512 devices in a mesh: dp: 4 (over y), seq: 8 (over x, core), vocab: 16 (over z).
Axes of the slice: x: 4, y: 4, z: 16, core: 2. Of those that a mesh axis runs over, the one named last changes fastest.
Arguments:
- teacher_logits: bfloat16 [8, 512, 75776], P('dp', 'seq', 'vocab'), may hold values from -50 to 220
- student_logits: bfloat16 [8, 512, 65536], P('dp', 'seq', 'vocab'), may hold values from -50 to 220
- alignment: int32 [8, 512], P('dp', 'seq'), may hold values from 0 to 511, as said below
- src_block: int32 [512, 2], replicated, may hold values from 0 to 591, as said below
- margin_weight: bfloat16 [512, 2, 128, 128], P('vocab', None, 'dp'), may hold values from 0.0019989014 to 0.029907227
Outputs:
- divergence: float32 [8, 512], P('dp', 'seq')
The draws below stay inside these ranges and needn't reach their ends.
Inputs may be any that keep to these rules, and one draw needn't show every extreme that they name: alignment[d, j] differs from j by at most 16; every document has a position aligned exactly 16 ahead and one exactly 16 behind. `src_block`: the student blocks of one vocab index name teacher blocks of any one vocab index at most 8 times in all, and this bound is reached in every draw; every teacher block is named; the 2 blocks of a student block differ.
All inputs are finite; a program needn't handle non-finite values.
Results may differ from the reference program's by a relative error of at most 0.0003.
Values may be sent and summed in bfloat16 or wider, within the bound.
No kernel may reach another device: no remote copies, remote signals or barrier semaphores. Data moves between devices by JAX's collectives and lax.ppermute only.
A program may use at most 64 MiB of HBM per device.

```python
import math
import jax
import jax.numpy as jnp
from jax import lax

BLK = 128
VTB_DEV = 37
VSB_DEV = 32
K = 2
L = 512
W = 16
DOCS = 8
VTB = 592
VSB = 512
VT = 75776
VS = 65536


def shaped_logits(key, base, spike_share):
    doc_total, length, columns = base.shape
    keys = jax.random.split(key, 7)
    row_scale = jnp.exp(jax.random.uniform(keys[0], (doc_total, length, 1), minval=math.log(0.7), maxval=math.log(2.2)))
    col_scale = jnp.exp(jax.random.uniform(keys[1], (1, 1, columns), minval=math.log(0.7), maxval=math.log(2.2)))
    values = 2.0 * base * row_scale * col_scale
    chosen = jax.random.uniform(keys[2], (doc_total, length, 1)) < spike_share
    summit = 120.0 + 100.0 * jax.random.uniform(keys[3], (doc_total, length, 1))
    spacing = 1.0 + 2.0 * jax.random.uniform(keys[4], (doc_total, length, 1))
    first_col = jax.random.randint(keys[5], (doc_total, length, 1), 0, columns)
    second_col = (first_col + 1 + jax.random.randint(keys[6], (doc_total, length, 1), 0, columns - 1)) % columns
    column_ids = jnp.arange(columns)[None, None, :]
    values = jnp.where(chosen & (column_ids == first_col), summit, values)
    values = jnp.where(chosen & (column_ids == second_col), summit - spacing, values)
    return values.astype(jnp.float32)


def draw_teacher_logits(key, part):
    key = jax.random.fold_in(key, 11)
    base_key, shape_key = jax.random.split(key)
    base = jnp.clip(jax.random.normal(base_key, (DOCS, L, VT)), -5.0, 5.0)
    return shaped_logits(shape_key, base, 0.0).astype(jnp.bfloat16)


def draw_student_logits(key, part):
    key = jax.random.fold_in(key, 12)
    base_key, shape_key = jax.random.split(key)
    base = jnp.clip(jax.random.normal(base_key, (DOCS, L, VS)), -5.0, 5.0)
    return shaped_logits(shape_key, base, 0.0).astype(jnp.bfloat16)


def draw_alignment(key, part):
    key = jax.random.fold_in(key, 31)
    offsets = jax.random.randint(key, (DOCS, L), -W, W + 1)
    positions = jnp.arange(L)[None, :]
    aligned = jnp.clip(positions + offsets, 0, L - 1)
    middle = L // 2
    aligned = aligned.at[:, middle].set(middle + W)
    aligned = aligned.at[:, middle + 1].set(middle + 1 - W)
    return aligned.astype(jnp.int32)


def draw_src_block(key, part):
    key = jax.random.fold_in(key, 41)
    k_extra, k_order, k_shift, k_start, k_place = jax.random.split(key, 5)
    vocab_count = VSB // VSB_DEV
    pair_count = K * VSB_DEV
    mean_load = pair_count // vocab_count
    half_count = vocab_count // 2
    extra = jax.random.randint(k_extra, (half_count,), 0, mean_load + 1)
    extra = extra.at[0].set(mean_load)
    signed = jnp.concatenate([extra, -extra])
    signed = signed[jax.random.permutation(k_order, vocab_count)]
    twist = jax.random.permutation(k_shift, vocab_count)
    target = jnp.arange(vocab_count)
    loads = mean_load + signed[(twist[:, None] - target[None, :]) % vocab_count]
    upto = jnp.cumsum(loads, axis=0)
    position = jnp.arange(pair_count)
    holder = jnp.sum(position[None, :, None] >= upto.T[:, None, :], axis=2).astype(jnp.int32)
    before = (upto - loads).T
    within = position[None, :] - jnp.take_along_axis(before, holder, axis=1)
    sent_before = (jnp.cumsum(loads, axis=1) - loads).T
    start_block = jax.random.randint(k_start, (vocab_count,), 0, VTB_DEV)
    local_block = (start_block[holder] + jnp.take_along_axis(sent_before, holder, axis=1) + within) % VTB_DEV
    teacher_id = holder * VTB_DEV + local_block
    order = jax.vmap(lambda part_key: jax.random.permutation(part_key, pair_count))(jax.random.split(k_place, vocab_count))
    placed = jnp.take_along_axis(teacher_id, order, axis=1)
    return placed.reshape(VSB, K).astype(jnp.int32)


def shard_levels(key, extent, pieces, low, top_value):
    factor_of, own = 1.0, jax.random.fold_in(key, 6)
    for dim, parts in pieces:
        draws = jnp.exp(jax.random.uniform(jax.random.fold_in(own, dim), (parts,), jnp.float32, low / len(pieces), top_value / len(pieces)))
        factor_of = factor_of * jnp.repeat(draws, extent[dim] // parts).reshape([-1 if axis == dim else 1 for axis in range(len(extent))])
    return factor_of


def setup_inputs(seed: int = 0) -> dict:
    streams_of = jax.random.split(jax.random.key(seed), 6)
    return {
        "teacher_logits": draw_teacher_logits(jax.random.fold_in(streams_of[5], 71), 0),
        "student_logits": draw_student_logits(jax.random.fold_in(streams_of[5], 71), 0),
        "alignment": draw_alignment(jax.random.fold_in(streams_of[5], 71), 0),
        "src_block": draw_src_block(jax.random.fold_in(streams_of[5], 71), 0),
        "margin_weight": jnp.clip(jnp.exp(math.log(0.029907227) - 2.7055024 * jax.random.uniform(streams_of[4], (VSB, K, BLK, BLK), jnp.float32) ** shard_levels(streams_of[4], (VSB, K, BLK, BLK), ((0, 16), (2, 4)), -0.2, 0.2)), 0.0019989014, 0.029907227).astype(jnp.bfloat16),
    }


def reference(teacher_logits, student_logits, alignment, src_block, margin_weight):
    weight_full = margin_weight.astype(jnp.float32)
    block_list = src_block.reshape(-1).astype(jnp.int32)

    def one_document(inputs):
        teacher_doc, student_doc, align_doc = inputs
        aligned = jnp.take(teacher_doc, align_doc.astype(jnp.int32), axis=0)
        teacher_float = aligned.astype(jnp.float32)
        teacher_peak = jnp.max(teacher_float, axis=1, keepdims=True)
        teacher_exp = jnp.exp(teacher_float - teacher_peak)
        teacher_prob = (teacher_exp / jnp.sum(teacher_exp, axis=1, keepdims=True)).astype(jnp.bfloat16)
        student_float = student_doc.astype(jnp.float32)
        student_peak = jnp.max(student_float, axis=1, keepdims=True)
        shifted = student_float - student_peak
        student_logprob = shifted - jnp.log(jnp.sum(jnp.exp(shifted), axis=1, keepdims=True))
        blocks = teacher_prob.reshape(L, VTB, BLK)
        picked = jnp.take(blocks, block_list, axis=1).reshape(L, VSB, K, BLK)
        mapped = jnp.einsum("jbkc,bkcd->jbd", picked.astype(jnp.float32), weight_full).reshape(L, VSB * BLK)
        total_mass = jnp.sum(mapped, axis=1, keepdims=True)
        normed = mapped / total_mass
        terms = jax.scipy.special.xlogy(normed, normed) - normed * student_logprob
        return jnp.sum(terms, axis=1)

    return lax.map(one_document, (teacher_logits, student_logits, alignment))
```

```python
import functools

import jax
import jax.numpy as jnp
from jax import lax
from jax.experimental import pallas as pl
from jax.experimental.pallas import tpu as pltpu
from jax.sharding import PartitionSpec as P

BLK = 128
K = 2
W = 16
ROWS = 104
PROFILE = (37, 37, 36, 31, 26, 20, 14, 6)
TINY = 1.2e-38


def halo(block, width):
    count = lax.axis_size("seq")
    forward = [(i, i + 1) for i in range(count - 1)]
    backward = [(target, source) for source, target in forward]
    low = lax.ppermute(block[:, block.shape[1] - width :], "seq", forward)
    high = lax.ppermute(block[:, :width], "seq", backward)
    return low, high


def ring_pairs(turn):
    seq_count, vocab_count = lax.axis_size("seq"), lax.axis_size("vocab")
    pairs = []
    for s in range(seq_count):
        step = turn if s % 2 == 0 else -turn
        for v in range(vocab_count):
            pairs.append((s * vocab_count + v, s * vocab_count + (v + step) % vocab_count))
    return pairs


def ways(distance, block, vocab_count):
    half = vocab_count // 2
    even = block % 2 == 0
    ahead = jnp.where(((distance >= 1) & (distance < half)) | ((distance == half) & even), distance, 0)
    behind = jnp.where((distance > half) | ((distance == half) & ~even), vocab_count - distance, 0)
    return ahead, behind


def reaches(need, block, holder, sign, vocab_count):
    targets = jnp.arange(vocab_count)[:, None]
    distance = (sign * (targets - holder[None, :]) + vocab_count) % vocab_count
    ahead, behind = ways(distance, block[None, :], vocab_count)
    return jnp.max(jnp.where(need, ahead, 0), axis=0), jnp.max(jnp.where(need, behind, 0), axis=0)


def ranks(reach):
    size = reach.shape[-1]
    key = reach * size - jnp.arange(size)
    return jnp.sum((key[..., None, :] > key[..., :, None]).astype(jnp.int32), axis=-1)


def pack_kernel(order_ref, own_ref, low_ref, high_ref, pick_ref, ahead_ref, behind_ref, home_ref, cand_ref, logit_ref):
    docs, positions, columns = own_ref.shape
    width = low_ref.shape[1]
    span = positions + 2 * width
    rows = pick_ref.shape[0]
    blocks = columns // BLK
    for doc in range(docs):
        cand_ref[doc * span : doc * span + width, :] = low_ref[doc]
        cand_ref[doc * span + width : doc * span + width + positions, :] = own_ref[doc]
        cand_ref[doc * span + width + positions : (doc + 1) * span, :] = high_ref[doc]
    pick = pick_ref[...]
    peak = jnp.full((rows, BLK), -jnp.inf, jnp.float32)
    for t in range(blocks):
        part = jnp.dot(pick, cand_ref[:, t * BLK : (t + 1) * BLK], preferred_element_type=jnp.float32)
        logit_ref[t] = part.astype(jnp.bfloat16)
        peak = jnp.maximum(peak, part)
    top = jnp.max(peak, axis=1, keepdims=True)
    total = jnp.zeros((rows, BLK), jnp.float32)
    for t in range(blocks):
        power = jnp.exp(logit_ref[t].astype(jnp.float32) - top)
        total = total + power
        home_ref[1 + t] = power.astype(jnp.bfloat16)
    total = jnp.sum(total, axis=1, keepdims=True)
    first = total.astype(jnp.bfloat16).astype(jnp.float32)
    second = (total - first).astype(jnp.bfloat16).astype(jnp.float32)
    third = total - first - second
    lane = lax.broadcasted_iota(jnp.int32, (rows, BLK), 1)
    stats = jnp.where(
        lane == 0, top, jnp.where(lane == 1, first, jnp.where(lane == 2, second, jnp.where(lane == 3, third, 0.0)))
    ).astype(jnp.bfloat16)
    home_ref[0] = stats
    ahead_ref[0] = stats
    behind_ref[0] = stats
    for i in range(ahead_ref.shape[0] - 1):
        ahead_ref[1 + i] = home_ref[1 + order_ref[0, i]]
        behind_ref[1 + i] = home_ref[1 + order_ref[1, i]]


def student_kernel(student_ref, top_ref, total_ref):
    docs, positions, columns = student_ref.shape
    rows = docs * positions
    peak = jnp.full((rows, BLK), -jnp.inf, jnp.float32)
    for b in range(columns // BLK):
        part = student_ref[:, :, b * BLK : (b + 1) * BLK].reshape(rows, BLK).astype(jnp.float32)
        peak = jnp.maximum(peak, part)
    top = jnp.max(peak, axis=1, keepdims=True)
    total = jnp.zeros((rows, BLK), jnp.float32)
    for b in range(columns // BLK):
        part = student_ref[:, :, b * BLK : (b + 1) * BLK].reshape(rows, BLK).astype(jnp.float32)
        total = total + jnp.exp(part - top)
    top_ref[...] = jnp.broadcast_to(top, (rows, BLK))
    total_ref[...] = jnp.broadcast_to(jnp.sum(total, axis=1, keepdims=True), (rows, BLK))


def map_kernel(steps, plan_ref, count_ref, *refs):
    sources = refs[: 2 * steps + 1]
    spread_ref, weight_ref, student_ref, top_ref, total_ref, out_ref, stage_ref, scale_ref = refs[2 * steps + 1 :]
    docs, positions, columns = student_ref.shape
    rows = docs * positions
    blocks = columns // BLK
    spread = spread_ref[...]
    for s, source in enumerate(sources):

        def bring(j, carry, s=s, source=source):
            pair = plan_ref[2, s * 8 + j]
            stage_ref[pair] = source[1 + plan_ref[0, pair]]
            return carry

        lax.fori_loop(0, count_ref[s], bring, 0)
    peaks, sums = [], []
    for source in sources:
        stats = jnp.dot(spread, source[0], preferred_element_type=jnp.float32)
        peaks.append(stats[:, 0:1])
        sums.append(stats[:, 1:2] + stats[:, 2:3] + stats[:, 3:4])
    peak = functools.reduce(jnp.maximum, peaks)
    powers = [jnp.exp(p - peak) for p in peaks]
    norm = sum(p * t for p, t in zip(powers[: 2 * steps], sums[: 2 * steps]))
    for s in range(len(sources)):
        scale_ref[s] = jnp.broadcast_to(powers[s] / norm, (rows, BLK))
    student_top = top_ref[...]
    mass = jnp.zeros((rows, BLK), jnp.float32)
    cross = jnp.zeros((rows, BLK), jnp.float32)
    for b in range(blocks):
        picked = jnp.concatenate([stage_ref[K * b], stage_ref[K * b + 1]], axis=1)
        prob = jnp.dot(spread, picked, preferred_element_type=jnp.float32).astype(jnp.bfloat16)
        mapped = scale_ref[plan_ref[1, K * b]] * jnp.dot(
            prob[:, :BLK], weight_ref[K * b], preferred_element_type=jnp.float32
        ) + scale_ref[plan_ref[1, K * b + 1]] * jnp.dot(
            prob[:, BLK:], weight_ref[K * b + 1], preferred_element_type=jnp.float32
        )
        logit = student_ref[:, :, b * BLK : (b + 1) * BLK].reshape(rows, BLK).astype(jnp.float32) - student_top
        mass = mass + mapped
        cross = cross + mapped * (jnp.log(jnp.maximum(mapped, TINY)) - logit)
    mass = jnp.sum(mass, axis=1, keepdims=True)
    cross = jnp.sum(cross, axis=1, keepdims=True)
    lane = lax.broadcasted_iota(jnp.int32, (rows, BLK), 1)
    table = jnp.where(
        lane == 0, mass, jnp.where(lane == 1, cross, jnp.where(lane == 2, student_top, total_ref[...]))
    )
    out_ref[...] = table.T[:8]


def whole(padded_parts, cand, src_block, weights, student_logits):
    doc_count, pos_count, student_cols = student_logits.shape
    teacher_cols = padded_parts[0].shape[2]
    teacher_blocks = teacher_cols // BLK
    student_blocks = student_cols // BLK
    row_count = doc_count * pos_count
    padded = jnp.concatenate(padded_parts, axis=1).reshape(-1, teacher_cols)
    teacher_float = jnp.take(padded, cand, axis=0).astype(jnp.float32)
    student_float = student_logits.reshape(row_count, student_cols).astype(jnp.float32)
    teacher_peak = jnp.max(teacher_float, axis=1)
    student_peak = jnp.max(student_float, axis=1)
    teacher_top, student_top = lax.pmax((teacher_peak, student_peak), "vocab")
    teacher_total, student_total = lax.psum(
        (
            jnp.sum(jnp.exp(teacher_float - teacher_top[:, None]), axis=1),
            jnp.sum(jnp.exp(student_float - student_top[:, None]), axis=1),
        ),
        "vocab",
    )
    teacher_prob = (jnp.exp(teacher_float - teacher_top[:, None]) / teacher_total[:, None]).astype(jnp.bfloat16)
    student_logprob = student_float - student_top[:, None] - jnp.log(student_total)[:, None]
    vocab_count = lax.axis_size("vocab")
    own_index = lax.axis_index("vocab")
    pair_count = student_blocks * K
    capacity = 2 * K * student_blocks // vocab_count
    pair_blocks = src_block.reshape(vocab_count, pair_count)
    holder = pair_blocks // teacher_blocks
    inside = pair_blocks % teacher_blocks
    same_holder = holder[:, :, None] == holder[:, None, :]
    before = jnp.arange(pair_count)[None, :] < jnp.arange(pair_count)[:, None]
    slot_rank = jnp.sum(same_holder & before[None, :, :], axis=2)
    chosen = (holder == own_index)[:, None, :] & (
        slot_rank[:, None, :] == jnp.arange(capacity)[None, :, None]
    )
    send_index = jnp.sum(jnp.where(chosen, inside[:, None, :], 0), axis=2)
    prob_blocks = teacher_prob.reshape(row_count, teacher_blocks, BLK)
    outgoing = jnp.take(prob_blocks, send_index.reshape(-1), axis=1).reshape(row_count, vocab_count, capacity, BLK)
    incoming = lax.all_to_all(outgoing, "vocab", split_axis=1, concat_axis=1, tiled=True)
    own_holder = jnp.take(holder, own_index, axis=0)
    own_rank = jnp.take(slot_rank, own_index, axis=0)
    recv_slot = own_holder * capacity + own_rank
    gathered = jnp.take(incoming.reshape(row_count, vocab_count * capacity, BLK), recv_slot, axis=1).reshape(
        row_count, student_blocks, K, BLK
    )
    mapped = jnp.einsum("rbkc,bkcd->rbd", gathered, weights, preferred_element_type=jnp.float32).reshape(
        row_count, student_cols
    )
    total_mass = lax.psum(jnp.sum(mapped, axis=1), "vocab")
    normed = mapped / total_mass[:, None]
    return lax.psum(
        jnp.sum(jax.scipy.special.xlogy(normed, normed) - normed * student_logprob, axis=1), "vocab"
    )


def shards(teacher_logits, student_logits, alignment, src_block, margin_weight):
    doc_count, pos_count, teacher_cols = teacher_logits.shape
    student_cols = student_logits.shape[2]
    teacher_blocks = teacher_cols // BLK
    student_blocks = student_cols // BLK
    row_count = doc_count * pos_count
    pair_count = student_blocks * K
    vocab_count = lax.axis_size("vocab")
    steps = vocab_count // 2
    sizes = tuple(min(size, teacher_blocks) for size in PROFILE)
    vocab_index = lax.axis_index("vocab")
    seq_index = lax.axis_index("seq")
    sign = 1 - 2 * (seq_index % 2)
    span = pos_count + 2 * W

    with jax.named_scope("halo"):
        low, high = halo(teacher_logits, W)
    with jax.named_scope("weights"):
        weights = lax.all_gather(margin_weight, "dp", axis=2, tiled=True)

    with jax.named_scope("rows"):
        cand = (alignment - seq_index * pos_count + W + jnp.arange(doc_count)[:, None] * span).reshape(-1)
        cand = jnp.clip(cand, 0, doc_count * span - 1)
        places = jnp.arange(doc_count * span)
        used = jnp.any(cand[:, None] == places[None, :], axis=0)
        place_rank = jnp.sum(used[:, None] & (places[:, None] < places[None, :]), axis=0)
        cand_rank = jnp.sum(used[None, :] & (places[None, :] < cand[:, None]), axis=1)
        row_ids = jnp.arange(ROWS)
        pick = ((row_ids[:, None] == place_rank[None, :]) & used[None, :]).astype(jnp.bfloat16)
        spread = (cand_rank[:, None] == row_ids[None, :]).astype(jnp.bfloat16)
        rows_fit = jnp.sum(used.astype(jnp.int32)) <= ROWS

    with jax.named_scope("send_order"):
        listed = src_block.reshape(vocab_count, pair_count)
        inner = jnp.arange(teacher_blocks)
        own_blocks = vocab_index * teacher_blocks + inner
        own_need = jnp.any(listed[:, :, None] == own_blocks[None, None, :], axis=1)
        own_reach = jnp.stack(
            reaches(own_need, own_blocks, jnp.full((teacher_blocks,), vocab_index), sign, vocab_count)
        )
        own_rank = ranks(own_reach)
        order = jnp.sum(
            jnp.where(own_rank[:, None, :] == inner[None, :, None], inner[None, None, :], 0), axis=2
        ).astype(jnp.int32)

    vmem = pl.BlockSpec(memory_space=pltpu.VMEM)
    smem = pl.BlockSpec(memory_space=pltpu.SMEM)
    big = pltpu.CompilerParams(vmem_limit_bytes=44 * 1024 * 1024)
    buffer = jax.ShapeDtypeStruct((1 + sizes[0], ROWS, BLK), jnp.bfloat16)
    with jax.named_scope("pack"):
        ahead, behind, home = pl.pallas_call(
            pack_kernel,
            out_shape=(buffer, buffer, jax.ShapeDtypeStruct((1 + teacher_blocks, ROWS, BLK), jnp.bfloat16)),
            in_specs=[smem] + [vmem] * 4,
            out_specs=(vmem,) * 3,
            scratch_shapes=[
                pltpu.VMEM((doc_count * span, teacher_cols), jnp.bfloat16),
                pltpu.VMEM((teacher_blocks, ROWS, BLK), jnp.bfloat16),
            ],
            compiler_params=big,
        )(order, teacher_logits, low, high, pick)

    with jax.named_scope("ring"):
        forward, backward = ring_pairs(1), ring_pairs(-1)
        came_ahead, came_behind = [], []
        for size in sizes:
            ahead = lax.ppermute(ahead[: 1 + size], ("seq", "vocab"), forward)
            behind = lax.ppermute(behind[: 1 + size], ("seq", "vocab"), backward)
            came_ahead.append(ahead)
            came_behind.append(behind)

    with jax.named_scope("student"):
        top, total = pl.pallas_call(
            student_kernel,
            out_shape=(jax.ShapeDtypeStruct((row_count, BLK), jnp.float32),) * 2,
            in_specs=[vmem],
            out_specs=(vmem,) * 2,
            compiler_params=big,
        )(student_logits)

    with jax.named_scope("receive_plan"):
        blocks = jnp.arange(vocab_count * teacher_blocks)
        block_holder = blocks // teacher_blocks
        need = jnp.any(listed[:, :, None] == blocks[None, None, :], axis=1)
        reach = jnp.stack(reaches(need, blocks, block_holder, sign, vocab_count)).reshape(
            2, vocab_count, teacher_blocks
        )
        fits = jnp.all(
            jnp.stack([jnp.sum((reach >= k + 1).astype(jnp.int32), axis=2) <= size for k, size in enumerate(sizes)])
        )
        all_rank = ranks(reach).reshape(2, 1, -1)
        mine = lax.dynamic_index_in_dim(listed, vocab_index, 0, keepdims=False)
        at_block = mine[:, None] == blocks[None, :]
        rank_of = jnp.sum(jnp.where(at_block[None], all_rank, 0), axis=2)
        distance = (sign * (vocab_index - mine // teacher_blocks) + vocab_count) % vocab_count
        go_ahead, go_behind = ways(distance, mine, vocab_count)
        source = jnp.where(go_ahead > 0, go_ahead, jnp.where(go_behind > 0, steps + go_behind, 0))
        limits = jnp.array((teacher_blocks,) + sizes + sizes, jnp.int32)
        source_ids = jnp.arange(2 * steps + 1)
        at_source = source[:, None] == source_ids[None, :]
        limit = jnp.sum(jnp.where(at_source, limits[None, :], 0), axis=1)
        place = jnp.where(go_ahead > 0, rank_of[0], jnp.where(go_behind > 0, rank_of[1], mine % teacher_blocks))
        place = jnp.clip(place, 0, limit - 1)
        pairs = jnp.arange(pair_count)
        turn = jnp.sum((source[:, None] == source[None, :]) & (pairs[None, :] < pairs[:, None]), axis=1)
        slots = jnp.arange((2 * steps + 1) * 8)
        pair_list = jnp.sum(jnp.where((source * 8 + turn)[None, :] == slots[:, None], pairs[None, :], 0), axis=1)
        count = jnp.minimum(jnp.sum(at_source.astype(jnp.int32), axis=0), 8).astype(jnp.int32)
        pad = lambda values: jnp.pad(values, (0, 256 - values.shape[0]))
        plan = jnp.stack([pad(place), pad(source), pad(pair_list)]).astype(jnp.int32)

    with jax.named_scope("map"):
        held = pl.pallas_call(
            functools.partial(map_kernel, steps),
            out_shape=jax.ShapeDtypeStruct((8, row_count), jnp.float32),
            in_specs=[smem] * 2 + [vmem] * (2 * steps + 1 + 5),
            out_specs=vmem,
            scratch_shapes=[
                pltpu.VMEM((pair_count, ROWS, BLK), jnp.bfloat16),
                pltpu.VMEM((2 * steps + 1, row_count, BLK), jnp.float32),
            ],
            compiler_params=big,
        )(
            plan,
            count,
            home,
            *came_ahead,
            *came_behind,
            spread,
            weights.reshape(pair_count, BLK, BLK),
            student_logits,
            top,
            total,
        )

    with jax.named_scope("finish"):
        sent = jnp.broadcast_to(held[None, :4], (vocab_count, 4, row_count))
        parts = lax.all_to_all(sent, "vocab", split_axis=0, concat_axis=0, tiled=True)
        mass_part, cross_part, top_part, total_part = (parts[:, i] for i in range(4))
        student_top = jnp.max(top_part, axis=0)
        log_total = student_top + jnp.log(jnp.sum(jnp.exp(top_part - student_top) * total_part, axis=0))
        mass = jnp.sum(mass_part, axis=0)
        result = jnp.sum(cross_part + mass_part * (log_total - top_part), axis=0) / mass - jnp.log(mass)

    result = lax.cond(
        rows_fit & fits,
        lambda *_: result,
        lambda *operands: whole(operands[:3], *operands[3:]),
        low,
        teacher_logits,
        high,
        cand,
        src_block,
        weights,
        student_logits,
    )
    return result.reshape(doc_count, pos_count)


def solution(mesh):
    in_specs = (
        P("dp", "seq", "vocab"),
        P("dp", "seq", "vocab"),
        P("dp", "seq"),
        P(),
        P("vocab", None, "dp", None),
    )
    out_specs = P("dp", "seq")
    return jax.shard_map(shards, mesh=mesh, in_specs=in_specs, out_specs=out_specs, check_vma=False)
```

```python
import functools

import jax
import jax.numpy as jnp
from jax import lax
from jax.experimental import pallas as pl
from jax.experimental.pallas import tpu as pltpu
from jax.sharding import PartitionSpec as P

BLK = 128
K = 2
W = 16
ROWS = 104
SLOTS = 21
TINY = 1.2e-38


def halo(block, width):
    count = lax.axis_size("seq")
    forward = [(i, i + 1) for i in range(count - 1)]
    backward = [(target, source) for source, target in forward]
    low = lax.ppermute(block[:, block.shape[1] - width :], "seq", forward)
    high = lax.ppermute(block[:, :width], "seq", backward)
    return low, high


def ring_pairs(turn):
    seq_count, vocab_count = lax.axis_size("seq"), lax.axis_size("vocab")
    pairs = []
    for s in range(seq_count):
        step = turn if s % 2 == 0 else -turn
        for v in range(vocab_count):
            pairs.append((s * vocab_count + v, s * vocab_count + (v + step) % vocab_count))
    return pairs


def ways(distance, block, vocab_count):
    half = vocab_count // 2
    even = block % 2 == 0
    ahead = jnp.where((distance >= 1) & ((distance < half) | ((distance == half) & even)), distance, 0)
    behind = jnp.where((distance > half) | ((distance == half) & ~even), vocab_count - distance, 0)
    return ahead, behind


def ones(mask):
    return jnp.where(mask, 1.0, 0.0).astype(jnp.bfloat16)


def plan_kernel(blocks, place_ref, holder_ref, holders_ref, inners_ref, send_ref, item_ref, fit_ref, book_ref):
    vocab_count, pair_count = holder_ref.shape
    half = vocab_count // 2
    steps = half
    home = blocks + 1
    me, sign = place_ref[0], place_ref[1]
    f32, i32 = jnp.float32, jnp.int32
    shape = (vocab_count, BLK)
    lane = lax.broadcasted_iota(i32, shape, 1)
    row = lax.broadcasted_iota(i32, shape, 0)

    reach = [jnp.zeros(shape, i32), jnp.zeros(shape, i32)]
    pair_lane = lax.broadcasted_iota(i32, (pair_count, BLK), 1)
    pair_row = lax.broadcasted_iota(i32, (vocab_count, pair_count), 0)
    for s in range(vocab_count):
        hits = jnp.dot(
            ones(pair_row == holder_ref[s : s + 1, :]),
            ones(pair_lane == inners_ref[:, s : s + 1]),
            preferred_element_type=f32,
        )
        distance = s - row
        distance = jnp.where(distance < 0, distance + vocab_count, distance)
        for way, length in enumerate(ways(distance, lane, vocab_count)):
            reach[way] = jnp.maximum(reach[way], jnp.where(hits > 0, length, 0))
    reach = [jnp.where(lane == blocks, half - way, reach[way]) for way in range(2)]

    square = (BLK, BLK)
    up, across = lax.broadcasted_iota(i32, square, 0), lax.broadcasted_iota(i32, square, 1)
    earlier = ones(up < across)
    left_up, left_across = (up & 7) + 1 - (up >> 3), (across & 7) + 1 - (across >> 3)
    goes_first = ones(
        (left_up > left_across) | ((left_up == left_across) & ((up >> 3) > (across >> 3)))
    )
    index, waiting, moved = [], [], [jnp.zeros(shape, f32)] * 2
    for way in range(2):
        masks = jnp.concatenate([ones(reach[way] == r) for r in range(1, half + 1)], axis=0)
        before = jnp.dot(masks, earlier, preferred_element_type=f32)
        place = jnp.zeros(shape, f32)
        count = jnp.zeros(shape, f32)
        for r in range(1, half + 1):
            same = reach[way] == r
            place = jnp.where(same, before[(r - 1) * vocab_count : r * vocab_count], place)
            total = jnp.sum(jnp.where(same, 1.0, 0.0), axis=1, keepdims=True)
            count = jnp.where(lane == r - 1, total, count)
        index.append(place)
        waiting.append(count)
    travels = (lane >= 8) & (lane < 8 * half) & ((lane & 7) + 1 > (lane >> 3))
    for f in range(steps):
        ahead_of = jnp.dot(
            jnp.concatenate(waiting, axis=0).astype(jnp.bfloat16), goes_first, preferred_element_type=f32
        )
        for way in range(2):
            first = ahead_of[way * vocab_count : (way + 1) * vocab_count]
            go = jnp.clip(SLOTS - first, 0.0, waiting[way])
            book_ref[(f * 2 + way) * 3] = moved[way]
            moved[way] = moved[way] + go
            book_ref[(f * 2 + way) * 3 + 1] = moved[way]
            book_ref[(f * 2 + way) * 3 + 2] = jnp.minimum(first, float(SLOTS))
            come = pltpu.roll(pltpu.roll(go, 8, 1), 1 if way == 0 else vocab_count - 1, 0)
            waiting[way] = waiting[way] - go + jnp.where(travels, come, 0.0)
    left = jnp.sum(waiting[0] + waiting[1], axis=1, keepdims=True)
    left = jnp.sum(jnp.broadcast_to(left, shape), axis=0, keepdims=True)
    fit_ref[...] = jnp.broadcast_to(left, fit_ref.shape).astype(i32)

    small = (vocab_count, vocab_count)
    target = lax.broadcasted_iota(i32, (BLK, 2 * BLK), 1).astype(f32)
    pointer, sends = [], []
    for way in range(2):
        step = 1 if way == 0 else -1
        back = me - step * lax.broadcasted_iota(i32, small, 0)
        back = jnp.where(back < 0, back + vocab_count, jnp.where(back >= vocab_count, back - vocab_count, back))
        pick = ones(back == lax.broadcasted_iota(i32, small, 1))
        far = jnp.dot(pick, reach[way].astype(f32).astype(jnp.bfloat16), preferred_element_type=f32).astype(i32)
        order = jnp.dot(pick, index[way].astype(jnp.bfloat16), preferred_element_type=f32)
        giver = me - step
        giver = jnp.where(giver < 0, giver + vocab_count, jnp.where(giver >= vocab_count, giver - vocab_count, giver))

        def slot(at, hops, valid):
            column = jnp.clip(hops * 8 + far - 1, 0, BLK - 1)
            where = jnp.full(shape, -1.0, f32)
            for f in range(steps):
                start, end, first = (
                    jnp.take_along_axis(
                        jnp.broadcast_to(book_ref[(f * 2 + way) * 3 + kind, pl.ds(at, 1), :], shape),
                        column,
                        axis=1,
                        mode="promise_in_bounds",
                    )
                    for kind in range(3)
                )
                now = valid & (start <= order) & (order < end)
                where = jnp.where(now, f * SLOTS + first + order - start, where)
            return where

        leave = slot(me, row, (far > row) & (row < half))
        arrive = slot(giver, row - 1, (far >= row) & (row >= 1) & (row <= half))
        point = jnp.where(row == 0, lane.astype(f32), jnp.maximum(home + arrive, 0.0))
        pointer.append(point)
        leave_turned = jnp.concatenate([leave, jnp.full((BLK - vocab_count, BLK), -1.0, f32)], axis=0).T
        chosen = jnp.zeros((1, 2 * BLK), f32)
        for h in range(half):
            chosen = chosen + jnp.dot(
                point[h : h + 1].astype(jnp.bfloat16),
                ones(leave_turned[:, h : h + 1] == target),
                preferred_element_type=f32,
            )
        sends.append(chosen.astype(i32))
    straight = sign > 0
    send_ref[0:1, :] = jnp.where(straight, sends[0], sends[1])
    send_ref[1:2, :] = jnp.where(straight, sends[1], sends[0])
    send_ref[2:8, :] = jnp.zeros((6, 2 * BLK), i32)

    mine_lane = lax.broadcasted_iota(i32, (pair_count, vocab_count), 1)
    holder = jnp.sum(jnp.where(mine_lane == me, holders_ref[...], 0), axis=1, keepdims=True)
    inner = jnp.sum(jnp.where(mine_lane == me, inners_ref[...], 0), axis=1, keepdims=True)
    distance = me - holder
    distance = jnp.where(distance < 0, distance + vocab_count, distance)
    hops = ways(distance, inner, vocab_count)
    scale = jnp.where(distance <= half, distance, 2 * vocab_count - distance)
    points = jnp.zeros((pair_count, 1), f32)
    for way in range(2):
        found = lax.dot_general(
            ones(pair_lane == inner),
            pointer[way].astype(jnp.bfloat16),
            (((1,), (1,)), ((), ())),
            preferred_element_type=f32,
        )
        points = points + jnp.sum(
            jnp.where((mine_lane == hops[way]) & (hops[way] > 0), found, 0.0), axis=1, keepdims=True
        )
    points = jnp.where(distance == 0, inner.astype(f32), points)
    by_stats = [jnp.sum(jnp.where(lane == blocks, p, 0.0), axis=1, keepdims=True) for p in pointer]
    hop = lax.broadcasted_iota(i32, (vocab_count, 1), 0)
    stat_ok = [hop <= half, (hop >= 1) & (hop < half)]
    points = jnp.concatenate(
        [points] + [jnp.where(ok, p, 0.0) for ok, p in zip(stat_ok, by_stats)], axis=0
    ).astype(i32)
    other = jnp.concatenate(
        [(hops[1] > 0).astype(i32), jnp.zeros((vocab_count, 1), i32), jnp.ones((vocab_count, 1), i32)], axis=0
    )
    other = jnp.where(straight, other, 1 - other)
    scale = jnp.concatenate([scale, jnp.zeros((2 * vocab_count, 1), i32)], axis=0)
    frame = jnp.zeros(points.shape, i32)
    for f in range(1, steps):
        frame = frame + (points >= home + f * SLOTS).astype(i32)
    away = points >= home
    source = jnp.where(away, 1 + frame + steps * other, 0)
    spot = jnp.where(away, points - home - frame * SLOTS, points)
    spot = jnp.clip(spot, 0, jnp.where(away, SLOTS - 1, home - 1))
    items = points.shape[0]
    item_lane = lax.broadcasted_iota(i32, (items, BLK), 1)
    table = jnp.where(
        item_lane == 0, spot, jnp.where(item_lane == 1, scale, jnp.where(item_lane == 2, source, 0))
    ).astype(f32)
    turned = jnp.concatenate([table, jnp.zeros((BLK - items, BLK), f32)], axis=0).T
    source_row = turned[2:3].astype(i32)
    item_up = lax.broadcasted_iota(i32, (items, BLK), 0)
    is_item = item_lane < items
    sooner = is_item & ((source_row < source) | ((source_row == source) & (item_lane < item_up)))
    rank = jnp.sum(sooner.astype(i32), axis=1, keepdims=True)
    item_ref[0:1, :] = turned[0:1].astype(i32)
    item_ref[1:2, :] = turned[1:2].astype(i32)
    item_ref[2:3, :] = jnp.sum(jnp.where(rank == item_lane, item_up, 0), axis=0, keepdims=True)
    item_ref[3:4, :] = jnp.sum((source < item_lane).astype(i32), axis=0, keepdims=True)
    item_ref[4:8, :] = jnp.zeros((4, BLK), i32)


def pack_kernel(send_ref, own_ref, low_ref, high_ref, pick_ref, home_ref, first_ref, second_ref, cand_ref, logit_ref):
    docs, positions, columns = own_ref.shape
    width = low_ref.shape[1]
    span = positions + 2 * width
    rows = pick_ref.shape[0]
    blocks = columns // BLK
    for doc in range(docs):
        cand_ref[doc * span : doc * span + width, :] = low_ref[doc]
        cand_ref[doc * span + width : doc * span + width + positions, :] = own_ref[doc]
        cand_ref[doc * span + width + positions : (doc + 1) * span, :] = high_ref[doc]
    pick = pick_ref[...]
    peak = jnp.full((rows, BLK), -jnp.inf, jnp.float32)
    for t in range(blocks):
        part = jnp.dot(pick, cand_ref[:, t * BLK : (t + 1) * BLK], preferred_element_type=jnp.float32)
        logit_ref[t] = part.astype(jnp.bfloat16)
        peak = jnp.maximum(peak, part)
    top = jnp.max(peak, axis=1, keepdims=True)
    total = jnp.zeros((rows, BLK), jnp.float32)
    for t in range(blocks):
        power = jnp.exp(logit_ref[t].astype(jnp.float32) - top)
        total = total + power
        home_ref[t] = power.astype(jnp.bfloat16)
    total = jnp.sum(total, axis=1, keepdims=True)
    first = total.astype(jnp.bfloat16).astype(jnp.float32)
    second = (total - first).astype(jnp.bfloat16).astype(jnp.float32)
    third = total - first - second
    lane = lax.broadcasted_iota(jnp.int32, (rows, BLK), 1)
    home_ref[blocks] = jnp.where(
        lane == 0, top, jnp.where(lane == 1, first, jnp.where(lane == 2, second, jnp.where(lane == 3, third, 0.0)))
    ).astype(jnp.bfloat16)
    for j in range(SLOTS):
        first_ref[j] = home_ref[send_ref[0, j]]
        second_ref[j] = home_ref[send_ref[1, j]]


def pass_kernel(chain, step, send_ref, home_ref, *refs):
    frames, out_ref = refs[:-1], refs[-1]
    home = home_ref.shape[0]

    def choose(j, carry):
        at = send_ref[chain, step * SLOTS + j]

        @pl.when(at < home)
        def _():
            out_ref[j] = home_ref[at]

        for f, frame in enumerate(frames):
            start = home + f * SLOTS

            @pl.when((at >= start) & (at < start + SLOTS))
            def _(frame=frame, start=start):
                out_ref[j] = frame[at - start]

        return carry

    lax.fori_loop(0, SLOTS, choose, 0)


def student_kernel(student_ref, top_ref, total_ref):
    docs, positions, columns = student_ref.shape
    rows = docs * positions
    peak = jnp.full((rows, BLK), -jnp.inf, jnp.float32)
    for b in range(columns // BLK):
        part = student_ref[:, :, b * BLK : (b + 1) * BLK].reshape(rows, BLK).astype(jnp.float32)
        peak = jnp.maximum(peak, part)
    top = jnp.max(peak, axis=1, keepdims=True)
    total = jnp.zeros((rows, BLK), jnp.float32)
    for b in range(columns // BLK):
        part = student_ref[:, :, b * BLK : (b + 1) * BLK].reshape(rows, BLK).astype(jnp.float32)
        total = total + jnp.exp(part - top)
    top_ref[...] = jnp.broadcast_to(top, (rows, BLK))
    total_ref[...] = jnp.broadcast_to(jnp.sum(total, axis=1, keepdims=True), (rows, BLK))


def map_kernel(steps, item_ref, *refs):
    sources = refs[: 2 * steps + 1]
    spread_ref, weight_ref, student_ref, top_ref, total_ref, out_ref, stage_ref, scale_ref = refs[2 * steps + 1 :]
    docs, positions, columns = student_ref.shape
    rows = docs * positions
    blocks = columns // BLK
    spread = spread_ref[...]
    for s, source in enumerate(sources):

        def bring(q, carry, source=source):
            item = item_ref[2, q]
            stage_ref[item] = source[item_ref[0, item]]
            return carry

        lax.fori_loop(item_ref[3, s], item_ref[3, s + 1], bring, 0)
    holders = [h for h in range(steps + 1)] + [2 * steps + h for h in range(1, steps)]
    peaks, sums = [], []
    for h in holders:
        stats = jnp.dot(spread, stage_ref[K * blocks + h], preferred_element_type=jnp.float32)
        peaks.append(stats[:, 0:1])
        sums.append(stats[:, 1:2] + stats[:, 2:3] + stats[:, 3:4])
    peak = functools.reduce(jnp.maximum, peaks)
    powers = [jnp.exp(p - peak) for p in peaks]
    norm = sum(p * t for p, t in zip(powers, sums))
    for h, power in zip(holders, powers):
        scale_ref[h] = jnp.broadcast_to(power / norm, (rows, BLK))
    student_top = top_ref[...]
    mass = jnp.zeros((rows, BLK), jnp.float32)
    cross = jnp.zeros((rows, BLK), jnp.float32)
    for b in range(blocks):
        picked = jnp.concatenate([stage_ref[K * b], stage_ref[K * b + 1]], axis=1)
        prob = jnp.dot(spread, picked, preferred_element_type=jnp.float32).astype(jnp.bfloat16)
        mapped = scale_ref[item_ref[1, K * b]] * jnp.dot(
            prob[:, :BLK], weight_ref[:, K * b].reshape(BLK, BLK), preferred_element_type=jnp.float32
        ) + scale_ref[item_ref[1, K * b + 1]] * jnp.dot(
            prob[:, BLK:], weight_ref[:, K * b + 1].reshape(BLK, BLK), preferred_element_type=jnp.float32
        )
        logit = student_ref[:, :, b * BLK : (b + 1) * BLK].reshape(rows, BLK).astype(jnp.float32) - student_top
        mass = mass + mapped
        cross = cross + mapped * (jnp.log(jnp.maximum(mapped, TINY)) - logit)
    mass = jnp.sum(mass, axis=1, keepdims=True)
    cross = jnp.sum(cross, axis=1, keepdims=True)
    lane = lax.broadcasted_iota(jnp.int32, (rows, BLK), 1)
    table = jnp.where(
        lane == 0, mass, jnp.where(lane == 1, cross, jnp.where(lane == 2, student_top, total_ref[...]))
    )
    out_ref[...] = table.T[:8]


def whole(padded_parts, cand, src_block, weights, student_logits):
    doc_count, pos_count, student_cols = student_logits.shape
    teacher_cols = padded_parts[0].shape[2]
    teacher_blocks = teacher_cols // BLK
    student_blocks = student_cols // BLK
    row_count = doc_count * pos_count
    padded = jnp.concatenate(padded_parts, axis=1).reshape(-1, teacher_cols)
    teacher_float = jnp.take(padded, cand, axis=0).astype(jnp.float32)
    student_float = student_logits.reshape(row_count, student_cols).astype(jnp.float32)
    teacher_peak = jnp.max(teacher_float, axis=1)
    student_peak = jnp.max(student_float, axis=1)
    teacher_top, student_top = lax.pmax((teacher_peak, student_peak), "vocab")
    teacher_total, student_total = lax.psum(
        (
            jnp.sum(jnp.exp(teacher_float - teacher_top[:, None]), axis=1),
            jnp.sum(jnp.exp(student_float - student_top[:, None]), axis=1),
        ),
        "vocab",
    )
    teacher_prob = (jnp.exp(teacher_float - teacher_top[:, None]) / teacher_total[:, None]).astype(jnp.bfloat16)
    student_logprob = student_float - student_top[:, None] - jnp.log(student_total)[:, None]
    vocab_count = lax.axis_size("vocab")
    own_index = lax.axis_index("vocab")
    pair_count = student_blocks * K
    capacity = 2 * K * student_blocks // vocab_count
    pair_blocks = src_block.reshape(vocab_count, pair_count)
    holder = pair_blocks // teacher_blocks
    inside = pair_blocks % teacher_blocks
    same_holder = holder[:, :, None] == holder[:, None, :]
    before = jnp.arange(pair_count)[None, :] < jnp.arange(pair_count)[:, None]
    slot_rank = jnp.sum(same_holder & before[None, :, :], axis=2)
    chosen = (holder == own_index)[:, None, :] & (
        slot_rank[:, None, :] == jnp.arange(capacity)[None, :, None]
    )
    send_index = jnp.sum(jnp.where(chosen, inside[:, None, :], 0), axis=2)
    prob_blocks = teacher_prob.reshape(row_count, teacher_blocks, BLK)
    outgoing = jnp.take(prob_blocks, send_index.reshape(-1), axis=1).reshape(row_count, vocab_count, capacity, BLK)
    incoming = lax.all_to_all(outgoing, "vocab", split_axis=1, concat_axis=1, tiled=True)
    own_holder = jnp.take(holder, own_index, axis=0)
    own_rank = jnp.take(slot_rank, own_index, axis=0)
    recv_slot = own_holder * capacity + own_rank
    gathered = jnp.take(incoming.reshape(row_count, vocab_count * capacity, BLK), recv_slot, axis=1).reshape(
        row_count, student_blocks, K, BLK
    )
    weights = weights.swapaxes(0, 1).reshape(student_blocks, K, BLK, BLK)
    mapped = jnp.einsum("rbkc,bkcd->rbd", gathered, weights, preferred_element_type=jnp.float32).reshape(
        row_count, student_cols
    )
    total_mass = lax.psum(jnp.sum(mapped, axis=1), "vocab")
    normed = mapped / total_mass[:, None]
    return lax.psum(
        jnp.sum(jax.scipy.special.xlogy(normed, normed) - normed * student_logprob, axis=1), "vocab"
    )


def shards(teacher_logits, student_logits, alignment, src_block, margin_weight):
    doc_count, pos_count, teacher_cols = teacher_logits.shape
    student_cols = student_logits.shape[2]
    teacher_blocks = teacher_cols // BLK
    student_blocks = student_cols // BLK
    row_count = doc_count * pos_count
    pair_count = student_blocks * K
    vocab_count = lax.axis_size("vocab")
    steps = vocab_count // 2
    home = teacher_blocks + 1
    vocab_index = lax.axis_index("vocab")
    seq_index = lax.axis_index("seq")
    sign = 1 - 2 * (seq_index % 2)
    span = pos_count + 2 * W

    with jax.named_scope("halo"):
        low, high = halo(teacher_logits, W)
    with jax.named_scope("weights"):
        weights = lax.all_gather(
            margin_weight.reshape(pair_count, -1, BLK), "dp", axis=0, tiled=False
        )

    with jax.named_scope("rows"):
        cand = (alignment - seq_index * pos_count + W + jnp.arange(doc_count)[:, None] * span).reshape(-1)
        cand = jnp.clip(cand, 0, doc_count * span - 1)
        places = jnp.arange(doc_count * span)
        used = jnp.any(cand[:, None] == places[None, :], axis=0)
        place_rank = jnp.sum(used[:, None] & (places[:, None] < places[None, :]), axis=0)
        cand_rank = jnp.sum(used[None, :] & (places[None, :] < cand[:, None]), axis=1)
        row_ids = jnp.arange(ROWS)
        pick = ((row_ids[:, None] == place_rank[None, :]) & used[None, :]).astype(jnp.bfloat16)
        spread = (cand_rank[:, None] == row_ids[None, :]).astype(jnp.bfloat16)
        rows_fit = jnp.sum(used.astype(jnp.int32)) <= ROWS

    vmem = pl.BlockSpec(memory_space=pltpu.VMEM)
    smem = pl.BlockSpec(memory_space=pltpu.SMEM)
    def room(mib):
        return pltpu.CompilerParams(vmem_limit_bytes=mib * 1024 * 1024)

    with jax.named_scope("plan"):
        listed = src_block.reshape(vocab_count, pair_count)
        holder, inner = listed // teacher_blocks, listed % teacher_blocks
        table = jax.ShapeDtypeStruct((8, BLK), jnp.int32)
        send, items, left = pl.pallas_call(
            functools.partial(plan_kernel, teacher_blocks),
            out_shape=(jax.ShapeDtypeStruct((8, 2 * BLK), jnp.int32), table, table),
            in_specs=[smem] + [vmem] * 3,
            out_specs=(vmem,) * 3,
            scratch_shapes=[pltpu.VMEM((6 * steps, vocab_count, BLK), jnp.float32)],
            compiler_params=room(16),
        )(jnp.stack([vocab_index, sign]).astype(jnp.int32), holder, holder.T, inner.T)

    def planes(count):
        return jax.ShapeDtypeStruct((count, ROWS, BLK), jnp.bfloat16)

    with jax.named_scope("pack"):
        own, ahead, behind = pl.pallas_call(
            pack_kernel,
            out_shape=(planes(home), planes(SLOTS), planes(SLOTS)),
            in_specs=[smem] + [vmem] * 4,
            out_specs=(vmem,) * 3,
            scratch_shapes=[
                pltpu.VMEM((doc_count * span, teacher_cols), jnp.bfloat16),
                pltpu.VMEM((teacher_blocks, ROWS, BLK), jnp.bfloat16),
            ],
            compiler_params=room(24),
        )(send, teacher_logits, low, high, pick)

    def chosen(chain, step, frames):
        return pl.pallas_call(
            functools.partial(pass_kernel, chain, step),
            out_shape=planes(SLOTS),
            in_specs=[smem] + [vmem] * (1 + len(frames)),
            out_specs=vmem,
            compiler_params=room(16),
        )(send, own, *frames)

    with jax.named_scope("ring"):
        forward, backward = ring_pairs(1), ring_pairs(-1)
        came_ahead, came_behind = [], []
        for step in range(steps):
            if step:
                ahead = chosen(0, step, came_ahead)
            came_ahead.append(lax.ppermute(ahead, ("seq", "vocab"), forward))
            if step:
                behind = chosen(1, step, came_behind)
            came_behind.append(lax.ppermute(behind, ("seq", "vocab"), backward))

    with jax.named_scope("student"):
        top, total = pl.pallas_call(
            student_kernel,
            out_shape=(jax.ShapeDtypeStruct((row_count, BLK), jnp.float32),) * 2,
            in_specs=[vmem],
            out_specs=(vmem,) * 2,
            compiler_params=room(16),
        )(student_logits)

    with jax.named_scope("map"):
        held = pl.pallas_call(
            functools.partial(map_kernel, steps),
            out_shape=jax.ShapeDtypeStruct((8, row_count), jnp.float32),
            in_specs=[smem] + [vmem] * (2 * steps + 1 + 5),
            out_specs=vmem,
            scratch_shapes=[
                pltpu.VMEM((pair_count + 2 * vocab_count, ROWS, BLK), jnp.bfloat16),
                pltpu.VMEM((3 * steps, row_count, BLK), jnp.float32),
            ],
            compiler_params=room(32),
        )(items, own, *came_ahead, *came_behind, spread, weights, student_logits, top, total)

    with jax.named_scope("finish"):
        sent = jnp.broadcast_to(held[None, :4], (vocab_count, 4, row_count))
        parts = lax.all_to_all(sent, "vocab", split_axis=0, concat_axis=0, tiled=True)
        mass_part, cross_part, top_part, total_part = (parts[:, i] for i in range(4))
        student_top = jnp.max(top_part, axis=0)
        log_total = student_top + jnp.log(jnp.sum(jnp.exp(top_part - student_top) * total_part, axis=0))
        mass = jnp.sum(mass_part, axis=0)
        result = jnp.sum(cross_part + mass_part * (log_total - top_part), axis=0) / mass - jnp.log(mass)

    result = lax.cond(
        rows_fit & (left[0, 0] == 0),
        lambda *_: result,
        lambda *operands: whole(operands[:3], *operands[3:]),
        low,
        teacher_logits,
        high,
        cand,
        src_block,
        weights,
        student_logits,
    )
    return result.reshape(doc_count, pos_count)


def solution(mesh):
    in_specs = (
        P("dp", "seq", "vocab"),
        P("dp", "seq", "vocab"),
        P("dp", "seq"),
        P(),
        P("vocab", None, "dp", None),
    )
    out_specs = P("dp", "seq")
    return jax.shard_map(shards, mesh=mesh, in_specs=in_specs, out_specs=out_specs, check_vma=False)
```

```python
import functools

import jax
import jax.numpy as jnp
from jax import lax
from jax.experimental import pallas as pl
from jax.experimental.pallas import tpu as pltpu
from jax.sharding import PartitionSpec as P

BLK = 128
K = 2
W = 16
ROWS = 104
SLOTS = 21
TINY = 1.2e-38


def halo(block, width):
    count = lax.axis_size("seq")
    forward = [(i, i + 1) for i in range(count - 1)]
    backward = [(target, source) for source, target in forward]
    low = lax.ppermute(block[:, block.shape[1] - width :], "seq", forward)
    high = lax.ppermute(block[:, :width], "seq", backward)
    return low, high


def ring_pairs(turn):
    seq_count, vocab_count = lax.axis_size("seq"), lax.axis_size("vocab")
    pairs = []
    for s in range(seq_count):
        step = turn if s % 2 == 0 else -turn
        for v in range(vocab_count):
            pairs.append((s * vocab_count + v, s * vocab_count + (v + step) % vocab_count))
    return pairs


def ways(distance, block, vocab_count):
    half = vocab_count // 2
    even = block % 2 == 0
    ahead = jnp.where((distance >= 1) & ((distance < half) | ((distance == half) & even)), distance, 0)
    behind = jnp.where((distance > half) | ((distance == half) & ~even), vocab_count - distance, 0)
    return ahead, behind


def ones(mask):
    return jnp.where(mask, 1.0, 0.0).astype(jnp.bfloat16)


def plan_kernel(blocks, place_ref, listed_ref, send_ref, item_ref, fit_ref, book_ref):
    vocab_count, pair_count = listed_ref.shape
    half = vocab_count // 2
    steps = half
    home = blocks + 1
    me, sign = place_ref[0], place_ref[1]
    f32, i32 = jnp.float32, jnp.int32
    shape = (vocab_count, BLK)

    def split(listed):
        holder = sum((listed >= h * blocks).astype(i32) for h in range(1, vocab_count))
        return holder, listed - holder * blocks

    listed = listed_ref[...]
    wide = jnp.concatenate([listed, jnp.zeros((vocab_count, BLK - pair_count), i32)], axis=1)
    tall = jnp.concatenate([wide, jnp.zeros((BLK - vocab_count, BLK), i32)], axis=0).astype(f32).T.astype(i32)
    row_holder, _ = split(listed)
    holders, inners = split(tall[:pair_count])
    lane = lax.broadcasted_iota(i32, shape, 1)
    row = lax.broadcasted_iota(i32, shape, 0)

    reach = [jnp.zeros(shape, i32), jnp.zeros(shape, i32)]
    pair_lane = lax.broadcasted_iota(i32, (pair_count, BLK), 1)
    pair_row = lax.broadcasted_iota(i32, (vocab_count, pair_count), 0)
    for s in range(vocab_count):
        hits = jnp.dot(
            ones(pair_row == row_holder[s : s + 1, :]),
            ones(pair_lane == inners[:, s : s + 1]),
            preferred_element_type=f32,
        )
        distance = s - row
        distance = jnp.where(distance < 0, distance + vocab_count, distance)
        for way, length in enumerate(ways(distance, lane, vocab_count)):
            reach[way] = jnp.maximum(reach[way], jnp.where(hits > 0, length, 0))
    reach = [jnp.where(lane == blocks, half - way, reach[way]) for way in range(2)]

    square = (BLK, BLK)
    up, across = lax.broadcasted_iota(i32, square, 0), lax.broadcasted_iota(i32, square, 1)
    earlier = ones(up < across)
    left_up, left_across = (up & 7) + 1 - (up >> 3), (across & 7) + 1 - (across >> 3)
    goes_first = ones(
        (left_up > left_across) | ((left_up == left_across) & ((up >> 3) > (across >> 3)))
    )
    index, waiting, moved = [], [], [jnp.zeros(shape, f32)] * 2
    for way in range(2):
        masks = jnp.concatenate([ones(reach[way] == r) for r in range(1, half + 1)], axis=0)
        before = jnp.dot(masks, earlier, preferred_element_type=f32)
        place = jnp.zeros(shape, f32)
        count = jnp.zeros(shape, f32)
        for r in range(1, half + 1):
            same = reach[way] == r
            place = jnp.where(same, before[(r - 1) * vocab_count : r * vocab_count], place)
            total = jnp.sum(jnp.where(same, 1.0, 0.0), axis=1, keepdims=True)
            count = jnp.where(lane == r - 1, total, count)
        index.append(place)
        waiting.append(count)
    travels = (lane >= 8) & (lane < 8 * half) & ((lane & 7) + 1 > (lane >> 3))
    for f in range(steps):
        ahead_of = jnp.dot(
            jnp.concatenate(waiting, axis=0).astype(jnp.bfloat16), goes_first, preferred_element_type=f32
        )
        for way in range(2):
            first = ahead_of[way * vocab_count : (way + 1) * vocab_count]
            go = jnp.clip(SLOTS - first, 0.0, waiting[way])
            book_ref[(f * 2 + way) * 3] = moved[way]
            moved[way] = moved[way] + go
            book_ref[(f * 2 + way) * 3 + 1] = moved[way]
            book_ref[(f * 2 + way) * 3 + 2] = jnp.minimum(first, float(SLOTS))
            come = pltpu.roll(pltpu.roll(go, 8, 1), 1 if way == 0 else vocab_count - 1, 0)
            waiting[way] = waiting[way] - go + jnp.where(travels, come, 0.0)
    left = jnp.sum(waiting[0] + waiting[1], axis=1, keepdims=True)
    left = jnp.sum(jnp.broadcast_to(left, shape), axis=0, keepdims=True)
    fit_ref[...] = jnp.broadcast_to(left, fit_ref.shape).astype(i32)

    small = (vocab_count, vocab_count)
    target = lax.broadcasted_iota(i32, (BLK, 2 * BLK), 1).astype(f32)
    pointer, sends = [], []
    for way in range(2):
        step = 1 if way == 0 else -1
        back = me - step * lax.broadcasted_iota(i32, small, 0)
        back = jnp.where(back < 0, back + vocab_count, jnp.where(back >= vocab_count, back - vocab_count, back))
        pick = ones(back == lax.broadcasted_iota(i32, small, 1))
        far = jnp.dot(pick, reach[way].astype(f32).astype(jnp.bfloat16), preferred_element_type=f32).astype(i32)
        order = jnp.dot(pick, index[way].astype(jnp.bfloat16), preferred_element_type=f32)
        giver = me - step
        giver = jnp.where(giver < 0, giver + vocab_count, jnp.where(giver >= vocab_count, giver - vocab_count, giver))

        def slot(at, hops, valid):
            column = jnp.clip(hops * 8 + far - 1, 0, BLK - 1)
            where = jnp.full(shape, -1.0, f32)
            for f in range(steps):
                start, end, first = (
                    jnp.take_along_axis(
                        jnp.broadcast_to(book_ref[(f * 2 + way) * 3 + kind, pl.ds(at, 1), :], shape),
                        column,
                        axis=1,
                        mode="promise_in_bounds",
                    )
                    for kind in range(3)
                )
                now = valid & (start <= order) & (order < end)
                where = jnp.where(now, f * SLOTS + first + order - start, where)
            return where

        leave = slot(me, row, (far > row) & (row < half))
        arrive = slot(giver, row - 1, (far >= row) & (row >= 1) & (row <= half))
        point = jnp.where(row == 0, lane.astype(f32), jnp.maximum(home + arrive, 0.0))
        pointer.append(point)
        leave_turned = jnp.concatenate([leave, jnp.full((BLK - vocab_count, BLK), -1.0, f32)], axis=0).T
        chosen = jnp.zeros((1, 2 * BLK), f32)
        for h in range(half):
            chosen = chosen + jnp.dot(
                point[h : h + 1].astype(jnp.bfloat16),
                ones(leave_turned[:, h : h + 1] == target),
                preferred_element_type=f32,
            )
        sends.append(chosen.astype(i32))
    straight = sign > 0
    send_ref[0:1, :] = jnp.where(straight, sends[0], sends[1])
    send_ref[1:2, :] = jnp.where(straight, sends[1], sends[0])
    send_ref[2:8, :] = jnp.zeros((6, 2 * BLK), i32)

    mine_lane = lax.broadcasted_iota(i32, (pair_count, vocab_count), 1)
    holder = jnp.sum(jnp.where(pair_lane == me, holders, 0), axis=1, keepdims=True)
    inner = jnp.sum(jnp.where(pair_lane == me, inners, 0), axis=1, keepdims=True)
    distance = me - holder
    distance = jnp.where(distance < 0, distance + vocab_count, distance)
    hops = ways(distance, inner, vocab_count)
    scale = jnp.where(distance <= half, distance, 2 * vocab_count - distance)
    points = jnp.zeros((pair_count, 1), f32)
    for way in range(2):
        found = lax.dot_general(
            ones(pair_lane == inner),
            pointer[way].astype(jnp.bfloat16),
            (((1,), (1,)), ((), ())),
            preferred_element_type=f32,
        )
        points = points + jnp.sum(
            jnp.where((mine_lane == hops[way]) & (hops[way] > 0), found, 0.0), axis=1, keepdims=True
        )
    points = jnp.where(distance == 0, inner.astype(f32), points)
    by_stats = [jnp.sum(jnp.where(lane == blocks, p, 0.0), axis=1, keepdims=True) for p in pointer]
    hop = lax.broadcasted_iota(i32, (vocab_count, 1), 0)
    stat_ok = [hop <= half, (hop >= 1) & (hop < half)]
    points = jnp.concatenate(
        [points] + [jnp.where(ok, p, 0.0) for ok, p in zip(stat_ok, by_stats)], axis=0
    ).astype(i32)
    other = jnp.concatenate(
        [(hops[1] > 0).astype(i32), jnp.zeros((vocab_count, 1), i32), jnp.ones((vocab_count, 1), i32)], axis=0
    )
    other = jnp.where(straight, other, 1 - other)
    scale = jnp.concatenate([scale, jnp.zeros((2 * vocab_count, 1), i32)], axis=0)
    frame = jnp.zeros(points.shape, i32)
    for f in range(1, steps):
        frame = frame + (points >= home + f * SLOTS).astype(i32)
    away = points >= home
    source = jnp.where(away, 1 + frame + steps * other, 0)
    spot = jnp.where(away, points - home - frame * SLOTS, points)
    spot = jnp.clip(spot, 0, jnp.where(away, SLOTS - 1, home - 1))
    items = points.shape[0]
    item_lane = lax.broadcasted_iota(i32, (items, BLK), 1)
    table = jnp.where(
        item_lane == 0, spot, jnp.where(item_lane == 1, scale, jnp.where(item_lane == 2, source, 0))
    ).astype(f32)
    turned = jnp.concatenate([table, jnp.zeros((BLK - items, BLK), f32)], axis=0).T
    source_row = turned[2:3].astype(i32)
    item_up = lax.broadcasted_iota(i32, (items, BLK), 0)
    is_item = item_lane < items
    sooner = is_item & ((source_row < source) | ((source_row == source) & (item_lane < item_up)))
    rank = jnp.sum(sooner.astype(i32), axis=1, keepdims=True)
    item_ref[0:1, :] = turned[0:1].astype(i32)
    item_ref[1:2, :] = turned[1:2].astype(i32)
    item_ref[2:3, :] = jnp.sum(jnp.where(rank == item_lane, item_up, 0), axis=0, keepdims=True)
    item_ref[3:4, :] = jnp.sum((source < item_lane).astype(i32), axis=0, keepdims=True)
    item_ref[4:8, :] = jnp.zeros((4, BLK), i32)


def pack_kernel(send_ref, own_ref, low_ref, high_ref, pick_ref, home_ref, first_ref, second_ref, cand_ref, logit_ref):
    docs, positions, columns = own_ref.shape
    width = low_ref.shape[1]
    span = positions + 2 * width
    rows = pick_ref.shape[0]
    blocks = columns // BLK
    for doc in range(docs):
        cand_ref[doc * span : doc * span + width, :] = low_ref[doc]
        cand_ref[doc * span + width : doc * span + width + positions, :] = own_ref[doc]
        cand_ref[doc * span + width + positions : (doc + 1) * span, :] = high_ref[doc]
    pick = pick_ref[...]
    peak = jnp.full((rows, BLK), -jnp.inf, jnp.float32)
    for t in range(blocks):
        part = jnp.dot(pick, cand_ref[:, t * BLK : (t + 1) * BLK], preferred_element_type=jnp.float32)
        logit_ref[t] = part.astype(jnp.bfloat16)
        peak = jnp.maximum(peak, part)
    top = jnp.max(peak, axis=1, keepdims=True)
    total = jnp.zeros((rows, BLK), jnp.float32)
    for t in range(blocks):
        power = jnp.exp(logit_ref[t].astype(jnp.float32) - top)
        total = total + power
        home_ref[t] = power.astype(jnp.bfloat16)
    total = jnp.sum(total, axis=1, keepdims=True)
    first = total.astype(jnp.bfloat16).astype(jnp.float32)
    second = (total - first).astype(jnp.bfloat16).astype(jnp.float32)
    third = total - first - second
    lane = lax.broadcasted_iota(jnp.int32, (rows, BLK), 1)
    home_ref[blocks] = jnp.where(
        lane == 0, top, jnp.where(lane == 1, first, jnp.where(lane == 2, second, jnp.where(lane == 3, third, 0.0)))
    ).astype(jnp.bfloat16)
    for j in range(SLOTS):
        first_ref[j] = home_ref[send_ref[0, j]]
        second_ref[j] = home_ref[send_ref[1, j]]


def ready_kernel(chain, step, send_ref, home_ref, *refs):
    frames, out_ref = refs[:-1], refs[-1]
    home = home_ref.shape[0]

    def choose(j, carry):
        at = send_ref[chain, step * SLOTS + j]

        def copy(low, high):
            if high - low == 1:
                if low == 0:
                    out_ref[j] = home_ref[at]
                elif low <= len(frames):
                    out_ref[j] = frames[low - 1][at - home - (low - 1) * SLOTS]
                return
            mid = (low + high) // 2
            split = home + (mid - 1) * SLOTS
            pl.when(at < split)(lambda: copy(low, mid))
            pl.when(at >= split)(lambda: copy(mid, high))

        copy(0, len(frames) + 2)
        return carry

    lax.fori_loop(0, SLOTS, choose, 0)


def pass_kernel(chain, step, home, send_ref, part_ref, newest_ref, out_ref):
    for j in range(SLOTS):
        at = send_ref[chain, step * SLOTS + j] - (home + (step - 1) * SLOTS)

        @pl.when(at >= 0)
        def _(j=j, at=at):
            out_ref[j] = newest_ref[at]

        @pl.when(at < 0)
        def _(j=j):
            out_ref[j] = part_ref[j]


def student_kernel(student_ref, top_ref, total_ref):
    docs, positions, columns = student_ref.shape
    rows = docs * positions
    peak = jnp.full((rows, BLK), -jnp.inf, jnp.float32)
    for b in range(columns // BLK):
        part = student_ref[:, :, b * BLK : (b + 1) * BLK].reshape(rows, BLK).astype(jnp.float32)
        peak = jnp.maximum(peak, part)
    top = jnp.max(peak, axis=1, keepdims=True)
    total = jnp.zeros((rows, BLK), jnp.float32)
    for b in range(columns // BLK):
        part = student_ref[:, :, b * BLK : (b + 1) * BLK].reshape(rows, BLK).astype(jnp.float32)
        total = total + jnp.exp(part - top)
    top_ref[...] = jnp.broadcast_to(top, (rows, BLK))
    total_ref[...] = jnp.broadcast_to(jnp.sum(total, axis=1, keepdims=True), (rows, BLK))


def map_kernel(steps, item_ref, *refs):
    sources = refs[: 2 * steps + 1]
    spread_ref, weight_ref, student_ref, top_ref, total_ref, out_ref, stage_ref, scale_ref = refs[2 * steps + 1 :]
    docs, positions, columns = student_ref.shape
    rows = docs * positions
    blocks = columns // BLK
    spread = spread_ref[...]
    for s, source in enumerate(sources):

        def bring(q, carry, source=source):
            item = item_ref[2, q]
            stage_ref[item] = source[item_ref[0, item]]
            return carry

        lax.fori_loop(item_ref[3, s], item_ref[3, s + 1], bring, 0)
    holders = [h for h in range(steps + 1)] + [2 * steps + h for h in range(1, steps)]
    peaks, sums = [], []
    for h in holders:
        stats = jnp.dot(spread, stage_ref[K * blocks + h], preferred_element_type=jnp.float32)
        peaks.append(stats[:, 0:1])
        sums.append(stats[:, 1:2] + stats[:, 2:3] + stats[:, 3:4])
    peak = functools.reduce(jnp.maximum, peaks)
    powers = [jnp.exp(p - peak) for p in peaks]
    norm = sum(p * t for p, t in zip(powers, sums))
    for h, power in zip(holders, powers):
        scale_ref[h] = jnp.broadcast_to(power / norm, (rows, BLK))
    student_top = top_ref[...]
    mass = jnp.zeros((rows, BLK), jnp.float32)
    cross = jnp.zeros((rows, BLK), jnp.float32)
    for b in range(blocks):
        picked = jnp.concatenate([stage_ref[K * b], stage_ref[K * b + 1]], axis=1)
        prob = jnp.dot(spread, picked, preferred_element_type=jnp.float32).astype(jnp.bfloat16)
        mapped = scale_ref[item_ref[1, K * b]] * jnp.dot(
            prob[:, :BLK], weight_ref[:, K * b].reshape(BLK, BLK), preferred_element_type=jnp.float32
        ) + scale_ref[item_ref[1, K * b + 1]] * jnp.dot(
            prob[:, BLK:], weight_ref[:, K * b + 1].reshape(BLK, BLK), preferred_element_type=jnp.float32
        )
        logit = student_ref[:, :, b * BLK : (b + 1) * BLK].reshape(rows, BLK).astype(jnp.float32) - student_top
        mass = mass + mapped
        cross = cross + mapped * (jnp.log(jnp.maximum(mapped, TINY)) - logit)
    mass = jnp.sum(mass, axis=1, keepdims=True)
    cross = jnp.sum(cross, axis=1, keepdims=True)
    lane = lax.broadcasted_iota(jnp.int32, (rows, BLK), 1)
    table = jnp.where(
        lane == 0, mass, jnp.where(lane == 1, cross, jnp.where(lane == 2, student_top, total_ref[...]))
    )
    out_ref[...] = table.T[:8]


def whole(padded_parts, cand, src_block, weights, student_logits):
    doc_count, pos_count, student_cols = student_logits.shape
    teacher_cols = padded_parts[0].shape[2]
    teacher_blocks = teacher_cols // BLK
    student_blocks = student_cols // BLK
    row_count = doc_count * pos_count
    padded = jnp.concatenate(padded_parts, axis=1).reshape(-1, teacher_cols)
    teacher_float = jnp.take(padded, cand, axis=0).astype(jnp.float32)
    student_float = student_logits.reshape(row_count, student_cols).astype(jnp.float32)
    teacher_peak = jnp.max(teacher_float, axis=1)
    student_peak = jnp.max(student_float, axis=1)
    teacher_top, student_top = lax.pmax((teacher_peak, student_peak), "vocab")
    teacher_total, student_total = lax.psum(
        (
            jnp.sum(jnp.exp(teacher_float - teacher_top[:, None]), axis=1),
            jnp.sum(jnp.exp(student_float - student_top[:, None]), axis=1),
        ),
        "vocab",
    )
    teacher_prob = (jnp.exp(teacher_float - teacher_top[:, None]) / teacher_total[:, None]).astype(jnp.bfloat16)
    student_logprob = student_float - student_top[:, None] - jnp.log(student_total)[:, None]
    vocab_count = lax.axis_size("vocab")
    own_index = lax.axis_index("vocab")
    pair_count = student_blocks * K
    capacity = 2 * K * student_blocks // vocab_count
    pair_blocks = src_block.reshape(vocab_count, pair_count)
    holder = pair_blocks // teacher_blocks
    inside = pair_blocks % teacher_blocks
    same_holder = holder[:, :, None] == holder[:, None, :]
    before = jnp.arange(pair_count)[None, :] < jnp.arange(pair_count)[:, None]
    slot_rank = jnp.sum(same_holder & before[None, :, :], axis=2)
    chosen = (holder == own_index)[:, None, :] & (
        slot_rank[:, None, :] == jnp.arange(capacity)[None, :, None]
    )
    send_index = jnp.sum(jnp.where(chosen, inside[:, None, :], 0), axis=2)
    prob_blocks = teacher_prob.reshape(row_count, teacher_blocks, BLK)
    outgoing = jnp.take(prob_blocks, send_index.reshape(-1), axis=1).reshape(row_count, vocab_count, capacity, BLK)
    incoming = lax.all_to_all(outgoing, "vocab", split_axis=1, concat_axis=1, tiled=True)
    own_holder = jnp.take(holder, own_index, axis=0)
    own_rank = jnp.take(slot_rank, own_index, axis=0)
    recv_slot = own_holder * capacity + own_rank
    gathered = jnp.take(incoming.reshape(row_count, vocab_count * capacity, BLK), recv_slot, axis=1).reshape(
        row_count, student_blocks, K, BLK
    )
    weights = weights.swapaxes(0, 1).reshape(student_blocks, K, BLK, BLK)
    mapped = jnp.einsum("rbkc,bkcd->rbd", gathered, weights, preferred_element_type=jnp.float32).reshape(
        row_count, student_cols
    )
    total_mass = lax.psum(jnp.sum(mapped, axis=1), "vocab")
    normed = mapped / total_mass[:, None]
    return lax.psum(
        jnp.sum(jax.scipy.special.xlogy(normed, normed) - normed * student_logprob, axis=1), "vocab"
    )


def shards(teacher_logits, student_logits, alignment, src_block, margin_weight):
    doc_count, pos_count, teacher_cols = teacher_logits.shape
    student_cols = student_logits.shape[2]
    teacher_blocks = teacher_cols // BLK
    student_blocks = student_cols // BLK
    row_count = doc_count * pos_count
    pair_count = student_blocks * K
    vocab_count = lax.axis_size("vocab")
    steps = vocab_count // 2
    home = teacher_blocks + 1
    vocab_index = lax.axis_index("vocab")
    seq_index = lax.axis_index("seq")
    sign = 1 - 2 * (seq_index % 2)
    span = pos_count + 2 * W

    with jax.named_scope("halo"):
        low, high = halo(teacher_logits, W)
    with jax.named_scope("weights"):
        weights = lax.all_gather(
            margin_weight.reshape(pair_count, -1, BLK), "dp", axis=0, tiled=False
        )

    with jax.named_scope("rows"):
        cand = (alignment - seq_index * pos_count + W + jnp.arange(doc_count)[:, None] * span).reshape(-1)
        cand = jnp.clip(cand, 0, doc_count * span - 1)
        places = jnp.arange(doc_count * span)
        used = jnp.any(cand[:, None] == places[None, :], axis=0)
        place_rank = jnp.sum(used[:, None] & (places[:, None] < places[None, :]), axis=0)
        cand_rank = jnp.sum(used[None, :] & (places[None, :] < cand[:, None]), axis=1)
        row_ids = jnp.arange(ROWS)
        pick = ((row_ids[:, None] == place_rank[None, :]) & used[None, :]).astype(jnp.bfloat16)
        spread = (cand_rank[:, None] == row_ids[None, :]).astype(jnp.bfloat16)
        rows_fit = jnp.sum(used.astype(jnp.int32)) <= ROWS

    vmem = pl.BlockSpec(memory_space=pltpu.VMEM)
    smem = pl.BlockSpec(memory_space=pltpu.SMEM)
    def room(mib):
        return pltpu.CompilerParams(vmem_limit_bytes=mib * 1024 * 1024)

    with jax.named_scope("plan"):
        listed = src_block.reshape(vocab_count, pair_count)
        table = jax.ShapeDtypeStruct((8, BLK), jnp.int32)
        send, items, left = pl.pallas_call(
            functools.partial(plan_kernel, teacher_blocks),
            out_shape=(jax.ShapeDtypeStruct((8, 2 * BLK), jnp.int32), table, table),
            in_specs=[smem, vmem],
            out_specs=(vmem,) * 3,
            scratch_shapes=[pltpu.VMEM((6 * steps, vocab_count, BLK), jnp.float32)],
            compiler_params=room(16),
        )(jnp.stack([vocab_index, sign]).astype(jnp.int32), listed)

    def planes(count):
        return jax.ShapeDtypeStruct((count, ROWS, BLK), jnp.bfloat16)

    with jax.named_scope("pack"):
        own, ahead, behind = pl.pallas_call(
            pack_kernel,
            out_shape=(planes(home), planes(SLOTS), planes(SLOTS)),
            in_specs=[smem] + [vmem] * 4,
            out_specs=(vmem,) * 3,
            scratch_shapes=[
                pltpu.VMEM((doc_count * span, teacher_cols), jnp.bfloat16),
                pltpu.VMEM((teacher_blocks, ROWS, BLK), jnp.bfloat16),
            ],
            compiler_params=room(24),
        )(send, teacher_logits, low, high, pick)

    def chosen(chain, step, frames):
        part = pl.pallas_call(
            functools.partial(ready_kernel, chain, step),
            out_shape=planes(SLOTS),
            in_specs=[smem] + [vmem] * len(frames),
            out_specs=vmem,
            compiler_params=room(12),
        )(send, own, *frames[:-1])
        return pl.pallas_call(
            functools.partial(pass_kernel, chain, step, home),
            out_shape=planes(SLOTS),
            in_specs=[smem] + [vmem] * 2,
            out_specs=vmem,
            compiler_params=room(8),
        )(send, part, frames[-1])

    with jax.named_scope("ring"):
        forward, backward = ring_pairs(1), ring_pairs(-1)
        came_ahead, came_behind = [], []
        for step in range(steps):
            if step:
                ahead = chosen(0, step, came_ahead)
            came_ahead.append(lax.ppermute(ahead, ("seq", "vocab"), forward))
            if step:
                behind = chosen(1, step, came_behind)
            came_behind.append(lax.ppermute(behind, ("seq", "vocab"), backward))

    with jax.named_scope("student"):
        top, total = pl.pallas_call(
            student_kernel,
            out_shape=(jax.ShapeDtypeStruct((row_count, BLK), jnp.float32),) * 2,
            in_specs=[vmem],
            out_specs=(vmem,) * 2,
            compiler_params=room(16),
        )(student_logits)

    with jax.named_scope("map"):
        held = pl.pallas_call(
            functools.partial(map_kernel, steps),
            out_shape=jax.ShapeDtypeStruct((8, row_count), jnp.float32),
            in_specs=[smem] + [vmem] * (2 * steps + 1 + 5),
            out_specs=vmem,
            scratch_shapes=[
                pltpu.VMEM((pair_count + 2 * vocab_count, ROWS, BLK), jnp.bfloat16),
                pltpu.VMEM((3 * steps, row_count, BLK), jnp.float32),
            ],
            compiler_params=room(20),
        )(items, own, *came_ahead, *came_behind, spread, weights, student_logits, top, total)

    with jax.named_scope("finish"):
        sent = jnp.broadcast_to(held[None, :4], (vocab_count, 4, row_count))
        parts = lax.all_to_all(sent, "vocab", split_axis=0, concat_axis=0, tiled=True)
        mass_part, cross_part, top_part, total_part = (parts[:, i] for i in range(4))
        student_top = jnp.max(top_part, axis=0)
        log_total = student_top + jnp.log(jnp.sum(jnp.exp(top_part - student_top) * total_part, axis=0))
        mass = jnp.sum(mass_part, axis=0)
        result = jnp.sum(cross_part + mass_part * (log_total - top_part), axis=0) / mass - jnp.log(mass)

    result = lax.cond(
        rows_fit & (left[0, 0] == 0),
        lambda *_: result,
        lambda *operands: whole(operands[:3], *operands[3:]),
        low,
        teacher_logits,
        high,
        cand,
        src_block,
        weights,
        student_logits,
    )
    return result.reshape(doc_count, pos_count)


def solution(mesh):
    in_specs = (
        P("dp", "seq", "vocab"),
        P("dp", "seq", "vocab"),
        P("dp", "seq"),
        P(),
        P("vocab", None, "dp", None),
    )
    out_specs = P("dp", "seq")
    return jax.shard_map(shards, mesh=mesh, in_specs=in_specs, out_specs=out_specs, check_vma=False)
```

```python
import functools

import jax
import jax.numpy as jnp
from jax import lax
from jax.experimental import pallas as pl
from jax.experimental.pallas import tpu as pltpu
from jax.sharding import PartitionSpec as P

BLK = 128
K = 2
W = 16
ROWS = 104
SLOTS = 21
TINY = 1.2e-38


def halo(block, width):
    count = lax.axis_size("seq")
    forward = [(i, i + 1) for i in range(count - 1)]
    backward = [(target, source) for source, target in forward]
    low = lax.ppermute(block[:, block.shape[1] - width :], "seq", forward)
    high = lax.ppermute(block[:, :width], "seq", backward)
    return low, high


def ring_pairs(turn):
    seq_count, vocab_count = lax.axis_size("seq"), lax.axis_size("vocab")
    pairs = []
    for s in range(seq_count):
        step = turn if s % 2 == 0 else -turn
        for v in range(vocab_count):
            pairs.append((s * vocab_count + v, s * vocab_count + (v + step) % vocab_count))
    return pairs


def ways(distance, block, share, vocab_count):
    half = vocab_count // 2
    first = (block * 5) % 8 < share
    ahead = jnp.where((distance >= 1) & ((distance < half) | ((distance == half) & first)), distance, 0)
    behind = jnp.where((distance > half) | ((distance == half) & ~first), vocab_count - distance, 0)
    return ahead, behind


def ones(mask):
    return jnp.where(mask, 1.0, 0.0).astype(jnp.bfloat16)


def plan_kernel(blocks, place_ref, listed_ref, send_ref, item_ref, fit_ref, book_ref):
    vocab_count, pair_count = listed_ref.shape
    half = vocab_count // 2
    steps = half
    home = blocks + 1
    me, sign = place_ref[0], place_ref[1]
    f32, i32 = jnp.float32, jnp.int32
    shape = (vocab_count, BLK)

    def split(listed):
        holder = sum((listed >= h * blocks).astype(i32) for h in range(1, vocab_count))
        return holder, listed - holder * blocks

    listed = listed_ref[...]
    wide = jnp.concatenate([listed, jnp.zeros((vocab_count, BLK - pair_count), i32)], axis=1)
    tall = jnp.concatenate([wide, jnp.zeros((BLK - vocab_count, BLK), i32)], axis=0).astype(f32).T.astype(i32)
    row_holder, _ = split(listed)
    holders, inners = split(tall[:pair_count])
    lane = lax.broadcasted_iota(i32, shape, 1)
    row = lax.broadcasted_iota(i32, shape, 0)

    reach = [jnp.zeros(shape, i32), jnp.zeros(shape, i32)]
    across = jnp.zeros(shape, i32)
    pair_lane = lax.broadcasted_iota(i32, (pair_count, BLK), 1)
    pair_row = lax.broadcasted_iota(i32, (vocab_count, pair_count), 0)
    for s in range(vocab_count):
        hits = jnp.dot(
            ones(pair_row == row_holder[s : s + 1, :]),
            ones(pair_lane == inners[:, s : s + 1]),
            preferred_element_type=f32,
        )
        distance = s - row
        distance = jnp.where(distance < 0, distance + vocab_count, distance)
        needed = hits > 0
        reach[0] = jnp.maximum(reach[0], jnp.where(needed & (distance < half), distance, 0))
        reach[1] = jnp.maximum(reach[1], jnp.where(needed & (distance > half), vocab_count - distance, 0))
        across = jnp.maximum(across, jnp.where(needed & (distance == half), 1, 0))
    order_key = (lane * 5) % 8
    share = jnp.zeros((1, 1), i32)
    for part in range(1, 9):
        first = (across > 0) & (order_key < part)
        more = jnp.where(first, half, reach[0]) - jnp.where((across > 0) & ~first, half, reach[1])
        more = jnp.sum(jnp.sum(more, axis=1, keepdims=True), axis=0, keepdims=True)
        share = share + (more <= 0).astype(i32)
    first = order_key < share
    reach[0] = jnp.where((across > 0) & first, half, reach[0])
    reach[1] = jnp.where((across > 0) & ~first, half, reach[1])
    reach = [jnp.where(lane == blocks, half - way, reach[way]) for way in range(2)]

    square = (BLK, BLK)
    up, over = lax.broadcasted_iota(i32, square, 0), lax.broadcasted_iota(i32, square, 1)
    earlier = ones(up < over)
    left_up, left_over = (up & 7) + 1 - (up >> 3), (over & 7) + 1 - (over >> 3)
    goes_first = ones((left_up > left_over) | ((left_up == left_over) & ((up >> 3) > (over >> 3))))
    index, waiting, moved = [], [], [jnp.zeros(shape, f32)] * 2
    for way in range(2):
        masks = jnp.concatenate([ones(reach[way] == r) for r in range(1, half + 1)], axis=0)
        before = jnp.dot(masks, earlier, preferred_element_type=f32)
        place = jnp.zeros(shape, f32)
        count = jnp.zeros(shape, f32)
        for r in range(1, half + 1):
            same = reach[way] == r
            place = jnp.where(same, before[(r - 1) * vocab_count : r * vocab_count], place)
            total = jnp.sum(jnp.where(same, 1.0, 0.0), axis=1, keepdims=True)
            count = jnp.where(lane == r - 1, total, count)
        index.append(place)
        waiting.append(count)
    travels = (lane >= 8) & (lane < 8 * half) & ((lane & 7) + 1 > (lane >> 3))
    for f in range(steps):
        ahead_of = jnp.dot(
            jnp.concatenate(waiting, axis=0).astype(jnp.bfloat16), goes_first, preferred_element_type=f32
        )
        for way in range(2):
            first = ahead_of[way * vocab_count : (way + 1) * vocab_count]
            go = jnp.clip(SLOTS - first, 0.0, waiting[way])
            book_ref[(f * 2 + way) * 3] = moved[way]
            moved[way] = moved[way] + go
            book_ref[(f * 2 + way) * 3 + 1] = moved[way]
            book_ref[(f * 2 + way) * 3 + 2] = jnp.minimum(first, float(SLOTS))
            come = pltpu.roll(pltpu.roll(go, 8, 1), 1 if way == 0 else vocab_count - 1, 0)
            waiting[way] = waiting[way] - go + jnp.where(travels, come, 0.0)
    left = jnp.sum(waiting[0] + waiting[1], axis=1, keepdims=True)
    left = jnp.sum(jnp.broadcast_to(left, shape), axis=0, keepdims=True)
    fit_ref[...] = jnp.broadcast_to(left, fit_ref.shape).astype(i32)

    small = (vocab_count, vocab_count)
    target = lax.broadcasted_iota(i32, (BLK, 2 * BLK), 1).astype(f32)
    pointer, sends = [], []
    for way in range(2):
        step = 1 if way == 0 else -1
        back = me - step * lax.broadcasted_iota(i32, small, 0)
        back = jnp.where(back < 0, back + vocab_count, jnp.where(back >= vocab_count, back - vocab_count, back))
        pick = ones(back == lax.broadcasted_iota(i32, small, 1))
        far = jnp.dot(pick, reach[way].astype(f32).astype(jnp.bfloat16), preferred_element_type=f32).astype(i32)
        order = jnp.dot(pick, index[way].astype(jnp.bfloat16), preferred_element_type=f32)
        giver = me - step
        giver = jnp.where(giver < 0, giver + vocab_count, jnp.where(giver >= vocab_count, giver - vocab_count, giver))

        def slot(at, hops, valid):
            column = jnp.clip(hops * 8 + far - 1, 0, BLK - 1)
            where = jnp.full(shape, -1.0, f32)
            for f in range(steps):
                start, end, first = (
                    jnp.take_along_axis(
                        jnp.broadcast_to(book_ref[(f * 2 + way) * 3 + kind, pl.ds(at, 1), :], shape),
                        column,
                        axis=1,
                        mode="promise_in_bounds",
                    )
                    for kind in range(3)
                )
                now = valid & (start <= order) & (order < end)
                where = jnp.where(now, f * SLOTS + first + order - start, where)
            return where

        leave = slot(me, row, (far > row) & (row < half))
        arrive = slot(giver, row - 1, (far >= row) & (row >= 1) & (row <= half))
        point = jnp.where(row == 0, lane.astype(f32), jnp.maximum(home + arrive, 0.0))
        pointer.append(point)
        leave_turned = jnp.concatenate([leave, jnp.full((BLK - vocab_count, BLK), -1.0, f32)], axis=0).T
        chosen = jnp.zeros((1, 2 * BLK), f32)
        for h in range(half):
            chosen = chosen + jnp.dot(
                point[h : h + 1].astype(jnp.bfloat16),
                ones(leave_turned[:, h : h + 1] == target),
                preferred_element_type=f32,
            )
        sends.append(chosen.astype(i32))
    straight = sign > 0
    send_ref[0:1, :] = jnp.where(straight, sends[0], sends[1])
    send_ref[1:2, :] = jnp.where(straight, sends[1], sends[0])
    send_ref[2:8, :] = jnp.zeros((6, 2 * BLK), i32)

    mine_lane = lax.broadcasted_iota(i32, (pair_count, vocab_count), 1)
    holder = jnp.sum(jnp.where(pair_lane == me, holders, 0), axis=1, keepdims=True)
    inner = jnp.sum(jnp.where(pair_lane == me, inners, 0), axis=1, keepdims=True)
    distance = me - holder
    distance = jnp.where(distance < 0, distance + vocab_count, distance)
    hops = ways(distance, inner, share, vocab_count)
    scale = jnp.where(distance <= half, distance, 2 * vocab_count - distance)
    points = jnp.zeros((pair_count, 1), f32)
    for way in range(2):
        found = lax.dot_general(
            ones(pair_lane == inner),
            pointer[way].astype(jnp.bfloat16),
            (((1,), (1,)), ((), ())),
            preferred_element_type=f32,
        )
        points = points + jnp.sum(
            jnp.where((mine_lane == hops[way]) & (hops[way] > 0), found, 0.0), axis=1, keepdims=True
        )
    points = jnp.where(distance == 0, inner.astype(f32), points)
    by_stats = [jnp.sum(jnp.where(lane == blocks, p, 0.0), axis=1, keepdims=True) for p in pointer]
    hop = lax.broadcasted_iota(i32, (vocab_count, 1), 0)
    stat_ok = [hop <= half, (hop >= 1) & (hop < half)]
    points = jnp.concatenate(
        [points] + [jnp.where(ok, p, 0.0) for ok, p in zip(stat_ok, by_stats)], axis=0
    ).astype(i32)
    other = jnp.concatenate(
        [(hops[1] > 0).astype(i32), jnp.zeros((vocab_count, 1), i32), jnp.ones((vocab_count, 1), i32)], axis=0
    )
    other = jnp.where(straight, other, 1 - other)
    scale = jnp.concatenate([scale, jnp.zeros((2 * vocab_count, 1), i32)], axis=0)
    frame = jnp.zeros(points.shape, i32)
    for f in range(1, steps):
        frame = frame + (points >= home + f * SLOTS).astype(i32)
    away = points >= home
    source = jnp.where(away, 1 + frame + steps * other, 0)
    spot = jnp.where(away, points - home - frame * SLOTS, points)
    spot = jnp.clip(spot, 0, jnp.where(away, SLOTS - 1, home - 1))
    items = points.shape[0]
    item_lane = lax.broadcasted_iota(i32, (items, BLK), 1)
    table = jnp.where(
        item_lane == 0, spot, jnp.where(item_lane == 1, scale, jnp.where(item_lane == 2, source, 0))
    ).astype(f32)
    turned = jnp.concatenate([table, jnp.zeros((BLK - items, BLK), f32)], axis=0).T
    source_row = turned[2:3].astype(i32)
    item_up = lax.broadcasted_iota(i32, (items, BLK), 0)
    is_item = item_lane < items
    sooner = is_item & ((source_row < source) | ((source_row == source) & (item_lane < item_up)))
    rank = jnp.sum(sooner.astype(i32), axis=1, keepdims=True)
    item_ref[0:1, :] = turned[0:1].astype(i32)
    item_ref[1:2, :] = turned[1:2].astype(i32)
    item_ref[2:3, :] = jnp.sum(jnp.where(rank == item_lane, item_up, 0), axis=0, keepdims=True)
    item_ref[3:4, :] = jnp.sum((source < item_lane).astype(i32), axis=0, keepdims=True)
    item_ref[4:8, :] = jnp.zeros((4, BLK), i32)


def scalars(table_ref, row, start, count):
    values = table_ref[row : row + 1, :]
    return [values[0, start + j] for j in range(count)]


def pack_kernel(send_ref, own_ref, low_ref, high_ref, pick_ref, home_ref, first_ref, second_ref, cand_ref, logit_ref):
    docs, positions, columns = own_ref.shape
    width = low_ref.shape[1]
    span = positions + 2 * width
    rows = pick_ref.shape[0]
    blocks = columns // BLK
    for doc in range(docs):
        cand_ref[doc * span : doc * span + width, :] = low_ref[doc]
        cand_ref[doc * span + width : doc * span + width + positions, :] = own_ref[doc]
        cand_ref[doc * span + width + positions : (doc + 1) * span, :] = high_ref[doc]
    pick = pick_ref[...]
    peak = jnp.full((rows, BLK), -jnp.inf, jnp.float32)
    for t in range(blocks):
        part = jnp.dot(pick, cand_ref[:, t * BLK : (t + 1) * BLK], preferred_element_type=jnp.float32)
        logit_ref[t] = part.astype(jnp.bfloat16)
        peak = jnp.maximum(peak, part)
    top = jnp.max(peak, axis=1, keepdims=True)
    total = jnp.zeros((rows, BLK), jnp.float32)
    for t in range(blocks):
        power = jnp.exp(logit_ref[t].astype(jnp.float32) - top)
        total = total + power
        home_ref[t] = power.astype(jnp.bfloat16)
    total = jnp.sum(total, axis=1, keepdims=True)
    first = total.astype(jnp.bfloat16).astype(jnp.float32)
    second = (total - first).astype(jnp.bfloat16).astype(jnp.float32)
    third = total - first - second
    lane = lax.broadcasted_iota(jnp.int32, (rows, BLK), 1)
    home_ref[blocks] = jnp.where(
        lane == 0, top, jnp.where(lane == 1, first, jnp.where(lane == 2, second, jnp.where(lane == 3, third, 0.0)))
    ).astype(jnp.bfloat16)
    for chain, out_ref in enumerate((first_ref, second_ref)):
        for j, at in enumerate(scalars(send_ref, chain, 0, SLOTS)):
            out_ref[j] = home_ref[at]


def ready_kernel(chain, step, send_ref, home_ref, *refs):
    frames, out_ref = refs[:-1], refs[-1]
    home = home_ref.shape[0]
    for j, at in enumerate(scalars(send_ref, chain, step * SLOTS, SLOTS)):

        def copy(low, high, j=j, at=at):
            if high - low == 1:
                if low == 0:
                    out_ref[j] = home_ref[at]
                elif low <= len(frames):
                    out_ref[j] = frames[low - 1][at - home - (low - 1) * SLOTS]
                return
            mid = (low + high) // 2
            split = home + (mid - 1) * SLOTS
            pl.when(at < split)(lambda: copy(low, mid))
            pl.when(at >= split)(lambda: copy(mid, high))

        copy(0, len(frames) + 2)


def pass_kernel(chain, step, home, send_ref, part_ref, newest_ref, out_ref):
    start = home + (step - 1) * SLOTS
    for j, at in enumerate(scalars(send_ref, chain, step * SLOTS, SLOTS)):
        newest = newest_ref[jnp.maximum(at - start, 0)]
        out_ref[j] = jnp.where(at >= start, newest, part_ref[j])


def stage_kernel(steps, item_ref, *refs):
    sources, stage_ref = refs[:-1], refs[-1]
    for s, source in zip([s for s in range(2 * steps + 1) if s not in (steps, 2 * steps)], sources):
        bring(item_ref, s, source, stage_ref)


def bring(item_ref, s, source_ref, stage_ref):
    def one(q, carry):
        item = item_ref[2, q]
        stage_ref[item] = source_ref[item_ref[0, item]]
        return carry

    lax.fori_loop(item_ref[3, s], item_ref[3, s + 1], one, 0)


def student_kernel(student_ref, top_ref, total_ref):
    docs, positions, columns = student_ref.shape
    rows = docs * positions
    peak = jnp.full((rows, BLK), -jnp.inf, jnp.float32)
    for b in range(columns // BLK):
        part = student_ref[:, :, b * BLK : (b + 1) * BLK].reshape(rows, BLK).astype(jnp.float32)
        peak = jnp.maximum(peak, part)
    top = jnp.max(peak, axis=1, keepdims=True)
    total = jnp.zeros((rows, BLK), jnp.float32)
    for b in range(columns // BLK):
        part = student_ref[:, :, b * BLK : (b + 1) * BLK].reshape(rows, BLK).astype(jnp.float32)
        total = total + jnp.exp(part - top)
    top_ref[...] = jnp.broadcast_to(top, (rows, BLK))
    total_ref[...] = jnp.broadcast_to(jnp.sum(total, axis=1, keepdims=True), (rows, BLK))


def map_kernel(
    steps,
    item_ref,
    held_ref,
    ahead_ref,
    behind_ref,
    spread_ref,
    weight_ref,
    student_ref,
    top_ref,
    total_ref,
    out_ref,
    stage_ref,
    scale_ref,
):
    docs, positions, columns = student_ref.shape
    rows = docs * positions
    blocks = columns // BLK
    spread = spread_ref[...]
    for i in range(stage_ref.shape[0]):
        stage_ref[i] = held_ref[i]
    bring(item_ref, steps, ahead_ref, stage_ref)
    bring(item_ref, 2 * steps, behind_ref, stage_ref)
    holders = [h for h in range(steps + 1)] + [2 * steps + h for h in range(1, steps)]
    peaks, sums = [], []
    for h in holders:
        stats = jnp.dot(spread, stage_ref[K * blocks + h], preferred_element_type=jnp.float32)
        peaks.append(stats[:, 0:1])
        sums.append(stats[:, 1:2] + stats[:, 2:3] + stats[:, 3:4])
    peak = functools.reduce(jnp.maximum, peaks)
    powers = [jnp.exp(p - peak) for p in peaks]
    norm = sum(p * t for p, t in zip(powers, sums))
    for h, power in zip(holders, powers):
        scale_ref[h] = jnp.broadcast_to(power / norm, (rows, BLK))
    student_top = top_ref[...]
    mass = jnp.zeros((rows, BLK), jnp.float32)
    cross = jnp.zeros((rows, BLK), jnp.float32)
    for b in range(blocks):
        picked = jnp.concatenate([stage_ref[K * b], stage_ref[K * b + 1]], axis=1)
        prob = jnp.dot(spread, picked, preferred_element_type=jnp.float32).astype(jnp.bfloat16)
        mapped = scale_ref[item_ref[1, K * b]] * jnp.dot(
            prob[:, :BLK], weight_ref[:, K * b].reshape(BLK, BLK), preferred_element_type=jnp.float32
        ) + scale_ref[item_ref[1, K * b + 1]] * jnp.dot(
            prob[:, BLK:], weight_ref[:, K * b + 1].reshape(BLK, BLK), preferred_element_type=jnp.float32
        )
        logit = student_ref[:, :, b * BLK : (b + 1) * BLK].reshape(rows, BLK).astype(jnp.float32) - student_top
        mass = mass + mapped
        cross = cross + mapped * (jnp.log(jnp.maximum(mapped, TINY)) - logit)
    mass = jnp.sum(mass, axis=1, keepdims=True)
    cross = jnp.sum(cross, axis=1, keepdims=True)
    lane = lax.broadcasted_iota(jnp.int32, (rows, BLK), 1)
    table = jnp.where(
        lane == 0, mass, jnp.where(lane == 1, cross, jnp.where(lane == 2, student_top, total_ref[...]))
    )
    out_ref[...] = table.T[:8]


def whole(padded_parts, cand, src_block, weights, student_logits):
    doc_count, pos_count, student_cols = student_logits.shape
    teacher_cols = padded_parts[0].shape[2]
    teacher_blocks = teacher_cols // BLK
    student_blocks = student_cols // BLK
    row_count = doc_count * pos_count
    padded = jnp.concatenate(padded_parts, axis=1).reshape(-1, teacher_cols)
    teacher_float = jnp.take(padded, cand, axis=0).astype(jnp.float32)
    student_float = student_logits.reshape(row_count, student_cols).astype(jnp.float32)
    teacher_peak = jnp.max(teacher_float, axis=1)
    student_peak = jnp.max(student_float, axis=1)
    teacher_top, student_top = lax.pmax((teacher_peak, student_peak), "vocab")
    teacher_total, student_total = lax.psum(
        (
            jnp.sum(jnp.exp(teacher_float - teacher_top[:, None]), axis=1),
            jnp.sum(jnp.exp(student_float - student_top[:, None]), axis=1),
        ),
        "vocab",
    )
    teacher_prob = (jnp.exp(teacher_float - teacher_top[:, None]) / teacher_total[:, None]).astype(jnp.bfloat16)
    student_logprob = student_float - student_top[:, None] - jnp.log(student_total)[:, None]
    vocab_count = lax.axis_size("vocab")
    own_index = lax.axis_index("vocab")
    pair_count = student_blocks * K
    capacity = 2 * K * student_blocks // vocab_count
    pair_blocks = src_block.reshape(vocab_count, pair_count)
    holder = pair_blocks // teacher_blocks
    inside = pair_blocks % teacher_blocks
    same_holder = holder[:, :, None] == holder[:, None, :]
    before = jnp.arange(pair_count)[None, :] < jnp.arange(pair_count)[:, None]
    slot_rank = jnp.sum(same_holder & before[None, :, :], axis=2)
    chosen = (holder == own_index)[:, None, :] & (
        slot_rank[:, None, :] == jnp.arange(capacity)[None, :, None]
    )
    send_index = jnp.sum(jnp.where(chosen, inside[:, None, :], 0), axis=2)
    prob_blocks = teacher_prob.reshape(row_count, teacher_blocks, BLK)
    outgoing = jnp.take(prob_blocks, send_index.reshape(-1), axis=1).reshape(row_count, vocab_count, capacity, BLK)
    incoming = lax.all_to_all(outgoing, "vocab", split_axis=1, concat_axis=1, tiled=True)
    own_holder = jnp.take(holder, own_index, axis=0)
    own_rank = jnp.take(slot_rank, own_index, axis=0)
    recv_slot = own_holder * capacity + own_rank
    gathered = jnp.take(incoming.reshape(row_count, vocab_count * capacity, BLK), recv_slot, axis=1).reshape(
        row_count, student_blocks, K, BLK
    )
    weights = weights.swapaxes(0, 1).reshape(student_blocks, K, BLK, BLK)
    mapped = jnp.einsum("rbkc,bkcd->rbd", gathered, weights, preferred_element_type=jnp.float32).reshape(
        row_count, student_cols
    )
    total_mass = lax.psum(jnp.sum(mapped, axis=1), "vocab")
    normed = mapped / total_mass[:, None]
    return lax.psum(
        jnp.sum(jax.scipy.special.xlogy(normed, normed) - normed * student_logprob, axis=1), "vocab"
    )


def shards(teacher_logits, student_logits, alignment, src_block, margin_weight):
    doc_count, pos_count, teacher_cols = teacher_logits.shape
    student_cols = student_logits.shape[2]
    teacher_blocks = teacher_cols // BLK
    student_blocks = student_cols // BLK
    row_count = doc_count * pos_count
    pair_count = student_blocks * K
    vocab_count = lax.axis_size("vocab")
    steps = vocab_count // 2
    home = teacher_blocks + 1
    vocab_index = lax.axis_index("vocab")
    seq_index = lax.axis_index("seq")
    sign = 1 - 2 * (seq_index % 2)
    span = pos_count + 2 * W

    with jax.named_scope("halo"):
        low, high = halo(teacher_logits, W)
    with jax.named_scope("weights"):
        weights = lax.all_gather(
            margin_weight.reshape(pair_count, -1, BLK), "dp", axis=0, tiled=False
        )

    with jax.named_scope("rows"):
        cand = (alignment - seq_index * pos_count + W + jnp.arange(doc_count)[:, None] * span).reshape(-1)
        cand = jnp.clip(cand, 0, doc_count * span - 1)
        places = jnp.arange(doc_count * span)
        used = jnp.any(cand[:, None] == places[None, :], axis=0)
        place_rank = jnp.sum(used[:, None] & (places[:, None] < places[None, :]), axis=0)
        cand_rank = jnp.sum(used[None, :] & (places[None, :] < cand[:, None]), axis=1)
        row_ids = jnp.arange(ROWS)
        pick = ((row_ids[:, None] == place_rank[None, :]) & used[None, :]).astype(jnp.bfloat16)
        spread = (cand_rank[:, None] == row_ids[None, :]).astype(jnp.bfloat16)
        rows_fit = jnp.sum(used.astype(jnp.int32)) <= ROWS

    vmem = pl.BlockSpec(memory_space=pltpu.VMEM)
    smem = pl.BlockSpec(memory_space=pltpu.SMEM)
    def room(mib):
        return pltpu.CompilerParams(vmem_limit_bytes=mib * 1024 * 1024)

    with jax.named_scope("plan"):
        listed = src_block.reshape(vocab_count, pair_count)
        table = jax.ShapeDtypeStruct((8, BLK), jnp.int32)
        send, items, left = pl.pallas_call(
            functools.partial(plan_kernel, teacher_blocks),
            out_shape=(jax.ShapeDtypeStruct((8, 2 * BLK), jnp.int32), table, table),
            in_specs=[smem, vmem],
            out_specs=(vmem,) * 3,
            scratch_shapes=[pltpu.VMEM((6 * steps, vocab_count, BLK), jnp.float32)],
            compiler_params=room(16),
        )(jnp.stack([vocab_index, sign]).astype(jnp.int32), listed)

    def planes(count):
        return jax.ShapeDtypeStruct((count, ROWS, BLK), jnp.bfloat16)

    with jax.named_scope("pack"):
        own, ahead, behind = pl.pallas_call(
            pack_kernel,
            out_shape=(planes(home), planes(SLOTS), planes(SLOTS)),
            in_specs=[vmem] * 5,
            out_specs=(vmem,) * 3,
            scratch_shapes=[
                pltpu.VMEM((doc_count * span, teacher_cols), jnp.bfloat16),
                pltpu.VMEM((teacher_blocks, ROWS, BLK), jnp.bfloat16),
            ],
            compiler_params=room(24),
        )(send, teacher_logits, low, high, pick)

    def chosen(chain, step, frames):
        part = pl.pallas_call(
            functools.partial(ready_kernel, chain, step),
            out_shape=planes(SLOTS),
            in_specs=[vmem] * (1 + len(frames)),
            out_specs=vmem,
            compiler_params=room(12),
        )(send, own, *frames[:-1])
        return pl.pallas_call(
            functools.partial(pass_kernel, chain, step, home),
            out_shape=planes(SLOTS),
            in_specs=[vmem] * 3,
            out_specs=vmem,
            compiler_params=room(8),
        )(send, part, frames[-1])

    with jax.named_scope("ring"):
        forward, backward = ring_pairs(1), ring_pairs(-1)
        came_ahead, came_behind = [], []
        for step in range(steps):
            if step:
                ahead = chosen(0, step, came_ahead)
            came_ahead.append(lax.ppermute(ahead, ("seq", "vocab"), forward))
            if step:
                behind = chosen(1, step, came_behind)
            came_behind.append(lax.ppermute(behind, ("seq", "vocab"), backward))

    with jax.named_scope("student"):
        top, total = pl.pallas_call(
            student_kernel,
            out_shape=(jax.ShapeDtypeStruct((row_count, BLK), jnp.float32),) * 2,
            in_specs=[vmem],
            out_specs=(vmem,) * 2,
            compiler_params=room(16),
        )(student_logits)

    with jax.named_scope("stage"):
        early = (own, *came_ahead[:-1], *came_behind[:-1])
        held = pl.pallas_call(
            functools.partial(stage_kernel, steps),
            out_shape=planes(pair_count + 2 * vocab_count),
            in_specs=[smem] + [vmem] * len(early),
            out_specs=vmem,
            compiler_params=room(20),
        )(items, *early)

    with jax.named_scope("map"):
        sums = pl.pallas_call(
            functools.partial(map_kernel, steps),
            out_shape=jax.ShapeDtypeStruct((8, row_count), jnp.float32),
            in_specs=[smem] + [vmem] * 8,
            out_specs=vmem,
            scratch_shapes=[
                pltpu.VMEM((pair_count + 2 * vocab_count, ROWS, BLK), jnp.bfloat16),
                pltpu.VMEM((3 * steps, row_count, BLK), jnp.float32),
            ],
            compiler_params=room(16),
        )(items, held, came_ahead[-1], came_behind[-1], spread, weights, student_logits, top, total)

    with jax.named_scope("finish"):
        sent = jnp.broadcast_to(sums[None, :4], (vocab_count, 4, row_count))
        parts = lax.all_to_all(sent, "vocab", split_axis=0, concat_axis=0, tiled=True)
        mass_part, cross_part, top_part, total_part = (parts[:, i] for i in range(4))
        student_top = jnp.max(top_part, axis=0)
        log_total = student_top + jnp.log(jnp.sum(jnp.exp(top_part - student_top) * total_part, axis=0))
        mass = jnp.sum(mass_part, axis=0)
        result = jnp.sum(cross_part + mass_part * (log_total - top_part), axis=0) / mass - jnp.log(mass)

    result = lax.cond(
        rows_fit & (left[0, 0] == 0),
        lambda *_: result,
        lambda *operands: whole(operands[:3], *operands[3:]),
        low,
        teacher_logits,
        high,
        cand,
        src_block,
        weights,
        student_logits,
    )
    return result.reshape(doc_count, pos_count)


def solution(mesh):
    in_specs = (
        P("dp", "seq", "vocab"),
        P("dp", "seq", "vocab"),
        P("dp", "seq"),
        P(),
        P("vocab", None, "dp", None),
    )
    out_specs = P("dp", "seq")
    return jax.shard_map(shards, mesh=mesh, in_specs=in_specs, out_specs=out_specs, check_vma=False)
```

```python
import functools

import jax
import jax.numpy as jnp
from jax import lax
from jax.experimental import pallas as pl
from jax.experimental.pallas import tpu as pltpu
from jax.sharding import PartitionSpec as P

BLK = 128
K = 2
W = 16
ROWS = 104
SLOTS = 21
TINY = 1.2e-38


def halo(block, width):
    count = lax.axis_size("seq")
    forward = [(i, i + 1) for i in range(count - 1)]
    backward = [(target, source) for source, target in forward]
    low = lax.ppermute(block[:, block.shape[1] - width :], "seq", forward)
    high = lax.ppermute(block[:, :width], "seq", backward)
    return low, high


def ring_pairs(turn):
    seq_count, vocab_count = lax.axis_size("seq"), lax.axis_size("vocab")
    pairs = []
    for s in range(seq_count):
        step = turn if s % 2 == 0 else -turn
        for v in range(vocab_count):
            pairs.append((s * vocab_count + v, s * vocab_count + (v + step) % vocab_count))
    return pairs


def ways(distance, block, share, vocab_count):
    half = vocab_count // 2
    first = (block * 5) % 8 < share
    ahead = jnp.where((distance >= 1) & ((distance < half) | ((distance == half) & first)), distance, 0)
    behind = jnp.where((distance > half) | ((distance == half) & ~first), vocab_count - distance, 0)
    return ahead, behind


def ones(mask):
    return jnp.where(mask, 1.0, 0.0).astype(jnp.bfloat16)


def plan_kernel(blocks, place_ref, listed_ref, send_ref, item_ref, fit_ref, book_ref):
    vocab_count, pair_count = listed_ref.shape
    half = vocab_count // 2
    steps = half
    home = blocks + 1
    me, sign = place_ref[0], place_ref[1]
    f32, i32 = jnp.float32, jnp.int32
    shape = (vocab_count, BLK)

    def split(listed):
        holder = sum((listed >= h * blocks).astype(i32) for h in range(1, vocab_count))
        return holder, listed - holder * blocks

    listed = listed_ref[...]
    wide = jnp.concatenate([listed, jnp.zeros((vocab_count, BLK - pair_count), i32)], axis=1)
    tall = jnp.concatenate([wide, jnp.zeros((BLK - vocab_count, BLK), i32)], axis=0).astype(f32).T.astype(i32)
    row_holder, _ = split(listed)
    holders, inners = split(tall[:pair_count])
    lane = lax.broadcasted_iota(i32, shape, 1)
    row = lax.broadcasted_iota(i32, shape, 0)

    reach = [jnp.zeros(shape, i32), jnp.zeros(shape, i32)]
    across = jnp.zeros(shape, i32)
    pair_lane = lax.broadcasted_iota(i32, (pair_count, BLK), 1)
    pair_row = lax.broadcasted_iota(i32, (vocab_count, pair_count), 0)
    for s in range(vocab_count):
        hits = jnp.dot(
            ones(pair_row == row_holder[s : s + 1, :]),
            ones(pair_lane == inners[:, s : s + 1]),
            preferred_element_type=f32,
        )
        distance = s - row
        distance = jnp.where(distance < 0, distance + vocab_count, distance)
        needed = hits > 0
        reach[0] = jnp.maximum(reach[0], jnp.where(needed & (distance < half), distance, 0))
        reach[1] = jnp.maximum(reach[1], jnp.where(needed & (distance > half), vocab_count - distance, 0))
        across = jnp.maximum(across, jnp.where(needed & (distance == half), 1, 0))
    order_key = (lane * 5) % 8
    share = jnp.zeros((1, 1), i32)
    for part in range(1, 9):
        first = (across > 0) & (order_key < part)
        more = jnp.where(first, half, reach[0]) - jnp.where((across > 0) & ~first, half, reach[1])
        more = jnp.sum(jnp.sum(more, axis=1, keepdims=True), axis=0, keepdims=True)
        share = share + (more <= 0).astype(i32)
    first = order_key < share
    reach[0] = jnp.where((across > 0) & first, half, reach[0])
    reach[1] = jnp.where((across > 0) & ~first, half, reach[1])
    reach = [jnp.where(lane == blocks, half - way, reach[way]) for way in range(2)]

    square = (BLK, BLK)
    up, over = lax.broadcasted_iota(i32, square, 0), lax.broadcasted_iota(i32, square, 1)
    earlier = ones(up < over)
    left_up, left_over = (up & 7) + 1 - (up >> 3), (over & 7) + 1 - (over >> 3)
    goes_first = ones((left_up > left_over) | ((left_up == left_over) & ((up >> 3) > (over >> 3))))
    index, waiting, moved = [], [], [jnp.zeros(shape, f32)] * 2
    for way in range(2):
        masks = jnp.concatenate([ones(reach[way] == r) for r in range(1, half + 1)], axis=0)
        before = jnp.dot(masks, earlier, preferred_element_type=f32)
        place = jnp.zeros(shape, f32)
        count = jnp.zeros(shape, f32)
        for r in range(1, half + 1):
            same = reach[way] == r
            place = jnp.where(same, before[(r - 1) * vocab_count : r * vocab_count], place)
            total = jnp.sum(jnp.where(same, 1.0, 0.0), axis=1, keepdims=True)
            count = jnp.where(lane == r - 1, total, count)
        index.append(place)
        waiting.append(count)
    travels = (lane >= 8) & (lane < 8 * half) & ((lane & 7) + 1 > (lane >> 3))
    for f in range(steps):
        ahead_of = jnp.dot(
            jnp.concatenate(waiting, axis=0).astype(jnp.bfloat16), goes_first, preferred_element_type=f32
        )
        for way in range(2):
            first = ahead_of[way * vocab_count : (way + 1) * vocab_count]
            go = jnp.clip(SLOTS - first, 0.0, waiting[way])
            book_ref[(f * 2 + way) * 3] = moved[way]
            moved[way] = moved[way] + go
            book_ref[(f * 2 + way) * 3 + 1] = moved[way]
            book_ref[(f * 2 + way) * 3 + 2] = jnp.minimum(first, float(SLOTS))
            come = pltpu.roll(pltpu.roll(go, 8, 1), 1 if way == 0 else vocab_count - 1, 0)
            waiting[way] = waiting[way] - go + jnp.where(travels, come, 0.0)
    left = jnp.sum(waiting[0] + waiting[1], axis=1, keepdims=True)
    left = jnp.sum(jnp.broadcast_to(left, shape), axis=0, keepdims=True)
    fit_ref[...] = jnp.broadcast_to(left, fit_ref.shape).astype(i32)

    small = (vocab_count, vocab_count)
    target = lax.broadcasted_iota(i32, (BLK, 2 * BLK), 1).astype(f32)
    pointer, sends = [], []
    for way in range(2):
        step = 1 if way == 0 else -1
        back = me - step * lax.broadcasted_iota(i32, small, 0)
        back = jnp.where(back < 0, back + vocab_count, jnp.where(back >= vocab_count, back - vocab_count, back))
        pick = ones(back == lax.broadcasted_iota(i32, small, 1))
        far = jnp.dot(pick, reach[way].astype(f32).astype(jnp.bfloat16), preferred_element_type=f32).astype(i32)
        order = jnp.dot(pick, index[way].astype(jnp.bfloat16), preferred_element_type=f32)
        giver = me - step
        giver = jnp.where(giver < 0, giver + vocab_count, jnp.where(giver >= vocab_count, giver - vocab_count, giver))

        def slot(at, hops, valid):
            column = jnp.clip(hops * 8 + far - 1, 0, BLK - 1)
            where = jnp.full(shape, -1.0, f32)
            for f in range(steps):
                start, end, first = (
                    jnp.take_along_axis(
                        jnp.broadcast_to(book_ref[(f * 2 + way) * 3 + kind, pl.ds(at, 1), :], shape),
                        column,
                        axis=1,
                        mode="promise_in_bounds",
                    )
                    for kind in range(3)
                )
                now = valid & (start <= order) & (order < end)
                where = jnp.where(now, f * SLOTS + first + order - start, where)
            return where

        leave = slot(me, row, (far > row) & (row < half))
        arrive = slot(giver, row - 1, (far >= row) & (row >= 1) & (row <= half))
        point = jnp.where(row == 0, lane.astype(f32), jnp.maximum(home + arrive, 0.0))
        pointer.append(point)
        leave_turned = jnp.concatenate([leave, jnp.full((BLK - vocab_count, BLK), -1.0, f32)], axis=0).T
        chosen = jnp.zeros((1, 2 * BLK), f32)
        for h in range(half):
            chosen = chosen + jnp.dot(
                point[h : h + 1].astype(jnp.bfloat16),
                ones(leave_turned[:, h : h + 1] == target),
                preferred_element_type=f32,
            )
        sends.append(chosen.astype(i32))
    straight = sign > 0
    send_ref[0:1, :] = jnp.where(straight, sends[0], sends[1])
    send_ref[1:2, :] = jnp.where(straight, sends[1], sends[0])
    send_ref[2:8, :] = jnp.zeros((6, 2 * BLK), i32)

    mine_lane = lax.broadcasted_iota(i32, (pair_count, vocab_count), 1)
    holder = jnp.sum(jnp.where(pair_lane == me, holders, 0), axis=1, keepdims=True)
    inner = jnp.sum(jnp.where(pair_lane == me, inners, 0), axis=1, keepdims=True)
    distance = me - holder
    distance = jnp.where(distance < 0, distance + vocab_count, distance)
    hops = ways(distance, inner, share, vocab_count)
    scale = jnp.where(distance <= half, distance, 2 * vocab_count - distance)
    points = jnp.zeros((pair_count, 1), f32)
    for way in range(2):
        found = lax.dot_general(
            ones(pair_lane == inner),
            pointer[way].astype(jnp.bfloat16),
            (((1,), (1,)), ((), ())),
            preferred_element_type=f32,
        )
        points = points + jnp.sum(
            jnp.where((mine_lane == hops[way]) & (hops[way] > 0), found, 0.0), axis=1, keepdims=True
        )
    points = jnp.where(distance == 0, inner.astype(f32), points)
    by_stats = [jnp.sum(jnp.where(lane == blocks, p, 0.0), axis=1, keepdims=True) for p in pointer]
    hop = lax.broadcasted_iota(i32, (vocab_count, 1), 0)
    stat_ok = [hop <= half, (hop >= 1) & (hop < half)]
    points = jnp.concatenate(
        [points] + [jnp.where(ok, p, 0.0) for ok, p in zip(stat_ok, by_stats)], axis=0
    ).astype(i32)
    other = jnp.concatenate(
        [(hops[1] > 0).astype(i32), jnp.zeros((vocab_count, 1), i32), jnp.ones((vocab_count, 1), i32)], axis=0
    )
    other = jnp.where(straight, other, 1 - other)
    scale = jnp.concatenate([scale, jnp.zeros((2 * vocab_count, 1), i32)], axis=0)
    frame = jnp.zeros(points.shape, i32)
    for f in range(1, steps):
        frame = frame + (points >= home + f * SLOTS).astype(i32)
    away = points >= home
    source = jnp.where(away, 1 + frame + steps * other, 0)
    spot = jnp.where(away, points - home - frame * SLOTS, points)
    spot = jnp.clip(spot, 0, jnp.where(away, SLOTS - 1, home - 1))
    items = points.shape[0]
    item_lane = lax.broadcasted_iota(i32, (items, BLK), 1)
    table = jnp.where(
        item_lane == 0, spot, jnp.where(item_lane == 1, scale, jnp.where(item_lane == 2, source, 0))
    ).astype(f32)
    turned = jnp.concatenate([table, jnp.zeros((BLK - items, BLK), f32)], axis=0).T
    source_row = turned[2:3].astype(i32)
    item_up = lax.broadcasted_iota(i32, (items, BLK), 0)
    is_item = item_lane < items
    sooner = is_item & ((source_row < source) | ((source_row == source) & (item_lane < item_up)))
    rank = jnp.sum(sooner.astype(i32), axis=1, keepdims=True)
    item_ref[0:1, :] = turned[0:1].astype(i32)
    item_ref[1:2, :] = turned[1:2].astype(i32)
    item_ref[2:3, :] = jnp.sum(jnp.where(rank == item_lane, item_up, 0), axis=0, keepdims=True)
    item_ref[3:4, :] = jnp.sum((source < item_lane).astype(i32), axis=0, keepdims=True)
    item_ref[4:8, :] = jnp.zeros((4, BLK), i32)


def scalars(table_ref, row, start, count):
    values = table_ref[row : row + 1, :]
    return [values[0, start + j] for j in range(count)]


def pack_kernel(send_ref, own_ref, low_ref, high_ref, pick_ref, home_ref, first_ref, second_ref, cand_ref, logit_ref):
    docs, positions, columns = own_ref.shape
    width = low_ref.shape[1]
    span = positions + 2 * width
    rows = pick_ref.shape[0]
    blocks = columns // BLK
    for doc in range(docs):
        cand_ref[doc * span : doc * span + width, :] = low_ref[doc]
        cand_ref[doc * span + width : doc * span + width + positions, :] = own_ref[doc]
        cand_ref[doc * span + width + positions : (doc + 1) * span, :] = high_ref[doc]
    pick = pick_ref[...]
    peak = jnp.full((rows, BLK), -jnp.inf, jnp.float32)
    for t in range(blocks):
        part = jnp.dot(pick, cand_ref[:, t * BLK : (t + 1) * BLK], preferred_element_type=jnp.float32)
        logit_ref[t] = part.astype(jnp.bfloat16)
        peak = jnp.maximum(peak, part)
    top = jnp.max(peak, axis=1, keepdims=True)
    total = jnp.zeros((rows, BLK), jnp.float32)
    for t in range(blocks):
        power = jnp.exp(logit_ref[t].astype(jnp.float32) - top)
        total = total + power
        home_ref[t] = power.astype(jnp.bfloat16)
    total = jnp.sum(total, axis=1, keepdims=True)
    first = total.astype(jnp.bfloat16).astype(jnp.float32)
    second = (total - first).astype(jnp.bfloat16).astype(jnp.float32)
    third = total - first - second
    lane = lax.broadcasted_iota(jnp.int32, (rows, BLK), 1)
    home_ref[blocks] = jnp.where(
        lane == 0, top, jnp.where(lane == 1, first, jnp.where(lane == 2, second, jnp.where(lane == 3, third, 0.0)))
    ).astype(jnp.bfloat16)
    for chain, out_ref in enumerate((first_ref, second_ref)):
        for j, at in enumerate(scalars(send_ref, chain, 0, SLOTS)):
            out_ref[j] = home_ref[at]


def ready_kernel(chain, step, send_ref, home_ref, *refs):
    frames, out_ref = refs[:-1], refs[-1]
    home = home_ref.shape[0]
    for j, at in enumerate(scalars(send_ref, chain, step * SLOTS, SLOTS)):

        def copy(low, high, j=j, at=at):
            if high - low == 1:
                if low == 0:
                    out_ref[j] = home_ref[at]
                elif low <= len(frames):
                    out_ref[j] = frames[low - 1][at - home - (low - 1) * SLOTS]
                return
            mid = (low + high) // 2
            split = home + (mid - 1) * SLOTS
            pl.when(at < split)(lambda: copy(low, mid))
            pl.when(at >= split)(lambda: copy(mid, high))

        copy(0, len(frames) + 2)


def pass_kernel(chain, step, home, send_ref, part_ref, newest_ref, out_ref):
    start = home + (step - 1) * SLOTS
    for j, at in enumerate(scalars(send_ref, chain, step * SLOTS, SLOTS)):
        newest = newest_ref[jnp.maximum(at - start, 0)]
        out_ref[j] = jnp.where(at >= start, newest, part_ref[j])


def stage_kernel(steps, item_ref, *refs):
    sources, stage_ref = refs[:-1], refs[-1]
    for s, source in zip([s for s in range(2 * steps + 1) if s not in (steps, 2 * steps)], sources):
        bring(item_ref, s, source, stage_ref)


def bring(item_ref, s, source_ref, stage_ref):
    def one(q, carry):
        item = item_ref[2, q]
        stage_ref[item] = source_ref[item_ref[0, item]]
        return carry

    lax.fori_loop(item_ref[3, s], item_ref[3, s + 1], one, 0)


def student_kernel(student_ref, top_ref, total_ref):
    docs, positions, columns = student_ref.shape
    rows = docs * positions
    peak = jnp.full((rows, BLK), -jnp.inf, jnp.float32)
    for b in range(columns // BLK):
        part = student_ref[:, :, b * BLK : (b + 1) * BLK].reshape(rows, BLK).astype(jnp.float32)
        peak = jnp.maximum(peak, part)
    top = jnp.max(peak, axis=1, keepdims=True)
    total = jnp.zeros((rows, BLK), jnp.float32)
    for b in range(columns // BLK):
        part = student_ref[:, :, b * BLK : (b + 1) * BLK].reshape(rows, BLK).astype(jnp.float32)
        total = total + jnp.exp(part - top)
    top_ref[...] = jnp.broadcast_to(top, (rows, BLK))
    total_ref[...] = jnp.broadcast_to(jnp.sum(total, axis=1, keepdims=True), (rows, BLK))


def map_kernel(
    steps,
    item_ref,
    held_ref,
    ahead_ref,
    behind_ref,
    spread_ref,
    weight_ref,
    student_ref,
    top_ref,
    total_ref,
    out_ref,
    stage_ref,
    scale_ref,
):
    docs, positions, columns = student_ref.shape
    rows = docs * positions
    blocks = columns // BLK
    spread = spread_ref[...]
    for i in range(stage_ref.shape[0]):
        stage_ref[i] = held_ref[i]
    bring(item_ref, steps, ahead_ref, stage_ref)
    bring(item_ref, 2 * steps, behind_ref, stage_ref)
    holders = [h for h in range(steps + 1)] + [2 * steps + h for h in range(1, steps)]
    peaks, sums = [], []
    for h in holders:
        stats = jnp.dot(spread, stage_ref[K * blocks + h], preferred_element_type=jnp.float32)
        peaks.append(stats[:, 0:1])
        sums.append(stats[:, 1:2] + stats[:, 2:3] + stats[:, 3:4])
    peak = functools.reduce(jnp.maximum, peaks)
    powers = [jnp.exp(p - peak) for p in peaks]
    norm = sum(p * t for p, t in zip(powers, sums))
    for h, power in zip(holders, powers):
        scale_ref[h] = jnp.broadcast_to(power / norm, (rows, BLK))
    student_top = top_ref[...]
    mass = jnp.zeros((rows, BLK), jnp.float32)
    cross = jnp.zeros((rows, BLK), jnp.float32)
    for b in range(blocks):
        picked = jnp.concatenate([stage_ref[K * b], stage_ref[K * b + 1]], axis=1)
        prob = jnp.dot(spread, picked, preferred_element_type=jnp.float32).astype(jnp.bfloat16)
        mapped = scale_ref[item_ref[1, K * b]] * jnp.dot(
            prob[:, :BLK], weight_ref[:, K * b].reshape(BLK, BLK), preferred_element_type=jnp.float32
        ) + scale_ref[item_ref[1, K * b + 1]] * jnp.dot(
            prob[:, BLK:], weight_ref[:, K * b + 1].reshape(BLK, BLK), preferred_element_type=jnp.float32
        )
        logit = student_ref[:, :, b * BLK : (b + 1) * BLK].reshape(rows, BLK).astype(jnp.float32) - student_top
        mass = mass + mapped
        cross = cross + mapped * (jnp.log(jnp.maximum(mapped, TINY)) - logit)
    mass = jnp.sum(mass, axis=1, keepdims=True)
    cross = jnp.sum(cross, axis=1, keepdims=True)
    lane = lax.broadcasted_iota(jnp.int32, (rows, BLK), 1)
    table = jnp.where(
        lane == 0, mass, jnp.where(lane == 1, cross, jnp.where(lane == 2, student_top, total_ref[...]))
    )
    out_ref[...] = table.T[:8]


def whole(padded_parts, cand, src_block, weights, student_logits):
    doc_count, pos_count, student_cols = student_logits.shape
    teacher_cols = padded_parts[0].shape[2]
    teacher_blocks = teacher_cols // BLK
    student_blocks = student_cols // BLK
    row_count = doc_count * pos_count
    padded = jnp.concatenate(padded_parts, axis=1).reshape(-1, teacher_cols)
    teacher_float = jnp.take(padded, cand, axis=0).astype(jnp.float32)
    student_float = student_logits.reshape(row_count, student_cols).astype(jnp.float32)
    teacher_peak = jnp.max(teacher_float, axis=1)
    student_peak = jnp.max(student_float, axis=1)
    teacher_top, student_top = lax.pmax((teacher_peak, student_peak), "vocab")
    teacher_total, student_total = lax.psum(
        (
            jnp.sum(jnp.exp(teacher_float - teacher_top[:, None]), axis=1),
            jnp.sum(jnp.exp(student_float - student_top[:, None]), axis=1),
        ),
        "vocab",
    )
    teacher_prob = (jnp.exp(teacher_float - teacher_top[:, None]) / teacher_total[:, None]).astype(jnp.bfloat16)
    student_logprob = student_float - student_top[:, None] - jnp.log(student_total)[:, None]
    vocab_count = lax.axis_size("vocab")
    own_index = lax.axis_index("vocab")
    pair_count = student_blocks * K
    capacity = 2 * K * student_blocks // vocab_count
    pair_blocks = src_block.reshape(vocab_count, pair_count)
    holder = pair_blocks // teacher_blocks
    inside = pair_blocks % teacher_blocks
    same_holder = holder[:, :, None] == holder[:, None, :]
    before = jnp.arange(pair_count)[None, :] < jnp.arange(pair_count)[:, None]
    slot_rank = jnp.sum(same_holder & before[None, :, :], axis=2)
    chosen = (holder == own_index)[:, None, :] & (
        slot_rank[:, None, :] == jnp.arange(capacity)[None, :, None]
    )
    send_index = jnp.sum(jnp.where(chosen, inside[:, None, :], 0), axis=2)
    prob_blocks = teacher_prob.reshape(row_count, teacher_blocks, BLK)
    outgoing = jnp.take(prob_blocks, send_index.reshape(-1), axis=1).reshape(row_count, vocab_count, capacity, BLK)
    incoming = lax.all_to_all(outgoing, "vocab", split_axis=1, concat_axis=1, tiled=True)
    own_holder = jnp.take(holder, own_index, axis=0)
    own_rank = jnp.take(slot_rank, own_index, axis=0)
    recv_slot = own_holder * capacity + own_rank
    gathered = jnp.take(incoming.reshape(row_count, vocab_count * capacity, BLK), recv_slot, axis=1).reshape(
        row_count, student_blocks, K, BLK
    )
    weights = weights.swapaxes(0, 1).reshape(student_blocks, K, BLK, BLK)
    mapped = jnp.einsum("rbkc,bkcd->rbd", gathered, weights, preferred_element_type=jnp.float32).reshape(
        row_count, student_cols
    )
    total_mass = lax.psum(jnp.sum(mapped, axis=1), "vocab")
    normed = mapped / total_mass[:, None]
    return lax.psum(
        jnp.sum(jax.scipy.special.xlogy(normed, normed) - normed * student_logprob, axis=1), "vocab"
    )


def shards(teacher_logits, student_logits, alignment, src_block, margin_weight):
    doc_count, pos_count, teacher_cols = teacher_logits.shape
    student_cols = student_logits.shape[2]
    teacher_blocks = teacher_cols // BLK
    student_blocks = student_cols // BLK
    row_count = doc_count * pos_count
    pair_count = student_blocks * K
    vocab_count = lax.axis_size("vocab")
    steps = vocab_count // 2
    home = teacher_blocks + 1
    vocab_index = lax.axis_index("vocab")
    seq_index = lax.axis_index("seq")
    sign = 1 - 2 * (seq_index % 2)
    span = pos_count + 2 * W

    with jax.named_scope("halo"):
        low, high = halo(teacher_logits, W)
    with jax.named_scope("weights"):
        weights = lax.all_gather(
            margin_weight.reshape(pair_count, -1, BLK), "dp", axis=0, tiled=False
        )

    with jax.named_scope("rows"):
        cand = (alignment - seq_index * pos_count + W + jnp.arange(doc_count)[:, None] * span).reshape(-1)
        cand = jnp.clip(cand, 0, doc_count * span - 1)
        places = jnp.arange(doc_count * span)
        used = jnp.any(cand[:, None] == places[None, :], axis=0)
        place_rank = jnp.sum(used[:, None] & (places[:, None] < places[None, :]), axis=0)
        cand_rank = jnp.sum(used[None, :] & (places[None, :] < cand[:, None]), axis=1)
        row_ids = jnp.arange(ROWS)
        pick = ((row_ids[:, None] == place_rank[None, :]) & used[None, :]).astype(jnp.bfloat16)
        spread = (cand_rank[:, None] == row_ids[None, :]).astype(jnp.bfloat16)
        rows_fit = jnp.sum(used.astype(jnp.int32)) <= ROWS

    vmem = pl.BlockSpec(memory_space=pltpu.VMEM)
    smem = pl.BlockSpec(memory_space=pltpu.SMEM)
    def room(mib):
        return pltpu.CompilerParams(vmem_limit_bytes=mib * 1024 * 1024)

    with jax.named_scope("plan"):
        listed = src_block.reshape(vocab_count, pair_count)
        table = jax.ShapeDtypeStruct((8, BLK), jnp.int32)
        send, items, left = pl.pallas_call(
            functools.partial(plan_kernel, teacher_blocks),
            out_shape=(jax.ShapeDtypeStruct((8, 2 * BLK), jnp.int32), table, table),
            in_specs=[smem, vmem],
            out_specs=(vmem,) * 3,
            scratch_shapes=[pltpu.VMEM((6 * steps, vocab_count, BLK), jnp.float32)],
            compiler_params=room(8),
        )(jnp.stack([vocab_index, sign]).astype(jnp.int32), listed)

    def planes(count):
        return jax.ShapeDtypeStruct((count, ROWS, BLK), jnp.bfloat16)

    with jax.named_scope("pack"):
        own, ahead, behind = pl.pallas_call(
            pack_kernel,
            out_shape=(planes(home), planes(SLOTS), planes(SLOTS)),
            in_specs=[vmem] * 5,
            out_specs=(vmem,) * 3,
            scratch_shapes=[
                pltpu.VMEM((doc_count * span, teacher_cols), jnp.bfloat16),
                pltpu.VMEM((teacher_blocks, ROWS, BLK), jnp.bfloat16),
            ],
            compiler_params=room(16),
        )(send, teacher_logits, low, high, pick)

    def chosen(chain, step, frames):
        part = pl.pallas_call(
            functools.partial(ready_kernel, chain, step),
            out_shape=planes(SLOTS),
            in_specs=[vmem] * (1 + len(frames)),
            out_specs=vmem,
            compiler_params=room(8),
        )(send, own, *frames[:-1])
        return pl.pallas_call(
            functools.partial(pass_kernel, chain, step, home),
            out_shape=planes(SLOTS),
            in_specs=[vmem] * 3,
            out_specs=vmem,
            compiler_params=room(4),
        )(send, part, frames[-1])

    with jax.named_scope("ring"):
        forward, backward = ring_pairs(1), ring_pairs(-1)
        came_ahead, came_behind = [], []
        for step in range(steps):
            if step:
                ahead = chosen(0, step, came_ahead)
            came_ahead.append(lax.ppermute(ahead, ("seq", "vocab"), forward))
            if step:
                behind = chosen(1, step, came_behind)
            came_behind.append(lax.ppermute(behind, ("seq", "vocab"), backward))

    with jax.named_scope("student"):
        top, total = pl.pallas_call(
            student_kernel,
            out_shape=(jax.ShapeDtypeStruct((row_count, BLK), jnp.float32),) * 2,
            in_specs=[vmem],
            out_specs=(vmem,) * 2,
            compiler_params=room(8),
        )(student_logits)

    with jax.named_scope("stage"):
        early = (own, *came_ahead[:-1], *came_behind[:-1])
        held = pl.pallas_call(
            functools.partial(stage_kernel, steps),
            out_shape=planes(pair_count + 2 * vocab_count),
            in_specs=[smem] + [vmem] * len(early),
            out_specs=vmem,
            compiler_params=room(16),
        )(items, *early)

    with jax.named_scope("map"):
        sums = pl.pallas_call(
            functools.partial(map_kernel, steps),
            out_shape=jax.ShapeDtypeStruct((8, row_count), jnp.float32),
            in_specs=[smem] + [vmem] * 8,
            out_specs=vmem,
            scratch_shapes=[
                pltpu.VMEM((pair_count + 2 * vocab_count, ROWS, BLK), jnp.bfloat16),
                pltpu.VMEM((3 * steps, row_count, BLK), jnp.float32),
            ],
            compiler_params=room(20),
        )(items, held, came_ahead[-1], came_behind[-1], spread, weights, student_logits, top, total)

    with jax.named_scope("finish"):
        sent = jnp.broadcast_to(sums[None, :4], (vocab_count, 4, row_count))
        parts = lax.all_to_all(sent, "vocab", split_axis=0, concat_axis=0, tiled=True)
        mass_part, cross_part, top_part, total_part = (parts[:, i] for i in range(4))
        student_top = jnp.max(top_part, axis=0)
        log_total = student_top + jnp.log(jnp.sum(jnp.exp(top_part - student_top) * total_part, axis=0))
        mass = jnp.sum(mass_part, axis=0)
        result = jnp.sum(cross_part + mass_part * (log_total - top_part), axis=0) / mass - jnp.log(mass)

    result = lax.cond(
        rows_fit & (left[0, 0] == 0),
        lambda *_: result,
        lambda *operands: whole(operands[:3], *operands[3:]),
        low,
        teacher_logits,
        high,
        cand,
        src_block,
        weights,
        student_logits,
    )
    return result.reshape(doc_count, pos_count)


def solution(mesh):
    in_specs = (
        P("dp", "seq", "vocab"),
        P("dp", "seq", "vocab"),
        P("dp", "seq"),
        P(),
        P("vocab", None, "dp", None),
    )
    out_specs = P("dp", "seq")
    return jax.shard_map(shards, mesh=mesh, in_specs=in_specs, out_specs=out_specs, check_vma=False)
```

```python
import functools

import jax
import jax.numpy as jnp
from jax import lax
from jax.experimental import pallas as pl
from jax.experimental.pallas import tpu as pltpu
from jax.sharding import PartitionSpec as P

BLK = 128
K = 2
W = 16
ROWS = 104
SLOTS = 22
DIRECT = 9
TINY = 1.2e-38


def halo(block, width):
    count = lax.axis_size("seq")
    forward = [(i, i + 1) for i in range(count - 1)]
    backward = [(target, source) for source, target in forward]
    low = lax.ppermute(block[:, block.shape[1] - width :], "seq", forward)
    high = lax.ppermute(block[:, :width], "seq", backward)
    return low, high


def ring_pairs(turn):
    seq_count, vocab_count = lax.axis_size("seq"), lax.axis_size("vocab")
    pairs = []
    for s in range(seq_count):
        step = turn if s % 2 == 0 else -turn
        for v in range(vocab_count):
            pairs.append((s * vocab_count + v, s * vocab_count + (v + step) % vocab_count))
    return pairs


def ones(mask):
    return jnp.where(mask, 1.0, 0.0).astype(jnp.bfloat16)


def split(listed, blocks, vocab_count):
    holder = sum((listed >= h * blocks).astype(jnp.int32) for h in range(1, vocab_count))
    return holder, listed - holder * blocks


def turn(table):
    rows, columns = table.shape
    table = table.astype(jnp.float32)
    if columns < BLK:
        table = jnp.concatenate([table, jnp.zeros((rows, BLK - columns), jnp.float32)], axis=1)
    if rows < BLK:
        table = jnp.concatenate([table, jnp.zeros((BLK - rows, BLK), jnp.float32)], axis=0)
    return table.T.astype(jnp.int32)


def earlier_lanes():
    square = (BLK, BLK)
    return ones(lax.broadcasted_iota(jnp.int32, square, 0) < lax.broadcasted_iota(jnp.int32, square, 1))


def plan_kernel(blocks, place_ref, listed_ref, after_ref, send_ref, item_ref, fit_ref, book_ref):
    vocab_count, pair_count = listed_ref.shape
    half = vocab_count // 2
    steps = half - 1
    home = blocks + 1
    beyond = home + steps * SLOTS
    me, sign = place_ref[0], place_ref[1]
    f32, i32 = jnp.float32, jnp.int32
    shape = (vocab_count, BLK)

    del after_ref
    listed = listed_ref[...]
    row_holder, _ = split(listed, blocks, vocab_count)
    holders, inners = split(turn(listed)[:pair_count], blocks, vocab_count)
    facing = me + half
    facing = jnp.where(facing >= vocab_count, facing - vocab_count, facing)
    lane = lax.broadcasted_iota(i32, shape, 1)
    row = lax.broadcasted_iota(i32, shape, 0)

    reach = [jnp.zeros(shape, i32), jnp.zeros(shape, i32)]
    across = jnp.zeros((1, BLK), i32)
    pair_lane = lax.broadcasted_iota(i32, (pair_count, BLK), 1)
    pair_row = lax.broadcasted_iota(i32, (vocab_count, pair_count), 0)
    for s in range(vocab_count):
        hits = jnp.dot(
            ones(pair_row == row_holder[s : s + 1, :]),
            ones(pair_lane == inners[:, s : s + 1]),
            preferred_element_type=f32,
        )
        distance = s - row
        distance = jnp.where(distance < 0, distance + vocab_count, distance)
        needed = hits > 0
        reach[0] = jnp.maximum(reach[0], jnp.where(needed & (distance < half), distance, 0))
        reach[1] = jnp.maximum(reach[1], jnp.where(needed & (distance > half), vocab_count - distance, 0))
        seen = jnp.max(jnp.where(needed & (row == facing), 1, 0), axis=0, keepdims=True)
        across = jnp.maximum(across, jnp.where(me == s, seen, 0))
    reach = [jnp.where(lane == blocks, steps, r) for r in reach]

    square = (BLK, BLK)
    up, over = lax.broadcasted_iota(i32, square, 0), lax.broadcasted_iota(i32, square, 1)
    earlier = earlier_lanes()
    left_up, left_over = (up & 7) + 1 - (up >> 3), (over & 7) + 1 - (over >> 3)
    goes_first = ones((left_up > left_over) | ((left_up == left_over) & ((up >> 3) > (over >> 3))))
    index, waiting, moved = [], [], [jnp.zeros(shape, f32)] * 2
    for way in range(2):
        masks = jnp.concatenate([ones(reach[way] == r) for r in range(1, steps + 1)], axis=0)
        before = jnp.dot(masks, earlier, preferred_element_type=f32)
        place = jnp.zeros(shape, f32)
        count = jnp.zeros(shape, f32)
        for r in range(1, steps + 1):
            same = reach[way] == r
            place = jnp.where(same, before[(r - 1) * vocab_count : r * vocab_count], place)
            total = jnp.sum(jnp.where(same, 1.0, 0.0), axis=1, keepdims=True)
            count = jnp.where(lane == r - 1, total, count)
        index.append(place)
        waiting.append(count)
    travels = (lane >= 8) & (lane < 8 * steps) & ((lane & 7) + 1 > (lane >> 3))
    for f in range(steps):
        ahead_of = jnp.dot(
            jnp.concatenate(waiting, axis=0).astype(jnp.bfloat16), goes_first, preferred_element_type=f32
        )
        for way in range(2):
            first = ahead_of[way * vocab_count : (way + 1) * vocab_count]
            go = jnp.clip(SLOTS - first, 0.0, waiting[way])
            book_ref[(f * 2 + way) * 3] = moved[way]
            moved[way] = moved[way] + go
            book_ref[(f * 2 + way) * 3 + 1] = moved[way]
            book_ref[(f * 2 + way) * 3 + 2] = jnp.minimum(first, float(SLOTS))
            come = pltpu.roll(pltpu.roll(go, 8, 1), 1 if way == 0 else vocab_count - 1, 0)
            waiting[way] = waiting[way] - go + jnp.where(travels, come, 0.0)
    left = jnp.sum(waiting[0] + waiting[1], axis=1, keepdims=True)
    left = jnp.sum(jnp.broadcast_to(left, shape), axis=0, keepdims=True)
    fit_ref[...] = jnp.broadcast_to(left, fit_ref.shape).astype(i32)

    small = (vocab_count, vocab_count)
    target = lax.broadcasted_iota(i32, (BLK, 2 * BLK), 1).astype(f32)
    pointer, sends = [], []
    for way in range(2):
        step = 1 if way == 0 else -1
        back = me - step * lax.broadcasted_iota(i32, small, 0)
        back = jnp.where(back < 0, back + vocab_count, jnp.where(back >= vocab_count, back - vocab_count, back))
        pick = ones(back == lax.broadcasted_iota(i32, small, 1))
        far = jnp.dot(pick, reach[way].astype(f32).astype(jnp.bfloat16), preferred_element_type=f32).astype(i32)
        order = jnp.dot(pick, index[way].astype(jnp.bfloat16), preferred_element_type=f32)
        giver = me - step
        giver = jnp.where(giver < 0, giver + vocab_count, jnp.where(giver >= vocab_count, giver - vocab_count, giver))

        def slot(at, hops, valid):
            column = jnp.clip(hops * 8 + far - 1, 0, BLK - 1)
            where = jnp.full(shape, -1.0, f32)
            for f in range(steps):
                start, end, first = (
                    jnp.take_along_axis(
                        jnp.broadcast_to(book_ref[(f * 2 + way) * 3 + kind, pl.ds(at, 1), :], shape),
                        column,
                        axis=1,
                        mode="promise_in_bounds",
                    )
                    for kind in range(3)
                )
                now = valid & (start <= order) & (order < end)
                where = jnp.where(now, f * SLOTS + first + order - start, where)
            return where

        leave = slot(me, row, (far > row) & (row < steps))
        arrive = slot(giver, row - 1, (far >= row) & (row >= 1) & (row <= steps))
        point = jnp.where(row == 0, lane.astype(f32), jnp.maximum(home + arrive, 0.0))
        pointer.append(point)
        leave_turned = jnp.concatenate([leave, jnp.full((BLK - vocab_count, BLK), -1.0, f32)], axis=0).T
        chosen = jnp.zeros((1, 2 * BLK), f32)
        for h in range(steps):
            chosen = chosen + jnp.dot(
                point[h : h + 1].astype(jnp.bfloat16),
                ones(leave_turned[:, h : h + 1] == target),
                preferred_element_type=f32,
            )
        sends.append(chosen.astype(i32))
    straight = sign > 0
    send_ref[0:1, :] = jnp.where(straight, sends[0], sends[1])
    send_ref[1:2, :] = jnp.where(straight, sends[1], sends[0])
    send_ref[2:8, :] = jnp.zeros((6, 2 * BLK), i32)

    mine_lane = lax.broadcasted_iota(i32, (pair_count, vocab_count), 1)
    holder = jnp.sum(jnp.where(pair_lane == me, holders, 0), axis=1, keepdims=True)
    inner = jnp.sum(jnp.where(pair_lane == me, inners, 0), axis=1, keepdims=True)
    distance = me - holder
    distance = jnp.where(distance < 0, distance + vocab_count, distance)
    hops = [
        jnp.where(distance < half, distance, 0),
        jnp.where(distance > half, vocab_count - distance, 0),
    ]
    scale = jnp.where(distance < half, distance, 2 * vocab_count - distance)
    lanes = lax.broadcasted_iota(i32, (1, BLK), 1)
    across = jnp.where(lanes == blocks, 1, across)
    met = beyond + jnp.dot(
        jnp.broadcast_to(ones(across > 0), (8, BLK)), earlier, preferred_element_type=f32
    )[:1]
    points = jnp.zeros((pair_count, 1), f32)
    for way in range(2):
        found = lax.dot_general(
            ones(pair_lane == inner),
            pointer[way].astype(jnp.bfloat16),
            (((1,), (1,)), ((), ())),
            preferred_element_type=f32,
        )
        points = points + jnp.sum(
            jnp.where((mine_lane == hops[way]) & (hops[way] > 0), found, 0.0), axis=1, keepdims=True
        )
    faced = jnp.sum(jnp.where(pair_lane == inner, met, 0.0), axis=1, keepdims=True)
    points = jnp.where(distance == half, faced, points)
    points = jnp.where(distance == 0, inner.astype(f32), points)
    by_stats = [jnp.sum(jnp.where(lane == blocks, p, 0.0), axis=1, keepdims=True) for p in pointer]
    hop = lax.broadcasted_iota(i32, (vocab_count, 1), 0)
    met_stats = jnp.sum(jnp.where(lanes == blocks, met, 0.0), axis=1, keepdims=True)
    by_stats[0] = jnp.where(hop < half, by_stats[0], 0.0)
    by_stats[1] = jnp.where((hop >= 1) & (hop < half), by_stats[1], jnp.where(hop == half, met_stats, 0.0))
    points = jnp.concatenate([points] + by_stats, axis=0).astype(i32)
    other = jnp.concatenate(
        [(hops[1] > 0).astype(i32), jnp.zeros((vocab_count, 1), i32), jnp.ones((vocab_count, 1), i32)], axis=0
    )
    other = jnp.where(straight, other, 1 - other)
    scale = jnp.concatenate([scale, jnp.zeros((2 * vocab_count, 1), i32)], axis=0)
    frame = jnp.zeros(points.shape, i32)
    for f in range(1, steps):
        frame = frame + (points >= home + f * SLOTS).astype(i32)
    away = points >= home
    direct = points >= beyond
    source = jnp.where(direct, 2 * steps + 1, jnp.where(away, 1 + frame + steps * other, 0))
    spot = jnp.where(direct, points - beyond, jnp.where(away, points - home - frame * SLOTS, points))
    spot = jnp.clip(spot, 0, jnp.where(direct, DIRECT - 1, jnp.where(away, SLOTS - 1, home - 1)))
    items = points.shape[0]
    item_lane = lax.broadcasted_iota(i32, (items, BLK), 1)
    table = jnp.where(
        item_lane == 0, spot, jnp.where(item_lane == 1, scale, jnp.where(item_lane == 2, source, 0))
    ).astype(f32)
    turned = jnp.concatenate([table, jnp.zeros((BLK - items, BLK), f32)], axis=0).T
    source_row = turned[2:3].astype(i32)
    item_up = lax.broadcasted_iota(i32, (items, BLK), 0)
    is_item = item_lane < items
    sooner = is_item & ((source_row < source) | ((source_row == source) & (item_lane < item_up)))
    rank = jnp.sum(sooner.astype(i32), axis=1, keepdims=True)
    item_ref[0:1, :] = turned[0:1].astype(i32)
    item_ref[1:2, :] = turned[1:2].astype(i32)
    item_ref[2:3, :] = jnp.sum(jnp.where(rank == item_lane, item_up, 0), axis=0, keepdims=True)
    item_ref[3:4, :] = jnp.sum((source < item_lane).astype(i32), axis=0, keepdims=True)
    item_ref[4:8, :] = jnp.zeros((4, BLK), i32)


def scalars(table_ref, row, start, count):
    values = table_ref[row : row + 1, :]
    return [values[0, start + j] for j in range(count)]


def in_order(place, valid, count):
    square = (BLK, BLK)
    up, over = lax.broadcasted_iota(jnp.int32, square, 0), lax.broadcasted_iota(jnp.int32, square, 1)
    lanes = jnp.sum(jnp.where((place == up) & valid, over, 0), axis=1, keepdims=True)
    row = turn(jnp.broadcast_to(lanes, square))[:1]
    return [row[0, j] for j in range(count)]


def first_choice(blocks, place_ref, listed_ref):
    vocab_count, pair_count = listed_ref.shape
    half = vocab_count // 2
    i32 = jnp.int32
    me, sign = place_ref[0:1, :], place_ref[1:2, :]
    holders, inners = split(turn(listed_ref[...])[:pair_count], blocks, vocab_count)
    pair_lane = lax.broadcasted_iota(i32, (pair_count, BLK), 1)
    lane = lax.broadcasted_iota(i32, (1, BLK), 1)
    reach = [jnp.zeros((1, BLK), i32), jnp.zeros((1, BLK), i32)]
    facing = jnp.where(lane == blocks, 1, 0)
    for s in range(vocab_count):
        hits = (pair_lane == inners[:, s : s + 1]) & (jnp.broadcast_to(holders[:, s : s + 1], pair_lane.shape) == me)
        seen = jnp.max(jnp.where(hits, 1, 0), axis=0, keepdims=True)
        distance = (s - me) * sign
        distance = jnp.where(distance < 0, distance + vocab_count, distance)
        reach[0] = jnp.maximum(reach[0], jnp.where(distance < half, distance * seen, 0))
        reach[1] = jnp.maximum(reach[1], jnp.where(distance > half, (vocab_count - distance) * seen, 0))
        facing = jnp.maximum(facing, jnp.where(distance == half, seen, 0))
    choices = []
    for far in reach:
        far = jnp.where(lane == blocks, half - 1, far)
        key = jnp.broadcast_to(far * BLK + (BLK - 1 - lane), (BLK, BLK))
        place = jnp.sum((turn(key) > key).astype(i32), axis=0, keepdims=True)
        choices.append(in_order(place, far > 0, SLOTS))
    place = jnp.dot(
        jnp.broadcast_to(ones(facing > 0), (8, BLK)), earlier_lanes(), preferred_element_type=jnp.float32
    )[:1].astype(i32)
    choices.append(in_order(place, facing > 0, DIRECT))
    return choices


def pack_kernel(
    place_ref,
    listed_ref,
    own_ref,
    low_ref,
    high_ref,
    pick_ref,
    home_ref,
    first_ref,
    second_ref,
    direct_ref,
    done_ref,
    cand_ref,
    logit_ref,
):
    docs, positions, columns = own_ref.shape
    width = low_ref.shape[1]
    span = positions + 2 * width
    rows = pick_ref.shape[0]
    blocks = columns // BLK
    for doc in range(docs):
        cand_ref[doc * span : doc * span + width, :] = low_ref[doc]
        cand_ref[doc * span + width : doc * span + width + positions, :] = own_ref[doc]
        cand_ref[doc * span + width + positions : (doc + 1) * span, :] = high_ref[doc]
    pick = pick_ref[...]
    peak = jnp.full((rows, BLK), -jnp.inf, jnp.float32)
    for t in range(blocks):
        part = jnp.dot(pick, cand_ref[:, t * BLK : (t + 1) * BLK], preferred_element_type=jnp.float32)
        logit_ref[t] = part.astype(jnp.bfloat16)
        peak = jnp.maximum(peak, part)
    top = jnp.max(peak, axis=1, keepdims=True)
    total = jnp.zeros((rows, BLK), jnp.float32)
    for t in range(blocks):
        power = jnp.exp(logit_ref[t].astype(jnp.float32) - top)
        total = total + power
        home_ref[t] = power.astype(jnp.bfloat16)
    total = jnp.sum(total, axis=1, keepdims=True)
    first = total.astype(jnp.bfloat16).astype(jnp.float32)
    second = (total - first).astype(jnp.bfloat16).astype(jnp.float32)
    third = total - first - second
    lane = lax.broadcasted_iota(jnp.int32, (rows, BLK), 1)
    home_ref[blocks] = jnp.where(
        lane == 0, top, jnp.where(lane == 1, first, jnp.where(lane == 2, second, jnp.where(lane == 3, third, 0.0)))
    ).astype(jnp.bfloat16)
    for out_ref, choice in zip((first_ref, second_ref, direct_ref), first_choice(blocks, place_ref, listed_ref)):
        for j, at in enumerate(choice):
            out_ref[j] = home_ref[at]
    done_ref[...] = jnp.zeros(done_ref.shape, jnp.int32)


def ready_kernel(chain, step, send_ref, home_ref, *refs):
    frames, out_ref = refs[:-1], refs[-1]
    home = home_ref.shape[0]
    for j, at in enumerate(scalars(send_ref, chain, step * SLOTS, SLOTS)):

        def copy(low, high, j=j, at=at):
            if high - low == 1:
                if low == 0:
                    out_ref[j] = home_ref[at]
                elif low <= len(frames):
                    out_ref[j] = frames[low - 1][at - home - (low - 1) * SLOTS]
                return
            mid = (low + high) // 2
            split = home + (mid - 1) * SLOTS
            pl.when(at < split)(lambda: copy(low, mid))
            pl.when(at >= split)(lambda: copy(mid, high))

        copy(0, len(frames) + 2)


def pass_kernel(chain, step, home, send_ref, part_ref, newest_ref, out_ref):
    start = home + (step - 1) * SLOTS
    for j, at in enumerate(scalars(send_ref, chain, step * SLOTS, SLOTS)):
        newest = newest_ref[jnp.maximum(at - start, 0)]
        out_ref[j] = jnp.where(at >= start, newest, part_ref[j])


def stage_kernel(steps, item_ref, *refs):
    sources, stage_ref = refs[:-1], refs[-1]
    for s, source in zip([s for s in range(2 * steps + 2) if s not in (steps, 2 * steps)], sources):
        bring(item_ref, s, source, stage_ref)


def bring(item_ref, s, source_ref, stage_ref):
    def one(q, carry):
        item = item_ref[2, q]
        stage_ref[item] = source_ref[item_ref[0, item]]
        return carry

    lax.fori_loop(item_ref[3, s], item_ref[3, s + 1], one, 0)


def student_kernel(student_ref, top_ref, total_ref):
    docs, positions, columns = student_ref.shape
    rows = docs * positions
    peak = jnp.full((rows, BLK), -jnp.inf, jnp.float32)
    for b in range(columns // BLK):
        part = student_ref[:, :, b * BLK : (b + 1) * BLK].reshape(rows, BLK).astype(jnp.float32)
        peak = jnp.maximum(peak, part)
    top = jnp.max(peak, axis=1, keepdims=True)
    total = jnp.zeros((rows, BLK), jnp.float32)
    for b in range(columns // BLK):
        part = student_ref[:, :, b * BLK : (b + 1) * BLK].reshape(rows, BLK).astype(jnp.float32)
        total = total + jnp.exp(part - top)
    top_ref[...] = jnp.broadcast_to(top, (rows, BLK))
    total_ref[...] = jnp.broadcast_to(jnp.sum(total, axis=1, keepdims=True), (rows, BLK))


def map_kernel(
    steps,
    item_ref,
    held_ref,
    ahead_ref,
    behind_ref,
    spread_ref,
    weight_ref,
    student_ref,
    top_ref,
    total_ref,
    out_ref,
    stage_ref,
    scale_ref,
):
    docs, positions, columns = student_ref.shape
    rows = docs * positions
    blocks = columns // BLK
    spread = spread_ref[...]
    for i in range(stage_ref.shape[0]):
        stage_ref[i] = held_ref[i]
    bring(item_ref, steps, ahead_ref, stage_ref)
    bring(item_ref, 2 * steps, behind_ref, stage_ref)
    facing = steps + 1
    holders = [h for h in range(facing)] + [2 * facing + h for h in range(1, facing + 1)]
    peaks, sums = [], []
    for h in holders:
        stats = jnp.dot(spread, stage_ref[K * blocks + h], preferred_element_type=jnp.float32)
        peaks.append(stats[:, 0:1])
        sums.append(stats[:, 1:2] + stats[:, 2:3] + stats[:, 3:4])
    peak = functools.reduce(jnp.maximum, peaks)
    powers = [jnp.exp(p - peak) for p in peaks]
    norm = sum(p * t for p, t in zip(powers, sums))
    for h, power in zip(holders, powers):
        scale_ref[h] = jnp.broadcast_to(power / norm, (rows, BLK))
    student_top = top_ref[...]
    mass = jnp.zeros((rows, BLK), jnp.float32)
    cross = jnp.zeros((rows, BLK), jnp.float32)
    for b in range(blocks):
        picked = jnp.concatenate([stage_ref[K * b], stage_ref[K * b + 1]], axis=1)
        prob = jnp.dot(spread, picked, preferred_element_type=jnp.float32).astype(jnp.bfloat16)
        mapped = scale_ref[item_ref[1, K * b]] * jnp.dot(
            prob[:, :BLK], weight_ref[:, K * b].reshape(BLK, BLK), preferred_element_type=jnp.float32
        ) + scale_ref[item_ref[1, K * b + 1]] * jnp.dot(
            prob[:, BLK:], weight_ref[:, K * b + 1].reshape(BLK, BLK), preferred_element_type=jnp.float32
        )
        logit = student_ref[:, :, b * BLK : (b + 1) * BLK].reshape(rows, BLK).astype(jnp.float32) - student_top
        mass = mass + mapped
        cross = cross + mapped * (jnp.log(jnp.maximum(mapped, TINY)) - logit)
    mass = jnp.sum(mass, axis=1, keepdims=True)
    cross = jnp.sum(cross, axis=1, keepdims=True)
    lane = lax.broadcasted_iota(jnp.int32, (rows, BLK), 1)
    table = jnp.where(
        lane == 0, mass, jnp.where(lane == 1, cross, jnp.where(lane == 2, student_top, total_ref[...]))
    )
    out_ref[...] = table.T[:8]


def whole(padded_parts, cand, src_block, weights, student_logits):
    doc_count, pos_count, student_cols = student_logits.shape
    teacher_cols = padded_parts[0].shape[2]
    teacher_blocks = teacher_cols // BLK
    student_blocks = student_cols // BLK
    row_count = doc_count * pos_count
    padded = jnp.concatenate(padded_parts, axis=1).reshape(-1, teacher_cols)
    teacher_float = jnp.take(padded, cand, axis=0).astype(jnp.float32)
    student_float = student_logits.reshape(row_count, student_cols).astype(jnp.float32)
    teacher_peak = jnp.max(teacher_float, axis=1)
    student_peak = jnp.max(student_float, axis=1)
    teacher_top, student_top = lax.pmax((teacher_peak, student_peak), "vocab")
    teacher_total, student_total = lax.psum(
        (
            jnp.sum(jnp.exp(teacher_float - teacher_top[:, None]), axis=1),
            jnp.sum(jnp.exp(student_float - student_top[:, None]), axis=1),
        ),
        "vocab",
    )
    teacher_prob = (jnp.exp(teacher_float - teacher_top[:, None]) / teacher_total[:, None]).astype(jnp.bfloat16)
    student_logprob = student_float - student_top[:, None] - jnp.log(student_total)[:, None]
    vocab_count = lax.axis_size("vocab")
    own_index = lax.axis_index("vocab")
    pair_count = student_blocks * K
    capacity = 2 * K * student_blocks // vocab_count
    pair_blocks = src_block.reshape(vocab_count, pair_count)
    holder = pair_blocks // teacher_blocks
    inside = pair_blocks % teacher_blocks
    same_holder = holder[:, :, None] == holder[:, None, :]
    before = jnp.arange(pair_count)[None, :] < jnp.arange(pair_count)[:, None]
    slot_rank = jnp.sum(same_holder & before[None, :, :], axis=2)
    chosen = (holder == own_index)[:, None, :] & (
        slot_rank[:, None, :] == jnp.arange(capacity)[None, :, None]
    )
    send_index = jnp.sum(jnp.where(chosen, inside[:, None, :], 0), axis=2)
    prob_blocks = teacher_prob.reshape(row_count, teacher_blocks, BLK)
    outgoing = jnp.take(prob_blocks, send_index.reshape(-1), axis=1).reshape(row_count, vocab_count, capacity, BLK)
    incoming = lax.all_to_all(outgoing, "vocab", split_axis=1, concat_axis=1, tiled=True)
    own_holder = jnp.take(holder, own_index, axis=0)
    own_rank = jnp.take(slot_rank, own_index, axis=0)
    recv_slot = own_holder * capacity + own_rank
    gathered = jnp.take(incoming.reshape(row_count, vocab_count * capacity, BLK), recv_slot, axis=1).reshape(
        row_count, student_blocks, K, BLK
    )
    weights = weights.swapaxes(0, 1).reshape(student_blocks, K, BLK, BLK)
    mapped = jnp.einsum("rbkc,bkcd->rbd", gathered, weights, preferred_element_type=jnp.float32).reshape(
        row_count, student_cols
    )
    total_mass = lax.psum(jnp.sum(mapped, axis=1), "vocab")
    normed = mapped / total_mass[:, None]
    return lax.psum(
        jnp.sum(jax.scipy.special.xlogy(normed, normed) - normed * student_logprob, axis=1), "vocab"
    )


def shards(teacher_logits, student_logits, alignment, src_block, margin_weight):
    doc_count, pos_count, teacher_cols = teacher_logits.shape
    student_cols = student_logits.shape[2]
    teacher_blocks = teacher_cols // BLK
    student_blocks = student_cols // BLK
    row_count = doc_count * pos_count
    pair_count = student_blocks * K
    vocab_count = lax.axis_size("vocab")
    steps = vocab_count // 2 - 1
    home = teacher_blocks + 1
    vocab_index = lax.axis_index("vocab")
    seq_index = lax.axis_index("seq")
    sign = 1 - 2 * (seq_index % 2)
    span = pos_count + 2 * W

    with jax.named_scope("halo"):
        low, high = halo(teacher_logits, W)
    with jax.named_scope("weights"):
        weights = lax.all_gather(
            margin_weight.reshape(pair_count, -1, BLK), "dp", axis=0, tiled=False
        )

    with jax.named_scope("rows"):
        cand = (alignment - seq_index * pos_count + W + jnp.arange(doc_count)[:, None] * span).reshape(-1)
        cand = jnp.clip(cand, 0, doc_count * span - 1)
        places = jnp.arange(doc_count * span)
        used = jnp.any(cand[:, None] == places[None, :], axis=0)
        place_rank = jnp.sum(used[:, None] & (places[:, None] < places[None, :]), axis=0)
        cand_rank = jnp.sum(used[None, :] & (places[None, :] < cand[:, None]), axis=1)
        row_ids = jnp.arange(ROWS)
        pick = ((row_ids[:, None] == place_rank[None, :]) & used[None, :]).astype(jnp.bfloat16)
        spread = (cand_rank[:, None] == row_ids[None, :]).astype(jnp.bfloat16)
        rows_fit = jnp.sum(used.astype(jnp.int32)) <= ROWS

    vmem = pl.BlockSpec(memory_space=pltpu.VMEM)
    smem = pl.BlockSpec(memory_space=pltpu.SMEM)
    def room(mib):
        return pltpu.CompilerParams(vmem_limit_bytes=mib * 1024 * 1024)

    def planes(count):
        return jax.ShapeDtypeStruct((count, ROWS, BLK), jnp.bfloat16)

    with jax.named_scope("pack"):
        listed = src_block.reshape(vocab_count, pair_count)
        place = jnp.stack([vocab_index, sign]).astype(jnp.int32)
        own, ahead, behind, direct, packed = pl.pallas_call(
            pack_kernel,
            out_shape=(
                planes(home),
                planes(SLOTS),
                planes(SLOTS),
                planes(DIRECT),
                jax.ShapeDtypeStruct((8, BLK), jnp.int32),
            ),
            in_specs=[vmem] * 6,
            out_specs=(vmem,) * 5,
            scratch_shapes=[
                pltpu.VMEM((doc_count * span, teacher_cols), jnp.bfloat16),
                pltpu.VMEM((teacher_blocks, ROWS, BLK), jnp.bfloat16),
            ],
            compiler_params=room(16),
        )(jnp.broadcast_to(place[:, None], (2, BLK)), listed, teacher_logits, low, high, pick)

    with jax.named_scope("plan"):
        table = jax.ShapeDtypeStruct((8, BLK), jnp.int32)
        send, items, left = pl.pallas_call(
            functools.partial(plan_kernel, teacher_blocks),
            out_shape=(jax.ShapeDtypeStruct((8, 2 * BLK), jnp.int32), table, table),
            in_specs=[smem, vmem, vmem],
            out_specs=(vmem,) * 3,
            scratch_shapes=[pltpu.VMEM((6 * steps, vocab_count, BLK), jnp.float32)],
            compiler_params=room(8),
        )(place, listed, packed)

    def chosen(chain, step, frames):
        part = pl.pallas_call(
            functools.partial(ready_kernel, chain, step),
            out_shape=planes(SLOTS),
            in_specs=[vmem] * (1 + len(frames)),
            out_specs=vmem,
            compiler_params=room(8),
        )(send, own, *frames[:-1])
        return pl.pallas_call(
            functools.partial(pass_kernel, chain, step, home),
            out_shape=planes(SLOTS),
            in_specs=[vmem] * 3,
            out_specs=vmem,
            compiler_params=room(4),
        )(send, part, frames[-1])

    with jax.named_scope("ring"):
        forward, backward = ring_pairs(1), ring_pairs(-1)
        came_ahead, came_behind = [], []
        for step in range(steps):
            if step:
                ahead = chosen(0, step, came_ahead)
            came_ahead.append(lax.ppermute(ahead, ("seq", "vocab"), forward))
            if step:
                behind = chosen(1, step, came_behind)
            came_behind.append(lax.ppermute(behind, ("seq", "vocab"), backward))
        across = [(v, (v + vocab_count // 2) % vocab_count) for v in range(vocab_count)]
        came_direct = lax.ppermute(direct, "vocab", across)

    with jax.named_scope("student"):
        top, total = pl.pallas_call(
            student_kernel,
            out_shape=(jax.ShapeDtypeStruct((row_count, BLK), jnp.float32),) * 2,
            in_specs=[vmem],
            out_specs=(vmem,) * 2,
            compiler_params=room(8),
        )(student_logits)

    with jax.named_scope("stage"):
        early = (own, *came_ahead[:-1], *came_behind[:-1], came_direct)
        held = pl.pallas_call(
            functools.partial(stage_kernel, steps),
            out_shape=planes(pair_count + 2 * vocab_count),
            in_specs=[smem] + [vmem] * len(early),
            out_specs=vmem,
            compiler_params=room(16),
        )(items, *early)

    with jax.named_scope("map"):
        sums = pl.pallas_call(
            functools.partial(map_kernel, steps),
            out_shape=jax.ShapeDtypeStruct((8, row_count), jnp.float32),
            in_specs=[smem] + [vmem] * 8,
            out_specs=vmem,
            scratch_shapes=[
                pltpu.VMEM((pair_count + 2 * vocab_count, ROWS, BLK), jnp.bfloat16),
                pltpu.VMEM((2 * vocab_count, row_count, BLK), jnp.float32),
            ],
            compiler_params=room(20),
        )(items, held, came_ahead[-1], came_behind[-1], spread, weights, student_logits, top, total)

    with jax.named_scope("finish"):
        sent = jnp.broadcast_to(sums[None, :4], (vocab_count, 4, row_count))
        parts = lax.all_to_all(sent, "vocab", split_axis=0, concat_axis=0, tiled=True)
        mass_part, cross_part, top_part, total_part = (parts[:, i] for i in range(4))
        student_top = jnp.max(top_part, axis=0)
        log_total = student_top + jnp.log(jnp.sum(jnp.exp(top_part - student_top) * total_part, axis=0))
        mass = jnp.sum(mass_part, axis=0)
        result = jnp.sum(cross_part + mass_part * (log_total - top_part), axis=0) / mass - jnp.log(mass)

    result = lax.cond(
        rows_fit & (left[0, 0] == 0),
        lambda *_: result,
        lambda *operands: whole(operands[:3], *operands[3:]),
        low,
        teacher_logits,
        high,
        cand,
        src_block,
        weights,
        student_logits,
    )
    return result.reshape(doc_count, pos_count)


def solution(mesh):
    in_specs = (
        P("dp", "seq", "vocab"),
        P("dp", "seq", "vocab"),
        P("dp", "seq"),
        P(),
        P("vocab", None, "dp", None),
    )
    out_specs = P("dp", "seq")
    return jax.shard_map(shards, mesh=mesh, in_specs=in_specs, out_specs=out_specs, check_vma=False)
```

```python
import functools

import jax
import jax.numpy as jnp
from jax import lax
from jax.experimental import pallas as pl
from jax.experimental.pallas import tpu as pltpu
from jax.sharding import PartitionSpec as P

BLK = 128
K = 2
W = 16
ROWS = 104
SLOTS = 21
TINY = 1.2e-38


def halo(block, width):
    count = lax.axis_size("seq")
    forward = [(i, i + 1) for i in range(count - 1)]
    backward = [(target, source) for source, target in forward]
    low = lax.ppermute(block[:, block.shape[1] - width :], "seq", forward)
    high = lax.ppermute(block[:, :width], "seq", backward)
    return low, high


def ring_pairs(turn):
    seq_count, vocab_count = lax.axis_size("seq"), lax.axis_size("vocab")
    pairs = []
    for s in range(seq_count):
        step = turn if s % 2 == 0 else -turn
        for v in range(vocab_count):
            pairs.append((s * vocab_count + v, s * vocab_count + (v + step) % vocab_count))
    return pairs


def tie_key(block):
    return (block * 5) & 7


def ways(distance, block, share, vocab_count):
    half = vocab_count // 2
    first = tie_key(block) < share
    ahead = jnp.where((distance >= 1) & ((distance < half) | ((distance == half) & first)), distance, 0)
    behind = jnp.where((distance > half) | ((distance == half) & ~first), vocab_count - distance, 0)
    return ahead, behind


def ones(mask):
    return jnp.where(mask, 1.0, 0.0).astype(jnp.bfloat16)


def tie_share(reach, facing, lane, half):
    share = jnp.zeros((reach[0].shape[0], 1), jnp.int32)
    for part in range(1, 9):
        first = tie_key(lane) < part
        more = jnp.where(facing & first, half, reach[0]) - jnp.where(facing & ~first, half, reach[1])
        share = share + (jnp.sum(more, axis=1, keepdims=True) <= 0).astype(jnp.int32)
    return share


def full_reach(reach, facing, lane, share, blocks, half):
    first = tie_key(lane) < share
    ahead = jnp.where(facing & first, half, reach[0])
    behind = jnp.where(facing & ~first, half, reach[1])
    return [jnp.where(lane == blocks, half, ahead), jnp.where(lane == blocks, half - 1, behind)]


def split(listed, blocks, vocab_count):
    holder = sum((listed >= h * blocks).astype(jnp.int32) for h in range(1, vocab_count))
    return holder, listed - holder * blocks


def turn(table):
    rows, columns = table.shape
    table = table.astype(jnp.float32)
    if columns < BLK:
        table = jnp.concatenate([table, jnp.zeros((rows, BLK - columns), jnp.float32)], axis=1)
    if rows < BLK:
        table = jnp.concatenate([table, jnp.zeros((BLK - rows, BLK), jnp.float32)], axis=0)
    return table.T.astype(jnp.int32)


def earlier_lanes():
    square = (BLK, BLK)
    return ones(lax.broadcasted_iota(jnp.int32, square, 0) < lax.broadcasted_iota(jnp.int32, square, 1))


def plan_kernel(blocks, place_ref, listed_ref, after_ref, send_ref, item_ref, fit_ref, book_ref):
    vocab_count, pair_count = listed_ref.shape
    half = vocab_count // 2
    steps = half
    home = blocks + 1
    me, sign = place_ref[0], place_ref[1]
    f32, i32 = jnp.float32, jnp.int32
    shape = (vocab_count, BLK)

    del after_ref
    listed = listed_ref[...]
    row_holder, _ = split(listed, blocks, vocab_count)
    holders, inners = split(turn(listed)[:pair_count], blocks, vocab_count)
    lane = lax.broadcasted_iota(i32, shape, 1)
    row = lax.broadcasted_iota(i32, shape, 0)

    reach = [jnp.zeros(shape, i32), jnp.zeros(shape, i32)]
    across = jnp.zeros(shape, i32)
    pair_lane = lax.broadcasted_iota(i32, (pair_count, BLK), 1)
    pair_row = lax.broadcasted_iota(i32, (vocab_count, pair_count), 0)
    for s in range(vocab_count):
        hits = jnp.dot(
            ones(pair_row == row_holder[s : s + 1, :]),
            ones(pair_lane == inners[:, s : s + 1]),
            preferred_element_type=f32,
        )
        distance = s - row
        distance = jnp.where(distance < 0, distance + vocab_count, distance)
        needed = hits > 0
        reach[0] = jnp.maximum(reach[0], jnp.where(needed & (distance < half), distance, 0))
        reach[1] = jnp.maximum(reach[1], jnp.where(needed & (distance > half), vocab_count - distance, 0))
        across = jnp.maximum(across, jnp.where(needed & (distance == half), 1, 0))
    share = tie_share(reach, across > 0, lane, half)
    reach = full_reach(reach, across > 0, lane, share, blocks, half)

    square = (BLK, BLK)
    up, over = lax.broadcasted_iota(i32, square, 0), lax.broadcasted_iota(i32, square, 1)
    earlier = earlier_lanes()
    left_up, left_over = (up & 7) + 1 - (up >> 3), (over & 7) + 1 - (over >> 3)
    goes_first = ones((left_up > left_over) | ((left_up == left_over) & ((up >> 3) > (over >> 3))))
    index, waiting, moved = [], [], [jnp.zeros(shape, f32)] * 2
    for way in range(2):
        masks = jnp.concatenate([ones(reach[way] == r) for r in range(1, half + 1)], axis=0)
        before = jnp.dot(masks, earlier, preferred_element_type=f32)
        place = jnp.zeros(shape, f32)
        count = jnp.zeros(shape, f32)
        for r in range(1, half + 1):
            same = reach[way] == r
            place = jnp.where(same, before[(r - 1) * vocab_count : r * vocab_count], place)
            total = jnp.sum(jnp.where(same, 1.0, 0.0), axis=1, keepdims=True)
            count = jnp.where(lane == r - 1, total, count)
        index.append(place)
        waiting.append(count)
    travels = (lane >= 8) & (lane < 8 * half) & ((lane & 7) + 1 > (lane >> 3))
    for f in range(steps):
        ahead_of = jnp.dot(
            jnp.concatenate(waiting, axis=0).astype(jnp.bfloat16), goes_first, preferred_element_type=f32
        )
        for way in range(2):
            first = ahead_of[way * vocab_count : (way + 1) * vocab_count]
            go = jnp.clip(SLOTS - first, 0.0, waiting[way])
            book_ref[(f * 2 + way) * 3] = moved[way]
            moved[way] = moved[way] + go
            book_ref[(f * 2 + way) * 3 + 1] = moved[way]
            book_ref[(f * 2 + way) * 3 + 2] = jnp.minimum(first, float(SLOTS))
            come = pltpu.roll(pltpu.roll(go, 8, 1), 1 if way == 0 else vocab_count - 1, 0)
            waiting[way] = waiting[way] - go + jnp.where(travels, come, 0.0)
    left = jnp.sum(waiting[0] + waiting[1], axis=1, keepdims=True)
    left = jnp.sum(jnp.broadcast_to(left, shape), axis=0, keepdims=True)
    fit_ref[...] = jnp.broadcast_to(left, fit_ref.shape).astype(i32)

    small = (vocab_count, vocab_count)
    target = lax.broadcasted_iota(i32, (BLK, 2 * BLK), 1).astype(f32)
    pointer, sends = [], []
    for way in range(2):
        step = 1 if way == 0 else -1
        back = me - step * lax.broadcasted_iota(i32, small, 0)
        back = jnp.where(back < 0, back + vocab_count, jnp.where(back >= vocab_count, back - vocab_count, back))
        pick = ones(back == lax.broadcasted_iota(i32, small, 1))
        far = jnp.dot(pick, reach[way].astype(f32).astype(jnp.bfloat16), preferred_element_type=f32).astype(i32)
        order = jnp.dot(pick, index[way].astype(jnp.bfloat16), preferred_element_type=f32)
        giver = me - step
        giver = jnp.where(giver < 0, giver + vocab_count, jnp.where(giver >= vocab_count, giver - vocab_count, giver))

        def slot(at, hops, valid):
            column = jnp.clip(hops * 8 + far - 1, 0, BLK - 1)
            where = jnp.full(shape, -1.0, f32)
            for f in range(steps):
                start, end, first = (
                    jnp.take_along_axis(
                        jnp.broadcast_to(book_ref[(f * 2 + way) * 3 + kind, pl.ds(at, 1), :], shape),
                        column,
                        axis=1,
                        mode="promise_in_bounds",
                    )
                    for kind in range(3)
                )
                now = valid & (start <= order) & (order < end)
                where = jnp.where(now, f * SLOTS + first + order - start, where)
            return where

        leave = slot(me, row, (far > row) & (row < half))
        arrive = slot(giver, row - 1, (far >= row) & (row >= 1) & (row <= half))
        point = jnp.where(row == 0, lane.astype(f32), jnp.maximum(home + arrive, 0.0))
        pointer.append(point)
        leave_turned = jnp.concatenate([leave, jnp.full((BLK - vocab_count, BLK), -1.0, f32)], axis=0).T
        chosen = jnp.zeros((1, 2 * BLK), f32)
        for h in range(half):
            chosen = chosen + jnp.dot(
                point[h : h + 1].astype(jnp.bfloat16),
                ones(leave_turned[:, h : h + 1] == target),
                preferred_element_type=f32,
            )
        sends.append(chosen.astype(i32))
    straight = sign > 0
    send_ref[0:1, :] = jnp.where(straight, sends[0], sends[1])
    send_ref[1:2, :] = jnp.where(straight, sends[1], sends[0])
    send_ref[2:8, :] = jnp.zeros((6, 2 * BLK), i32)

    mine_lane = lax.broadcasted_iota(i32, (pair_count, vocab_count), 1)
    holder = jnp.sum(jnp.where(pair_lane == me, holders, 0), axis=1, keepdims=True)
    inner = jnp.sum(jnp.where(pair_lane == me, inners, 0), axis=1, keepdims=True)
    distance = me - holder
    distance = jnp.where(distance < 0, distance + vocab_count, distance)
    share = turn(jnp.broadcast_to(share, shape))[:1]
    share = jnp.sum(jnp.where(pair_lane == holder, share, 0), axis=1, keepdims=True)
    hops = ways(distance, inner, share, vocab_count)
    scale = jnp.where(distance <= half, distance, 2 * vocab_count - distance)
    points = jnp.zeros((pair_count, 1), f32)
    for way in range(2):
        found = lax.dot_general(
            ones(pair_lane == inner),
            pointer[way].astype(jnp.bfloat16),
            (((1,), (1,)), ((), ())),
            preferred_element_type=f32,
        )
        points = points + jnp.sum(
            jnp.where((mine_lane == hops[way]) & (hops[way] > 0), found, 0.0), axis=1, keepdims=True
        )
    points = jnp.where(distance == 0, inner.astype(f32), points)
    by_stats = [jnp.sum(jnp.where(lane == blocks, p, 0.0), axis=1, keepdims=True) for p in pointer]
    hop = lax.broadcasted_iota(i32, (vocab_count, 1), 0)
    stat_ok = [hop <= half, (hop >= 1) & (hop < half)]
    points = jnp.concatenate(
        [points] + [jnp.where(ok, p, 0.0) for ok, p in zip(stat_ok, by_stats)], axis=0
    ).astype(i32)
    other = jnp.concatenate(
        [(hops[1] > 0).astype(i32), jnp.zeros((vocab_count, 1), i32), jnp.ones((vocab_count, 1), i32)], axis=0
    )
    other = jnp.where(straight, other, 1 - other)
    scale = jnp.concatenate([scale, jnp.zeros((2 * vocab_count, 1), i32)], axis=0)
    frame = jnp.zeros(points.shape, i32)
    for f in range(1, steps):
        frame = frame + (points >= home + f * SLOTS).astype(i32)
    away = points >= home
    source = jnp.where(away, 1 + frame + steps * other, 0)
    spot = jnp.where(away, points - home - frame * SLOTS, points)
    spot = jnp.clip(spot, 0, jnp.where(away, SLOTS - 1, home - 1))
    items = points.shape[0]
    item_lane = lax.broadcasted_iota(i32, (items, BLK), 1)
    table = jnp.where(
        item_lane == 0, spot, jnp.where(item_lane == 1, scale, jnp.where(item_lane == 2, source, 0))
    ).astype(f32)
    turned = jnp.concatenate([table, jnp.zeros((BLK - items, BLK), f32)], axis=0).T
    source_row = turned[2:3].astype(i32)
    item_up = lax.broadcasted_iota(i32, (items, BLK), 0)
    is_item = item_lane < items
    sooner = is_item & ((source_row < source) | ((source_row == source) & (item_lane < item_up)))
    rank = jnp.sum(sooner.astype(i32), axis=1, keepdims=True)
    item_ref[0:1, :] = turned[0:1].astype(i32)
    item_ref[1:2, :] = turned[1:2].astype(i32)
    item_ref[2:3, :] = jnp.sum(jnp.where(rank == item_lane, item_up, 0), axis=0, keepdims=True)
    item_ref[3:4, :] = jnp.sum((source < item_lane).astype(i32), axis=0, keepdims=True)
    item_ref[4:8, :] = jnp.zeros((4, BLK), i32)


def scalars(table_ref, row, start, count):
    values = table_ref[row : row + 1, :]
    return [values[0, start + j] for j in range(count)]


def in_order(place, valid, count):
    square = (BLK, BLK)
    up, over = lax.broadcasted_iota(jnp.int32, square, 0), lax.broadcasted_iota(jnp.int32, square, 1)
    lanes = jnp.sum(jnp.where((place == up) & valid, over, 0), axis=1, keepdims=True)
    row = turn(jnp.broadcast_to(lanes, square))[:1]
    return [row[0, j] for j in range(count)]


def first_choice(blocks, place_ref, listed_ref):
    vocab_count, pair_count = listed_ref.shape
    half = vocab_count // 2
    i32 = jnp.int32
    me, sign = place_ref[0:1, :], place_ref[1:2, :]
    holders, inners = split(turn(listed_ref[...])[:pair_count], blocks, vocab_count)
    pair_lane = lax.broadcasted_iota(i32, (pair_count, BLK), 1)
    lane = lax.broadcasted_iota(i32, (1, BLK), 1)
    reach = [jnp.zeros((1, BLK), i32), jnp.zeros((1, BLK), i32)]
    facing = jnp.zeros((1, BLK), i32)
    for s in range(vocab_count):
        hits = (pair_lane == inners[:, s : s + 1]) & (jnp.broadcast_to(holders[:, s : s + 1], pair_lane.shape) == me)
        seen = jnp.max(jnp.where(hits, 1, 0), axis=0, keepdims=True)
        distance = s - me
        distance = jnp.where(distance < 0, distance + vocab_count, distance)
        reach[0] = jnp.maximum(reach[0], jnp.where(distance < half, distance * seen, 0))
        reach[1] = jnp.maximum(reach[1], jnp.where(distance > half, (vocab_count - distance) * seen, 0))
        facing = jnp.maximum(facing, jnp.where(distance == half, seen, 0))
    share = tie_share(reach, facing > 0, lane, half)
    reach = full_reach(reach, facing > 0, lane, share, blocks, half)
    choices = []
    for one, other in (reach, reach[::-1]):
        far = jnp.where(sign > 0, one, other)
        key = jnp.broadcast_to(far * BLK + (BLK - 1 - lane), (BLK, BLK))
        place = jnp.sum((turn(key) > key).astype(i32), axis=0, keepdims=True)
        choices.append(in_order(place, far > 0, SLOTS))
    return choices


def pack_kernel(
    place_ref,
    listed_ref,
    own_ref,
    low_ref,
    high_ref,
    pick_ref,
    home_ref,
    first_ref,
    second_ref,
    done_ref,
    cand_ref,
    logit_ref,
):
    docs, positions, columns = own_ref.shape
    width = low_ref.shape[1]
    span = positions + 2 * width
    rows = pick_ref.shape[0]
    blocks = columns // BLK
    for doc in range(docs):
        cand_ref[doc * span : doc * span + width, :] = low_ref[doc]
        cand_ref[doc * span + width : doc * span + width + positions, :] = own_ref[doc]
        cand_ref[doc * span + width + positions : (doc + 1) * span, :] = high_ref[doc]
    pick = pick_ref[...]
    peak = jnp.full((rows, BLK), -jnp.inf, jnp.float32)
    for t in range(blocks):
        part = jnp.dot(pick, cand_ref[:, t * BLK : (t + 1) * BLK], preferred_element_type=jnp.float32)
        logit_ref[t] = part.astype(jnp.bfloat16)
        peak = jnp.maximum(peak, part)
    top = jnp.max(peak, axis=1, keepdims=True)
    total = jnp.zeros((rows, BLK), jnp.float32)
    for t in range(blocks):
        power = jnp.exp(logit_ref[t].astype(jnp.float32) - top)
        total = total + power
        home_ref[t] = power.astype(jnp.bfloat16)
    total = jnp.sum(total, axis=1, keepdims=True)
    first = total.astype(jnp.bfloat16).astype(jnp.float32)
    second = (total - first).astype(jnp.bfloat16).astype(jnp.float32)
    third = total - first - second
    lane = lax.broadcasted_iota(jnp.int32, (rows, BLK), 1)
    home_ref[blocks] = jnp.where(
        lane == 0, top, jnp.where(lane == 1, first, jnp.where(lane == 2, second, jnp.where(lane == 3, third, 0.0)))
    ).astype(jnp.bfloat16)
    for out_ref, choice in zip((first_ref, second_ref), first_choice(blocks, place_ref, listed_ref)):
        for j, at in enumerate(choice):
            out_ref[j] = home_ref[at]
    done_ref[...] = jnp.zeros(done_ref.shape, jnp.int32)


def ready_kernel(chain, step, send_ref, home_ref, *refs):
    frames, out_ref = refs[:-1], refs[-1]
    home = home_ref.shape[0]
    for j, at in enumerate(scalars(send_ref, chain, step * SLOTS, SLOTS)):

        def copy(low, high, j=j, at=at):
            if high - low == 1:
                if low == 0:
                    out_ref[j] = home_ref[at]
                elif low <= len(frames):
                    out_ref[j] = frames[low - 1][at - home - (low - 1) * SLOTS]
                return
            mid = (low + high) // 2
            split = home + (mid - 1) * SLOTS
            pl.when(at < split)(lambda: copy(low, mid))
            pl.when(at >= split)(lambda: copy(mid, high))

        copy(0, len(frames) + 2)


def pass_kernel(chain, step, home, send_ref, part_ref, newest_ref, out_ref):
    start = home + (step - 1) * SLOTS
    for j, at in enumerate(scalars(send_ref, chain, step * SLOTS, SLOTS)):
        newest = newest_ref[jnp.maximum(at - start, 0)]
        out_ref[j] = jnp.where(at >= start, newest, part_ref[j])


def stage_kernel(steps, item_ref, *refs):
    sources, stage_ref = refs[:-1], refs[-1]
    for s, source in zip([s for s in range(2 * steps + 1) if s not in (steps, 2 * steps)], sources):
        bring(item_ref, s, source, stage_ref)


def bring(item_ref, s, source_ref, stage_ref):
    def one(q, carry):
        item = item_ref[2, q]
        stage_ref[item] = source_ref[item_ref[0, item]]
        return carry

    lax.fori_loop(item_ref[3, s], item_ref[3, s + 1], one, 0)


def student_kernel(student_ref, top_ref, total_ref):
    docs, positions, columns = student_ref.shape
    rows = docs * positions
    peak = jnp.full((rows, BLK), -jnp.inf, jnp.float32)
    for b in range(columns // BLK):
        part = student_ref[:, :, b * BLK : (b + 1) * BLK].reshape(rows, BLK).astype(jnp.float32)
        peak = jnp.maximum(peak, part)
    top = jnp.max(peak, axis=1, keepdims=True)
    total = jnp.zeros((rows, BLK), jnp.float32)
    for b in range(columns // BLK):
        part = student_ref[:, :, b * BLK : (b + 1) * BLK].reshape(rows, BLK).astype(jnp.float32)
        total = total + jnp.exp(part - top)
    top_ref[...] = jnp.broadcast_to(top, (rows, BLK))
    total_ref[...] = jnp.broadcast_to(jnp.sum(total, axis=1, keepdims=True), (rows, BLK))


def map_kernel(
    steps,
    item_ref,
    held_ref,
    ahead_ref,
    behind_ref,
    spread_ref,
    weight_ref,
    student_ref,
    top_ref,
    total_ref,
    out_ref,
    stage_ref,
    scale_ref,
):
    docs, positions, columns = student_ref.shape
    rows = docs * positions
    blocks = columns // BLK
    spread = spread_ref[...]
    for i in range(stage_ref.shape[0]):
        stage_ref[i] = held_ref[i]
    bring(item_ref, steps, ahead_ref, stage_ref)
    bring(item_ref, 2 * steps, behind_ref, stage_ref)
    holders = [h for h in range(steps + 1)] + [2 * steps + h for h in range(1, steps)]
    peaks, sums = [], []
    for h in holders:
        stats = jnp.dot(spread, stage_ref[K * blocks + h], preferred_element_type=jnp.float32)
        peaks.append(stats[:, 0:1])
        sums.append(stats[:, 1:2] + stats[:, 2:3] + stats[:, 3:4])
    peak = functools.reduce(jnp.maximum, peaks)
    powers = [jnp.exp(p - peak) for p in peaks]
    norm = sum(p * t for p, t in zip(powers, sums))
    for h, power in zip(holders, powers):
        scale_ref[h] = jnp.broadcast_to(power / norm, (rows, BLK))
    student_top = top_ref[...]
    mass = jnp.zeros((rows, BLK), jnp.float32)
    cross = jnp.zeros((rows, BLK), jnp.float32)
    for b in range(blocks):
        picked = jnp.concatenate([stage_ref[K * b], stage_ref[K * b + 1]], axis=1)
        prob = jnp.dot(spread, picked, preferred_element_type=jnp.float32).astype(jnp.bfloat16)
        mapped = scale_ref[item_ref[1, K * b]] * jnp.dot(
            prob[:, :BLK], weight_ref[:, K * b].reshape(BLK, BLK), preferred_element_type=jnp.float32
        ) + scale_ref[item_ref[1, K * b + 1]] * jnp.dot(
            prob[:, BLK:], weight_ref[:, K * b + 1].reshape(BLK, BLK), preferred_element_type=jnp.float32
        )
        logit = student_ref[:, :, b * BLK : (b + 1) * BLK].reshape(rows, BLK).astype(jnp.float32) - student_top
        mass = mass + mapped
        cross = cross + mapped * (jnp.log(jnp.maximum(mapped, TINY)) - logit)
    mass = jnp.sum(mass, axis=1, keepdims=True)
    cross = jnp.sum(cross, axis=1, keepdims=True)
    lane = lax.broadcasted_iota(jnp.int32, (rows, BLK), 1)
    table = jnp.where(
        lane == 0, mass, jnp.where(lane == 1, cross, jnp.where(lane == 2, student_top, total_ref[...]))
    )
    out_ref[...] = table.T[:8]


def whole(padded_parts, cand, src_block, weights, student_logits):
    doc_count, pos_count, student_cols = student_logits.shape
    teacher_cols = padded_parts[0].shape[2]
    teacher_blocks = teacher_cols // BLK
    student_blocks = student_cols // BLK
    row_count = doc_count * pos_count
    padded = jnp.concatenate(padded_parts, axis=1).reshape(-1, teacher_cols)
    teacher_float = jnp.take(padded, cand, axis=0).astype(jnp.float32)
    student_float = student_logits.reshape(row_count, student_cols).astype(jnp.float32)
    teacher_peak = jnp.max(teacher_float, axis=1)
    student_peak = jnp.max(student_float, axis=1)
    teacher_top, student_top = lax.pmax((teacher_peak, student_peak), "vocab")
    teacher_total, student_total = lax.psum(
        (
            jnp.sum(jnp.exp(teacher_float - teacher_top[:, None]), axis=1),
            jnp.sum(jnp.exp(student_float - student_top[:, None]), axis=1),
        ),
        "vocab",
    )
    teacher_prob = (jnp.exp(teacher_float - teacher_top[:, None]) / teacher_total[:, None]).astype(jnp.bfloat16)
    student_logprob = student_float - student_top[:, None] - jnp.log(student_total)[:, None]
    vocab_count = lax.axis_size("vocab")
    own_index = lax.axis_index("vocab")
    pair_count = student_blocks * K
    capacity = 2 * K * student_blocks // vocab_count
    pair_blocks = src_block.reshape(vocab_count, pair_count)
    holder = pair_blocks // teacher_blocks
    inside = pair_blocks % teacher_blocks
    same_holder = holder[:, :, None] == holder[:, None, :]
    before = jnp.arange(pair_count)[None, :] < jnp.arange(pair_count)[:, None]
    slot_rank = jnp.sum(same_holder & before[None, :, :], axis=2)
    chosen = (holder == own_index)[:, None, :] & (
        slot_rank[:, None, :] == jnp.arange(capacity)[None, :, None]
    )
    send_index = jnp.sum(jnp.where(chosen, inside[:, None, :], 0), axis=2)
    prob_blocks = teacher_prob.reshape(row_count, teacher_blocks, BLK)
    outgoing = jnp.take(prob_blocks, send_index.reshape(-1), axis=1).reshape(row_count, vocab_count, capacity, BLK)
    incoming = lax.all_to_all(outgoing, "vocab", split_axis=1, concat_axis=1, tiled=True)
    own_holder = jnp.take(holder, own_index, axis=0)
    own_rank = jnp.take(slot_rank, own_index, axis=0)
    recv_slot = own_holder * capacity + own_rank
    gathered = jnp.take(incoming.reshape(row_count, vocab_count * capacity, BLK), recv_slot, axis=1).reshape(
        row_count, student_blocks, K, BLK
    )
    weights = weights.swapaxes(0, 1).reshape(student_blocks, K, BLK, BLK)
    mapped = jnp.einsum("rbkc,bkcd->rbd", gathered, weights, preferred_element_type=jnp.float32).reshape(
        row_count, student_cols
    )
    total_mass = lax.psum(jnp.sum(mapped, axis=1), "vocab")
    normed = mapped / total_mass[:, None]
    return lax.psum(
        jnp.sum(jax.scipy.special.xlogy(normed, normed) - normed * student_logprob, axis=1), "vocab"
    )


def shards(teacher_logits, student_logits, alignment, src_block, margin_weight):
    doc_count, pos_count, teacher_cols = teacher_logits.shape
    student_cols = student_logits.shape[2]
    teacher_blocks = teacher_cols // BLK
    student_blocks = student_cols // BLK
    row_count = doc_count * pos_count
    pair_count = student_blocks * K
    vocab_count = lax.axis_size("vocab")
    steps = vocab_count // 2
    home = teacher_blocks + 1
    vocab_index = lax.axis_index("vocab")
    seq_index = lax.axis_index("seq")
    sign = 1 - 2 * (seq_index % 2)
    span = pos_count + 2 * W

    with jax.named_scope("halo"):
        low, high = halo(teacher_logits, W)
    with jax.named_scope("weights"):
        weights = lax.all_gather(
            margin_weight.reshape(pair_count, -1, BLK), "dp", axis=0, tiled=False
        )

    with jax.named_scope("rows"):
        cand = (alignment - seq_index * pos_count + W + jnp.arange(doc_count)[:, None] * span).reshape(-1)
        cand = jnp.clip(cand, 0, doc_count * span - 1)
        places = jnp.arange(doc_count * span)
        used = jnp.any(cand[:, None] == places[None, :], axis=0)
        place_rank = jnp.sum(used[:, None] & (places[:, None] < places[None, :]), axis=0)
        cand_rank = jnp.sum(used[None, :] & (places[None, :] < cand[:, None]), axis=1)
        row_ids = jnp.arange(ROWS)
        pick = ((row_ids[:, None] == place_rank[None, :]) & used[None, :]).astype(jnp.bfloat16)
        spread = (cand_rank[:, None] == row_ids[None, :]).astype(jnp.bfloat16)
        rows_fit = jnp.sum(used.astype(jnp.int32)) <= ROWS

    vmem = pl.BlockSpec(memory_space=pltpu.VMEM)
    smem = pl.BlockSpec(memory_space=pltpu.SMEM)
    def room(mib):
        return pltpu.CompilerParams(vmem_limit_bytes=mib * 1024 * 1024)

    def planes(count):
        return jax.ShapeDtypeStruct((count, ROWS, BLK), jnp.bfloat16)

    with jax.named_scope("pack"):
        listed = src_block.reshape(vocab_count, pair_count)
        place = jnp.stack([vocab_index, sign]).astype(jnp.int32)
        own, ahead, behind, packed = pl.pallas_call(
            pack_kernel,
            out_shape=(planes(home), planes(SLOTS), planes(SLOTS), jax.ShapeDtypeStruct((8, BLK), jnp.int32)),
            in_specs=[vmem] * 6,
            out_specs=(vmem,) * 4,
            scratch_shapes=[
                pltpu.VMEM((doc_count * span, teacher_cols), jnp.bfloat16),
                pltpu.VMEM((teacher_blocks, ROWS, BLK), jnp.bfloat16),
            ],
            compiler_params=room(16),
        )(jnp.broadcast_to(place[:, None], (2, BLK)), listed, teacher_logits, low, high, pick)

    with jax.named_scope("plan"):
        table = jax.ShapeDtypeStruct((8, BLK), jnp.int32)
        send, items, left = pl.pallas_call(
            functools.partial(plan_kernel, teacher_blocks),
            out_shape=(jax.ShapeDtypeStruct((8, 2 * BLK), jnp.int32), table, table),
            in_specs=[smem, vmem, vmem],
            out_specs=(vmem,) * 3,
            scratch_shapes=[pltpu.VMEM((6 * steps, vocab_count, BLK), jnp.float32)],
            compiler_params=room(8),
        )(place, listed, packed)

    def chosen(chain, step, frames):
        part = pl.pallas_call(
            functools.partial(ready_kernel, chain, step),
            out_shape=planes(SLOTS),
            in_specs=[vmem] * (1 + len(frames)),
            out_specs=vmem,
            compiler_params=room(8),
        )(send, own, *frames[:-1])
        return pl.pallas_call(
            functools.partial(pass_kernel, chain, step, home),
            out_shape=planes(SLOTS),
            in_specs=[vmem] * 3,
            out_specs=vmem,
            compiler_params=room(4),
        )(send, part, frames[-1])

    with jax.named_scope("ring"):
        forward, backward = ring_pairs(1), ring_pairs(-1)
        came_ahead, came_behind = [], []
        for step in range(steps):
            if step:
                ahead = chosen(0, step, came_ahead)
            came_ahead.append(lax.ppermute(ahead, ("seq", "vocab"), forward))
            if step:
                behind = chosen(1, step, came_behind)
            came_behind.append(lax.ppermute(behind, ("seq", "vocab"), backward))

    with jax.named_scope("student"):
        top, total = pl.pallas_call(
            student_kernel,
            out_shape=(jax.ShapeDtypeStruct((row_count, BLK), jnp.float32),) * 2,
            in_specs=[vmem],
            out_specs=(vmem,) * 2,
            compiler_params=room(8),
        )(student_logits)

    with jax.named_scope("stage"):
        early = (own, *came_ahead[:-1], *came_behind[:-1])
        held = pl.pallas_call(
            functools.partial(stage_kernel, steps),
            out_shape=planes(pair_count + 2 * vocab_count),
            in_specs=[smem] + [vmem] * len(early),
            out_specs=vmem,
            compiler_params=room(16),
        )(items, *early)

    with jax.named_scope("map"):
        sums = pl.pallas_call(
            functools.partial(map_kernel, steps),
            out_shape=jax.ShapeDtypeStruct((8, row_count), jnp.float32),
            in_specs=[smem] + [vmem] * 8,
            out_specs=vmem,
            scratch_shapes=[
                pltpu.VMEM((pair_count + 2 * vocab_count, ROWS, BLK), jnp.bfloat16),
                pltpu.VMEM((3 * steps, row_count, BLK), jnp.float32),
            ],
            compiler_params=room(20),
        )(items, held, came_ahead[-1], came_behind[-1], spread, weights, student_logits, top, total)

    with jax.named_scope("finish"):
        sent = jnp.broadcast_to(sums[None, :4], (vocab_count, 4, row_count))
        parts = lax.all_to_all(sent, "vocab", split_axis=0, concat_axis=0, tiled=True)
        mass_part, cross_part, top_part, total_part = (parts[:, i] for i in range(4))
        student_top = jnp.max(top_part, axis=0)
        log_total = student_top + jnp.log(jnp.sum(jnp.exp(top_part - student_top) * total_part, axis=0))
        mass = jnp.sum(mass_part, axis=0)
        result = jnp.sum(cross_part + mass_part * (log_total - top_part), axis=0) / mass - jnp.log(mass)

    result = lax.cond(
        rows_fit & (left[0, 0] == 0),
        lambda *_: result,
        lambda *operands: whole(operands[:3], *operands[3:]),
        low,
        teacher_logits,
        high,
        cand,
        src_block,
        weights,
        student_logits,
    )
    return result.reshape(doc_count, pos_count)


def solution(mesh):
    in_specs = (
        P("dp", "seq", "vocab"),
        P("dp", "seq", "vocab"),
        P("dp", "seq"),
        P(),
        P("vocab", None, "dp", None),
    )
    out_specs = P("dp", "seq")
    return jax.shard_map(shards, mesh=mesh, in_specs=in_specs, out_specs=out_specs, check_vma=False)
```

```python
import functools

import jax
import jax.numpy as jnp
from jax import lax
from jax.experimental import pallas as pl
from jax.experimental.pallas import tpu as pltpu
from jax.sharding import PartitionSpec as P

BLK = 128
K = 2
W = 16
ROWS = 104
SIZES = ((21,) * 8, (12, 23, 23, 23, 22, 22, 22, 22))
STARTS = tuple(tuple(sum(sizes[:f]) for f in range(len(sizes))) for sizes in SIZES)
TINY = 1.2e-38


def halo(block, width):
    count = lax.axis_size("seq")
    forward = [(i, i + 1) for i in range(count - 1)]
    backward = [(target, source) for source, target in forward]
    low = lax.ppermute(block[:, block.shape[1] - width :], "seq", forward)
    high = lax.ppermute(block[:, :width], "seq", backward)
    return low, high


def ring_pairs(turn):
    seq_count, vocab_count = lax.axis_size("seq"), lax.axis_size("vocab")
    pairs = []
    for s in range(seq_count):
        step = turn if s % 2 == 0 else -turn
        for v in range(vocab_count):
            pairs.append((s * vocab_count + v, s * vocab_count + (v + step) % vocab_count))
    return pairs


def tie_key(block):
    return (block * 5) & 7


def ways(distance, block, share, vocab_count):
    half = vocab_count // 2
    first = tie_key(block) < share
    ahead = jnp.where((distance >= 1) & ((distance < half) | ((distance == half) & first)), distance, 0)
    behind = jnp.where((distance > half) | ((distance == half) & ~first), vocab_count - distance, 0)
    return ahead, behind


def ones(mask):
    return jnp.where(mask, 1.0, 0.0).astype(jnp.bfloat16)


def tie_share(reach, facing, lane, half):
    share = jnp.zeros((reach[0].shape[0], 1), jnp.int32)
    for part in range(1, 9):
        first = tie_key(lane) < part
        more = jnp.where(facing & first, half, reach[0]) - jnp.where(facing & ~first, half, reach[1])
        share = share + (jnp.sum(more, axis=1, keepdims=True) <= 0).astype(jnp.int32)
    return share


def full_reach(reach, facing, lane, share, blocks, half):
    first = tie_key(lane) < share
    ahead = jnp.where(facing & first, half, reach[0])
    behind = jnp.where(facing & ~first, half, reach[1])
    return [jnp.where(lane == blocks, half, ahead), jnp.where(lane == blocks, half - 1, behind)]


def split(listed, blocks, vocab_count):
    holder = sum((listed >= h * blocks).astype(jnp.int32) for h in range(1, vocab_count))
    return holder, listed - holder * blocks


def turn(table):
    rows, columns = table.shape
    table = table.astype(jnp.float32)
    if columns < BLK:
        table = jnp.concatenate([table, jnp.zeros((rows, BLK - columns), jnp.float32)], axis=1)
    if rows < BLK:
        table = jnp.concatenate([table, jnp.zeros((BLK - rows, BLK), jnp.float32)], axis=0)
    return table.T.astype(jnp.int32)


def earlier_lanes():
    square = (BLK, BLK)
    return ones(lax.broadcasted_iota(jnp.int32, square, 0) < lax.broadcasted_iota(jnp.int32, square, 1))


def plan_kernel(blocks, place_ref, listed_ref, after_ref, send_ref, item_ref, fit_ref, book_ref):
    vocab_count, pair_count = listed_ref.shape
    half = vocab_count // 2
    steps = half
    home = blocks + 1
    me, sign = place_ref[0], place_ref[1]
    f32, i32 = jnp.float32, jnp.int32
    shape = (vocab_count, BLK)
    straight = sign > 0

    def of_chain(table, way, f):
        return jnp.where(straight, float(table[way][f]), float(table[1 - way][f]))


    del after_ref
    listed = listed_ref[...]
    row_holder, _ = split(listed, blocks, vocab_count)
    holders, inners = split(turn(listed)[:pair_count], blocks, vocab_count)
    lane = lax.broadcasted_iota(i32, shape, 1)
    row = lax.broadcasted_iota(i32, shape, 0)

    reach = [jnp.zeros(shape, i32), jnp.zeros(shape, i32)]
    across = jnp.zeros(shape, i32)
    pair_lane = lax.broadcasted_iota(i32, (pair_count, BLK), 1)
    pair_row = lax.broadcasted_iota(i32, (vocab_count, pair_count), 0)
    for s in range(vocab_count):
        hits = jnp.dot(
            ones(pair_row == row_holder[s : s + 1, :]),
            ones(pair_lane == inners[:, s : s + 1]),
            preferred_element_type=f32,
        )
        distance = s - row
        distance = jnp.where(distance < 0, distance + vocab_count, distance)
        needed = hits > 0
        reach[0] = jnp.maximum(reach[0], jnp.where(needed & (distance < half), distance, 0))
        reach[1] = jnp.maximum(reach[1], jnp.where(needed & (distance > half), vocab_count - distance, 0))
        across = jnp.maximum(across, jnp.where(needed & (distance == half), 1, 0))
    share = tie_share(reach, across > 0, lane, half)
    reach = full_reach(reach, across > 0, lane, share, blocks, half)

    square = (BLK, BLK)
    up, over = lax.broadcasted_iota(i32, square, 0), lax.broadcasted_iota(i32, square, 1)
    earlier = earlier_lanes()
    left_up, left_over = (up & 7) + 1 - (up >> 3), (over & 7) + 1 - (over >> 3)
    goes_first = ones((left_up > left_over) | ((left_up == left_over) & ((up >> 3) > (over >> 3))))
    index, waiting, moved = [], [], [jnp.zeros(shape, f32)] * 2
    for way in range(2):
        masks = jnp.concatenate([ones(reach[way] == r) for r in range(1, half + 1)], axis=0)
        before = jnp.dot(masks, earlier, preferred_element_type=f32)
        place = jnp.zeros(shape, f32)
        count = jnp.zeros(shape, f32)
        for r in range(1, half + 1):
            same = reach[way] == r
            place = jnp.where(same, before[(r - 1) * vocab_count : r * vocab_count], place)
            total = jnp.sum(jnp.where(same, 1.0, 0.0), axis=1, keepdims=True)
            count = jnp.where(lane == r - 1, total, count)
        index.append(place)
        waiting.append(count)
    travels = (lane >= 8) & (lane < 8 * half) & ((lane & 7) + 1 > (lane >> 3))
    for f in range(steps):
        ahead_of = jnp.dot(
            jnp.concatenate(waiting, axis=0).astype(jnp.bfloat16), goes_first, preferred_element_type=f32
        )
        for way in range(2):
            first = ahead_of[way * vocab_count : (way + 1) * vocab_count]
            size = of_chain(SIZES, way, f)
            go = jnp.clip(size - first, 0.0, waiting[way])
            book_ref[(f * 2 + way) * 3] = moved[way]
            moved[way] = moved[way] + go
            book_ref[(f * 2 + way) * 3 + 1] = moved[way]
            book_ref[(f * 2 + way) * 3 + 2] = jnp.minimum(first, size)
            come = pltpu.roll(pltpu.roll(go, 8, 1), 1 if way == 0 else vocab_count - 1, 0)
            waiting[way] = waiting[way] - go + jnp.where(travels, come, 0.0)
    left = jnp.sum(waiting[0] + waiting[1], axis=1, keepdims=True)
    left = jnp.sum(jnp.broadcast_to(left, shape), axis=0, keepdims=True)
    fit_ref[...] = jnp.broadcast_to(left, fit_ref.shape).astype(i32)

    small = (vocab_count, vocab_count)
    target = lax.broadcasted_iota(i32, (BLK, 2 * BLK), 1).astype(f32)
    pointer, sends = [], []
    for way in range(2):
        step = 1 if way == 0 else -1
        back = me - step * lax.broadcasted_iota(i32, small, 0)
        back = jnp.where(back < 0, back + vocab_count, jnp.where(back >= vocab_count, back - vocab_count, back))
        pick = ones(back == lax.broadcasted_iota(i32, small, 1))
        far = jnp.dot(pick, reach[way].astype(f32).astype(jnp.bfloat16), preferred_element_type=f32).astype(i32)
        order = jnp.dot(pick, index[way].astype(jnp.bfloat16), preferred_element_type=f32)
        giver = me - step
        giver = jnp.where(giver < 0, giver + vocab_count, jnp.where(giver >= vocab_count, giver - vocab_count, giver))

        def slot(at, hops, valid):
            column = jnp.clip(hops * 8 + far - 1, 0, BLK - 1)
            where = jnp.full(shape, -1.0, f32)
            for f in range(steps):
                start, end, first = (
                    jnp.take_along_axis(
                        jnp.broadcast_to(book_ref[(f * 2 + way) * 3 + kind, pl.ds(at, 1), :], shape),
                        column,
                        axis=1,
                        mode="promise_in_bounds",
                    )
                    for kind in range(3)
                )
                now = valid & (start <= order) & (order < end)
                where = jnp.where(now, of_chain(STARTS, way, f) + first + order - start, where)
            return where

        leave = slot(me, row, (far > row) & (row < half))
        arrive = slot(giver, row - 1, (far >= row) & (row >= 1) & (row <= half))
        point = jnp.where(row == 0, lane.astype(f32), jnp.maximum(home + arrive, 0.0))
        pointer.append(point)
        leave_turned = jnp.concatenate([leave, jnp.full((BLK - vocab_count, BLK), -1.0, f32)], axis=0).T
        chosen = jnp.zeros((1, 2 * BLK), f32)
        for h in range(half):
            chosen = chosen + jnp.dot(
                point[h : h + 1].astype(jnp.bfloat16),
                ones(leave_turned[:, h : h + 1] == target),
                preferred_element_type=f32,
            )
        sends.append(chosen.astype(i32))
    send_ref[0:1, :] = jnp.where(straight, sends[0], sends[1])
    send_ref[1:2, :] = jnp.where(straight, sends[1], sends[0])
    send_ref[2:8, :] = jnp.zeros((6, 2 * BLK), i32)

    mine_lane = lax.broadcasted_iota(i32, (pair_count, vocab_count), 1)
    holder = jnp.sum(jnp.where(pair_lane == me, holders, 0), axis=1, keepdims=True)
    inner = jnp.sum(jnp.where(pair_lane == me, inners, 0), axis=1, keepdims=True)
    distance = me - holder
    distance = jnp.where(distance < 0, distance + vocab_count, distance)
    share = turn(jnp.broadcast_to(share, shape))[:1]
    share = jnp.sum(jnp.where(pair_lane == holder, share, 0), axis=1, keepdims=True)
    hops = ways(distance, inner, share, vocab_count)
    scale = jnp.where(distance <= half, distance, 2 * vocab_count - distance)
    points = jnp.zeros((pair_count, 1), f32)
    for way in range(2):
        found = lax.dot_general(
            ones(pair_lane == inner),
            pointer[way].astype(jnp.bfloat16),
            (((1,), (1,)), ((), ())),
            preferred_element_type=f32,
        )
        points = points + jnp.sum(
            jnp.where((mine_lane == hops[way]) & (hops[way] > 0), found, 0.0), axis=1, keepdims=True
        )
    points = jnp.where(distance == 0, inner.astype(f32), points)
    by_stats = [jnp.sum(jnp.where(lane == blocks, p, 0.0), axis=1, keepdims=True) for p in pointer]
    hop = lax.broadcasted_iota(i32, (vocab_count, 1), 0)
    stat_ok = [hop <= half, (hop >= 1) & (hop < half)]
    points = jnp.concatenate(
        [points] + [jnp.where(ok, p, 0.0) for ok, p in zip(stat_ok, by_stats)], axis=0
    ).astype(i32)
    other = jnp.concatenate(
        [(hops[1] > 0).astype(i32), jnp.zeros((vocab_count, 1), i32), jnp.ones((vocab_count, 1), i32)], axis=0
    )
    other = jnp.where(straight, other, 1 - other)
    scale = jnp.concatenate([scale, jnp.zeros((2 * vocab_count, 1), i32)], axis=0)
    frame = jnp.zeros(points.shape, i32)
    base = jnp.full(points.shape, home, i32)
    limit = jnp.where(other == 1, SIZES[1][0], SIZES[0][0])
    for f in range(1, steps):
        reached = points >= home + jnp.where(other == 1, STARTS[1][f], STARTS[0][f])
        frame = frame + reached.astype(i32)
        base = jnp.where(reached, home + jnp.where(other == 1, STARTS[1][f], STARTS[0][f]), base)
        limit = jnp.where(reached, jnp.where(other == 1, SIZES[1][f], SIZES[0][f]), limit)
    away = points >= home
    source = jnp.where(away, 1 + frame + steps * other, 0)
    spot = jnp.where(away, points - base, points)
    spot = jnp.clip(spot, 0, jnp.where(away, limit, home) - 1)
    items = points.shape[0]
    item_lane = lax.broadcasted_iota(i32, (items, BLK), 1)
    table = jnp.where(
        item_lane == 0, spot, jnp.where(item_lane == 1, scale, jnp.where(item_lane == 2, source, 0))
    ).astype(f32)
    turned = jnp.concatenate([table, jnp.zeros((BLK - items, BLK), f32)], axis=0).T
    source_row = turned[2:3].astype(i32)
    item_up = lax.broadcasted_iota(i32, (items, BLK), 0)
    is_item = item_lane < items
    sooner = is_item & ((source_row < source) | ((source_row == source) & (item_lane < item_up)))
    rank = jnp.sum(sooner.astype(i32), axis=1, keepdims=True)
    item_ref[0:1, :] = turned[0:1].astype(i32)
    item_ref[1:2, :] = turned[1:2].astype(i32)
    item_ref[2:3, :] = jnp.sum(jnp.where(rank == item_lane, item_up, 0), axis=0, keepdims=True)
    item_ref[3:4, :] = jnp.sum((source < item_lane).astype(i32), axis=0, keepdims=True)
    item_ref[4:8, :] = jnp.zeros((4, BLK), i32)


def scalars(table_ref, row, start, count):
    values = table_ref[row : row + 1, :]
    return [values[0, start + j] for j in range(count)]


def in_order(place, valid, count):
    square = (BLK, BLK)
    up, over = lax.broadcasted_iota(jnp.int32, square, 0), lax.broadcasted_iota(jnp.int32, square, 1)
    lanes = jnp.sum(jnp.where((place == up) & valid, over, 0), axis=1, keepdims=True)
    row = turn(jnp.broadcast_to(lanes, square))[:1]
    return [row[0, j] for j in range(count)]


def first_choice(blocks, place_ref, listed_ref):
    vocab_count, pair_count = listed_ref.shape
    half = vocab_count // 2
    i32 = jnp.int32
    me, sign = place_ref[0:1, :], place_ref[1:2, :]
    holders, inners = split(turn(listed_ref[...])[:pair_count], blocks, vocab_count)
    pair_lane = lax.broadcasted_iota(i32, (pair_count, BLK), 1)
    lane = lax.broadcasted_iota(i32, (1, BLK), 1)
    reach = [jnp.zeros((1, BLK), i32), jnp.zeros((1, BLK), i32)]
    facing = jnp.zeros((1, BLK), i32)
    for s in range(vocab_count):
        hits = (pair_lane == inners[:, s : s + 1]) & (jnp.broadcast_to(holders[:, s : s + 1], pair_lane.shape) == me)
        seen = jnp.max(jnp.where(hits, 1, 0), axis=0, keepdims=True)
        distance = s - me
        distance = jnp.where(distance < 0, distance + vocab_count, distance)
        reach[0] = jnp.maximum(reach[0], jnp.where(distance < half, distance * seen, 0))
        reach[1] = jnp.maximum(reach[1], jnp.where(distance > half, (vocab_count - distance) * seen, 0))
        facing = jnp.maximum(facing, jnp.where(distance == half, seen, 0))
    share = tie_share(reach, facing > 0, lane, half)
    reach = full_reach(reach, facing > 0, lane, share, blocks, half)
    choices = []
    for sizes, one, other in zip(SIZES, reach, reach[::-1]):
        far = jnp.where(sign > 0, one, other)
        key = jnp.broadcast_to(far * BLK + (BLK - 1 - lane), (BLK, BLK))
        place = jnp.sum((turn(key) > key).astype(i32), axis=0, keepdims=True)
        choices.append(in_order(place, far > 0, sizes[0]))
    return choices


def pack_kernel(
    place_ref,
    listed_ref,
    own_ref,
    low_ref,
    high_ref,
    pick_ref,
    home_ref,
    first_ref,
    second_ref,
    done_ref,
    cand_ref,
    logit_ref,
):
    docs, positions, columns = own_ref.shape
    width = low_ref.shape[1]
    span = positions + 2 * width
    rows = pick_ref.shape[0]
    blocks = columns // BLK
    for doc in range(docs):
        cand_ref[doc * span : doc * span + width, :] = low_ref[doc]
        cand_ref[doc * span + width : doc * span + width + positions, :] = own_ref[doc]
        cand_ref[doc * span + width + positions : (doc + 1) * span, :] = high_ref[doc]
    pick = pick_ref[...]
    peak = jnp.full((rows, BLK), -jnp.inf, jnp.float32)
    for t in range(blocks):
        part = jnp.dot(pick, cand_ref[:, t * BLK : (t + 1) * BLK], preferred_element_type=jnp.float32)
        logit_ref[t] = part.astype(jnp.bfloat16)
        peak = jnp.maximum(peak, part)
    top = jnp.max(peak, axis=1, keepdims=True)
    total = jnp.zeros((rows, BLK), jnp.float32)
    for t in range(blocks):
        power = jnp.exp(logit_ref[t].astype(jnp.float32) - top)
        total = total + power
        home_ref[t] = power.astype(jnp.bfloat16)
    total = jnp.sum(total, axis=1, keepdims=True)
    first = total.astype(jnp.bfloat16).astype(jnp.float32)
    second = (total - first).astype(jnp.bfloat16).astype(jnp.float32)
    third = total - first - second
    lane = lax.broadcasted_iota(jnp.int32, (rows, BLK), 1)
    home_ref[blocks] = jnp.where(
        lane == 0, top, jnp.where(lane == 1, first, jnp.where(lane == 2, second, jnp.where(lane == 3, third, 0.0)))
    ).astype(jnp.bfloat16)
    for out_ref, choice in zip((first_ref, second_ref), first_choice(blocks, place_ref, listed_ref)):
        for j, at in enumerate(choice):
            out_ref[j] = home_ref[at]
    done_ref[...] = jnp.zeros(done_ref.shape, jnp.int32)


def ready_kernel(chain, step, after_ref, send_ref, home_ref, *refs):
    del after_ref
    frames, out_ref = refs[:-1], refs[-1]
    home = home_ref.shape[0]
    for j, at in enumerate(scalars(send_ref, chain, STARTS[chain][step], SIZES[chain][step])):

        def copy(low, high, j=j, at=at):
            if high - low == 1:
                if low == 0:
                    out_ref[j] = home_ref[at]
                elif low <= len(frames):
                    out_ref[j] = frames[low - 1][at - home - STARTS[chain][low - 1]]
                return
            mid = (low + high) // 2
            split = home + STARTS[chain][mid - 1]
            pl.when(at < split)(lambda: copy(low, mid))
            pl.when(at >= split)(lambda: copy(mid, high))

        copy(0, len(frames) + 2)


def pass_kernel(chain, step, home, send_ref, part_ref, newest_ref, out_ref):
    start = home + STARTS[chain][step - 1]
    for j, at in enumerate(scalars(send_ref, chain, STARTS[chain][step], SIZES[chain][step])):
        newest = newest_ref[jnp.maximum(at - start, 0)]
        out_ref[j] = jnp.where(at >= start, newest, part_ref[j])


def stage_kernel(steps, item_ref, *refs):
    sources, stage_ref = refs[:-1], refs[-1]
    for s, source in zip([s for s in range(2 * steps + 1) if s not in (steps, 2 * steps)], sources):
        bring(item_ref, s, source, stage_ref)


def bring(item_ref, s, source_ref, stage_ref):
    def one(q, carry):
        item = item_ref[2, q]
        stage_ref[item] = source_ref[item_ref[0, item]]
        return carry

    lax.fori_loop(item_ref[3, s], item_ref[3, s + 1], one, 0)


def student_kernel(student_ref, top_ref, total_ref):
    docs, positions, columns = student_ref.shape
    rows = docs * positions
    peak = jnp.full((rows, BLK), -jnp.inf, jnp.float32)
    for b in range(columns // BLK):
        part = student_ref[:, :, b * BLK : (b + 1) * BLK].reshape(rows, BLK).astype(jnp.float32)
        peak = jnp.maximum(peak, part)
    top = jnp.max(peak, axis=1, keepdims=True)
    total = jnp.zeros((rows, BLK), jnp.float32)
    for b in range(columns // BLK):
        part = student_ref[:, :, b * BLK : (b + 1) * BLK].reshape(rows, BLK).astype(jnp.float32)
        total = total + jnp.exp(part - top)
    top_ref[...] = jnp.broadcast_to(top, (rows, BLK))
    total_ref[...] = jnp.broadcast_to(jnp.sum(total, axis=1, keepdims=True), (rows, BLK))


def map_kernel(
    steps,
    item_ref,
    held_ref,
    ahead_ref,
    behind_ref,
    spread_ref,
    weight_ref,
    student_ref,
    top_ref,
    total_ref,
    out_ref,
    stage_ref,
    scale_ref,
):
    docs, positions, columns = student_ref.shape
    rows = docs * positions
    blocks = columns // BLK
    spread = spread_ref[...]
    for i in range(stage_ref.shape[0]):
        stage_ref[i] = held_ref[i]
    bring(item_ref, steps, ahead_ref, stage_ref)
    bring(item_ref, 2 * steps, behind_ref, stage_ref)
    holders = [h for h in range(steps + 1)] + [2 * steps + h for h in range(1, steps)]
    peaks, sums = [], []
    for h in holders:
        stats = jnp.dot(spread, stage_ref[K * blocks + h], preferred_element_type=jnp.float32)
        peaks.append(stats[:, 0:1])
        sums.append(stats[:, 1:2] + stats[:, 2:3] + stats[:, 3:4])
    peak = functools.reduce(jnp.maximum, peaks)
    powers = [jnp.exp(p - peak) for p in peaks]
    norm = sum(p * t for p, t in zip(powers, sums))
    for h, power in zip(holders, powers):
        scale_ref[h] = jnp.broadcast_to(power / norm, (rows, BLK))
    student_top = top_ref[...]
    mass = jnp.zeros((rows, BLK), jnp.float32)
    cross = jnp.zeros((rows, BLK), jnp.float32)
    for b in range(blocks):
        picked = jnp.concatenate([stage_ref[K * b], stage_ref[K * b + 1]], axis=1)
        prob = jnp.dot(spread, picked, preferred_element_type=jnp.float32).astype(jnp.bfloat16)
        mapped = scale_ref[item_ref[1, K * b]] * jnp.dot(
            prob[:, :BLK], weight_ref[:, K * b].reshape(BLK, BLK), preferred_element_type=jnp.float32
        ) + scale_ref[item_ref[1, K * b + 1]] * jnp.dot(
            prob[:, BLK:], weight_ref[:, K * b + 1].reshape(BLK, BLK), preferred_element_type=jnp.float32
        )
        logit = student_ref[:, :, b * BLK : (b + 1) * BLK].reshape(rows, BLK).astype(jnp.float32) - student_top
        mass = mass + mapped
        cross = cross + mapped * (jnp.log(jnp.maximum(mapped, TINY)) - logit)
    mass = jnp.sum(mass, axis=1, keepdims=True)
    cross = jnp.sum(cross, axis=1, keepdims=True)
    lane = lax.broadcasted_iota(jnp.int32, (rows, BLK), 1)
    table = jnp.where(
        lane == 0, mass, jnp.where(lane == 1, cross, jnp.where(lane == 2, student_top, total_ref[...]))
    )
    out_ref[...] = table.T[:8]


def whole(padded_parts, cand, src_block, weights, student_logits):
    doc_count, pos_count, student_cols = student_logits.shape
    teacher_cols = padded_parts[0].shape[2]
    teacher_blocks = teacher_cols // BLK
    student_blocks = student_cols // BLK
    row_count = doc_count * pos_count
    padded = jnp.concatenate(padded_parts, axis=1).reshape(-1, teacher_cols)
    teacher_float = jnp.take(padded, cand, axis=0).astype(jnp.float32)
    student_float = student_logits.reshape(row_count, student_cols).astype(jnp.float32)
    teacher_peak = jnp.max(teacher_float, axis=1)
    student_peak = jnp.max(student_float, axis=1)
    teacher_top, student_top = lax.pmax((teacher_peak, student_peak), "vocab")
    teacher_total, student_total = lax.psum(
        (
            jnp.sum(jnp.exp(teacher_float - teacher_top[:, None]), axis=1),
            jnp.sum(jnp.exp(student_float - student_top[:, None]), axis=1),
        ),
        "vocab",
    )
    teacher_prob = (jnp.exp(teacher_float - teacher_top[:, None]) / teacher_total[:, None]).astype(jnp.bfloat16)
    student_logprob = student_float - student_top[:, None] - jnp.log(student_total)[:, None]
    vocab_count = lax.axis_size("vocab")
    own_index = lax.axis_index("vocab")
    pair_count = student_blocks * K
    capacity = 2 * K * student_blocks // vocab_count
    pair_blocks = src_block.reshape(vocab_count, pair_count)
    holder = pair_blocks // teacher_blocks
    inside = pair_blocks % teacher_blocks
    same_holder = holder[:, :, None] == holder[:, None, :]
    before = jnp.arange(pair_count)[None, :] < jnp.arange(pair_count)[:, None]
    slot_rank = jnp.sum(same_holder & before[None, :, :], axis=2)
    chosen = (holder == own_index)[:, None, :] & (
        slot_rank[:, None, :] == jnp.arange(capacity)[None, :, None]
    )
    send_index = jnp.sum(jnp.where(chosen, inside[:, None, :], 0), axis=2)
    prob_blocks = teacher_prob.reshape(row_count, teacher_blocks, BLK)
    outgoing = jnp.take(prob_blocks, send_index.reshape(-1), axis=1).reshape(row_count, vocab_count, capacity, BLK)
    incoming = lax.all_to_all(outgoing, "vocab", split_axis=1, concat_axis=1, tiled=True)
    own_holder = jnp.take(holder, own_index, axis=0)
    own_rank = jnp.take(slot_rank, own_index, axis=0)
    recv_slot = own_holder * capacity + own_rank
    gathered = jnp.take(incoming.reshape(row_count, vocab_count * capacity, BLK), recv_slot, axis=1).reshape(
        row_count, student_blocks, K, BLK
    )
    weights = weights.swapaxes(0, 1).reshape(student_blocks, K, BLK, BLK)
    mapped = jnp.einsum("rbkc,bkcd->rbd", gathered, weights, preferred_element_type=jnp.float32).reshape(
        row_count, student_cols
    )
    total_mass = lax.psum(jnp.sum(mapped, axis=1), "vocab")
    normed = mapped / total_mass[:, None]
    return lax.psum(
        jnp.sum(jax.scipy.special.xlogy(normed, normed) - normed * student_logprob, axis=1), "vocab"
    )


def shards(teacher_logits, student_logits, alignment, src_block, margin_weight):
    doc_count, pos_count, teacher_cols = teacher_logits.shape
    student_cols = student_logits.shape[2]
    teacher_blocks = teacher_cols // BLK
    student_blocks = student_cols // BLK
    row_count = doc_count * pos_count
    pair_count = student_blocks * K
    vocab_count = lax.axis_size("vocab")
    steps = vocab_count // 2
    home = teacher_blocks + 1
    vocab_index = lax.axis_index("vocab")
    seq_index = lax.axis_index("seq")
    sign = 1 - 2 * (seq_index % 2)
    span = pos_count + 2 * W

    with jax.named_scope("halo"):
        low, high = halo(teacher_logits, W)
    with jax.named_scope("weights"):
        weights = lax.all_gather(
            margin_weight.reshape(pair_count, -1, BLK), "dp", axis=0, tiled=False
        )

    with jax.named_scope("rows"):
        cand = (alignment - seq_index * pos_count + W + jnp.arange(doc_count)[:, None] * span).reshape(-1)
        cand = jnp.clip(cand, 0, doc_count * span - 1)
        places = jnp.arange(doc_count * span)
        used = jnp.any(cand[:, None] == places[None, :], axis=0)
        place_rank = jnp.sum(used[:, None] & (places[:, None] < places[None, :]), axis=0)
        cand_rank = jnp.sum(used[None, :] & (places[None, :] < cand[:, None]), axis=1)
        row_ids = jnp.arange(ROWS)
        pick = ((row_ids[:, None] == place_rank[None, :]) & used[None, :]).astype(jnp.bfloat16)
        spread = (cand_rank[:, None] == row_ids[None, :]).astype(jnp.bfloat16)
        rows_fit = jnp.sum(used.astype(jnp.int32)) <= ROWS

    vmem = pl.BlockSpec(memory_space=pltpu.VMEM)
    smem = pl.BlockSpec(memory_space=pltpu.SMEM)
    anywhere = pl.BlockSpec(memory_space=pl.ANY)
    def room(mib):
        return pltpu.CompilerParams(vmem_limit_bytes=mib * 1024 * 1024)

    def planes(count):
        return jax.ShapeDtypeStruct((count, ROWS, BLK), jnp.bfloat16)

    with jax.named_scope("pack"):
        listed = src_block.reshape(vocab_count, pair_count)
        place = jnp.stack([vocab_index, sign]).astype(jnp.int32)
        own, ahead, behind, packed = pl.pallas_call(
            pack_kernel,
            out_shape=(planes(home), planes(SIZES[0][0]), planes(SIZES[1][0]), jax.ShapeDtypeStruct((8, BLK), jnp.int32)),
            in_specs=[vmem] * 6,
            out_specs=(vmem,) * 4,
            scratch_shapes=[
                pltpu.VMEM((doc_count * span, teacher_cols), jnp.bfloat16),
                pltpu.VMEM((teacher_blocks, ROWS, BLK), jnp.bfloat16),
            ],
            compiler_params=room(16),
        )(jnp.broadcast_to(place[:, None], (2, BLK)), listed, teacher_logits, low, high, pick)

    with jax.named_scope("plan"):
        table = jax.ShapeDtypeStruct((8, BLK), jnp.int32)
        send, items, left = pl.pallas_call(
            functools.partial(plan_kernel, teacher_blocks),
            out_shape=(jax.ShapeDtypeStruct((8, 2 * BLK), jnp.int32), table, table),
            in_specs=[smem, vmem, vmem],
            out_specs=(vmem,) * 3,
            scratch_shapes=[pltpu.VMEM((6 * steps, vocab_count, BLK), jnp.float32)],
            compiler_params=room(8),
        )(place, listed, packed)

    def ready(chain, step, after, frames):
        return pl.pallas_call(
            functools.partial(ready_kernel, chain, step),
            out_shape=planes(SIZES[chain][step]),
            in_specs=[anywhere] + [vmem] * (2 + len(frames)),
            out_specs=vmem,
            compiler_params=room(8),
        )(after, send, own, *frames)

    def passed(chain, step, part, newest):
        return pl.pallas_call(
            functools.partial(pass_kernel, chain, step, home),
            out_shape=planes(SIZES[chain][step]),
            in_specs=[vmem] * 3,
            out_specs=vmem,
            compiler_params=room(4),
        )(send, part, newest)

    with jax.named_scope("ring"):
        forward, backward = ring_pairs(1), ring_pairs(-1)
        came_behind = [lax.ppermute(behind, ("seq", "vocab"), backward)]
        came_ahead = [lax.ppermute(ahead, ("seq", "vocab"), forward)]
        for step in range(1, steps):
            part = ready(1, step, ahead, came_behind[:-1])
            behind = passed(1, step, part, came_behind[-1])
            came_behind.append(lax.ppermute(behind, ("seq", "vocab"), backward))
            part = ready(0, step, behind, came_ahead[:-1])
            ahead = passed(0, step, part, came_ahead[-1])
            came_ahead.append(lax.ppermute(ahead, ("seq", "vocab"), forward))

    with jax.named_scope("student"):
        top, total = pl.pallas_call(
            student_kernel,
            out_shape=(jax.ShapeDtypeStruct((row_count, BLK), jnp.float32),) * 2,
            in_specs=[vmem],
            out_specs=(vmem,) * 2,
            compiler_params=room(8),
        )(student_logits)

    with jax.named_scope("stage"):
        early = (own, *came_ahead[:-1], *came_behind[:-1])
        held = pl.pallas_call(
            functools.partial(stage_kernel, steps),
            out_shape=planes(pair_count + 2 * vocab_count),
            in_specs=[smem] + [vmem] * len(early),
            out_specs=vmem,
            compiler_params=room(16),
        )(items, *early)

    with jax.named_scope("map"):
        sums = pl.pallas_call(
            functools.partial(map_kernel, steps),
            out_shape=jax.ShapeDtypeStruct((8, row_count), jnp.float32),
            in_specs=[smem] + [vmem] * 8,
            out_specs=vmem,
            scratch_shapes=[
                pltpu.VMEM((pair_count + 2 * vocab_count, ROWS, BLK), jnp.bfloat16),
                pltpu.VMEM((3 * steps, row_count, BLK), jnp.float32),
            ],
            compiler_params=room(20),
        )(items, held, came_ahead[-1], came_behind[-1], spread, weights, student_logits, top, total)

    with jax.named_scope("finish"):
        sent = jnp.broadcast_to(sums[None, :4], (vocab_count, 4, row_count))
        parts = lax.all_to_all(sent, "vocab", split_axis=0, concat_axis=0, tiled=True)
        mass_part, cross_part, top_part, total_part = (parts[:, i] for i in range(4))
        student_top = jnp.max(top_part, axis=0)
        log_total = student_top + jnp.log(jnp.sum(jnp.exp(top_part - student_top) * total_part, axis=0))
        mass = jnp.sum(mass_part, axis=0)
        result = jnp.sum(cross_part + mass_part * (log_total - top_part), axis=0) / mass - jnp.log(mass)

    result = lax.cond(
        rows_fit & (left[0, 0] == 0),
        lambda *_: result,
        lambda *operands: whole(operands[:3], *operands[3:]),
        low,
        teacher_logits,
        high,
        cand,
        src_block,
        weights,
        student_logits,
    )
    return result.reshape(doc_count, pos_count)


def solution(mesh):
    in_specs = (
        P("dp", "seq", "vocab"),
        P("dp", "seq", "vocab"),
        P("dp", "seq"),
        P(),
        P("vocab", None, "dp", None),
    )
    out_specs = P("dp", "seq")
    return jax.shard_map(shards, mesh=mesh, in_specs=in_specs, out_specs=out_specs, check_vma=False)
```

```python
import functools

import jax
import jax.numpy as jnp
from jax import lax
from jax.experimental import pallas as pl
from jax.experimental.pallas import tpu as pltpu
from jax.sharding import PartitionSpec as P

BLK = 128
K = 2
W = 16
ROWS = 104
SIZES = ((21,) * 8, (12, 23, 23, 23, 22, 22, 22, 22))
STARTS = tuple(tuple(sum(sizes[:f]) for f in range(len(sizes))) for sizes in SIZES)
TINY = 1.2e-38


def halo(block, width):
    count = lax.axis_size("seq")
    forward = [(i, (i + 1) % count) for i in range(count)]
    backward = [(target, source) for source, target in forward]
    low = lax.ppermute(block[:, block.shape[1] - width :], "seq", forward)
    high = lax.ppermute(block[:, :width], "seq", backward)
    return low, high


def ring_pairs(turn):
    seq_count, vocab_count = lax.axis_size("seq"), lax.axis_size("vocab")
    pairs = []
    for s in range(seq_count):
        step = turn if s % 2 == 0 else -turn
        for v in range(vocab_count):
            pairs.append((s * vocab_count + v, s * vocab_count + (v + step) % vocab_count))
    return pairs


def tie_key(block):
    return (block * 5) & 7


def ways(distance, block, share, vocab_count):
    half = vocab_count // 2
    first = tie_key(block) < share
    ahead = jnp.where((distance >= 1) & ((distance < half) | ((distance == half) & first)), distance, 0)
    behind = jnp.where((distance > half) | ((distance == half) & ~first), vocab_count - distance, 0)
    return ahead, behind


def ones(mask):
    return jnp.where(mask, 1.0, 0.0).astype(jnp.bfloat16)


def tie_share(reach, facing, lane, half):
    share = jnp.zeros((reach[0].shape[0], 1), jnp.int32)
    for part in range(1, 9):
        first = tie_key(lane) < part
        more = jnp.where(facing & first, half, reach[0]) - jnp.where(facing & ~first, half, reach[1])
        share = share + (jnp.sum(more, axis=1, keepdims=True) <= 0).astype(jnp.int32)
    return share


def full_reach(reach, facing, lane, share, blocks, half):
    first = tie_key(lane) < share
    ahead = jnp.where(facing & first, half, reach[0])
    behind = jnp.where(facing & ~first, half, reach[1])
    return [jnp.where(lane == blocks, half, ahead), jnp.where(lane == blocks, half - 1, behind)]


def split(listed, blocks, vocab_count):
    holder = sum((listed >= h * blocks).astype(jnp.int32) for h in range(1, vocab_count))
    return holder, listed - holder * blocks


def turn(table):
    rows, columns = table.shape
    table = table.astype(jnp.float32)
    if columns < BLK:
        table = jnp.concatenate([table, jnp.zeros((rows, BLK - columns), jnp.float32)], axis=1)
    if rows < BLK:
        table = jnp.concatenate([table, jnp.zeros((BLK - rows, BLK), jnp.float32)], axis=0)
    return table.T.astype(jnp.int32)


def earlier_lanes():
    square = (BLK, BLK)
    return ones(lax.broadcasted_iota(jnp.int32, square, 0) < lax.broadcasted_iota(jnp.int32, square, 1))


def plan_kernel(blocks, place_ref, listed_ref, after_ref, send_ref, item_ref, fit_ref, book_ref):
    vocab_count, pair_count = listed_ref.shape
    half = vocab_count // 2
    steps = half
    home = blocks + 1
    me, sign = place_ref[0], place_ref[1]
    f32, i32 = jnp.float32, jnp.int32
    shape = (vocab_count, BLK)
    straight = sign > 0

    def of_chain(table, way, f):
        return jnp.where(straight, float(table[way][f]), float(table[1 - way][f]))


    del after_ref
    listed = listed_ref[...]
    row_holder, _ = split(listed, blocks, vocab_count)
    holders, inners = split(turn(listed)[:pair_count], blocks, vocab_count)
    lane = lax.broadcasted_iota(i32, shape, 1)
    row = lax.broadcasted_iota(i32, shape, 0)

    reach = [jnp.zeros(shape, i32), jnp.zeros(shape, i32)]
    across = jnp.zeros(shape, i32)
    pair_lane = lax.broadcasted_iota(i32, (pair_count, BLK), 1)
    pair_row = lax.broadcasted_iota(i32, (vocab_count, pair_count), 0)
    for s in range(vocab_count):
        hits = jnp.dot(
            ones(pair_row == row_holder[s : s + 1, :]),
            ones(pair_lane == inners[:, s : s + 1]),
            preferred_element_type=f32,
        )
        distance = s - row
        distance = jnp.where(distance < 0, distance + vocab_count, distance)
        needed = hits > 0
        reach[0] = jnp.maximum(reach[0], jnp.where(needed & (distance < half), distance, 0))
        reach[1] = jnp.maximum(reach[1], jnp.where(needed & (distance > half), vocab_count - distance, 0))
        across = jnp.maximum(across, jnp.where(needed & (distance == half), 1, 0))
    share = tie_share(reach, across > 0, lane, half)
    reach = full_reach(reach, across > 0, lane, share, blocks, half)

    square = (BLK, BLK)
    up, over = lax.broadcasted_iota(i32, square, 0), lax.broadcasted_iota(i32, square, 1)
    earlier = earlier_lanes()
    left_up, left_over = (up & 7) + 1 - (up >> 3), (over & 7) + 1 - (over >> 3)
    goes_first = ones((left_up > left_over) | ((left_up == left_over) & ((up >> 3) > (over >> 3))))
    index, waiting, moved = [], [], [jnp.zeros(shape, f32)] * 2
    for way in range(2):
        masks = jnp.concatenate([ones(reach[way] == r) for r in range(1, half + 1)], axis=0)
        before = jnp.dot(masks, earlier, preferred_element_type=f32)
        place = jnp.zeros(shape, f32)
        count = jnp.zeros(shape, f32)
        for r in range(1, half + 1):
            same = reach[way] == r
            place = jnp.where(same, before[(r - 1) * vocab_count : r * vocab_count], place)
            total = jnp.sum(jnp.where(same, 1.0, 0.0), axis=1, keepdims=True)
            count = jnp.where(lane == r - 1, total, count)
        index.append(place)
        waiting.append(count)
    travels = (lane >= 8) & (lane < 8 * half) & ((lane & 7) + 1 > (lane >> 3))
    for f in range(steps):
        ahead_of = jnp.dot(
            jnp.concatenate(waiting, axis=0).astype(jnp.bfloat16), goes_first, preferred_element_type=f32
        )
        for way in range(2):
            first = ahead_of[way * vocab_count : (way + 1) * vocab_count]
            size = of_chain(SIZES, way, f)
            go = jnp.clip(size - first, 0.0, waiting[way])
            book_ref[(f * 2 + way) * 3] = moved[way]
            moved[way] = moved[way] + go
            book_ref[(f * 2 + way) * 3 + 1] = moved[way]
            book_ref[(f * 2 + way) * 3 + 2] = jnp.minimum(first, size)
            come = pltpu.roll(pltpu.roll(go, 8, 1), 1 if way == 0 else vocab_count - 1, 0)
            waiting[way] = waiting[way] - go + jnp.where(travels, come, 0.0)
    left = jnp.sum(waiting[0] + waiting[1], axis=1, keepdims=True)
    left = jnp.sum(jnp.broadcast_to(left, shape), axis=0, keepdims=True)
    fit_ref[...] = jnp.broadcast_to(left, fit_ref.shape).astype(i32)

    small = (vocab_count, vocab_count)
    target = lax.broadcasted_iota(i32, (BLK, 2 * BLK), 1).astype(f32)
    pointer, sends = [], []
    for way in range(2):
        step = 1 if way == 0 else -1
        back = me - step * lax.broadcasted_iota(i32, small, 0)
        back = jnp.where(back < 0, back + vocab_count, jnp.where(back >= vocab_count, back - vocab_count, back))
        pick = ones(back == lax.broadcasted_iota(i32, small, 1))
        far = jnp.dot(pick, reach[way].astype(f32).astype(jnp.bfloat16), preferred_element_type=f32).astype(i32)
        order = jnp.dot(pick, index[way].astype(jnp.bfloat16), preferred_element_type=f32)
        giver = me - step
        giver = jnp.where(giver < 0, giver + vocab_count, jnp.where(giver >= vocab_count, giver - vocab_count, giver))

        def slot(at, hops, valid):
            column = jnp.clip(hops * 8 + far - 1, 0, BLK - 1)
            where = jnp.full(shape, -1.0, f32)
            for f in range(steps):
                start, end, first = (
                    jnp.take_along_axis(
                        jnp.broadcast_to(book_ref[(f * 2 + way) * 3 + kind, pl.ds(at, 1), :], shape),
                        column,
                        axis=1,
                        mode="promise_in_bounds",
                    )
                    for kind in range(3)
                )
                now = valid & (start <= order) & (order < end)
                where = jnp.where(now, of_chain(STARTS, way, f) + first + order - start, where)
            return where

        leave = slot(me, row, (far > row) & (row < half))
        arrive = slot(giver, row - 1, (far >= row) & (row >= 1) & (row <= half))
        point = jnp.where(row == 0, lane.astype(f32), jnp.maximum(home + arrive, 0.0))
        pointer.append(point)
        leave_turned = jnp.concatenate([leave, jnp.full((BLK - vocab_count, BLK), -1.0, f32)], axis=0).T
        chosen = jnp.zeros((1, 2 * BLK), f32)
        for h in range(half):
            chosen = chosen + jnp.dot(
                point[h : h + 1].astype(jnp.bfloat16),
                ones(leave_turned[:, h : h + 1] == target),
                preferred_element_type=f32,
            )
        sends.append(chosen.astype(i32))
    send_ref[0:1, :] = jnp.where(straight, sends[0], sends[1])
    send_ref[1:2, :] = jnp.where(straight, sends[1], sends[0])
    send_ref[2:8, :] = jnp.zeros((6, 2 * BLK), i32)

    mine_lane = lax.broadcasted_iota(i32, (pair_count, vocab_count), 1)
    holder = jnp.sum(jnp.where(pair_lane == me, holders, 0), axis=1, keepdims=True)
    inner = jnp.sum(jnp.where(pair_lane == me, inners, 0), axis=1, keepdims=True)
    distance = me - holder
    distance = jnp.where(distance < 0, distance + vocab_count, distance)
    share = turn(jnp.broadcast_to(share, shape))[:1]
    share = jnp.sum(jnp.where(pair_lane == holder, share, 0), axis=1, keepdims=True)
    hops = ways(distance, inner, share, vocab_count)
    scale = jnp.where(distance <= half, distance, 2 * vocab_count - distance)
    points = jnp.zeros((pair_count, 1), f32)
    for way in range(2):
        found = lax.dot_general(
            ones(pair_lane == inner),
            pointer[way].astype(jnp.bfloat16),
            (((1,), (1,)), ((), ())),
            preferred_element_type=f32,
        )
        points = points + jnp.sum(
            jnp.where((mine_lane == hops[way]) & (hops[way] > 0), found, 0.0), axis=1, keepdims=True
        )
    points = jnp.where(distance == 0, inner.astype(f32), points)
    by_stats = [jnp.sum(jnp.where(lane == blocks, p, 0.0), axis=1, keepdims=True) for p in pointer]
    hop = lax.broadcasted_iota(i32, (vocab_count, 1), 0)
    stat_ok = [hop <= half, (hop >= 1) & (hop < half)]
    points = jnp.concatenate(
        [points] + [jnp.where(ok, p, 0.0) for ok, p in zip(stat_ok, by_stats)], axis=0
    ).astype(i32)
    other = jnp.concatenate(
        [(hops[1] > 0).astype(i32), jnp.zeros((vocab_count, 1), i32), jnp.ones((vocab_count, 1), i32)], axis=0
    )
    other = jnp.where(straight, other, 1 - other)
    scale = jnp.concatenate([scale, jnp.zeros((2 * vocab_count, 1), i32)], axis=0)
    frame = jnp.zeros(points.shape, i32)
    base = jnp.full(points.shape, home, i32)
    limit = jnp.where(other == 1, SIZES[1][0], SIZES[0][0])
    for f in range(1, steps):
        reached = points >= home + jnp.where(other == 1, STARTS[1][f], STARTS[0][f])
        frame = frame + reached.astype(i32)
        base = jnp.where(reached, home + jnp.where(other == 1, STARTS[1][f], STARTS[0][f]), base)
        limit = jnp.where(reached, jnp.where(other == 1, SIZES[1][f], SIZES[0][f]), limit)
    away = points >= home
    source = jnp.where(away, 1 + frame + steps * other, 0)
    spot = jnp.where(away, points - base, points)
    spot = jnp.clip(spot, 0, jnp.where(away, limit, home) - 1)
    items = points.shape[0]
    item_lane = lax.broadcasted_iota(i32, (items, BLK), 1)
    table = jnp.where(
        item_lane == 0, spot, jnp.where(item_lane == 1, scale, jnp.where(item_lane == 2, source, 0))
    ).astype(f32)
    turned = jnp.concatenate([table, jnp.zeros((BLK - items, BLK), f32)], axis=0).T
    source_row = turned[2:3].astype(i32)
    item_up = lax.broadcasted_iota(i32, (items, BLK), 0)
    is_item = item_lane < items
    sooner = is_item & ((source_row < source) | ((source_row == source) & (item_lane < item_up)))
    rank = jnp.sum(sooner.astype(i32), axis=1, keepdims=True)
    item_ref[0:1, :] = turned[0:1].astype(i32)
    item_ref[1:2, :] = turned[1:2].astype(i32)
    item_ref[2:3, :] = jnp.sum(jnp.where(rank == item_lane, item_up, 0), axis=0, keepdims=True)
    item_ref[3:4, :] = jnp.sum((source < item_lane).astype(i32), axis=0, keepdims=True)
    item_ref[4:8, :] = jnp.zeros((4, BLK), i32)


def scalars(table_ref, row, start, count):
    values = table_ref[row : row + 1, :]
    return [values[0, start + j] for j in range(count)]


def in_order(place, valid, count):
    square = (BLK, BLK)
    up, over = lax.broadcasted_iota(jnp.int32, square, 0), lax.broadcasted_iota(jnp.int32, square, 1)
    lanes = jnp.sum(jnp.where((place == up) & valid, over, 0), axis=1, keepdims=True)
    row = turn(jnp.broadcast_to(lanes, square))[:1]
    return [row[0, j] for j in range(count)]


def first_choice(blocks, place_ref, listed_ref):
    vocab_count, pair_count = listed_ref.shape
    half = vocab_count // 2
    i32 = jnp.int32
    me, sign = place_ref[0:1, :], place_ref[1:2, :]
    holders, inners = split(turn(listed_ref[...])[:pair_count], blocks, vocab_count)
    pair_lane = lax.broadcasted_iota(i32, (pair_count, BLK), 1)
    lane = lax.broadcasted_iota(i32, (1, BLK), 1)
    reach = [jnp.zeros((1, BLK), i32), jnp.zeros((1, BLK), i32)]
    facing = jnp.zeros((1, BLK), i32)
    for s in range(vocab_count):
        hits = (pair_lane == inners[:, s : s + 1]) & (jnp.broadcast_to(holders[:, s : s + 1], pair_lane.shape) == me)
        seen = jnp.max(jnp.where(hits, 1, 0), axis=0, keepdims=True)
        distance = s - me
        distance = jnp.where(distance < 0, distance + vocab_count, distance)
        reach[0] = jnp.maximum(reach[0], jnp.where(distance < half, distance * seen, 0))
        reach[1] = jnp.maximum(reach[1], jnp.where(distance > half, (vocab_count - distance) * seen, 0))
        facing = jnp.maximum(facing, jnp.where(distance == half, seen, 0))
    share = tie_share(reach, facing > 0, lane, half)
    reach = full_reach(reach, facing > 0, lane, share, blocks, half)
    choices = []
    for sizes, one, other in zip(SIZES, reach, reach[::-1]):
        far = jnp.where(sign > 0, one, other)
        key = jnp.broadcast_to(far * BLK + (BLK - 1 - lane), (BLK, BLK))
        place = jnp.sum((turn(key) > key).astype(i32), axis=0, keepdims=True)
        choices.append(in_order(place, far > 0, sizes[0]))
    return choices


def pack_kernel(
    place_ref,
    listed_ref,
    own_ref,
    low_ref,
    high_ref,
    pick_ref,
    home_ref,
    first_ref,
    second_ref,
    done_ref,
    cand_ref,
    logit_ref,
):
    docs, positions, columns = own_ref.shape
    width = low_ref.shape[1]
    span = positions + 2 * width
    rows = pick_ref.shape[0]
    blocks = columns // BLK
    for doc in range(docs):
        cand_ref[doc * span : doc * span + width, :] = low_ref[doc]
        cand_ref[doc * span + width : doc * span + width + positions, :] = own_ref[doc]
        cand_ref[doc * span + width + positions : (doc + 1) * span, :] = high_ref[doc]
    pick = pick_ref[...]
    peak = jnp.full((rows, BLK), -jnp.inf, jnp.float32)
    for t in range(blocks):
        part = jnp.dot(pick, cand_ref[:, t * BLK : (t + 1) * BLK], preferred_element_type=jnp.float32)
        logit_ref[t] = part.astype(jnp.bfloat16)
        peak = jnp.maximum(peak, part)
    top = jnp.max(peak, axis=1, keepdims=True)
    total = jnp.zeros((rows, BLK), jnp.float32)
    for t in range(blocks):
        power = jnp.exp(logit_ref[t].astype(jnp.float32) - top)
        total = total + power
        home_ref[t] = power.astype(jnp.bfloat16)
    total = jnp.sum(total, axis=1, keepdims=True)
    first = total.astype(jnp.bfloat16).astype(jnp.float32)
    second = (total - first).astype(jnp.bfloat16).astype(jnp.float32)
    third = total - first - second
    lane = lax.broadcasted_iota(jnp.int32, (rows, BLK), 1)
    home_ref[blocks] = jnp.where(
        lane == 0, top, jnp.where(lane == 1, first, jnp.where(lane == 2, second, jnp.where(lane == 3, third, 0.0)))
    ).astype(jnp.bfloat16)
    for out_ref, choice in zip((first_ref, second_ref), first_choice(blocks, place_ref, listed_ref)):
        for j, at in enumerate(choice):
            out_ref[j] = home_ref[at]
    done_ref[...] = jnp.zeros(done_ref.shape, jnp.int32)


def ready_kernel(chain, step, after_ref, send_ref, home_ref, *refs):
    del after_ref
    frames, out_ref = refs[:-1], refs[-1]
    home = home_ref.shape[0]
    for j, at in enumerate(scalars(send_ref, chain, STARTS[chain][step], SIZES[chain][step])):

        def copy(low, high, j=j, at=at):
            if high - low == 1:
                if low == 0:
                    out_ref[j] = home_ref[at]
                elif low <= len(frames):
                    out_ref[j] = frames[low - 1][at - home - STARTS[chain][low - 1]]
                return
            mid = (low + high) // 2
            split = home + STARTS[chain][mid - 1]
            pl.when(at < split)(lambda: copy(low, mid))
            pl.when(at >= split)(lambda: copy(mid, high))

        copy(0, len(frames) + 2)


def pass_kernel(chain, step, home, send_ref, part_ref, newest_ref, out_ref):
    start = home + STARTS[chain][step - 1]
    for j, at in enumerate(scalars(send_ref, chain, STARTS[chain][step], SIZES[chain][step])):
        newest = newest_ref[jnp.maximum(at - start, 0)]
        out_ref[j] = jnp.where(at >= start, newest, part_ref[j])


def stage_kernel(steps, item_ref, *refs):
    sources, stage_ref = refs[:-1], refs[-1]
    for s, source in zip([s for s in range(2 * steps + 1) if s not in (steps, 2 * steps)], sources):
        bring(item_ref, s, source, stage_ref)


def bring(item_ref, s, source_ref, stage_ref):
    def one(q, carry):
        item = item_ref[2, q]
        stage_ref[item] = source_ref[item_ref[0, item]]
        return carry

    lax.fori_loop(item_ref[3, s], item_ref[3, s + 1], one, 0)


def student_kernel(student_ref, top_ref, total_ref):
    docs, positions, columns = student_ref.shape
    rows = docs * positions
    peak = jnp.full((rows, BLK), -jnp.inf, jnp.float32)
    for b in range(columns // BLK):
        part = student_ref[:, :, b * BLK : (b + 1) * BLK].reshape(rows, BLK).astype(jnp.float32)
        peak = jnp.maximum(peak, part)
    top = jnp.max(peak, axis=1, keepdims=True)
    total = jnp.zeros((rows, BLK), jnp.float32)
    for b in range(columns // BLK):
        part = student_ref[:, :, b * BLK : (b + 1) * BLK].reshape(rows, BLK).astype(jnp.float32)
        total = total + jnp.exp(part - top)
    top_ref[...] = jnp.broadcast_to(top, (rows, BLK))
    total_ref[...] = jnp.broadcast_to(jnp.sum(total, axis=1, keepdims=True), (rows, BLK))


def map_kernel(
    steps,
    item_ref,
    held_ref,
    ahead_ref,
    behind_ref,
    spread_ref,
    weight_ref,
    student_ref,
    top_ref,
    total_ref,
    out_ref,
    stage_ref,
    scale_ref,
):
    docs, positions, columns = student_ref.shape
    rows = docs * positions
    blocks = columns // BLK
    spread = spread_ref[...]
    for i in range(stage_ref.shape[0]):
        stage_ref[i] = held_ref[i]
    bring(item_ref, steps, ahead_ref, stage_ref)
    bring(item_ref, 2 * steps, behind_ref, stage_ref)
    holders = [h for h in range(steps + 1)] + [2 * steps + h for h in range(1, steps)]
    peaks, sums = [], []
    for h in holders:
        stats = jnp.dot(spread, stage_ref[K * blocks + h], preferred_element_type=jnp.float32)
        peaks.append(stats[:, 0:1])
        sums.append(stats[:, 1:2] + stats[:, 2:3] + stats[:, 3:4])
    peak = functools.reduce(jnp.maximum, peaks)
    powers = [jnp.exp(p - peak) for p in peaks]
    norm = sum(p * t for p, t in zip(powers, sums))
    for h, power in zip(holders, powers):
        scale_ref[h] = jnp.broadcast_to(power / norm, (rows, BLK))
    student_top = top_ref[...]
    mass = jnp.zeros((rows, BLK), jnp.float32)
    cross = jnp.zeros((rows, BLK), jnp.float32)
    for b in range(blocks):
        picked = jnp.concatenate([stage_ref[K * b], stage_ref[K * b + 1]], axis=1)
        prob = jnp.dot(spread, picked, preferred_element_type=jnp.float32).astype(jnp.bfloat16)
        mapped = scale_ref[item_ref[1, K * b]] * jnp.dot(
            prob[:, :BLK], weight_ref[:, K * b].reshape(BLK, BLK), preferred_element_type=jnp.float32
        ) + scale_ref[item_ref[1, K * b + 1]] * jnp.dot(
            prob[:, BLK:], weight_ref[:, K * b + 1].reshape(BLK, BLK), preferred_element_type=jnp.float32
        )
        logit = student_ref[:, :, b * BLK : (b + 1) * BLK].reshape(rows, BLK).astype(jnp.float32) - student_top
        mass = mass + mapped
        cross = cross + mapped * (jnp.log(jnp.maximum(mapped, TINY)) - logit)
    mass = jnp.sum(mass, axis=1, keepdims=True)
    cross = jnp.sum(cross, axis=1, keepdims=True)
    lane = lax.broadcasted_iota(jnp.int32, (rows, BLK), 1)
    table = jnp.where(
        lane == 0, mass, jnp.where(lane == 1, cross, jnp.where(lane == 2, student_top, total_ref[...]))
    )
    out_ref[...] = table.T[:8]


def whole(padded_parts, cand, src_block, weights, student_logits):
    doc_count, pos_count, student_cols = student_logits.shape
    teacher_cols = padded_parts[0].shape[2]
    teacher_blocks = teacher_cols // BLK
    student_blocks = student_cols // BLK
    row_count = doc_count * pos_count
    padded = jnp.concatenate(padded_parts, axis=1).reshape(-1, teacher_cols)
    teacher_float = jnp.take(padded, cand, axis=0).astype(jnp.float32)
    student_float = student_logits.reshape(row_count, student_cols).astype(jnp.float32)
    teacher_peak = jnp.max(teacher_float, axis=1)
    student_peak = jnp.max(student_float, axis=1)
    teacher_top, student_top = lax.pmax((teacher_peak, student_peak), "vocab")
    teacher_total, student_total = lax.psum(
        (
            jnp.sum(jnp.exp(teacher_float - teacher_top[:, None]), axis=1),
            jnp.sum(jnp.exp(student_float - student_top[:, None]), axis=1),
        ),
        "vocab",
    )
    teacher_prob = (jnp.exp(teacher_float - teacher_top[:, None]) / teacher_total[:, None]).astype(jnp.bfloat16)
    student_logprob = student_float - student_top[:, None] - jnp.log(student_total)[:, None]
    vocab_count = lax.axis_size("vocab")
    own_index = lax.axis_index("vocab")
    pair_count = student_blocks * K
    capacity = 2 * K * student_blocks // vocab_count
    pair_blocks = src_block.reshape(vocab_count, pair_count)
    holder = pair_blocks // teacher_blocks
    inside = pair_blocks % teacher_blocks
    same_holder = holder[:, :, None] == holder[:, None, :]
    before = jnp.arange(pair_count)[None, :] < jnp.arange(pair_count)[:, None]
    slot_rank = jnp.sum(same_holder & before[None, :, :], axis=2)
    chosen = (holder == own_index)[:, None, :] & (
        slot_rank[:, None, :] == jnp.arange(capacity)[None, :, None]
    )
    send_index = jnp.sum(jnp.where(chosen, inside[:, None, :], 0), axis=2)
    prob_blocks = teacher_prob.reshape(row_count, teacher_blocks, BLK)
    outgoing = jnp.take(prob_blocks, send_index.reshape(-1), axis=1).reshape(row_count, vocab_count, capacity, BLK)
    incoming = lax.all_to_all(outgoing, "vocab", split_axis=1, concat_axis=1, tiled=True)
    own_holder = jnp.take(holder, own_index, axis=0)
    own_rank = jnp.take(slot_rank, own_index, axis=0)
    recv_slot = own_holder * capacity + own_rank
    gathered = jnp.take(incoming.reshape(row_count, vocab_count * capacity, BLK), recv_slot, axis=1).reshape(
        row_count, student_blocks, K, BLK
    )
    weights = weights.swapaxes(0, 1).reshape(student_blocks, K, BLK, BLK)
    mapped = jnp.einsum("rbkc,bkcd->rbd", gathered, weights, preferred_element_type=jnp.float32).reshape(
        row_count, student_cols
    )
    total_mass = lax.psum(jnp.sum(mapped, axis=1), "vocab")
    normed = mapped / total_mass[:, None]
    return lax.psum(
        jnp.sum(jax.scipy.special.xlogy(normed, normed) - normed * student_logprob, axis=1), "vocab"
    )


def shards(teacher_logits, student_logits, alignment, src_block, margin_weight):
    doc_count, pos_count, teacher_cols = teacher_logits.shape
    student_cols = student_logits.shape[2]
    teacher_blocks = teacher_cols // BLK
    student_blocks = student_cols // BLK
    row_count = doc_count * pos_count
    pair_count = student_blocks * K
    vocab_count = lax.axis_size("vocab")
    steps = vocab_count // 2
    home = teacher_blocks + 1
    vocab_index = lax.axis_index("vocab")
    seq_index = lax.axis_index("seq")
    sign = 1 - 2 * (seq_index % 2)
    span = pos_count + 2 * W

    with jax.named_scope("halo"):
        low, high = halo(teacher_logits, W)
    with jax.named_scope("weights"):
        weights = lax.all_gather(
            margin_weight.reshape(pair_count, -1, BLK), "dp", axis=0, tiled=False
        )

    with jax.named_scope("rows"):
        cand = (alignment - seq_index * pos_count + W + jnp.arange(doc_count)[:, None] * span).reshape(-1)
        cand = jnp.clip(cand, 0, doc_count * span - 1)
        places = jnp.arange(doc_count * span)
        used = jnp.any(cand[:, None] == places[None, :], axis=0)
        place_rank = jnp.sum(used[:, None] & (places[:, None] < places[None, :]), axis=0)
        cand_rank = jnp.sum(used[None, :] & (places[None, :] < cand[:, None]), axis=1)
        row_ids = jnp.arange(ROWS)
        pick = ((row_ids[:, None] == place_rank[None, :]) & used[None, :]).astype(jnp.bfloat16)
        spread = (cand_rank[:, None] == row_ids[None, :]).astype(jnp.bfloat16)
        rows_fit = jnp.sum(used.astype(jnp.int32)) <= ROWS

    vmem = pl.BlockSpec(memory_space=pltpu.VMEM)
    smem = pl.BlockSpec(memory_space=pltpu.SMEM)
    anywhere = pl.BlockSpec(memory_space=pl.ANY)
    room = pltpu.CompilerParams(vmem_limit_bytes=20 * 1024 * 1024)

    def planes(count):
        return jax.ShapeDtypeStruct((count, ROWS, BLK), jnp.bfloat16)

    with jax.named_scope("pack"):
        listed = src_block.reshape(vocab_count, pair_count)
        place = jnp.stack([vocab_index, sign]).astype(jnp.int32)
        own, ahead, behind, packed = pl.pallas_call(
            pack_kernel,
            out_shape=(planes(home), planes(SIZES[0][0]), planes(SIZES[1][0]), jax.ShapeDtypeStruct((8, BLK), jnp.int32)),
            in_specs=[vmem] * 6,
            out_specs=(vmem,) * 4,
            scratch_shapes=[
                pltpu.VMEM((doc_count * span, teacher_cols), jnp.bfloat16),
                pltpu.VMEM((teacher_blocks, ROWS, BLK), jnp.bfloat16),
            ],
            compiler_params=room,
        )(jnp.broadcast_to(place[:, None], (2, BLK)), listed, teacher_logits, low, high, pick)

    with jax.named_scope("plan"):
        table = jax.ShapeDtypeStruct((8, BLK), jnp.int32)
        send, items, left = pl.pallas_call(
            functools.partial(plan_kernel, teacher_blocks),
            out_shape=(jax.ShapeDtypeStruct((8, 2 * BLK), jnp.int32), table, table),
            in_specs=[smem, vmem, vmem],
            out_specs=(vmem,) * 3,
            scratch_shapes=[pltpu.VMEM((6 * steps, vocab_count, BLK), jnp.float32)],
            compiler_params=room,
        )(place, listed, packed)

    def ready(chain, step, after, frames):
        return pl.pallas_call(
            functools.partial(ready_kernel, chain, step),
            out_shape=planes(SIZES[chain][step]),
            in_specs=[anywhere] + [vmem] * (2 + len(frames)),
            out_specs=vmem,
            compiler_params=room,
        )(after, send, own, *frames)

    def passed(chain, step, part, newest):
        return pl.pallas_call(
            functools.partial(pass_kernel, chain, step, home),
            out_shape=planes(SIZES[chain][step]),
            in_specs=[vmem] * 3,
            out_specs=vmem,
            compiler_params=room,
        )(send, part, newest)

    with jax.named_scope("ring"):
        forward, backward = ring_pairs(1), ring_pairs(-1)
        came_behind = [lax.ppermute(behind, ("seq", "vocab"), backward)]
        came_ahead = [lax.ppermute(ahead, ("seq", "vocab"), forward)]
        for step in range(1, steps):
            part = ready(1, step, ahead, came_behind[:-1])
            behind = passed(1, step, part, came_behind[-1])
            came_behind.append(lax.ppermute(behind, ("seq", "vocab"), backward))
            part = ready(0, step, behind, came_ahead[:-1])
            ahead = passed(0, step, part, came_ahead[-1])
            came_ahead.append(lax.ppermute(ahead, ("seq", "vocab"), forward))

    with jax.named_scope("student"):
        top, total = pl.pallas_call(
            student_kernel,
            out_shape=(jax.ShapeDtypeStruct((row_count, BLK), jnp.float32),) * 2,
            in_specs=[vmem],
            out_specs=(vmem,) * 2,
            compiler_params=room,
        )(student_logits)

    with jax.named_scope("stage"):
        early = (own, *came_ahead[:-1], *came_behind[:-1])
        held = pl.pallas_call(
            functools.partial(stage_kernel, steps),
            out_shape=planes(pair_count + 2 * vocab_count),
            in_specs=[smem] + [vmem] * len(early),
            out_specs=vmem,
            compiler_params=room,
        )(items, *early)

    with jax.named_scope("map"):
        sums = pl.pallas_call(
            functools.partial(map_kernel, steps),
            out_shape=jax.ShapeDtypeStruct((8, row_count), jnp.float32),
            in_specs=[smem] + [vmem] * 8,
            out_specs=vmem,
            scratch_shapes=[
                pltpu.VMEM((pair_count + 2 * vocab_count, ROWS, BLK), jnp.bfloat16),
                pltpu.VMEM((3 * steps, row_count, BLK), jnp.float32),
            ],
            compiler_params=room,
        )(items, held, came_ahead[-1], came_behind[-1], spread, weights, student_logits, top, total)

    with jax.named_scope("finish"):
        sent = jnp.broadcast_to(sums[None, :4], (vocab_count, 4, row_count))
        parts = lax.all_to_all(sent, "vocab", split_axis=0, concat_axis=0, tiled=True)
        mass_part, cross_part, top_part, total_part = (parts[:, i] for i in range(4))
        student_top = jnp.max(top_part, axis=0)
        log_total = student_top + jnp.log(jnp.sum(jnp.exp(top_part - student_top) * total_part, axis=0))
        mass = jnp.sum(mass_part, axis=0)
        result = jnp.sum(cross_part + mass_part * (log_total - top_part), axis=0) / mass - jnp.log(mass)

    result = lax.cond(
        rows_fit & (left[0, 0] == 0),
        lambda *_: result,
        lambda *operands: whole(operands[:3], *operands[3:]),
        low,
        teacher_logits,
        high,
        cand,
        src_block,
        weights,
        student_logits,
    )
    return result.reshape(doc_count, pos_count)


def solution(mesh):
    in_specs = (
        P("dp", "seq", "vocab"),
        P("dp", "seq", "vocab"),
        P("dp", "seq"),
        P(),
        P("vocab", None, "dp", None),
    )
    out_specs = P("dp", "seq")
    return jax.shard_map(shards, mesh=mesh, in_specs=in_specs, out_specs=out_specs, check_vma=False)
```

```python
import functools

import jax
import jax.numpy as jnp
from jax import lax
from jax.experimental import pallas as pl
from jax.experimental.pallas import tpu as pltpu
from jax.sharding import PartitionSpec as P

BLK = 128
K = 2
W = 16
ROWS = 104
SIZES = ((30, 21, 20, 20, 20, 20, 20, 20), (12, 23, 23, 23, 22, 22, 22, 22))
STARTS = tuple(tuple(sum(sizes[:f]) for f in range(len(sizes))) for sizes in SIZES)
TINY = 1.2e-38


def halo(block, width):
    count = lax.axis_size("seq")
    forward = [(i, (i + 1) % count) for i in range(count)]
    backward = [(target, source) for source, target in forward]
    low = lax.ppermute(block[:, block.shape[1] - width :], "seq", forward)
    high = lax.ppermute(block[:, :width], "seq", backward)
    return low, high


def ring_pairs(turn):
    seq_count, vocab_count = lax.axis_size("seq"), lax.axis_size("vocab")
    pairs = []
    for s in range(seq_count):
        step = turn if s % 2 == 0 else -turn
        for v in range(vocab_count):
            pairs.append((s * vocab_count + v, s * vocab_count + (v + step) % vocab_count))
    return pairs


def tie_key(block):
    return (block * 5) & 7


def ways(distance, block, share, vocab_count):
    half = vocab_count // 2
    first = tie_key(block) < share
    ahead = jnp.where((distance >= 1) & ((distance < half) | ((distance == half) & first)), distance, 0)
    behind = jnp.where((distance > half) | ((distance == half) & ~first), vocab_count - distance, 0)
    return ahead, behind


def ones(mask):
    return jnp.where(mask, 1.0, 0.0).astype(jnp.bfloat16)


def tie_share(reach, facing, lane, half):
    share = jnp.zeros((reach[0].shape[0], 1), jnp.int32)
    for part in range(1, 9):
        first = tie_key(lane) < part
        more = jnp.where(facing & first, half, reach[0]) - jnp.where(facing & ~first, half, reach[1])
        share = share + (jnp.sum(more, axis=1, keepdims=True) <= 0).astype(jnp.int32)
    return share


def full_reach(reach, facing, lane, share, blocks, half):
    first = tie_key(lane) < share
    ahead = jnp.where(facing & first, half, reach[0])
    behind = jnp.where(facing & ~first, half, reach[1])
    return [jnp.where(lane == blocks, half, ahead), jnp.where(lane == blocks, half - 1, behind)]


def split(listed, blocks, vocab_count):
    holder = sum((listed >= h * blocks).astype(jnp.int32) for h in range(1, vocab_count))
    return holder, listed - holder * blocks


def turn(table):
    rows, columns = table.shape
    table = table.astype(jnp.float32)
    if columns < BLK:
        table = jnp.concatenate([table, jnp.zeros((rows, BLK - columns), jnp.float32)], axis=1)
    if rows < BLK:
        table = jnp.concatenate([table, jnp.zeros((BLK - rows, BLK), jnp.float32)], axis=0)
    return table.T.astype(jnp.int32)


def earlier_lanes():
    square = (BLK, BLK)
    return ones(lax.broadcasted_iota(jnp.int32, square, 0) < lax.broadcasted_iota(jnp.int32, square, 1))


def plan_kernel(blocks, place_ref, listed_ref, after_ref, send_ref, item_ref, fit_ref, book_ref):
    vocab_count, pair_count = listed_ref.shape
    half = vocab_count // 2
    steps = half
    home = blocks + 1
    me, sign = place_ref[0], place_ref[1]
    f32, i32 = jnp.float32, jnp.int32
    shape = (vocab_count, BLK)
    straight = sign > 0

    def of_chain(table, way, f):
        return jnp.where(straight, float(table[way][f]), float(table[1 - way][f]))


    del after_ref
    listed = listed_ref[...]
    row_holder, _ = split(listed, blocks, vocab_count)
    holders, inners = split(turn(listed)[:pair_count], blocks, vocab_count)
    lane = lax.broadcasted_iota(i32, shape, 1)
    row = lax.broadcasted_iota(i32, shape, 0)

    reach = [jnp.zeros(shape, i32), jnp.zeros(shape, i32)]
    across = jnp.zeros(shape, i32)
    pair_lane = lax.broadcasted_iota(i32, (pair_count, BLK), 1)
    pair_row = lax.broadcasted_iota(i32, (vocab_count, pair_count), 0)
    for s in range(vocab_count):
        hits = jnp.dot(
            ones(pair_row == row_holder[s : s + 1, :]),
            ones(pair_lane == inners[:, s : s + 1]),
            preferred_element_type=f32,
        )
        distance = s - row
        distance = jnp.where(distance < 0, distance + vocab_count, distance)
        needed = hits > 0
        reach[0] = jnp.maximum(reach[0], jnp.where(needed & (distance < half), distance, 0))
        reach[1] = jnp.maximum(reach[1], jnp.where(needed & (distance > half), vocab_count - distance, 0))
        across = jnp.maximum(across, jnp.where(needed & (distance == half), 1, 0))
    share = tie_share(reach, across > 0, lane, half)
    reach = full_reach(reach, across > 0, lane, share, blocks, half)

    square = (BLK, BLK)
    up, over = lax.broadcasted_iota(i32, square, 0), lax.broadcasted_iota(i32, square, 1)
    earlier = earlier_lanes()
    left_up, left_over = (up & 7) + 1 - (up >> 3), (over & 7) + 1 - (over >> 3)
    goes_first = ones((left_up > left_over) | ((left_up == left_over) & ((up >> 3) > (over >> 3))))
    index, waiting, moved = [], [], [jnp.zeros(shape, f32)] * 2
    for way in range(2):
        masks = jnp.concatenate([ones(reach[way] == r) for r in range(1, half + 1)], axis=0)
        before = jnp.dot(masks, earlier, preferred_element_type=f32)
        place = jnp.zeros(shape, f32)
        count = jnp.zeros(shape, f32)
        for r in range(1, half + 1):
            same = reach[way] == r
            place = jnp.where(same, before[(r - 1) * vocab_count : r * vocab_count], place)
            total = jnp.sum(jnp.where(same, 1.0, 0.0), axis=1, keepdims=True)
            count = jnp.where(lane == r - 1, total, count)
        index.append(place)
        waiting.append(count)
    travels = (lane >= 8) & (lane < 8 * half) & ((lane & 7) + 1 > (lane >> 3))
    for f in range(steps):
        ahead_of = jnp.dot(
            jnp.concatenate(waiting, axis=0).astype(jnp.bfloat16), goes_first, preferred_element_type=f32
        )
        for way in range(2):
            first = ahead_of[way * vocab_count : (way + 1) * vocab_count]
            size = of_chain(SIZES, way, f)
            go = jnp.clip(size - first, 0.0, waiting[way])
            book_ref[(f * 2 + way) * 3] = moved[way]
            moved[way] = moved[way] + go
            book_ref[(f * 2 + way) * 3 + 1] = moved[way]
            book_ref[(f * 2 + way) * 3 + 2] = jnp.minimum(first, size)
            come = pltpu.roll(pltpu.roll(go, 8, 1), 1 if way == 0 else vocab_count - 1, 0)
            waiting[way] = waiting[way] - go + jnp.where(travels, come, 0.0)
    left = jnp.sum(waiting[0] + waiting[1], axis=1, keepdims=True)
    left = jnp.sum(jnp.broadcast_to(left, shape), axis=0, keepdims=True)
    fit_ref[...] = jnp.broadcast_to(left, fit_ref.shape).astype(i32)

    small = (vocab_count, vocab_count)
    target = lax.broadcasted_iota(i32, (BLK, 2 * BLK), 1).astype(f32)
    pointer, sends = [], []
    for way in range(2):
        step = 1 if way == 0 else -1
        back = me - step * lax.broadcasted_iota(i32, small, 0)
        back = jnp.where(back < 0, back + vocab_count, jnp.where(back >= vocab_count, back - vocab_count, back))
        pick = ones(back == lax.broadcasted_iota(i32, small, 1))
        far = jnp.dot(pick, reach[way].astype(f32).astype(jnp.bfloat16), preferred_element_type=f32).astype(i32)
        order = jnp.dot(pick, index[way].astype(jnp.bfloat16), preferred_element_type=f32)
        giver = me - step
        giver = jnp.where(giver < 0, giver + vocab_count, jnp.where(giver >= vocab_count, giver - vocab_count, giver))

        def slot(at, hops, valid):
            column = jnp.clip(hops * 8 + far - 1, 0, BLK - 1)
            where = jnp.full(shape, -1.0, f32)
            for f in range(steps):
                start, end, first = (
                    jnp.take_along_axis(
                        jnp.broadcast_to(book_ref[(f * 2 + way) * 3 + kind, pl.ds(at, 1), :], shape),
                        column,
                        axis=1,
                        mode="promise_in_bounds",
                    )
                    for kind in range(3)
                )
                now = valid & (start <= order) & (order < end)
                where = jnp.where(now, of_chain(STARTS, way, f) + first + order - start, where)
            return where

        leave = slot(me, row, (far > row) & (row < half))
        arrive = slot(giver, row - 1, (far >= row) & (row >= 1) & (row <= half))
        point = jnp.where(row == 0, lane.astype(f32), jnp.maximum(home + arrive, 0.0))
        pointer.append(point)
        leave_turned = jnp.concatenate([leave, jnp.full((BLK - vocab_count, BLK), -1.0, f32)], axis=0).T
        chosen = jnp.zeros((1, 2 * BLK), f32)
        for h in range(half):
            chosen = chosen + jnp.dot(
                point[h : h + 1].astype(jnp.bfloat16),
                ones(leave_turned[:, h : h + 1] == target),
                preferred_element_type=f32,
            )
        sends.append(chosen.astype(i32))
    send_ref[0:1, :] = jnp.where(straight, sends[0], sends[1])
    send_ref[1:2, :] = jnp.where(straight, sends[1], sends[0])
    send_ref[2:8, :] = jnp.zeros((6, 2 * BLK), i32)

    mine_lane = lax.broadcasted_iota(i32, (pair_count, vocab_count), 1)
    holder = jnp.sum(jnp.where(pair_lane == me, holders, 0), axis=1, keepdims=True)
    inner = jnp.sum(jnp.where(pair_lane == me, inners, 0), axis=1, keepdims=True)
    distance = me - holder
    distance = jnp.where(distance < 0, distance + vocab_count, distance)
    share = turn(jnp.broadcast_to(share, shape))[:1]
    share = jnp.sum(jnp.where(pair_lane == holder, share, 0), axis=1, keepdims=True)
    hops = ways(distance, inner, share, vocab_count)
    scale = jnp.where(distance <= half, distance, 2 * vocab_count - distance)
    points = jnp.zeros((pair_count, 1), f32)
    for way in range(2):
        found = lax.dot_general(
            ones(pair_lane == inner),
            pointer[way].astype(jnp.bfloat16),
            (((1,), (1,)), ((), ())),
            preferred_element_type=f32,
        )
        points = points + jnp.sum(
            jnp.where((mine_lane == hops[way]) & (hops[way] > 0), found, 0.0), axis=1, keepdims=True
        )
    points = jnp.where(distance == 0, inner.astype(f32), points)
    by_stats = [jnp.sum(jnp.where(lane == blocks, p, 0.0), axis=1, keepdims=True) for p in pointer]
    hop = lax.broadcasted_iota(i32, (vocab_count, 1), 0)
    stat_ok = [hop <= half, (hop >= 1) & (hop < half)]
    points = jnp.concatenate(
        [points] + [jnp.where(ok, p, 0.0) for ok, p in zip(stat_ok, by_stats)], axis=0
    ).astype(i32)
    other = jnp.concatenate(
        [(hops[1] > 0).astype(i32), jnp.zeros((vocab_count, 1), i32), jnp.ones((vocab_count, 1), i32)], axis=0
    )
    other = jnp.where(straight, other, 1 - other)
    scale = jnp.concatenate([scale, jnp.zeros((2 * vocab_count, 1), i32)], axis=0)
    frame = jnp.zeros(points.shape, i32)
    base = jnp.full(points.shape, home, i32)
    limit = jnp.where(other == 1, SIZES[1][0], SIZES[0][0])
    for f in range(1, steps):
        reached = points >= home + jnp.where(other == 1, STARTS[1][f], STARTS[0][f])
        frame = frame + reached.astype(i32)
        base = jnp.where(reached, home + jnp.where(other == 1, STARTS[1][f], STARTS[0][f]), base)
        limit = jnp.where(reached, jnp.where(other == 1, SIZES[1][f], SIZES[0][f]), limit)
    away = points >= home
    source = jnp.where(away, 1 + frame + steps * other, 0)
    spot = jnp.where(away, points - base, points)
    spot = jnp.clip(spot, 0, jnp.where(away, limit, home) - 1)
    items = points.shape[0]
    item_lane = lax.broadcasted_iota(i32, (items, BLK), 1)
    table = jnp.where(
        item_lane == 0, spot, jnp.where(item_lane == 1, scale, jnp.where(item_lane == 2, source, 0))
    ).astype(f32)
    turned = jnp.concatenate([table, jnp.zeros((BLK - items, BLK), f32)], axis=0).T
    source_row = turned[2:3].astype(i32)
    item_up = lax.broadcasted_iota(i32, (items, BLK), 0)
    is_item = item_lane < items
    sooner = is_item & ((source_row < source) | ((source_row == source) & (item_lane < item_up)))
    rank = jnp.sum(sooner.astype(i32), axis=1, keepdims=True)
    item_ref[0:1, :] = turned[0:1].astype(i32)
    item_ref[1:2, :] = turned[1:2].astype(i32)
    item_ref[2:3, :] = jnp.sum(jnp.where(rank == item_lane, item_up, 0), axis=0, keepdims=True)
    item_ref[3:4, :] = jnp.sum((source < item_lane).astype(i32), axis=0, keepdims=True)
    item_ref[4:8, :] = jnp.zeros((4, BLK), i32)


def scalars(table_ref, row, start, count):
    values = table_ref[row : row + 1, :]
    return [values[0, start + j] for j in range(count)]


def in_order(place, valid, count):
    square = (BLK, BLK)
    up, over = lax.broadcasted_iota(jnp.int32, square, 0), lax.broadcasted_iota(jnp.int32, square, 1)
    lanes = jnp.sum(jnp.where((place == up) & valid, over, 0), axis=1, keepdims=True)
    row = turn(jnp.broadcast_to(lanes, square))[:1]
    return [row[0, j] for j in range(count)]


def first_choice(blocks, place_ref, listed_ref):
    vocab_count, pair_count = listed_ref.shape
    half = vocab_count // 2
    i32 = jnp.int32
    me, sign = place_ref[0:1, :], place_ref[1:2, :]
    holders, inners = split(turn(listed_ref[...])[:pair_count], blocks, vocab_count)
    pair_lane = lax.broadcasted_iota(i32, (pair_count, BLK), 1)
    lane = lax.broadcasted_iota(i32, (1, BLK), 1)
    reach = [jnp.zeros((1, BLK), i32), jnp.zeros((1, BLK), i32)]
    facing = jnp.zeros((1, BLK), i32)
    for s in range(vocab_count):
        hits = (pair_lane == inners[:, s : s + 1]) & (jnp.broadcast_to(holders[:, s : s + 1], pair_lane.shape) == me)
        seen = jnp.max(jnp.where(hits, 1, 0), axis=0, keepdims=True)
        distance = s - me
        distance = jnp.where(distance < 0, distance + vocab_count, distance)
        reach[0] = jnp.maximum(reach[0], jnp.where(distance < half, distance * seen, 0))
        reach[1] = jnp.maximum(reach[1], jnp.where(distance > half, (vocab_count - distance) * seen, 0))
        facing = jnp.maximum(facing, jnp.where(distance == half, seen, 0))
    share = tie_share(reach, facing > 0, lane, half)
    reach = full_reach(reach, facing > 0, lane, share, blocks, half)
    choices = []
    for sizes, one, other in zip(SIZES, reach, reach[::-1]):
        far = jnp.where(sign > 0, one, other)
        key = jnp.broadcast_to(far * BLK + (BLK - 1 - lane), (BLK, BLK))
        place = jnp.sum((turn(key) > key).astype(i32), axis=0, keepdims=True)
        choices.append(in_order(place, far > 0, sizes[0]))
    return choices


def pack_kernel(
    place_ref,
    listed_ref,
    own_ref,
    low_ref,
    high_ref,
    pick_ref,
    home_ref,
    first_ref,
    second_ref,
    done_ref,
    cand_ref,
    logit_ref,
):
    docs, positions, columns = own_ref.shape
    width = low_ref.shape[1]
    span = positions + 2 * width
    rows = pick_ref.shape[0]
    blocks = columns // BLK
    for doc in range(docs):
        cand_ref[doc * span : doc * span + width, :] = low_ref[doc]
        cand_ref[doc * span + width : doc * span + width + positions, :] = own_ref[doc]
        cand_ref[doc * span + width + positions : (doc + 1) * span, :] = high_ref[doc]
    pick = pick_ref[...]
    peak = jnp.full((rows, BLK), -jnp.inf, jnp.float32)
    for t in range(blocks):
        part = jnp.dot(pick, cand_ref[:, t * BLK : (t + 1) * BLK], preferred_element_type=jnp.float32)
        logit_ref[t] = part.astype(jnp.bfloat16)
        peak = jnp.maximum(peak, part)
    top = jnp.max(peak, axis=1, keepdims=True)
    total = jnp.zeros((rows, BLK), jnp.float32)
    for t in range(blocks):
        power = jnp.exp(logit_ref[t].astype(jnp.float32) - top)
        total = total + power
        home_ref[t] = power.astype(jnp.bfloat16)
    total = jnp.sum(total, axis=1, keepdims=True)
    first = total.astype(jnp.bfloat16).astype(jnp.float32)
    second = (total - first).astype(jnp.bfloat16).astype(jnp.float32)
    third = total - first - second
    lane = lax.broadcasted_iota(jnp.int32, (rows, BLK), 1)
    home_ref[blocks] = jnp.where(
        lane == 0, top, jnp.where(lane == 1, first, jnp.where(lane == 2, second, jnp.where(lane == 3, third, 0.0)))
    ).astype(jnp.bfloat16)
    for out_ref, choice in zip((first_ref, second_ref), first_choice(blocks, place_ref, listed_ref)):
        for j, at in enumerate(choice):
            out_ref[j] = home_ref[at]
    done_ref[...] = jnp.zeros(done_ref.shape, jnp.int32)


def ready_kernel(chain, step, after_ref, send_ref, home_ref, *refs):
    del after_ref
    frames, out_ref = refs[:-1], refs[-1]
    home = home_ref.shape[0]
    for j, at in enumerate(scalars(send_ref, chain, STARTS[chain][step], SIZES[chain][step])):

        def copy(low, high, j=j, at=at):
            if high - low == 1:
                if low == 0:
                    out_ref[j] = home_ref[at]
                elif low <= len(frames):
                    out_ref[j] = frames[low - 1][at - home - STARTS[chain][low - 1]]
                return
            mid = (low + high) // 2
            split = home + STARTS[chain][mid - 1]
            pl.when(at < split)(lambda: copy(low, mid))
            pl.when(at >= split)(lambda: copy(mid, high))

        copy(0, len(frames) + 2)


def pass_kernel(chain, step, home, send_ref, part_ref, newest_ref, out_ref):
    start = home + STARTS[chain][step - 1]
    for j, at in enumerate(scalars(send_ref, chain, STARTS[chain][step], SIZES[chain][step])):
        newest = newest_ref[jnp.maximum(at - start, 0)]
        out_ref[j] = jnp.where(at >= start, newest, part_ref[j])


def stage_kernel(steps, item_ref, *refs):
    sources, stage_ref = refs[:-1], refs[-1]
    for s, source in zip([s for s in range(2 * steps + 1) if s not in (steps, 2 * steps)], sources):
        bring(item_ref, s, source, stage_ref)


def bring(item_ref, s, source_ref, stage_ref):
    def one(q, carry):
        item = item_ref[2, q]
        stage_ref[item] = source_ref[item_ref[0, item]]
        return carry

    lax.fori_loop(item_ref[3, s], item_ref[3, s + 1], one, 0)


def student_kernel(student_ref, top_ref, total_ref):
    docs, positions, columns = student_ref.shape
    rows = docs * positions
    peak = jnp.full((rows, BLK), -jnp.inf, jnp.float32)
    for b in range(columns // BLK):
        part = student_ref[:, :, b * BLK : (b + 1) * BLK].reshape(rows, BLK).astype(jnp.float32)
        peak = jnp.maximum(peak, part)
    top = jnp.max(peak, axis=1, keepdims=True)
    total = jnp.zeros((rows, BLK), jnp.float32)
    for b in range(columns // BLK):
        part = student_ref[:, :, b * BLK : (b + 1) * BLK].reshape(rows, BLK).astype(jnp.float32)
        total = total + jnp.exp(part - top)
    top_ref[...] = jnp.broadcast_to(top, (rows, BLK))
    total_ref[...] = jnp.broadcast_to(jnp.sum(total, axis=1, keepdims=True), (rows, BLK))


def map_kernel(
    steps,
    item_ref,
    held_ref,
    ahead_ref,
    behind_ref,
    spread_ref,
    weight_ref,
    student_ref,
    top_ref,
    total_ref,
    out_ref,
    stage_ref,
    scale_ref,
):
    docs, positions, columns = student_ref.shape
    rows = docs * positions
    blocks = columns // BLK
    spread = spread_ref[...]
    for i in range(stage_ref.shape[0]):
        stage_ref[i] = held_ref[i]
    bring(item_ref, steps, ahead_ref, stage_ref)
    bring(item_ref, 2 * steps, behind_ref, stage_ref)
    holders = [h for h in range(steps + 1)] + [2 * steps + h for h in range(1, steps)]
    peaks, sums = [], []
    for h in holders:
        stats = jnp.dot(spread, stage_ref[K * blocks + h], preferred_element_type=jnp.float32)
        peaks.append(stats[:, 0:1])
        sums.append(stats[:, 1:2] + stats[:, 2:3] + stats[:, 3:4])
    peak = functools.reduce(jnp.maximum, peaks)
    powers = [jnp.exp(p - peak) for p in peaks]
    norm = sum(p * t for p, t in zip(powers, sums))
    for h, power in zip(holders, powers):
        scale_ref[h] = jnp.broadcast_to(power / norm, (rows, BLK))
    student_top = top_ref[...]
    mass = jnp.zeros((rows, BLK), jnp.float32)
    cross = jnp.zeros((rows, BLK), jnp.float32)
    for b in range(blocks):
        picked = jnp.concatenate([stage_ref[K * b], stage_ref[K * b + 1]], axis=1)
        prob = jnp.dot(spread, picked, preferred_element_type=jnp.float32).astype(jnp.bfloat16)
        mapped = scale_ref[item_ref[1, K * b]] * jnp.dot(
            prob[:, :BLK], weight_ref[:, K * b].reshape(BLK, BLK), preferred_element_type=jnp.float32
        ) + scale_ref[item_ref[1, K * b + 1]] * jnp.dot(
            prob[:, BLK:], weight_ref[:, K * b + 1].reshape(BLK, BLK), preferred_element_type=jnp.float32
        )
        logit = student_ref[:, :, b * BLK : (b + 1) * BLK].reshape(rows, BLK).astype(jnp.float32) - student_top
        mass = mass + mapped
        cross = cross + mapped * (jnp.log(jnp.maximum(mapped, TINY)) - logit)
    mass = jnp.sum(mass, axis=1, keepdims=True)
    cross = jnp.sum(cross, axis=1, keepdims=True)
    lane = lax.broadcasted_iota(jnp.int32, (rows, BLK), 1)
    table = jnp.where(
        lane == 0, mass, jnp.where(lane == 1, cross, jnp.where(lane == 2, student_top, total_ref[...]))
    )
    out_ref[...] = table.T[:8]


def whole(padded_parts, cand, src_block, weights, student_logits):
    doc_count, pos_count, student_cols = student_logits.shape
    teacher_cols = padded_parts[0].shape[2]
    teacher_blocks = teacher_cols // BLK
    student_blocks = student_cols // BLK
    row_count = doc_count * pos_count
    padded = jnp.concatenate(padded_parts, axis=1).reshape(-1, teacher_cols)
    teacher_float = jnp.take(padded, cand, axis=0).astype(jnp.float32)
    student_float = student_logits.reshape(row_count, student_cols).astype(jnp.float32)
    teacher_peak = jnp.max(teacher_float, axis=1)
    student_peak = jnp.max(student_float, axis=1)
    teacher_top, student_top = lax.pmax((teacher_peak, student_peak), "vocab")
    teacher_total, student_total = lax.psum(
        (
            jnp.sum(jnp.exp(teacher_float - teacher_top[:, None]), axis=1),
            jnp.sum(jnp.exp(student_float - student_top[:, None]), axis=1),
        ),
        "vocab",
    )
    teacher_prob = (jnp.exp(teacher_float - teacher_top[:, None]) / teacher_total[:, None]).astype(jnp.bfloat16)
    student_logprob = student_float - student_top[:, None] - jnp.log(student_total)[:, None]
    vocab_count = lax.axis_size("vocab")
    own_index = lax.axis_index("vocab")
    pair_count = student_blocks * K
    capacity = 2 * K * student_blocks // vocab_count
    pair_blocks = src_block.reshape(vocab_count, pair_count)
    holder = pair_blocks // teacher_blocks
    inside = pair_blocks % teacher_blocks
    same_holder = holder[:, :, None] == holder[:, None, :]
    before = jnp.arange(pair_count)[None, :] < jnp.arange(pair_count)[:, None]
    slot_rank = jnp.sum(same_holder & before[None, :, :], axis=2)
    chosen = (holder == own_index)[:, None, :] & (
        slot_rank[:, None, :] == jnp.arange(capacity)[None, :, None]
    )
    send_index = jnp.sum(jnp.where(chosen, inside[:, None, :], 0), axis=2)
    prob_blocks = teacher_prob.reshape(row_count, teacher_blocks, BLK)
    outgoing = jnp.take(prob_blocks, send_index.reshape(-1), axis=1).reshape(row_count, vocab_count, capacity, BLK)
    incoming = lax.all_to_all(outgoing, "vocab", split_axis=1, concat_axis=1, tiled=True)
    own_holder = jnp.take(holder, own_index, axis=0)
    own_rank = jnp.take(slot_rank, own_index, axis=0)
    recv_slot = own_holder * capacity + own_rank
    gathered = jnp.take(incoming.reshape(row_count, vocab_count * capacity, BLK), recv_slot, axis=1).reshape(
        row_count, student_blocks, K, BLK
    )
    weights = weights.swapaxes(0, 1).reshape(student_blocks, K, BLK, BLK)
    mapped = jnp.einsum("rbkc,bkcd->rbd", gathered, weights, preferred_element_type=jnp.float32).reshape(
        row_count, student_cols
    )
    total_mass = lax.psum(jnp.sum(mapped, axis=1), "vocab")
    normed = mapped / total_mass[:, None]
    return lax.psum(
        jnp.sum(jax.scipy.special.xlogy(normed, normed) - normed * student_logprob, axis=1), "vocab"
    )


def shards(teacher_logits, student_logits, alignment, src_block, margin_weight):
    doc_count, pos_count, teacher_cols = teacher_logits.shape
    student_cols = student_logits.shape[2]
    teacher_blocks = teacher_cols // BLK
    student_blocks = student_cols // BLK
    row_count = doc_count * pos_count
    pair_count = student_blocks * K
    vocab_count = lax.axis_size("vocab")
    steps = vocab_count // 2
    home = teacher_blocks + 1
    vocab_index = lax.axis_index("vocab")
    seq_index = lax.axis_index("seq")
    sign = 1 - 2 * (seq_index % 2)
    span = pos_count + 2 * W

    with jax.named_scope("halo"):
        low, high = halo(teacher_logits, W)
    with jax.named_scope("weights"):
        weights = lax.all_gather(
            margin_weight.reshape(pair_count, -1, BLK), "dp", axis=0, tiled=False
        )

    with jax.named_scope("rows"):
        cand = (alignment - seq_index * pos_count + W + jnp.arange(doc_count)[:, None] * span).reshape(-1)
        cand = jnp.clip(cand, 0, doc_count * span - 1)
        places = jnp.arange(doc_count * span)
        used = jnp.any(cand[:, None] == places[None, :], axis=0)
        place_rank = jnp.sum(used[:, None] & (places[:, None] < places[None, :]), axis=0)
        cand_rank = jnp.sum(used[None, :] & (places[None, :] < cand[:, None]), axis=1)
        row_ids = jnp.arange(ROWS)
        pick = ((row_ids[:, None] == place_rank[None, :]) & used[None, :]).astype(jnp.bfloat16)
        spread = (cand_rank[:, None] == row_ids[None, :]).astype(jnp.bfloat16)
        rows_fit = jnp.sum(used.astype(jnp.int32)) <= ROWS

    vmem = pl.BlockSpec(memory_space=pltpu.VMEM)
    smem = pl.BlockSpec(memory_space=pltpu.SMEM)
    anywhere = pl.BlockSpec(memory_space=pl.ANY)
    room = pltpu.CompilerParams(vmem_limit_bytes=20 * 1024 * 1024)

    def planes(count):
        return jax.ShapeDtypeStruct((count, ROWS, BLK), jnp.bfloat16)

    with jax.named_scope("pack"):
        listed = src_block.reshape(vocab_count, pair_count)
        place = jnp.stack([vocab_index, sign]).astype(jnp.int32)
        own, ahead, behind, packed = pl.pallas_call(
            pack_kernel,
            out_shape=(planes(home), planes(SIZES[0][0]), planes(SIZES[1][0]), jax.ShapeDtypeStruct((8, BLK), jnp.int32)),
            in_specs=[vmem] * 6,
            out_specs=(vmem,) * 4,
            scratch_shapes=[
                pltpu.VMEM((doc_count * span, teacher_cols), jnp.bfloat16),
                pltpu.VMEM((teacher_blocks, ROWS, BLK), jnp.bfloat16),
            ],
            compiler_params=room,
        )(jnp.broadcast_to(place[:, None], (2, BLK)), listed, teacher_logits, low, high, pick)

    with jax.named_scope("plan"):
        table = jax.ShapeDtypeStruct((8, BLK), jnp.int32)
        send, items, left = pl.pallas_call(
            functools.partial(plan_kernel, teacher_blocks),
            out_shape=(jax.ShapeDtypeStruct((8, 2 * BLK), jnp.int32), table, table),
            in_specs=[smem, vmem, vmem],
            out_specs=(vmem,) * 3,
            scratch_shapes=[pltpu.VMEM((6 * steps, vocab_count, BLK), jnp.float32)],
            compiler_params=room,
        )(place, listed, packed)

    def ready(chain, step, after, frames):
        return pl.pallas_call(
            functools.partial(ready_kernel, chain, step),
            out_shape=planes(SIZES[chain][step]),
            in_specs=[anywhere] + [vmem] * (2 + len(frames)),
            out_specs=vmem,
            compiler_params=room,
        )(after, send, own, *frames)

    def passed(chain, step, part, newest):
        return pl.pallas_call(
            functools.partial(pass_kernel, chain, step, home),
            out_shape=planes(SIZES[chain][step]),
            in_specs=[vmem] * 3,
            out_specs=vmem,
            compiler_params=room,
        )(send, part, newest)

    with jax.named_scope("ring"):
        forward, backward = ring_pairs(1), ring_pairs(-1)
        came_behind = [lax.ppermute(behind, ("seq", "vocab"), backward)]
        came_ahead = [lax.ppermute(ahead, ("seq", "vocab"), forward)]
        for step in range(1, steps):
            part = ready(1, step, ahead, came_behind[:-1])
            behind = passed(1, step, part, came_behind[-1])
            came_behind.append(lax.ppermute(behind, ("seq", "vocab"), backward))
            part = ready(0, step, behind, came_ahead[:-1])
            ahead = passed(0, step, part, came_ahead[-1])
            came_ahead.append(lax.ppermute(ahead, ("seq", "vocab"), forward))

    with jax.named_scope("student"):
        top, total = pl.pallas_call(
            student_kernel,
            out_shape=(jax.ShapeDtypeStruct((row_count, BLK), jnp.float32),) * 2,
            in_specs=[vmem],
            out_specs=(vmem,) * 2,
            compiler_params=room,
        )(student_logits)

    with jax.named_scope("stage"):
        early = (own, *came_ahead[:-1], *came_behind[:-1])
        held = pl.pallas_call(
            functools.partial(stage_kernel, steps),
            out_shape=planes(pair_count + 2 * vocab_count),
            in_specs=[smem] + [vmem] * len(early),
            out_specs=vmem,
            compiler_params=room,
        )(items, *early)

    with jax.named_scope("map"):
        sums = pl.pallas_call(
            functools.partial(map_kernel, steps),
            out_shape=jax.ShapeDtypeStruct((8, row_count), jnp.float32),
            in_specs=[smem] + [vmem] * 8,
            out_specs=vmem,
            scratch_shapes=[
                pltpu.VMEM((pair_count + 2 * vocab_count, ROWS, BLK), jnp.bfloat16),
                pltpu.VMEM((3 * steps, row_count, BLK), jnp.float32),
            ],
            compiler_params=room,
        )(items, held, came_ahead[-1], came_behind[-1], spread, weights, student_logits, top, total)

    with jax.named_scope("finish"):
        sent = jnp.broadcast_to(sums[None, :4], (vocab_count, 4, row_count))
        parts = lax.all_to_all(sent, "vocab", split_axis=0, concat_axis=0, tiled=True)
        mass_part, cross_part, top_part, total_part = (parts[:, i] for i in range(4))
        student_top = jnp.max(top_part, axis=0)
        log_total = student_top + jnp.log(jnp.sum(jnp.exp(top_part - student_top) * total_part, axis=0))
        mass = jnp.sum(mass_part, axis=0)
        result = jnp.sum(cross_part + mass_part * (log_total - top_part), axis=0) / mass - jnp.log(mass)

    result = lax.cond(
        rows_fit & (left[0, 0] == 0),
        lambda *_: result,
        lambda *operands: whole(operands[:3], *operands[3:]),
        low,
        teacher_logits,
        high,
        cand,
        src_block,
        weights,
        student_logits,
    )
    return result.reshape(doc_count, pos_count)


def solution(mesh):
    in_specs = (
        P("dp", "seq", "vocab"),
        P("dp", "seq", "vocab"),
        P("dp", "seq"),
        P(),
        P("vocab", None, "dp", None),
    )
    out_specs = P("dp", "seq")
    return jax.shard_map(shards, mesh=mesh, in_specs=in_specs, out_specs=out_specs, check_vma=False)
```

```python
import functools

import jax
import jax.numpy as jnp
from jax import lax
from jax.experimental import pallas as pl
from jax.experimental.pallas import tpu as pltpu
from jax.sharding import PartitionSpec as P

BLK = 128
K = 2
W = 16
ROWS = 104
SIZES = ((24, 21, 21, 21, 20, 20, 20, 20), (14, 22, 22, 22, 22, 22, 22, 22))
STARTS = tuple(tuple(sum(sizes[:f]) for f in range(len(sizes))) for sizes in SIZES)
TINY = 1.2e-38


def halo(block, width):
    count = lax.axis_size("seq")
    forward = [(i, (i + 1) % count) for i in range(count)]
    backward = [(target, source) for source, target in forward]
    low = lax.ppermute(block[:, block.shape[1] - width :], "seq", forward)
    high = lax.ppermute(block[:, :width], "seq", backward)
    return low, high


def ring_pairs(turn):
    seq_count, vocab_count = lax.axis_size("seq"), lax.axis_size("vocab")
    pairs = []
    for s in range(seq_count):
        step = turn if s % 2 == 0 else -turn
        for v in range(vocab_count):
            pairs.append((s * vocab_count + v, s * vocab_count + (v + step) % vocab_count))
    return pairs


def tie_key(block):
    return (block * 5) & 7


def ways(distance, block, share, vocab_count):
    half = vocab_count // 2
    first = tie_key(block) < share
    ahead = jnp.where((distance >= 1) & ((distance < half) | ((distance == half) & first)), distance, 0)
    behind = jnp.where((distance > half) | ((distance == half) & ~first), vocab_count - distance, 0)
    return ahead, behind


def ones(mask):
    return jnp.where(mask, 1.0, 0.0).astype(jnp.bfloat16)


def tie_share(reach, facing, lane, half):
    share = jnp.zeros((reach[0].shape[0], 1), jnp.int32)
    for part in range(1, 9):
        first = tie_key(lane) < part
        more = jnp.where(facing & first, half, reach[0]) - jnp.where(facing & ~first, half, reach[1])
        share = share + (jnp.sum(more, axis=1, keepdims=True) <= 0).astype(jnp.int32)
    return share


def full_reach(reach, facing, lane, share, blocks, half):
    first = tie_key(lane) < share
    ahead = jnp.where(facing & first, half, reach[0])
    behind = jnp.where(facing & ~first, half, reach[1])
    return [jnp.where(lane == blocks, half, ahead), jnp.where(lane == blocks, half - 1, behind)]


def split(listed, blocks, vocab_count):
    holder = sum((listed >= h * blocks).astype(jnp.int32) for h in range(1, vocab_count))
    return holder, listed - holder * blocks


def turn(table):
    rows, columns = table.shape
    table = table.astype(jnp.float32)
    if columns < BLK:
        table = jnp.concatenate([table, jnp.zeros((rows, BLK - columns), jnp.float32)], axis=1)
    if rows < BLK:
        table = jnp.concatenate([table, jnp.zeros((BLK - rows, BLK), jnp.float32)], axis=0)
    return table.T.astype(jnp.int32)


def earlier_lanes():
    square = (BLK, BLK)
    return ones(lax.broadcasted_iota(jnp.int32, square, 0) < lax.broadcasted_iota(jnp.int32, square, 1))


def plan_kernel(blocks, place_ref, listed_ref, after_ref, send_ref, item_ref, fit_ref, book_ref):
    vocab_count, pair_count = listed_ref.shape
    half = vocab_count // 2
    steps = half
    home = blocks + 1
    me, sign = place_ref[0], place_ref[1]
    f32, i32 = jnp.float32, jnp.int32
    shape = (vocab_count, BLK)
    straight = sign > 0

    def of_chain(table, way, f):
        return jnp.where(straight, float(table[way][f]), float(table[1 - way][f]))


    del after_ref
    listed = listed_ref[...]
    row_holder, _ = split(listed, blocks, vocab_count)
    holders, inners = split(turn(listed)[:pair_count], blocks, vocab_count)
    lane = lax.broadcasted_iota(i32, shape, 1)
    row = lax.broadcasted_iota(i32, shape, 0)

    reach = [jnp.zeros(shape, i32), jnp.zeros(shape, i32)]
    across = jnp.zeros(shape, i32)
    pair_lane = lax.broadcasted_iota(i32, (pair_count, BLK), 1)
    pair_row = lax.broadcasted_iota(i32, (vocab_count, pair_count), 0)
    for s in range(vocab_count):
        hits = jnp.dot(
            ones(pair_row == row_holder[s : s + 1, :]),
            ones(pair_lane == inners[:, s : s + 1]),
            preferred_element_type=f32,
        )
        distance = s - row
        distance = jnp.where(distance < 0, distance + vocab_count, distance)
        needed = hits > 0
        reach[0] = jnp.maximum(reach[0], jnp.where(needed & (distance < half), distance, 0))
        reach[1] = jnp.maximum(reach[1], jnp.where(needed & (distance > half), vocab_count - distance, 0))
        across = jnp.maximum(across, jnp.where(needed & (distance == half), 1, 0))
    share = tie_share(reach, across > 0, lane, half)
    reach = full_reach(reach, across > 0, lane, share, blocks, half)

    square = (BLK, BLK)
    up, over = lax.broadcasted_iota(i32, square, 0), lax.broadcasted_iota(i32, square, 1)
    earlier = earlier_lanes()
    left_up, left_over = (up & 7) + 1 - (up >> 3), (over & 7) + 1 - (over >> 3)
    goes_first = ones((left_up > left_over) | ((left_up == left_over) & ((up >> 3) > (over >> 3))))
    index, waiting, moved = [], [], [jnp.zeros(shape, f32)] * 2
    for way in range(2):
        masks = jnp.concatenate([ones(reach[way] == r) for r in range(1, half + 1)], axis=0)
        before = jnp.dot(masks, earlier, preferred_element_type=f32)
        place = jnp.zeros(shape, f32)
        count = jnp.zeros(shape, f32)
        for r in range(1, half + 1):
            same = reach[way] == r
            place = jnp.where(same, before[(r - 1) * vocab_count : r * vocab_count], place)
            total = jnp.sum(jnp.where(same, 1.0, 0.0), axis=1, keepdims=True)
            count = jnp.where(lane == r - 1, total, count)
        index.append(place)
        waiting.append(count)
    travels = (lane >= 8) & (lane < 8 * half) & ((lane & 7) + 1 > (lane >> 3))
    for f in range(steps):
        ahead_of = jnp.dot(
            jnp.concatenate(waiting, axis=0).astype(jnp.bfloat16), goes_first, preferred_element_type=f32
        )
        for way in range(2):
            first = ahead_of[way * vocab_count : (way + 1) * vocab_count]
            size = of_chain(SIZES, way, f)
            go = jnp.clip(size - first, 0.0, waiting[way])
            book_ref[(f * 2 + way) * 3] = moved[way]
            moved[way] = moved[way] + go
            book_ref[(f * 2 + way) * 3 + 1] = moved[way]
            book_ref[(f * 2 + way) * 3 + 2] = jnp.minimum(first, size)
            come = pltpu.roll(pltpu.roll(go, 8, 1), 1 if way == 0 else vocab_count - 1, 0)
            waiting[way] = waiting[way] - go + jnp.where(travels, come, 0.0)
    left = jnp.sum(waiting[0] + waiting[1], axis=1, keepdims=True)
    left = jnp.sum(jnp.broadcast_to(left, shape), axis=0, keepdims=True)
    fit_ref[...] = jnp.broadcast_to(left, fit_ref.shape).astype(i32)

    small = (vocab_count, vocab_count)
    target = lax.broadcasted_iota(i32, (BLK, 2 * BLK), 1).astype(f32)
    pointer, sends = [], []
    for way in range(2):
        step = 1 if way == 0 else -1
        back = me - step * lax.broadcasted_iota(i32, small, 0)
        back = jnp.where(back < 0, back + vocab_count, jnp.where(back >= vocab_count, back - vocab_count, back))
        pick = ones(back == lax.broadcasted_iota(i32, small, 1))
        far = jnp.dot(pick, reach[way].astype(f32).astype(jnp.bfloat16), preferred_element_type=f32).astype(i32)
        order = jnp.dot(pick, index[way].astype(jnp.bfloat16), preferred_element_type=f32)
        giver = me - step
        giver = jnp.where(giver < 0, giver + vocab_count, jnp.where(giver >= vocab_count, giver - vocab_count, giver))

        def slot(at, hops, valid):
            column = jnp.clip(hops * 8 + far - 1, 0, BLK - 1)
            where = jnp.full(shape, -1.0, f32)
            for f in range(steps):
                start, end, first = (
                    jnp.take_along_axis(
                        jnp.broadcast_to(book_ref[(f * 2 + way) * 3 + kind, pl.ds(at, 1), :], shape),
                        column,
                        axis=1,
                        mode="promise_in_bounds",
                    )
                    for kind in range(3)
                )
                now = valid & (start <= order) & (order < end)
                where = jnp.where(now, of_chain(STARTS, way, f) + first + order - start, where)
            return where

        leave = slot(me, row, (far > row) & (row < half))
        arrive = slot(giver, row - 1, (far >= row) & (row >= 1) & (row <= half))
        point = jnp.where(row == 0, lane.astype(f32), jnp.maximum(home + arrive, 0.0))
        pointer.append(point)
        leave_turned = jnp.concatenate([leave, jnp.full((BLK - vocab_count, BLK), -1.0, f32)], axis=0).T
        chosen = jnp.zeros((1, 2 * BLK), f32)
        for h in range(half):
            chosen = chosen + jnp.dot(
                point[h : h + 1].astype(jnp.bfloat16),
                ones(leave_turned[:, h : h + 1] == target),
                preferred_element_type=f32,
            )
        sends.append(chosen.astype(i32))
    send_ref[0:1, :] = jnp.where(straight, sends[0], sends[1])
    send_ref[1:2, :] = jnp.where(straight, sends[1], sends[0])
    send_ref[2:8, :] = jnp.zeros((6, 2 * BLK), i32)

    mine_lane = lax.broadcasted_iota(i32, (pair_count, vocab_count), 1)
    holder = jnp.sum(jnp.where(pair_lane == me, holders, 0), axis=1, keepdims=True)
    inner = jnp.sum(jnp.where(pair_lane == me, inners, 0), axis=1, keepdims=True)
    distance = me - holder
    distance = jnp.where(distance < 0, distance + vocab_count, distance)
    share = turn(jnp.broadcast_to(share, shape))[:1]
    share = jnp.sum(jnp.where(pair_lane == holder, share, 0), axis=1, keepdims=True)
    hops = ways(distance, inner, share, vocab_count)
    scale = jnp.where(distance <= half, distance, 2 * vocab_count - distance)
    points = jnp.zeros((pair_count, 1), f32)
    for way in range(2):
        found = lax.dot_general(
            ones(pair_lane == inner),
            pointer[way].astype(jnp.bfloat16),
            (((1,), (1,)), ((), ())),
            preferred_element_type=f32,
        )
        points = points + jnp.sum(
            jnp.where((mine_lane == hops[way]) & (hops[way] > 0), found, 0.0), axis=1, keepdims=True
        )
    points = jnp.where(distance == 0, inner.astype(f32), points)
    by_stats = [jnp.sum(jnp.where(lane == blocks, p, 0.0), axis=1, keepdims=True) for p in pointer]
    hop = lax.broadcasted_iota(i32, (vocab_count, 1), 0)
    stat_ok = [hop <= half, (hop >= 1) & (hop < half)]
    points = jnp.concatenate(
        [points] + [jnp.where(ok, p, 0.0) for ok, p in zip(stat_ok, by_stats)], axis=0
    ).astype(i32)
    other = jnp.concatenate(
        [(hops[1] > 0).astype(i32), jnp.zeros((vocab_count, 1), i32), jnp.ones((vocab_count, 1), i32)], axis=0
    )
    other = jnp.where(straight, other, 1 - other)
    scale = jnp.concatenate([scale, jnp.zeros((2 * vocab_count, 1), i32)], axis=0)
    frame = jnp.zeros(points.shape, i32)
    base = jnp.full(points.shape, home, i32)
    limit = jnp.where(other == 1, SIZES[1][0], SIZES[0][0])
    for f in range(1, steps):
        reached = points >= home + jnp.where(other == 1, STARTS[1][f], STARTS[0][f])
        frame = frame + reached.astype(i32)
        base = jnp.where(reached, home + jnp.where(other == 1, STARTS[1][f], STARTS[0][f]), base)
        limit = jnp.where(reached, jnp.where(other == 1, SIZES[1][f], SIZES[0][f]), limit)
    away = points >= home
    source = jnp.where(away, 1 + frame + steps * other, 0)
    spot = jnp.where(away, points - base, points)
    spot = jnp.clip(spot, 0, jnp.where(away, limit, home) - 1)
    items = points.shape[0]
    item_lane = lax.broadcasted_iota(i32, (items, BLK), 1)
    table = jnp.where(
        item_lane == 0, spot, jnp.where(item_lane == 1, scale, jnp.where(item_lane == 2, source, 0))
    ).astype(f32)
    turned = jnp.concatenate([table, jnp.zeros((BLK - items, BLK), f32)], axis=0).T
    source_row = turned[2:3].astype(i32)
    item_up = lax.broadcasted_iota(i32, (items, BLK), 0)
    is_item = item_lane < items
    sooner = is_item & ((source_row < source) | ((source_row == source) & (item_lane < item_up)))
    rank = jnp.sum(sooner.astype(i32), axis=1, keepdims=True)
    item_ref[0:1, :] = turned[0:1].astype(i32)
    item_ref[1:2, :] = turned[1:2].astype(i32)
    item_ref[2:3, :] = jnp.sum(jnp.where(rank == item_lane, item_up, 0), axis=0, keepdims=True)
    item_ref[3:4, :] = jnp.sum((source < item_lane).astype(i32), axis=0, keepdims=True)
    item_ref[4:8, :] = jnp.zeros((4, BLK), i32)


def scalars(table_ref, row, start, count):
    values = table_ref[row : row + 1, :]
    return [values[0, start + j] for j in range(count)]


def in_order(place, valid, count):
    square = (BLK, BLK)
    up, over = lax.broadcasted_iota(jnp.int32, square, 0), lax.broadcasted_iota(jnp.int32, square, 1)
    lanes = jnp.sum(jnp.where((place == up) & valid, over, 0), axis=1, keepdims=True)
    row = turn(jnp.broadcast_to(lanes, square))[:1]
    return [row[0, j] for j in range(count)]


def first_choice(blocks, place_ref, listed_ref):
    vocab_count, pair_count = listed_ref.shape
    half = vocab_count // 2
    i32 = jnp.int32
    me, sign = place_ref[0:1, :], place_ref[1:2, :]
    holders, inners = split(turn(listed_ref[...])[:pair_count], blocks, vocab_count)
    pair_lane = lax.broadcasted_iota(i32, (pair_count, BLK), 1)
    lane = lax.broadcasted_iota(i32, (1, BLK), 1)
    reach = [jnp.zeros((1, BLK), i32), jnp.zeros((1, BLK), i32)]
    facing = jnp.zeros((1, BLK), i32)
    for s in range(vocab_count):
        hits = (pair_lane == inners[:, s : s + 1]) & (jnp.broadcast_to(holders[:, s : s + 1], pair_lane.shape) == me)
        seen = jnp.max(jnp.where(hits, 1, 0), axis=0, keepdims=True)
        distance = s - me
        distance = jnp.where(distance < 0, distance + vocab_count, distance)
        reach[0] = jnp.maximum(reach[0], jnp.where(distance < half, distance * seen, 0))
        reach[1] = jnp.maximum(reach[1], jnp.where(distance > half, (vocab_count - distance) * seen, 0))
        facing = jnp.maximum(facing, jnp.where(distance == half, seen, 0))
    share = tie_share(reach, facing > 0, lane, half)
    reach = full_reach(reach, facing > 0, lane, share, blocks, half)
    choices = []
    for sizes, one, other in zip(SIZES, reach, reach[::-1]):
        far = jnp.where(sign > 0, one, other)
        key = jnp.broadcast_to(far * BLK + (BLK - 1 - lane), (BLK, BLK))
        place = jnp.sum((turn(key) > key).astype(i32), axis=0, keepdims=True)
        choices.append(in_order(place, far > 0, sizes[0]))
    return choices


def pack_kernel(
    place_ref,
    listed_ref,
    own_ref,
    low_ref,
    high_ref,
    pick_ref,
    home_ref,
    first_ref,
    second_ref,
    done_ref,
    cand_ref,
    logit_ref,
):
    docs, positions, columns = own_ref.shape
    width = low_ref.shape[1]
    span = positions + 2 * width
    rows = pick_ref.shape[0]
    blocks = columns // BLK
    for doc in range(docs):
        cand_ref[doc * span : doc * span + width, :] = low_ref[doc]
        cand_ref[doc * span + width : doc * span + width + positions, :] = own_ref[doc]
        cand_ref[doc * span + width + positions : (doc + 1) * span, :] = high_ref[doc]
    pick = pick_ref[...]
    peak = jnp.full((rows, BLK), -jnp.inf, jnp.float32)
    for t in range(blocks):
        part = jnp.dot(pick, cand_ref[:, t * BLK : (t + 1) * BLK], preferred_element_type=jnp.float32)
        logit_ref[t] = part.astype(jnp.bfloat16)
        peak = jnp.maximum(peak, part)
    top = jnp.max(peak, axis=1, keepdims=True)
    total = jnp.zeros((rows, BLK), jnp.float32)
    for t in range(blocks):
        power = jnp.exp(logit_ref[t].astype(jnp.float32) - top)
        total = total + power
        home_ref[t] = power.astype(jnp.bfloat16)
    total = jnp.sum(total, axis=1, keepdims=True)
    first = total.astype(jnp.bfloat16).astype(jnp.float32)
    second = (total - first).astype(jnp.bfloat16).astype(jnp.float32)
    third = total - first - second
    lane = lax.broadcasted_iota(jnp.int32, (rows, BLK), 1)
    home_ref[blocks] = jnp.where(
        lane == 0, top, jnp.where(lane == 1, first, jnp.where(lane == 2, second, jnp.where(lane == 3, third, 0.0)))
    ).astype(jnp.bfloat16)
    for out_ref, choice in zip((first_ref, second_ref), first_choice(blocks, place_ref, listed_ref)):
        for j, at in enumerate(choice):
            out_ref[j] = home_ref[at]
    done_ref[...] = jnp.zeros(done_ref.shape, jnp.int32)


def ready_kernel(chain, step, after_ref, send_ref, home_ref, *refs):
    del after_ref
    frames, out_ref = refs[:-1], refs[-1]
    home = home_ref.shape[0]
    for j, at in enumerate(scalars(send_ref, chain, STARTS[chain][step], SIZES[chain][step])):

        def copy(low, high, j=j, at=at):
            if high - low == 1:
                if low == 0:
                    out_ref[j] = home_ref[at]
                elif low <= len(frames):
                    out_ref[j] = frames[low - 1][at - home - STARTS[chain][low - 1]]
                return
            mid = (low + high) // 2
            split = home + STARTS[chain][mid - 1]
            pl.when(at < split)(lambda: copy(low, mid))
            pl.when(at >= split)(lambda: copy(mid, high))

        copy(0, len(frames) + 2)


def pass_kernel(chain, step, home, send_ref, part_ref, newest_ref, out_ref):
    start = home + STARTS[chain][step - 1]
    for j, at in enumerate(scalars(send_ref, chain, STARTS[chain][step], SIZES[chain][step])):
        newest = newest_ref[jnp.maximum(at - start, 0)]
        out_ref[j] = jnp.where(at >= start, newest, part_ref[j])


def stage_kernel(steps, item_ref, *refs):
    sources, stage_ref = refs[:-1], refs[-1]
    for s, source in zip([s for s in range(2 * steps + 1) if s not in (steps, 2 * steps)], sources):
        bring(item_ref, s, source, stage_ref)


def bring(item_ref, s, source_ref, stage_ref):
    def one(q, carry):
        item = item_ref[2, q]
        stage_ref[item] = source_ref[item_ref[0, item]]
        return carry

    lax.fori_loop(item_ref[3, s], item_ref[3, s + 1], one, 0)


def student_kernel(student_ref, top_ref, total_ref):
    docs, positions, columns = student_ref.shape
    rows = docs * positions
    peak = jnp.full((rows, BLK), -jnp.inf, jnp.float32)
    for b in range(columns // BLK):
        part = student_ref[:, :, b * BLK : (b + 1) * BLK].reshape(rows, BLK).astype(jnp.float32)
        peak = jnp.maximum(peak, part)
    top = jnp.max(peak, axis=1, keepdims=True)
    total = jnp.zeros((rows, BLK), jnp.float32)
    for b in range(columns // BLK):
        part = student_ref[:, :, b * BLK : (b + 1) * BLK].reshape(rows, BLK).astype(jnp.float32)
        total = total + jnp.exp(part - top)
    top_ref[...] = jnp.broadcast_to(top, (rows, BLK))
    total_ref[...] = jnp.broadcast_to(jnp.sum(total, axis=1, keepdims=True), (rows, BLK))


def map_kernel(
    steps,
    item_ref,
    held_ref,
    ahead_ref,
    behind_ref,
    spread_ref,
    weight_ref,
    student_ref,
    top_ref,
    total_ref,
    out_ref,
    stage_ref,
    scale_ref,
):
    docs, positions, columns = student_ref.shape
    rows = docs * positions
    blocks = columns // BLK
    spread = spread_ref[...]
    for i in range(stage_ref.shape[0]):
        stage_ref[i] = held_ref[i]
    bring(item_ref, steps, ahead_ref, stage_ref)
    bring(item_ref, 2 * steps, behind_ref, stage_ref)
    holders = [h for h in range(steps + 1)] + [2 * steps + h for h in range(1, steps)]
    peaks, sums = [], []
    for h in holders:
        stats = jnp.dot(spread, stage_ref[K * blocks + h], preferred_element_type=jnp.float32)
        peaks.append(stats[:, 0:1])
        sums.append(stats[:, 1:2] + stats[:, 2:3] + stats[:, 3:4])
    peak = functools.reduce(jnp.maximum, peaks)
    powers = [jnp.exp(p - peak) for p in peaks]
    norm = sum(p * t for p, t in zip(powers, sums))
    for h, power in zip(holders, powers):
        scale_ref[h] = jnp.broadcast_to(power / norm, (rows, BLK))
    student_top = top_ref[...]
    mass = jnp.zeros((rows, BLK), jnp.float32)
    cross = jnp.zeros((rows, BLK), jnp.float32)
    for b in range(blocks):
        picked = jnp.concatenate([stage_ref[K * b], stage_ref[K * b + 1]], axis=1)
        prob = jnp.dot(spread, picked, preferred_element_type=jnp.float32).astype(jnp.bfloat16)
        mapped = scale_ref[item_ref[1, K * b]] * jnp.dot(
            prob[:, :BLK], weight_ref[:, K * b].reshape(BLK, BLK), preferred_element_type=jnp.float32
        ) + scale_ref[item_ref[1, K * b + 1]] * jnp.dot(
            prob[:, BLK:], weight_ref[:, K * b + 1].reshape(BLK, BLK), preferred_element_type=jnp.float32
        )
        logit = student_ref[:, :, b * BLK : (b + 1) * BLK].reshape(rows, BLK).astype(jnp.float32) - student_top
        mass = mass + mapped
        cross = cross + mapped * (jnp.log(jnp.maximum(mapped, TINY)) - logit)
    mass = jnp.sum(mass, axis=1, keepdims=True)
    cross = jnp.sum(cross, axis=1, keepdims=True)
    lane = lax.broadcasted_iota(jnp.int32, (rows, BLK), 1)
    table = jnp.where(
        lane == 0, mass, jnp.where(lane == 1, cross, jnp.where(lane == 2, student_top, total_ref[...]))
    )
    parts = table.T[:4]
    for v in range(out_ref.shape[0]):
        out_ref[v] = parts


def whole(padded_parts, cand, src_block, weights, student_logits):
    doc_count, pos_count, student_cols = student_logits.shape
    teacher_cols = padded_parts[0].shape[2]
    teacher_blocks = teacher_cols // BLK
    student_blocks = student_cols // BLK
    row_count = doc_count * pos_count
    padded = jnp.concatenate(padded_parts, axis=1).reshape(-1, teacher_cols)
    teacher_float = jnp.take(padded, cand, axis=0).astype(jnp.float32)
    student_float = student_logits.reshape(row_count, student_cols).astype(jnp.float32)
    teacher_peak = jnp.max(teacher_float, axis=1)
    student_peak = jnp.max(student_float, axis=1)
    teacher_top, student_top = lax.pmax((teacher_peak, student_peak), "vocab")
    teacher_total, student_total = lax.psum(
        (
            jnp.sum(jnp.exp(teacher_float - teacher_top[:, None]), axis=1),
            jnp.sum(jnp.exp(student_float - student_top[:, None]), axis=1),
        ),
        "vocab",
    )
    teacher_prob = (jnp.exp(teacher_float - teacher_top[:, None]) / teacher_total[:, None]).astype(jnp.bfloat16)
    student_logprob = student_float - student_top[:, None] - jnp.log(student_total)[:, None]
    vocab_count = lax.axis_size("vocab")
    own_index = lax.axis_index("vocab")
    pair_count = student_blocks * K
    capacity = 2 * K * student_blocks // vocab_count
    pair_blocks = src_block.reshape(vocab_count, pair_count)
    holder = pair_blocks // teacher_blocks
    inside = pair_blocks % teacher_blocks
    same_holder = holder[:, :, None] == holder[:, None, :]
    before = jnp.arange(pair_count)[None, :] < jnp.arange(pair_count)[:, None]
    slot_rank = jnp.sum(same_holder & before[None, :, :], axis=2)
    chosen = (holder == own_index)[:, None, :] & (
        slot_rank[:, None, :] == jnp.arange(capacity)[None, :, None]
    )
    send_index = jnp.sum(jnp.where(chosen, inside[:, None, :], 0), axis=2)
    prob_blocks = teacher_prob.reshape(row_count, teacher_blocks, BLK)
    outgoing = jnp.take(prob_blocks, send_index.reshape(-1), axis=1).reshape(row_count, vocab_count, capacity, BLK)
    incoming = lax.all_to_all(outgoing, "vocab", split_axis=1, concat_axis=1, tiled=True)
    own_holder = jnp.take(holder, own_index, axis=0)
    own_rank = jnp.take(slot_rank, own_index, axis=0)
    recv_slot = own_holder * capacity + own_rank
    gathered = jnp.take(incoming.reshape(row_count, vocab_count * capacity, BLK), recv_slot, axis=1).reshape(
        row_count, student_blocks, K, BLK
    )
    weights = weights.swapaxes(0, 1).reshape(student_blocks, K, BLK, BLK)
    mapped = jnp.einsum("rbkc,bkcd->rbd", gathered, weights, preferred_element_type=jnp.float32).reshape(
        row_count, student_cols
    )
    total_mass = lax.psum(jnp.sum(mapped, axis=1), "vocab")
    normed = mapped / total_mass[:, None]
    return lax.psum(
        jnp.sum(jax.scipy.special.xlogy(normed, normed) - normed * student_logprob, axis=1), "vocab"
    )


def shards(teacher_logits, student_logits, alignment, src_block, margin_weight):
    doc_count, pos_count, teacher_cols = teacher_logits.shape
    student_cols = student_logits.shape[2]
    teacher_blocks = teacher_cols // BLK
    student_blocks = student_cols // BLK
    row_count = doc_count * pos_count
    pair_count = student_blocks * K
    vocab_count = lax.axis_size("vocab")
    steps = vocab_count // 2
    home = teacher_blocks + 1
    vocab_index = lax.axis_index("vocab")
    seq_index = lax.axis_index("seq")
    sign = 1 - 2 * (seq_index % 2)
    span = pos_count + 2 * W

    with jax.named_scope("halo"):
        low, high = halo(teacher_logits, W)
    with jax.named_scope("weights"):
        weights = lax.all_gather(
            margin_weight.reshape(pair_count, -1, BLK), "dp", axis=0, tiled=False
        )

    with jax.named_scope("rows"):
        cand = (alignment - seq_index * pos_count + W + jnp.arange(doc_count)[:, None] * span).reshape(-1)
        cand = jnp.clip(cand, 0, doc_count * span - 1)
        places = jnp.arange(doc_count * span)
        used = jnp.any(cand[:, None] == places[None, :], axis=0)
        place_rank = jnp.sum(used[:, None] & (places[:, None] < places[None, :]), axis=0)
        cand_rank = jnp.sum(used[None, :] & (places[None, :] < cand[:, None]), axis=1)
        row_ids = jnp.arange(ROWS)
        pick = ((row_ids[:, None] == place_rank[None, :]) & used[None, :]).astype(jnp.bfloat16)
        spread = (cand_rank[:, None] == row_ids[None, :]).astype(jnp.bfloat16)
        rows_fit = jnp.sum(used.astype(jnp.int32)) <= ROWS

    vmem = pl.BlockSpec(memory_space=pltpu.VMEM)
    smem = pl.BlockSpec(memory_space=pltpu.SMEM)
    anywhere = pl.BlockSpec(memory_space=pl.ANY)
    room = pltpu.CompilerParams(vmem_limit_bytes=20 * 1024 * 1024)

    def planes(count):
        return jax.ShapeDtypeStruct((count, ROWS, BLK), jnp.bfloat16)

    with jax.named_scope("pack"):
        listed = src_block.reshape(vocab_count, pair_count)
        place = jnp.stack([vocab_index, sign]).astype(jnp.int32)
        own, ahead, behind, packed = pl.pallas_call(
            pack_kernel,
            out_shape=(planes(home), planes(SIZES[0][0]), planes(SIZES[1][0]), jax.ShapeDtypeStruct((8, BLK), jnp.int32)),
            in_specs=[vmem] * 6,
            out_specs=(vmem,) * 4,
            scratch_shapes=[
                pltpu.VMEM((doc_count * span, teacher_cols), jnp.bfloat16),
                pltpu.VMEM((teacher_blocks, ROWS, BLK), jnp.bfloat16),
            ],
            compiler_params=room,
        )(jnp.broadcast_to(place[:, None], (2, BLK)), listed, teacher_logits, low, high, pick)

    with jax.named_scope("plan"):
        table = jax.ShapeDtypeStruct((8, BLK), jnp.int32)
        send, items, left = pl.pallas_call(
            functools.partial(plan_kernel, teacher_blocks),
            out_shape=(jax.ShapeDtypeStruct((8, 2 * BLK), jnp.int32), table, table),
            in_specs=[smem, vmem, vmem],
            out_specs=(vmem,) * 3,
            scratch_shapes=[pltpu.VMEM((6 * steps, vocab_count, BLK), jnp.float32)],
            compiler_params=room,
        )(place, listed, packed)

    def ready(chain, step, after, frames):
        return pl.pallas_call(
            functools.partial(ready_kernel, chain, step),
            out_shape=planes(SIZES[chain][step]),
            in_specs=[anywhere] + [vmem] * (2 + len(frames)),
            out_specs=vmem,
            compiler_params=room,
        )(after, send, own, *frames)

    def passed(chain, step, part, newest):
        return pl.pallas_call(
            functools.partial(pass_kernel, chain, step, home),
            out_shape=planes(SIZES[chain][step]),
            in_specs=[vmem] * 3,
            out_specs=vmem,
            compiler_params=room,
        )(send, part, newest)

    with jax.named_scope("ring"):
        forward, backward = ring_pairs(1), ring_pairs(-1)
        came_behind = [lax.ppermute(behind, ("seq", "vocab"), backward)]
        came_ahead = [lax.ppermute(ahead, ("seq", "vocab"), forward)]
        for step in range(1, steps):
            part = ready(1, step, ahead, came_behind[:-1])
            behind = passed(1, step, part, came_behind[-1])
            came_behind.append(lax.ppermute(behind, ("seq", "vocab"), backward))
            part = ready(0, step, behind, came_ahead[:-1])
            ahead = passed(0, step, part, came_ahead[-1])
            came_ahead.append(lax.ppermute(ahead, ("seq", "vocab"), forward))

    with jax.named_scope("student"):
        top, total = pl.pallas_call(
            student_kernel,
            out_shape=(jax.ShapeDtypeStruct((row_count, BLK), jnp.float32),) * 2,
            in_specs=[vmem],
            out_specs=(vmem,) * 2,
            compiler_params=room,
        )(student_logits)

    with jax.named_scope("stage"):
        early = (own, *came_ahead[:-1], *came_behind[:-1])
        held = pl.pallas_call(
            functools.partial(stage_kernel, steps),
            out_shape=planes(pair_count + 2 * vocab_count),
            in_specs=[smem] + [vmem] * len(early),
            out_specs=vmem,
            compiler_params=room,
        )(items, *early)

    with jax.named_scope("map"):
        sums = pl.pallas_call(
            functools.partial(map_kernel, steps),
            out_shape=jax.ShapeDtypeStruct((vocab_count, 4, row_count), jnp.float32),
            in_specs=[smem] + [vmem] * 8,
            out_specs=vmem,
            scratch_shapes=[
                pltpu.VMEM((pair_count + 2 * vocab_count, ROWS, BLK), jnp.bfloat16),
                pltpu.VMEM((3 * steps, row_count, BLK), jnp.float32),
            ],
            compiler_params=room,
        )(items, held, came_ahead[-1], came_behind[-1], spread, weights, student_logits, top, total)

    with jax.named_scope("finish"):
        parts = lax.all_to_all(sums, "vocab", split_axis=0, concat_axis=0, tiled=True)
        mass_part, cross_part, top_part, total_part = (parts[:, i] for i in range(4))
        student_top = jnp.max(top_part, axis=0)
        log_total = student_top + jnp.log(jnp.sum(jnp.exp(top_part - student_top) * total_part, axis=0))
        mass = jnp.sum(mass_part, axis=0)
        result = jnp.sum(cross_part + mass_part * (log_total - top_part), axis=0) / mass - jnp.log(mass)

    result = lax.cond(
        rows_fit & (left[0, 0] == 0),
        lambda *_: result,
        lambda *operands: whole(operands[:3], *operands[3:]),
        low,
        teacher_logits,
        high,
        cand,
        src_block,
        weights,
        student_logits,
    )
    return result.reshape(doc_count, pos_count)


def solution(mesh):
    in_specs = (
        P("dp", "seq", "vocab"),
        P("dp", "seq", "vocab"),
        P("dp", "seq"),
        P(),
        P("vocab", None, "dp", None),
    )
    out_specs = P("dp", "seq")
    return jax.shard_map(shards, mesh=mesh, in_specs=in_specs, out_specs=out_specs, check_vma=False)
```

```python
import functools

import jax
import jax.numpy as jnp
from jax import lax
from jax.experimental import pallas as pl
from jax.experimental.pallas import tpu as pltpu
from jax.sharding import PartitionSpec as P

BLK = 128
K = 2
W = 16
ROWS = 104
SIZES = ((24, 21, 21, 21, 20, 20, 20, 20), (10, 23, 23, 23, 23, 22, 22, 22))
STARTS = tuple(tuple(sum(sizes[:f]) for f in range(len(sizes))) for sizes in SIZES)
TINY = 1.2e-38


def halo(block, width):
    count = lax.axis_size("seq")
    forward = [(i, (i + 1) % count) for i in range(count)]
    backward = [(target, source) for source, target in forward]
    low = lax.ppermute(block[:, block.shape[1] - width :], "seq", forward)
    high = lax.ppermute(block[:, :width], "seq", backward)
    return low, high


def ring_pairs(turn):
    seq_count, vocab_count = lax.axis_size("seq"), lax.axis_size("vocab")
    pairs = []
    for s in range(seq_count):
        step = turn if s % 2 == 0 else -turn
        for v in range(vocab_count):
            pairs.append((s * vocab_count + v, s * vocab_count + (v + step) % vocab_count))
    return pairs


def tie_key(block):
    return (block * 5) & 7


def ways(distance, block, share, vocab_count):
    half = vocab_count // 2
    first = tie_key(block) < share
    ahead = jnp.where((distance >= 1) & ((distance < half) | ((distance == half) & first)), distance, 0)
    behind = jnp.where((distance > half) | ((distance == half) & ~first), vocab_count - distance, 0)
    return ahead, behind


def ones(mask):
    return jnp.where(mask, 1.0, 0.0).astype(jnp.bfloat16)


def tie_share(reach, facing, lane, half):
    share = jnp.zeros((reach[0].shape[0], 1), jnp.int32)
    for part in range(1, 9):
        first = tie_key(lane) < part
        more = jnp.where(facing & first, half, reach[0]) - jnp.where(facing & ~first, half, reach[1])
        share = share + (jnp.sum(more, axis=1, keepdims=True) <= 0).astype(jnp.int32)
    return share


def full_reach(reach, facing, lane, share, blocks, half):
    first = tie_key(lane) < share
    ahead = jnp.where(facing & first, half, reach[0])
    behind = jnp.where(facing & ~first, half, reach[1])
    return [jnp.where(lane == blocks, half, ahead), jnp.where(lane == blocks, half - 1, behind)]


def split(listed, blocks, vocab_count):
    holder = sum((listed >= h * blocks).astype(jnp.int32) for h in range(1, vocab_count))
    return holder, listed - holder * blocks


def turn(table):
    rows, columns = table.shape
    table = table.astype(jnp.float32)
    if columns < BLK:
        table = jnp.concatenate([table, jnp.zeros((rows, BLK - columns), jnp.float32)], axis=1)
    if rows < BLK:
        table = jnp.concatenate([table, jnp.zeros((BLK - rows, BLK), jnp.float32)], axis=0)
    return table.T.astype(jnp.int32)


def earlier_lanes():
    square = (BLK, BLK)
    return ones(lax.broadcasted_iota(jnp.int32, square, 0) < lax.broadcasted_iota(jnp.int32, square, 1))


def plan_kernel(blocks, place_ref, listed_ref, after_ref, send_ref, item_ref, fit_ref, book_ref):
    vocab_count, pair_count = listed_ref.shape
    half = vocab_count // 2
    steps = half
    home = blocks + 1
    me, sign = place_ref[0], place_ref[1]
    f32, i32 = jnp.float32, jnp.int32
    shape = (vocab_count, BLK)
    straight = sign > 0

    def of_chain(table, way, f):
        return jnp.where(straight, float(table[way][f]), float(table[1 - way][f]))


    del after_ref
    listed = listed_ref[...]
    row_holder, _ = split(listed, blocks, vocab_count)
    holders, inners = split(turn(listed)[:pair_count], blocks, vocab_count)
    lane = lax.broadcasted_iota(i32, shape, 1)
    row = lax.broadcasted_iota(i32, shape, 0)

    reach = [jnp.zeros(shape, i32), jnp.zeros(shape, i32)]
    across = jnp.zeros(shape, i32)
    pair_lane = lax.broadcasted_iota(i32, (pair_count, BLK), 1)
    pair_row = lax.broadcasted_iota(i32, (vocab_count, pair_count), 0)
    for s in range(vocab_count):
        hits = jnp.dot(
            ones(pair_row == row_holder[s : s + 1, :]),
            ones(pair_lane == inners[:, s : s + 1]),
            preferred_element_type=f32,
        )
        distance = s - row
        distance = jnp.where(distance < 0, distance + vocab_count, distance)
        needed = hits > 0
        reach[0] = jnp.maximum(reach[0], jnp.where(needed & (distance < half), distance, 0))
        reach[1] = jnp.maximum(reach[1], jnp.where(needed & (distance > half), vocab_count - distance, 0))
        across = jnp.maximum(across, jnp.where(needed & (distance == half), 1, 0))
    share = tie_share(reach, across > 0, lane, half)
    reach = full_reach(reach, across > 0, lane, share, blocks, half)

    square = (BLK, BLK)
    up, over = lax.broadcasted_iota(i32, square, 0), lax.broadcasted_iota(i32, square, 1)
    earlier = earlier_lanes()
    left_up, left_over = (up & 7) + 1 - (up >> 3), (over & 7) + 1 - (over >> 3)
    goes_first = ones((left_up > left_over) | ((left_up == left_over) & ((up >> 3) > (over >> 3))))
    index, waiting, moved = [], [], [jnp.zeros(shape, f32)] * 2
    for way in range(2):
        masks = jnp.concatenate([ones(reach[way] == r) for r in range(1, half + 1)], axis=0)
        before = jnp.dot(masks, earlier, preferred_element_type=f32)
        place = jnp.zeros(shape, f32)
        count = jnp.zeros(shape, f32)
        for r in range(1, half + 1):
            same = reach[way] == r
            place = jnp.where(same, before[(r - 1) * vocab_count : r * vocab_count], place)
            total = jnp.sum(jnp.where(same, 1.0, 0.0), axis=1, keepdims=True)
            count = jnp.where(lane == r - 1, total, count)
        index.append(place)
        waiting.append(count)
    travels = (lane >= 8) & (lane < 8 * half) & ((lane & 7) + 1 > (lane >> 3))
    for f in range(steps):
        ahead_of = jnp.dot(
            jnp.concatenate(waiting, axis=0).astype(jnp.bfloat16), goes_first, preferred_element_type=f32
        )
        for way in range(2):
            first = ahead_of[way * vocab_count : (way + 1) * vocab_count]
            size = of_chain(SIZES, way, f)
            go = jnp.clip(size - first, 0.0, waiting[way])
            book_ref[(f * 2 + way) * 3] = moved[way]
            moved[way] = moved[way] + go
            book_ref[(f * 2 + way) * 3 + 1] = moved[way]
            book_ref[(f * 2 + way) * 3 + 2] = jnp.minimum(first, size)
            come = pltpu.roll(pltpu.roll(go, 8, 1), 1 if way == 0 else vocab_count - 1, 0)
            waiting[way] = waiting[way] - go + jnp.where(travels, come, 0.0)
    left = jnp.sum(waiting[0] + waiting[1], axis=1, keepdims=True)
    left = jnp.sum(jnp.broadcast_to(left, shape), axis=0, keepdims=True)
    fit_ref[...] = jnp.broadcast_to(left, fit_ref.shape).astype(i32)

    small = (vocab_count, vocab_count)
    target = lax.broadcasted_iota(i32, (BLK, 2 * BLK), 1).astype(f32)
    pointer, sends = [], []
    for way in range(2):
        step = 1 if way == 0 else -1
        back = me - step * lax.broadcasted_iota(i32, small, 0)
        back = jnp.where(back < 0, back + vocab_count, jnp.where(back >= vocab_count, back - vocab_count, back))
        pick = ones(back == lax.broadcasted_iota(i32, small, 1))
        far = jnp.dot(pick, reach[way].astype(f32).astype(jnp.bfloat16), preferred_element_type=f32).astype(i32)
        order = jnp.dot(pick, index[way].astype(jnp.bfloat16), preferred_element_type=f32)
        giver = me - step
        giver = jnp.where(giver < 0, giver + vocab_count, jnp.where(giver >= vocab_count, giver - vocab_count, giver))

        def slot(at, hops, valid):
            column = jnp.clip(hops * 8 + far - 1, 0, BLK - 1)
            where = jnp.full(shape, -1.0, f32)
            for f in range(steps):
                start, end, first = (
                    jnp.take_along_axis(
                        jnp.broadcast_to(book_ref[(f * 2 + way) * 3 + kind, pl.ds(at, 1), :], shape),
                        column,
                        axis=1,
                        mode="promise_in_bounds",
                    )
                    for kind in range(3)
                )
                now = valid & (start <= order) & (order < end)
                where = jnp.where(now, of_chain(STARTS, way, f) + first + order - start, where)
            return where

        leave = slot(me, row, (far > row) & (row < half))
        arrive = slot(giver, row - 1, (far >= row) & (row >= 1) & (row <= half))
        point = jnp.where(row == 0, lane.astype(f32), jnp.maximum(home + arrive, 0.0))
        pointer.append(point)
        leave_turned = jnp.concatenate([leave, jnp.full((BLK - vocab_count, BLK), -1.0, f32)], axis=0).T
        chosen = jnp.zeros((1, 2 * BLK), f32)
        for h in range(half):
            chosen = chosen + jnp.dot(
                point[h : h + 1].astype(jnp.bfloat16),
                ones(leave_turned[:, h : h + 1] == target),
                preferred_element_type=f32,
            )
        sends.append(chosen.astype(i32))
    send_ref[0:1, :] = jnp.where(straight, sends[0], sends[1])
    send_ref[1:2, :] = jnp.where(straight, sends[1], sends[0])
    send_ref[2:8, :] = jnp.zeros((6, 2 * BLK), i32)

    mine_lane = lax.broadcasted_iota(i32, (pair_count, vocab_count), 1)
    holder = jnp.sum(jnp.where(pair_lane == me, holders, 0), axis=1, keepdims=True)
    inner = jnp.sum(jnp.where(pair_lane == me, inners, 0), axis=1, keepdims=True)
    distance = me - holder
    distance = jnp.where(distance < 0, distance + vocab_count, distance)
    share = turn(jnp.broadcast_to(share, shape))[:1]
    share = jnp.sum(jnp.where(pair_lane == holder, share, 0), axis=1, keepdims=True)
    hops = ways(distance, inner, share, vocab_count)
    scale = jnp.where(distance <= half, distance, 2 * vocab_count - distance)
    points = jnp.zeros((pair_count, 1), f32)
    for way in range(2):
        found = lax.dot_general(
            ones(pair_lane == inner),
            pointer[way].astype(jnp.bfloat16),
            (((1,), (1,)), ((), ())),
            preferred_element_type=f32,
        )
        points = points + jnp.sum(
            jnp.where((mine_lane == hops[way]) & (hops[way] > 0), found, 0.0), axis=1, keepdims=True
        )
    points = jnp.where(distance == 0, inner.astype(f32), points)
    by_stats = [jnp.sum(jnp.where(lane == blocks, p, 0.0), axis=1, keepdims=True) for p in pointer]
    hop = lax.broadcasted_iota(i32, (vocab_count, 1), 0)
    stat_ok = [hop <= half, (hop >= 1) & (hop < half)]
    points = jnp.concatenate(
        [points] + [jnp.where(ok, p, 0.0) for ok, p in zip(stat_ok, by_stats)], axis=0
    ).astype(i32)
    other = jnp.concatenate(
        [(hops[1] > 0).astype(i32), jnp.zeros((vocab_count, 1), i32), jnp.ones((vocab_count, 1), i32)], axis=0
    )
    other = jnp.where(straight, other, 1 - other)
    scale = jnp.concatenate([scale, jnp.zeros((2 * vocab_count, 1), i32)], axis=0)
    frame = jnp.zeros(points.shape, i32)
    base = jnp.full(points.shape, home, i32)
    limit = jnp.where(other == 1, SIZES[1][0], SIZES[0][0])
    for f in range(1, steps):
        reached = points >= home + jnp.where(other == 1, STARTS[1][f], STARTS[0][f])
        frame = frame + reached.astype(i32)
        base = jnp.where(reached, home + jnp.where(other == 1, STARTS[1][f], STARTS[0][f]), base)
        limit = jnp.where(reached, jnp.where(other == 1, SIZES[1][f], SIZES[0][f]), limit)
    away = points >= home
    source = jnp.where(away, 1 + frame + steps * other, 0)
    spot = jnp.where(away, points - base, points)
    spot = jnp.clip(spot, 0, jnp.where(away, limit, home) - 1)
    items = points.shape[0]
    item_lane = lax.broadcasted_iota(i32, (items, BLK), 1)
    table = jnp.where(
        item_lane == 0, spot, jnp.where(item_lane == 1, scale, jnp.where(item_lane == 2, source, 0))
    ).astype(f32)
    turned = jnp.concatenate([table, jnp.zeros((BLK - items, BLK), f32)], axis=0).T
    source_row = turned[2:3].astype(i32)
    item_up = lax.broadcasted_iota(i32, (items, BLK), 0)
    is_item = item_lane < items
    sooner = is_item & ((source_row < source) | ((source_row == source) & (item_lane < item_up)))
    rank = jnp.sum(sooner.astype(i32), axis=1, keepdims=True)
    item_ref[0:1, :] = turned[0:1].astype(i32)
    item_ref[1:2, :] = turned[1:2].astype(i32)
    item_ref[2:3, :] = jnp.sum(jnp.where(rank == item_lane, item_up, 0), axis=0, keepdims=True)
    item_ref[3:4, :] = jnp.sum((source < item_lane).astype(i32), axis=0, keepdims=True)
    item_ref[4:8, :] = jnp.zeros((4, BLK), i32)


def scalars(table_ref, row, start, count):
    values = table_ref[row : row + 1, :]
    return [values[0, start + j] for j in range(count)]


def in_order(place, valid, count):
    square = (BLK, BLK)
    up, over = lax.broadcasted_iota(jnp.int32, square, 0), lax.broadcasted_iota(jnp.int32, square, 1)
    lanes = jnp.sum(jnp.where((place == up) & valid, over, 0), axis=1, keepdims=True)
    row = turn(jnp.broadcast_to(lanes, square))[:1]
    return [row[0, j] for j in range(count)]


def first_choice(blocks, place_ref, listed_ref):
    vocab_count, pair_count = listed_ref.shape
    half = vocab_count // 2
    i32 = jnp.int32
    me, sign = place_ref[0:1, :], place_ref[1:2, :]
    holders, inners = split(turn(listed_ref[...])[:pair_count], blocks, vocab_count)
    pair_lane = lax.broadcasted_iota(i32, (pair_count, BLK), 1)
    lane = lax.broadcasted_iota(i32, (1, BLK), 1)
    reach = [jnp.zeros((1, BLK), i32), jnp.zeros((1, BLK), i32)]
    facing = jnp.zeros((1, BLK), i32)
    for s in range(vocab_count):
        hits = (pair_lane == inners[:, s : s + 1]) & (jnp.broadcast_to(holders[:, s : s + 1], pair_lane.shape) == me)
        seen = jnp.max(jnp.where(hits, 1, 0), axis=0, keepdims=True)
        distance = s - me
        distance = jnp.where(distance < 0, distance + vocab_count, distance)
        reach[0] = jnp.maximum(reach[0], jnp.where(distance < half, distance * seen, 0))
        reach[1] = jnp.maximum(reach[1], jnp.where(distance > half, (vocab_count - distance) * seen, 0))
        facing = jnp.maximum(facing, jnp.where(distance == half, seen, 0))
    share = tie_share(reach, facing > 0, lane, half)
    reach = full_reach(reach, facing > 0, lane, share, blocks, half)
    choices = []
    for sizes, one, other in zip(SIZES, reach, reach[::-1]):
        far = jnp.where(sign > 0, one, other)
        key = jnp.broadcast_to(far * BLK + (BLK - 1 - lane), (BLK, BLK))
        place = jnp.sum((turn(key) > key).astype(i32), axis=0, keepdims=True)
        choices.append(in_order(place, far > 0, sizes[0]))
    return choices


def pack_kernel(
    place_ref,
    listed_ref,
    own_ref,
    low_ref,
    high_ref,
    pick_ref,
    home_ref,
    first_ref,
    second_ref,
    done_ref,
    cand_ref,
    logit_ref,
):
    docs, positions, columns = own_ref.shape
    width = low_ref.shape[1]
    span = positions + 2 * width
    rows = pick_ref.shape[0]
    blocks = columns // BLK
    for doc in range(docs):
        cand_ref[doc * span : doc * span + width, :] = low_ref[doc]
        cand_ref[doc * span + width : doc * span + width + positions, :] = own_ref[doc]
        cand_ref[doc * span + width + positions : (doc + 1) * span, :] = high_ref[doc]
    pick = pick_ref[...]
    peak = jnp.full((rows, BLK), -jnp.inf, jnp.float32)
    for t in range(blocks):
        part = jnp.dot(pick, cand_ref[:, t * BLK : (t + 1) * BLK], preferred_element_type=jnp.float32)
        logit_ref[t] = part.astype(jnp.bfloat16)
        peak = jnp.maximum(peak, part)
    top = jnp.max(peak, axis=1, keepdims=True)
    total = jnp.zeros((rows, BLK), jnp.float32)
    for t in range(blocks):
        power = jnp.exp(logit_ref[t].astype(jnp.float32) - top)
        total = total + power
        home_ref[t] = power.astype(jnp.bfloat16)
    total = jnp.sum(total, axis=1, keepdims=True)
    first = total.astype(jnp.bfloat16).astype(jnp.float32)
    second = (total - first).astype(jnp.bfloat16).astype(jnp.float32)
    third = total - first - second
    lane = lax.broadcasted_iota(jnp.int32, (rows, BLK), 1)
    home_ref[blocks] = jnp.where(
        lane < 32, top, jnp.where(lane < 64, first, jnp.where(lane < 96, second, third))
    ).astype(jnp.bfloat16)
    for out_ref, choice in zip((first_ref, second_ref), first_choice(blocks, place_ref, listed_ref)):
        for j, at in enumerate(choice):
            out_ref[j] = home_ref[at]
    done_ref[...] = jnp.zeros(done_ref.shape, jnp.int32)


def ready_kernel(chain, step, after_ref, send_ref, home_ref, *refs):
    del after_ref
    frames, out_ref = refs[:-1], refs[-1]
    home = home_ref.shape[0]
    for j, at in enumerate(scalars(send_ref, chain, STARTS[chain][step], SIZES[chain][step])):

        def copy(low, high, j=j, at=at):
            if high - low == 1:
                if low == 0:
                    out_ref[j] = home_ref[at]
                elif low <= len(frames):
                    out_ref[j] = frames[low - 1][at - home - STARTS[chain][low - 1]]
                return
            mid = (low + high) // 2
            split = home + STARTS[chain][mid - 1]
            pl.when(at < split)(lambda: copy(low, mid))
            pl.when(at >= split)(lambda: copy(mid, high))

        copy(0, len(frames) + 2)


def pass_kernel(chain, step, home, send_ref, part_ref, newest_ref, out_ref):
    start = home + STARTS[chain][step - 1]
    for j, at in enumerate(scalars(send_ref, chain, STARTS[chain][step], SIZES[chain][step])):
        newest = newest_ref[jnp.maximum(at - start, 0)]
        out_ref[j] = jnp.where(at >= start, newest, part_ref[j])


def stage_kernel(steps, item_ref, *refs):
    sources, stage_ref = refs[:-1], refs[-1]
    for s, source in zip([s for s in range(2 * steps + 1) if s not in (steps, 2 * steps)], sources):
        bring(item_ref, s, source, stage_ref)


def bring(item_ref, s, source_ref, stage_ref):
    def one(q, carry):
        item = item_ref[2, q]
        stage_ref[item] = source_ref[item_ref[0, item]]
        return carry

    lax.fori_loop(item_ref[3, s], item_ref[3, s + 1], one, 0)


def student_kernel(student_ref, top_ref, total_ref):
    docs, positions, columns = student_ref.shape
    rows = docs * positions
    peak = jnp.full((rows, BLK), -jnp.inf, jnp.float32)
    for b in range(columns // BLK):
        part = student_ref[:, :, b * BLK : (b + 1) * BLK].reshape(rows, BLK).astype(jnp.float32)
        peak = jnp.maximum(peak, part)
    top = jnp.max(peak, axis=1, keepdims=True)
    total = jnp.zeros((rows, BLK), jnp.float32)
    for b in range(columns // BLK):
        part = student_ref[:, :, b * BLK : (b + 1) * BLK].reshape(rows, BLK).astype(jnp.float32)
        total = total + jnp.exp(part - top)
    top_ref[...] = jnp.broadcast_to(top, (rows, BLK))
    total_ref[...] = jnp.broadcast_to(jnp.sum(total, axis=1, keepdims=True), (rows, BLK))


def map_kernel(
    steps,
    item_ref,
    held_ref,
    ahead_ref,
    behind_ref,
    spread_ref,
    weight_ref,
    student_ref,
    top_ref,
    total_ref,
    out_ref,
    stage_ref,
    scale_ref,
):
    docs, positions, columns = student_ref.shape
    rows = docs * positions
    blocks = columns // BLK
    spread = spread_ref[...]
    for i in range(stage_ref.shape[0]):
        stage_ref[i] = held_ref[i]
    bring(item_ref, steps, ahead_ref, stage_ref)
    bring(item_ref, 2 * steps, behind_ref, stage_ref)
    holders = [h for h in range(steps + 1)] + [2 * steps + h for h in range(1, steps)]
    lane = lax.broadcasted_iota(jnp.int32, (spread.shape[1], BLK), 1)
    stats = jnp.zeros((spread.shape[1], BLK), jnp.float32)
    for i, h in enumerate(holders):
        stats = jnp.where((lane & 31) == i, stage_ref[K * blocks + h].astype(jnp.float32), stats)
    stats = jnp.dot(spread, stats.astype(jnp.bfloat16), preferred_element_type=jnp.float32)
    held = lax.broadcasted_iota(jnp.int32, (rows, BLK), 1) < len(holders)
    peak = jnp.max(jnp.where(held, stats, -jnp.inf), axis=1, keepdims=True)
    power = jnp.where(held, jnp.exp(jnp.where(held, stats, peak) - peak), 0.0)
    sums = pltpu.roll(stats, 96, 1) + pltpu.roll(stats, 64, 1) + pltpu.roll(stats, 32, 1)
    scale = power / jnp.sum(power * sums, axis=1, keepdims=True)
    for i, h in enumerate(holders):
        scale_ref[h] = jnp.broadcast_to(scale[:, i : i + 1], (rows, BLK))
    student_top = top_ref[...]
    mass = jnp.zeros((rows, BLK), jnp.float32)
    cross = jnp.zeros((rows, BLK), jnp.float32)
    for b in range(blocks):
        picked = jnp.concatenate([stage_ref[K * b], stage_ref[K * b + 1]], axis=1)
        prob = jnp.dot(spread, picked, preferred_element_type=jnp.float32).astype(jnp.bfloat16)
        mapped = scale_ref[item_ref[1, K * b]] * jnp.dot(
            prob[:, :BLK], weight_ref[:, K * b].reshape(BLK, BLK), preferred_element_type=jnp.float32
        ) + scale_ref[item_ref[1, K * b + 1]] * jnp.dot(
            prob[:, BLK:], weight_ref[:, K * b + 1].reshape(BLK, BLK), preferred_element_type=jnp.float32
        )
        logit = student_ref[:, :, b * BLK : (b + 1) * BLK].reshape(rows, BLK).astype(jnp.float32) - student_top
        mass = mass + mapped
        cross = cross + mapped * (jnp.log(jnp.maximum(mapped, TINY)) - logit)
    mass = jnp.sum(mass, axis=1, keepdims=True)
    cross = jnp.sum(cross, axis=1, keepdims=True)
    lane = lax.broadcasted_iota(jnp.int32, (rows, BLK), 1)
    table = jnp.where(
        lane == 0, mass, jnp.where(lane == 1, cross, jnp.where(lane == 2, student_top, total_ref[...]))
    )
    parts = table.T[:4]
    for v in range(out_ref.shape[0]):
        out_ref[v] = parts


def whole(padded_parts, cand, src_block, weights, student_logits):
    doc_count, pos_count, student_cols = student_logits.shape
    teacher_cols = padded_parts[0].shape[2]
    teacher_blocks = teacher_cols // BLK
    student_blocks = student_cols // BLK
    row_count = doc_count * pos_count
    padded = jnp.concatenate(padded_parts, axis=1).reshape(-1, teacher_cols)
    teacher_float = jnp.take(padded, cand, axis=0).astype(jnp.float32)
    student_float = student_logits.reshape(row_count, student_cols).astype(jnp.float32)
    teacher_peak = jnp.max(teacher_float, axis=1)
    student_peak = jnp.max(student_float, axis=1)
    teacher_top, student_top = lax.pmax((teacher_peak, student_peak), "vocab")
    teacher_total, student_total = lax.psum(
        (
            jnp.sum(jnp.exp(teacher_float - teacher_top[:, None]), axis=1),
            jnp.sum(jnp.exp(student_float - student_top[:, None]), axis=1),
        ),
        "vocab",
    )
    teacher_prob = (jnp.exp(teacher_float - teacher_top[:, None]) / teacher_total[:, None]).astype(jnp.bfloat16)
    student_logprob = student_float - student_top[:, None] - jnp.log(student_total)[:, None]
    vocab_count = lax.axis_size("vocab")
    own_index = lax.axis_index("vocab")
    pair_count = student_blocks * K
    capacity = 2 * K * student_blocks // vocab_count
    pair_blocks = src_block.reshape(vocab_count, pair_count)
    holder = pair_blocks // teacher_blocks
    inside = pair_blocks % teacher_blocks
    same_holder = holder[:, :, None] == holder[:, None, :]
    before = jnp.arange(pair_count)[None, :] < jnp.arange(pair_count)[:, None]
    slot_rank = jnp.sum(same_holder & before[None, :, :], axis=2)
    chosen = (holder == own_index)[:, None, :] & (
        slot_rank[:, None, :] == jnp.arange(capacity)[None, :, None]
    )
    send_index = jnp.sum(jnp.where(chosen, inside[:, None, :], 0), axis=2)
    prob_blocks = teacher_prob.reshape(row_count, teacher_blocks, BLK)
    outgoing = jnp.take(prob_blocks, send_index.reshape(-1), axis=1).reshape(row_count, vocab_count, capacity, BLK)
    incoming = lax.all_to_all(outgoing, "vocab", split_axis=1, concat_axis=1, tiled=True)
    own_holder = jnp.take(holder, own_index, axis=0)
    own_rank = jnp.take(slot_rank, own_index, axis=0)
    recv_slot = own_holder * capacity + own_rank
    gathered = jnp.take(incoming.reshape(row_count, vocab_count * capacity, BLK), recv_slot, axis=1).reshape(
        row_count, student_blocks, K, BLK
    )
    weights = weights.swapaxes(0, 1).reshape(student_blocks, K, BLK, BLK)
    mapped = jnp.einsum("rbkc,bkcd->rbd", gathered, weights, preferred_element_type=jnp.float32).reshape(
        row_count, student_cols
    )
    total_mass = lax.psum(jnp.sum(mapped, axis=1), "vocab")
    normed = mapped / total_mass[:, None]
    return lax.psum(
        jnp.sum(jax.scipy.special.xlogy(normed, normed) - normed * student_logprob, axis=1), "vocab"
    )


def shards(teacher_logits, student_logits, alignment, src_block, margin_weight):
    doc_count, pos_count, teacher_cols = teacher_logits.shape
    student_cols = student_logits.shape[2]
    teacher_blocks = teacher_cols // BLK
    student_blocks = student_cols // BLK
    row_count = doc_count * pos_count
    pair_count = student_blocks * K
    vocab_count = lax.axis_size("vocab")
    steps = vocab_count // 2
    home = teacher_blocks + 1
    vocab_index = lax.axis_index("vocab")
    seq_index = lax.axis_index("seq")
    sign = 1 - 2 * (seq_index % 2)
    span = pos_count + 2 * W

    with jax.named_scope("halo"):
        low, high = halo(teacher_logits, W)
    with jax.named_scope("weights"):
        weights = lax.all_gather(
            margin_weight.reshape(pair_count, -1, BLK), "dp", axis=0, tiled=False
        )

    with jax.named_scope("rows"):
        cand = (alignment - seq_index * pos_count + W + jnp.arange(doc_count)[:, None] * span).reshape(-1)
        cand = jnp.clip(cand, 0, doc_count * span - 1)
        places = jnp.arange(doc_count * span)
        used = jnp.any(cand[:, None] == places[None, :], axis=0)
        place_rank = jnp.sum(used[:, None] & (places[:, None] < places[None, :]), axis=0)
        cand_rank = jnp.sum(used[None, :] & (places[None, :] < cand[:, None]), axis=1)
        row_ids = jnp.arange(ROWS)
        pick = ((row_ids[:, None] == place_rank[None, :]) & used[None, :]).astype(jnp.bfloat16)
        spread = (cand_rank[:, None] == row_ids[None, :]).astype(jnp.bfloat16)
        rows_fit = jnp.sum(used.astype(jnp.int32)) <= ROWS

    vmem = pl.BlockSpec(memory_space=pltpu.VMEM)
    smem = pl.BlockSpec(memory_space=pltpu.SMEM)
    anywhere = pl.BlockSpec(memory_space=pl.ANY)
    room = pltpu.CompilerParams(vmem_limit_bytes=20 * 1024 * 1024)

    def planes(count):
        return jax.ShapeDtypeStruct((count, ROWS, BLK), jnp.bfloat16)

    with jax.named_scope("pack"):
        listed = src_block.reshape(vocab_count, pair_count)
        place = jnp.stack([vocab_index, sign]).astype(jnp.int32)
        own, ahead, behind, packed = pl.pallas_call(
            pack_kernel,
            out_shape=(planes(home), planes(SIZES[0][0]), planes(SIZES[1][0]), jax.ShapeDtypeStruct((8, BLK), jnp.int32)),
            in_specs=[vmem] * 6,
            out_specs=(vmem,) * 4,
            scratch_shapes=[
                pltpu.VMEM((doc_count * span, teacher_cols), jnp.bfloat16),
                pltpu.VMEM((teacher_blocks, ROWS, BLK), jnp.bfloat16),
            ],
            compiler_params=room,
        )(jnp.broadcast_to(place[:, None], (2, BLK)), listed, teacher_logits, low, high, pick)

    with jax.named_scope("plan"):
        table = jax.ShapeDtypeStruct((8, BLK), jnp.int32)
        send, items, left = pl.pallas_call(
            functools.partial(plan_kernel, teacher_blocks),
            out_shape=(jax.ShapeDtypeStruct((8, 2 * BLK), jnp.int32), table, table),
            in_specs=[smem, vmem, vmem],
            out_specs=(vmem,) * 3,
            scratch_shapes=[pltpu.VMEM((6 * steps, vocab_count, BLK), jnp.float32)],
            compiler_params=room,
        )(place, listed, packed)

    def ready(chain, step, after, frames):
        return pl.pallas_call(
            functools.partial(ready_kernel, chain, step),
            out_shape=planes(SIZES[chain][step]),
            in_specs=[anywhere] + [vmem] * (2 + len(frames)),
            out_specs=vmem,
            compiler_params=room,
        )(after, send, own, *frames)

    def passed(chain, step, part, newest):
        return pl.pallas_call(
            functools.partial(pass_kernel, chain, step, home),
            out_shape=planes(SIZES[chain][step]),
            in_specs=[vmem] * 3,
            out_specs=vmem,
            compiler_params=room,
        )(send, part, newest)

    with jax.named_scope("ring"):
        forward, backward = ring_pairs(1), ring_pairs(-1)
        came_behind = [lax.ppermute(behind, ("seq", "vocab"), backward)]
        came_ahead = [lax.ppermute(ahead, ("seq", "vocab"), forward)]
        for step in range(1, steps):
            part = ready(1, step, ahead, came_behind[:-1])
            behind = passed(1, step, part, came_behind[-1])
            came_behind.append(lax.ppermute(behind, ("seq", "vocab"), backward))
            part = ready(0, step, behind, came_ahead[:-1])
            ahead = passed(0, step, part, came_ahead[-1])
            came_ahead.append(lax.ppermute(ahead, ("seq", "vocab"), forward))

    with jax.named_scope("student"):
        top, total = pl.pallas_call(
            student_kernel,
            out_shape=(jax.ShapeDtypeStruct((row_count, BLK), jnp.float32),) * 2,
            in_specs=[vmem],
            out_specs=(vmem,) * 2,
            compiler_params=room,
        )(student_logits)

    with jax.named_scope("stage"):
        early = (own, *came_ahead[:-1], *came_behind[:-1])
        held = pl.pallas_call(
            functools.partial(stage_kernel, steps),
            out_shape=planes(pair_count + 2 * vocab_count),
            in_specs=[smem] + [vmem] * len(early),
            out_specs=vmem,
            compiler_params=room,
        )(items, *early)

    with jax.named_scope("map"):
        sums = pl.pallas_call(
            functools.partial(map_kernel, steps),
            out_shape=jax.ShapeDtypeStruct((vocab_count, 4, row_count), jnp.float32),
            in_specs=[smem] + [vmem] * 8,
            out_specs=vmem,
            scratch_shapes=[
                pltpu.VMEM((pair_count + 2 * vocab_count, ROWS, BLK), jnp.bfloat16),
                pltpu.VMEM((3 * steps, row_count, BLK), jnp.float32),
            ],
            compiler_params=room,
        )(items, held, came_ahead[-1], came_behind[-1], spread, weights, student_logits, top, total)

    with jax.named_scope("finish"):
        parts = lax.all_to_all(sums, "vocab", split_axis=0, concat_axis=0, tiled=True)
        mass_part, cross_part, top_part, total_part = (parts[:, i] for i in range(4))
        student_top = jnp.max(top_part, axis=0)
        log_total = student_top + jnp.log(jnp.sum(jnp.exp(top_part - student_top) * total_part, axis=0))
        mass = jnp.sum(mass_part, axis=0)
        result = jnp.sum(cross_part + mass_part * (log_total - top_part), axis=0) / mass - jnp.log(mass)

    result = lax.cond(
        rows_fit & (left[0, 0] == 0),
        lambda *_: result,
        lambda *operands: whole(operands[:3], *operands[3:]),
        low,
        teacher_logits,
        high,
        cand,
        src_block,
        weights,
        student_logits,
    )
    return result.reshape(doc_count, pos_count)


def solution(mesh):
    in_specs = (
        P("dp", "seq", "vocab"),
        P("dp", "seq", "vocab"),
        P("dp", "seq"),
        P(),
        P("vocab", None, "dp", None),
    )
    out_specs = P("dp", "seq")
    return jax.shard_map(shards, mesh=mesh, in_specs=in_specs, out_specs=out_specs, check_vma=False)
```

```python
import functools

import jax
import jax.numpy as jnp
from jax import lax
from jax.experimental import pallas as pl
from jax.experimental.pallas import tpu as pltpu
from jax.sharding import PartitionSpec as P

BLK = 128
K = 2
W = 16
ROWS = 104
SIZES = ((24, 21, 21, 21, 20, 20, 20, 20), (10, 23, 23, 23, 23, 22, 22, 22))
STARTS = tuple(tuple(sum(sizes[:f]) for f in range(len(sizes))) for sizes in SIZES)
TINY = 1.2e-38


def halo(block, width):
    count = lax.axis_size("seq")
    forward = [(i, (i + 1) % count) for i in range(count)]
    backward = [(target, source) for source, target in forward]
    low = lax.ppermute(block[:, block.shape[1] - width :], "seq", forward)
    high = lax.ppermute(block[:, :width], "seq", backward)
    return low, high


def ring_pairs(turn):
    seq_count, vocab_count = lax.axis_size("seq"), lax.axis_size("vocab")
    pairs = []
    for s in range(seq_count):
        step = turn if s % 2 == 0 else -turn
        for v in range(vocab_count):
            pairs.append((s * vocab_count + v, s * vocab_count + (v + step) % vocab_count))
    return pairs


def tie_key(block):
    return (block * 5) & 7


def ways(distance, block, share, vocab_count):
    half = vocab_count // 2
    first = tie_key(block) < share
    ahead = jnp.where((distance >= 1) & ((distance < half) | ((distance == half) & first)), distance, 0)
    behind = jnp.where((distance > half) | ((distance == half) & ~first), vocab_count - distance, 0)
    return ahead, behind


def ones(mask):
    return jnp.where(mask, 1.0, 0.0).astype(jnp.bfloat16)


def tie_share(reach, facing, lane, half):
    share = jnp.zeros((reach[0].shape[0], 1), jnp.int32)
    for part in range(1, 9):
        first = tie_key(lane) < part
        more = jnp.where(facing & first, half, reach[0]) - jnp.where(facing & ~first, half, reach[1])
        share = share + (jnp.sum(more, axis=1, keepdims=True) <= 0).astype(jnp.int32)
    return share


def full_reach(reach, facing, lane, share, blocks, half):
    first = tie_key(lane) < share
    ahead = jnp.where(facing & first, half, reach[0])
    behind = jnp.where(facing & ~first, half, reach[1])
    return [jnp.where(lane == blocks, half, ahead), jnp.where(lane == blocks, half - 1, behind)]


def split(listed, blocks, vocab_count):
    holder = sum((listed >= h * blocks).astype(jnp.int32) for h in range(1, vocab_count))
    return holder, listed - holder * blocks


def turn(table):
    rows, columns = table.shape
    table = table.astype(jnp.float32)
    if columns < BLK:
        table = jnp.concatenate([table, jnp.zeros((rows, BLK - columns), jnp.float32)], axis=1)
    if rows < BLK:
        table = jnp.concatenate([table, jnp.zeros((BLK - rows, BLK), jnp.float32)], axis=0)
    return table.T.astype(jnp.int32)


def earlier_lanes():
    square = (BLK, BLK)
    return ones(lax.broadcasted_iota(jnp.int32, square, 0) < lax.broadcasted_iota(jnp.int32, square, 1))


def plan_kernel(blocks, place_ref, listed_ref, after_ref, send_ref, item_ref, fit_ref, book_ref):
    vocab_count, pair_count = listed_ref.shape
    half = vocab_count // 2
    steps = half
    home = blocks + 1
    me, sign = place_ref[0], place_ref[1]
    f32, i32 = jnp.float32, jnp.int32
    shape = (vocab_count, BLK)
    straight = sign > 0

    def of_chain(table, way, f):
        return jnp.where(straight, float(table[way][f]), float(table[1 - way][f]))


    del after_ref
    listed = listed_ref[...]
    row_holder, _ = split(listed, blocks, vocab_count)
    holders, inners = split(turn(listed)[:pair_count], blocks, vocab_count)
    lane = lax.broadcasted_iota(i32, shape, 1)
    row = lax.broadcasted_iota(i32, shape, 0)

    reach = [jnp.zeros(shape, i32), jnp.zeros(shape, i32)]
    across = jnp.zeros(shape, i32)
    pair_lane = lax.broadcasted_iota(i32, (pair_count, BLK), 1)
    pair_row = lax.broadcasted_iota(i32, (vocab_count, pair_count), 0)
    for s in range(vocab_count):
        hits = jnp.dot(
            ones(pair_row == row_holder[s : s + 1, :]),
            ones(pair_lane == inners[:, s : s + 1]),
            preferred_element_type=f32,
        )
        distance = s - row
        distance = jnp.where(distance < 0, distance + vocab_count, distance)
        needed = hits > 0
        reach[0] = jnp.maximum(reach[0], jnp.where(needed & (distance < half), distance, 0))
        reach[1] = jnp.maximum(reach[1], jnp.where(needed & (distance > half), vocab_count - distance, 0))
        across = jnp.maximum(across, jnp.where(needed & (distance == half), 1, 0))
    share = tie_share(reach, across > 0, lane, half)
    reach = full_reach(reach, across > 0, lane, share, blocks, half)

    square = (BLK, BLK)
    up, over = lax.broadcasted_iota(i32, square, 0), lax.broadcasted_iota(i32, square, 1)
    earlier = earlier_lanes()
    left_up, left_over = (up & 7) + 1 - (up >> 3), (over & 7) + 1 - (over >> 3)
    goes_first = ones((left_up > left_over) | ((left_up == left_over) & ((up >> 3) > (over >> 3))))
    index, waiting, moved = [], [], [jnp.zeros(shape, f32)] * 2
    for way in range(2):
        masks = jnp.concatenate([ones(reach[way] == r) for r in range(1, half + 1)], axis=0)
        before = jnp.dot(masks, earlier, preferred_element_type=f32)
        place = jnp.zeros(shape, f32)
        count = jnp.zeros(shape, f32)
        for r in range(1, half + 1):
            same = reach[way] == r
            place = jnp.where(same, before[(r - 1) * vocab_count : r * vocab_count], place)
            total = jnp.sum(jnp.where(same, 1.0, 0.0), axis=1, keepdims=True)
            count = jnp.where(lane == r - 1, total, count)
        index.append(place)
        waiting.append(count)
    travels = (lane >= 8) & (lane < 8 * half) & ((lane & 7) + 1 > (lane >> 3))
    for f in range(steps):
        ahead_of = jnp.dot(
            jnp.concatenate(waiting, axis=0).astype(jnp.bfloat16), goes_first, preferred_element_type=f32
        )
        for way in range(2):
            first = ahead_of[way * vocab_count : (way + 1) * vocab_count]
            size = of_chain(SIZES, way, f)
            go = jnp.clip(size - first, 0.0, waiting[way])
            book_ref[(f * 2 + way) * 3] = moved[way]
            moved[way] = moved[way] + go
            book_ref[(f * 2 + way) * 3 + 1] = moved[way]
            book_ref[(f * 2 + way) * 3 + 2] = jnp.minimum(first, size)
            come = pltpu.roll(pltpu.roll(go, 8, 1), 1 if way == 0 else vocab_count - 1, 0)
            waiting[way] = waiting[way] - go + jnp.where(travels, come, 0.0)
    left = jnp.sum(waiting[0] + waiting[1], axis=1, keepdims=True)
    left = jnp.sum(jnp.broadcast_to(left, shape), axis=0, keepdims=True)
    fit_ref[...] = jnp.broadcast_to(left, fit_ref.shape).astype(i32)

    small = (vocab_count, vocab_count)
    target = lax.broadcasted_iota(i32, (BLK, 2 * BLK), 1).astype(f32)
    pointer, sends = [], []
    for way in range(2):
        step = 1 if way == 0 else -1
        back = me - step * lax.broadcasted_iota(i32, small, 0)
        back = jnp.where(back < 0, back + vocab_count, jnp.where(back >= vocab_count, back - vocab_count, back))
        pick = ones(back == lax.broadcasted_iota(i32, small, 1))
        far = jnp.dot(pick, reach[way].astype(f32).astype(jnp.bfloat16), preferred_element_type=f32).astype(i32)
        order = jnp.dot(pick, index[way].astype(jnp.bfloat16), preferred_element_type=f32)
        giver = me - step
        giver = jnp.where(giver < 0, giver + vocab_count, jnp.where(giver >= vocab_count, giver - vocab_count, giver))

        def slot(at, hops, valid):
            column = jnp.clip(hops * 8 + far - 1, 0, BLK - 1)
            where = jnp.full(shape, -1.0, f32)
            for f in range(steps):
                start, end, first = (
                    jnp.take_along_axis(
                        jnp.broadcast_to(book_ref[(f * 2 + way) * 3 + kind, pl.ds(at, 1), :], shape),
                        column,
                        axis=1,
                        mode="promise_in_bounds",
                    )
                    for kind in range(3)
                )
                now = valid & (start <= order) & (order < end)
                where = jnp.where(now, of_chain(STARTS, way, f) + first + order - start, where)
            return where

        leave = slot(me, row, (far > row) & (row < half))
        arrive = slot(giver, row - 1, (far >= row) & (row >= 1) & (row <= half))
        point = jnp.where(row == 0, lane.astype(f32), jnp.maximum(home + arrive, 0.0))
        pointer.append(point)
        leave_turned = jnp.concatenate([leave, jnp.full((BLK - vocab_count, BLK), -1.0, f32)], axis=0).T
        chosen = jnp.zeros((1, 2 * BLK), f32)
        for h in range(half):
            chosen = chosen + jnp.dot(
                point[h : h + 1].astype(jnp.bfloat16),
                ones(leave_turned[:, h : h + 1] == target),
                preferred_element_type=f32,
            )
        sends.append(chosen.astype(i32))
    send_ref[0:1, :] = jnp.where(straight, sends[0], sends[1])
    send_ref[1:2, :] = jnp.where(straight, sends[1], sends[0])
    send_ref[2:8, :] = jnp.zeros((6, 2 * BLK), i32)

    mine_lane = lax.broadcasted_iota(i32, (pair_count, vocab_count), 1)
    holder = jnp.sum(jnp.where(pair_lane == me, holders, 0), axis=1, keepdims=True)
    inner = jnp.sum(jnp.where(pair_lane == me, inners, 0), axis=1, keepdims=True)
    distance = me - holder
    distance = jnp.where(distance < 0, distance + vocab_count, distance)
    share = turn(jnp.broadcast_to(share, shape))[:1]
    share = jnp.sum(jnp.where(pair_lane == holder, share, 0), axis=1, keepdims=True)
    hops = ways(distance, inner, share, vocab_count)
    points = jnp.zeros((pair_count, 1), f32)
    for way in range(2):
        found = lax.dot_general(
            ones(pair_lane == inner),
            pointer[way].astype(jnp.bfloat16),
            (((1,), (1,)), ((), ())),
            preferred_element_type=f32,
        )
        points = points + jnp.sum(
            jnp.where((mine_lane == hops[way]) & (hops[way] > 0), found, 0.0), axis=1, keepdims=True
        )
    points = jnp.where(distance == 0, inner.astype(f32), points)
    by_stats = [jnp.sum(jnp.where(lane == blocks, p, 0.0), axis=1, keepdims=True) for p in pointer]
    hop = lax.broadcasted_iota(i32, (vocab_count, 1), 0)
    mirror = ones(lax.broadcasted_iota(i32, small, 0) + lax.broadcasted_iota(i32, small, 1) == vocab_count)
    mirrored = jnp.dot(
        mirror, jnp.broadcast_to(by_stats[1], shape).astype(jnp.bfloat16), preferred_element_type=f32
    )[:, :1]
    points = jnp.concatenate([points, jnp.where(hop <= half, by_stats[0], mirrored)], axis=0).astype(i32)
    other = jnp.concatenate([(hops[1] > 0).astype(i32), (hop > half).astype(i32)], axis=0)
    other = jnp.where(straight, other, 1 - other)
    scale = jnp.concatenate([distance, jnp.zeros((vocab_count, 1), i32)], axis=0)
    frame = jnp.zeros(points.shape, i32)
    base = jnp.full(points.shape, home, i32)
    limit = jnp.where(other == 1, SIZES[1][0], SIZES[0][0])
    for f in range(1, steps):
        reached = points >= home + jnp.where(other == 1, STARTS[1][f], STARTS[0][f])
        frame = frame + reached.astype(i32)
        base = jnp.where(reached, home + jnp.where(other == 1, STARTS[1][f], STARTS[0][f]), base)
        limit = jnp.where(reached, jnp.where(other == 1, SIZES[1][f], SIZES[0][f]), limit)
    away = points >= home
    source = jnp.where(away, 1 + frame + steps * other, 0)
    spot = jnp.where(away, points - base, points)
    spot = jnp.clip(spot, 0, jnp.where(away, limit, home) - 1)
    items = points.shape[0]
    item_lane = lax.broadcasted_iota(i32, (items, BLK), 1)
    table = jnp.where(
        item_lane == 0, spot, jnp.where(item_lane == 1, scale, jnp.where(item_lane == 2, source, 0))
    ).astype(f32)
    turned = jnp.concatenate([table, jnp.zeros((BLK - items, BLK), f32)], axis=0).T
    source_row = turned[2:3].astype(i32)
    item_up = lax.broadcasted_iota(i32, (items, BLK), 0)
    is_item = item_lane < items
    sooner = is_item & ((source_row < source) | ((source_row == source) & (item_lane < item_up)))
    rank = jnp.sum(sooner.astype(i32), axis=1, keepdims=True)
    item_ref[0:1, :] = turned[0:1].astype(i32)
    item_ref[1:2, :] = turned[1:2].astype(i32)
    item_ref[2:3, :] = jnp.sum(jnp.where(rank == item_lane, item_up, 0), axis=0, keepdims=True)
    item_ref[3:4, :] = jnp.sum((source < item_lane).astype(i32), axis=0, keepdims=True)
    item_ref[4:8, :] = jnp.zeros((4, BLK), i32)


def scalars(table_ref, row, start, count):
    values = table_ref[row : row + 1, :]
    return [values[0, start + j] for j in range(count)]


def in_order(place, valid, count):
    square = (BLK, BLK)
    up, over = lax.broadcasted_iota(jnp.int32, square, 0), lax.broadcasted_iota(jnp.int32, square, 1)
    lanes = jnp.sum(jnp.where((place == up) & valid, over, 0), axis=1, keepdims=True)
    row = turn(jnp.broadcast_to(lanes, square))[:1]
    return [row[0, j] for j in range(count)]


def first_choice(blocks, place_ref, listed_ref):
    vocab_count, pair_count = listed_ref.shape
    half = vocab_count // 2
    i32 = jnp.int32
    me, sign = place_ref[0:1, :], place_ref[1:2, :]
    holders, inners = split(turn(listed_ref[...])[:pair_count], blocks, vocab_count)
    pair_lane = lax.broadcasted_iota(i32, (pair_count, BLK), 1)
    lane = lax.broadcasted_iota(i32, (1, BLK), 1)
    reach = [jnp.zeros((1, BLK), i32), jnp.zeros((1, BLK), i32)]
    facing = jnp.zeros((1, BLK), i32)
    for s in range(vocab_count):
        hits = (pair_lane == inners[:, s : s + 1]) & (jnp.broadcast_to(holders[:, s : s + 1], pair_lane.shape) == me)
        seen = jnp.max(jnp.where(hits, 1, 0), axis=0, keepdims=True)
        distance = s - me
        distance = jnp.where(distance < 0, distance + vocab_count, distance)
        reach[0] = jnp.maximum(reach[0], jnp.where(distance < half, distance * seen, 0))
        reach[1] = jnp.maximum(reach[1], jnp.where(distance > half, (vocab_count - distance) * seen, 0))
        facing = jnp.maximum(facing, jnp.where(distance == half, seen, 0))
    share = tie_share(reach, facing > 0, lane, half)
    reach = full_reach(reach, facing > 0, lane, share, blocks, half)
    choices = []
    for sizes, one, other in zip(SIZES, reach, reach[::-1]):
        far = jnp.where(sign > 0, one, other)
        key = jnp.broadcast_to(far * BLK + (BLK - 1 - lane), (BLK, BLK))
        place = jnp.sum((turn(key) > key).astype(i32), axis=0, keepdims=True)
        choices.append(in_order(place, far > 0, sizes[0]))
    return choices


def pack_kernel(
    place_ref,
    listed_ref,
    own_ref,
    low_ref,
    high_ref,
    pick_ref,
    home_ref,
    first_ref,
    second_ref,
    done_ref,
    cand_ref,
    logit_ref,
):
    docs, positions, columns = own_ref.shape
    width = low_ref.shape[1]
    span = positions + 2 * width
    rows = pick_ref.shape[0]
    blocks = columns // BLK
    for doc in range(docs):
        cand_ref[doc * span : doc * span + width, :] = low_ref[doc]
        cand_ref[doc * span + width : doc * span + width + positions, :] = own_ref[doc]
        cand_ref[doc * span + width + positions : (doc + 1) * span, :] = high_ref[doc]
    pick = pick_ref[...]
    peak = jnp.full((rows, BLK), -jnp.inf, jnp.float32)
    for t in range(blocks):
        part = jnp.dot(pick, cand_ref[:, t * BLK : (t + 1) * BLK], preferred_element_type=jnp.float32)
        logit_ref[t] = part.astype(jnp.bfloat16)
        peak = jnp.maximum(peak, part)
    top = jnp.max(peak, axis=1, keepdims=True)
    total = jnp.zeros((rows, BLK), jnp.float32)
    for t in range(blocks):
        power = jnp.exp(logit_ref[t].astype(jnp.float32) - top)
        total = total + power
        home_ref[t] = power.astype(jnp.bfloat16)
    total = jnp.sum(total, axis=1, keepdims=True)
    first = total.astype(jnp.bfloat16).astype(jnp.float32)
    second = (total - first).astype(jnp.bfloat16).astype(jnp.float32)
    third = total - first - second
    lane = lax.broadcasted_iota(jnp.int32, (rows, BLK), 1)
    home_ref[blocks] = jnp.where(
        lane < 32, top, jnp.where(lane < 64, first, jnp.where(lane < 96, second, third))
    ).astype(jnp.bfloat16)
    for out_ref, choice in zip((first_ref, second_ref), first_choice(blocks, place_ref, listed_ref)):
        for j, at in enumerate(choice):
            out_ref[j] = home_ref[at]
    done_ref[...] = jnp.zeros(done_ref.shape, jnp.int32)


def ready_kernel(chain, step, after_ref, send_ref, home_ref, *refs):
    del after_ref
    frames, out_ref = refs[:-1], refs[-1]
    home = home_ref.shape[0]
    for j, at in enumerate(scalars(send_ref, chain, STARTS[chain][step], SIZES[chain][step])):

        def copy(low, high, j=j, at=at):
            if high - low == 1:
                if low == 0:
                    out_ref[j] = home_ref[at]
                elif low <= len(frames):
                    out_ref[j] = frames[low - 1][at - home - STARTS[chain][low - 1]]
                return
            mid = (low + high) // 2
            split = home + STARTS[chain][mid - 1]
            pl.when(at < split)(lambda: copy(low, mid))
            pl.when(at >= split)(lambda: copy(mid, high))

        copy(0, len(frames) + 2)


def pass_kernel(chain, step, home, send_ref, part_ref, newest_ref, out_ref):
    start = home + STARTS[chain][step - 1]
    for j, at in enumerate(scalars(send_ref, chain, STARTS[chain][step], SIZES[chain][step])):
        newest = newest_ref[jnp.maximum(at - start, 0)]
        out_ref[j] = jnp.where(at >= start, newest, part_ref[j])


def stage_kernel(steps, item_ref, *refs):
    sources, stage_ref = refs[:-1], refs[-1]
    for s, source in zip([s for s in range(2 * steps + 1) if s not in (steps, 2 * steps)], sources):
        bring(item_ref, s, source, stage_ref)


def bring(item_ref, s, source_ref, stage_ref):
    def one(q, carry):
        item = item_ref[2, q]
        stage_ref[item] = source_ref[item_ref[0, item]]
        return carry

    lax.fori_loop(item_ref[3, s], item_ref[3, s + 1], one, 0)


def student_kernel(student_ref, top_ref, total_ref):
    docs, positions, columns = student_ref.shape
    rows = docs * positions
    peak = jnp.full((rows, BLK), -jnp.inf, jnp.float32)
    for b in range(columns // BLK):
        part = student_ref[:, :, b * BLK : (b + 1) * BLK].reshape(rows, BLK).astype(jnp.float32)
        peak = jnp.maximum(peak, part)
    top = jnp.max(peak, axis=1, keepdims=True)
    total = jnp.zeros((rows, BLK), jnp.float32)
    for b in range(columns // BLK):
        part = student_ref[:, :, b * BLK : (b + 1) * BLK].reshape(rows, BLK).astype(jnp.float32)
        total = total + jnp.exp(part - top)
    top_ref[...] = jnp.broadcast_to(top, (rows, BLK))
    total_ref[...] = jnp.broadcast_to(jnp.sum(total, axis=1, keepdims=True), (rows, BLK))


def map_kernel(
    steps,
    item_ref,
    held_ref,
    ahead_ref,
    behind_ref,
    spread_ref,
    weight_ref,
    student_ref,
    top_ref,
    total_ref,
    out_ref,
    stage_ref,
    scale_ref,
):
    docs, positions, columns = student_ref.shape
    rows = docs * positions
    blocks = columns // BLK
    spread = spread_ref[...]
    for i in range(stage_ref.shape[0]):
        stage_ref[i] = held_ref[i]
    bring(item_ref, steps, ahead_ref, stage_ref)
    bring(item_ref, 2 * steps, behind_ref, stage_ref)
    holders = range(2 * steps)
    lane = lax.broadcasted_iota(jnp.int32, (spread.shape[1], BLK), 1)
    stats = jnp.zeros((spread.shape[1], BLK), jnp.float32)
    for i, h in enumerate(holders):
        stats = jnp.where((lane & 31) == i, stage_ref[K * blocks + h].astype(jnp.float32), stats)
    stats = jnp.dot(spread, stats.astype(jnp.bfloat16), preferred_element_type=jnp.float32)
    held = lax.broadcasted_iota(jnp.int32, (rows, BLK), 1) < len(holders)
    peak = jnp.max(jnp.where(held, stats, -jnp.inf), axis=1, keepdims=True)
    power = jnp.where(held, jnp.exp(jnp.where(held, stats, peak) - peak), 0.0)
    sums = pltpu.roll(stats, 96, 1) + pltpu.roll(stats, 64, 1) + pltpu.roll(stats, 32, 1)
    scale = power / jnp.sum(power * sums, axis=1, keepdims=True)
    for i, h in enumerate(holders):
        scale_ref[h] = jnp.broadcast_to(scale[:, i : i + 1], (rows, BLK))
    student_top = top_ref[...]
    mass = jnp.zeros((rows, BLK), jnp.float32)
    cross = jnp.zeros((rows, BLK), jnp.float32)
    for b in range(blocks):
        picked = jnp.concatenate([stage_ref[K * b], stage_ref[K * b + 1]], axis=1)
        prob = jnp.dot(spread, picked, preferred_element_type=jnp.float32).astype(jnp.bfloat16)
        mapped = scale_ref[item_ref[1, K * b]] * jnp.dot(
            prob[:, :BLK], weight_ref[:, K * b].reshape(BLK, BLK), preferred_element_type=jnp.float32
        ) + scale_ref[item_ref[1, K * b + 1]] * jnp.dot(
            prob[:, BLK:], weight_ref[:, K * b + 1].reshape(BLK, BLK), preferred_element_type=jnp.float32
        )
        logit = student_ref[:, :, b * BLK : (b + 1) * BLK].reshape(rows, BLK).astype(jnp.float32) - student_top
        mass = mass + mapped
        cross = cross + mapped * (jnp.log(jnp.maximum(mapped, TINY)) - logit)
    mass = jnp.sum(mass, axis=1, keepdims=True)
    cross = jnp.sum(cross, axis=1, keepdims=True)
    lane = lax.broadcasted_iota(jnp.int32, (rows, BLK), 1)
    table = jnp.where(
        lane == 0, mass, jnp.where(lane == 1, cross, jnp.where(lane == 2, student_top, total_ref[...]))
    )
    parts = table.T[:4]
    for v in range(out_ref.shape[0]):
        out_ref[v] = parts


def whole(padded_parts, cand, src_block, weights, student_logits):
    doc_count, pos_count, student_cols = student_logits.shape
    teacher_cols = padded_parts[0].shape[2]
    teacher_blocks = teacher_cols // BLK
    student_blocks = student_cols // BLK
    row_count = doc_count * pos_count
    padded = jnp.concatenate(padded_parts, axis=1).reshape(-1, teacher_cols)
    teacher_float = jnp.take(padded, cand, axis=0).astype(jnp.float32)
    student_float = student_logits.reshape(row_count, student_cols).astype(jnp.float32)
    teacher_peak = jnp.max(teacher_float, axis=1)
    student_peak = jnp.max(student_float, axis=1)
    teacher_top, student_top = lax.pmax((teacher_peak, student_peak), "vocab")
    teacher_total, student_total = lax.psum(
        (
            jnp.sum(jnp.exp(teacher_float - teacher_top[:, None]), axis=1),
            jnp.sum(jnp.exp(student_float - student_top[:, None]), axis=1),
        ),
        "vocab",
    )
    teacher_prob = (jnp.exp(teacher_float - teacher_top[:, None]) / teacher_total[:, None]).astype(jnp.bfloat16)
    student_logprob = student_float - student_top[:, None] - jnp.log(student_total)[:, None]
    vocab_count = lax.axis_size("vocab")
    own_index = lax.axis_index("vocab")
    pair_count = student_blocks * K
    capacity = 2 * K * student_blocks // vocab_count
    pair_blocks = src_block.reshape(vocab_count, pair_count)
    holder = pair_blocks // teacher_blocks
    inside = pair_blocks % teacher_blocks
    same_holder = holder[:, :, None] == holder[:, None, :]
    before = jnp.arange(pair_count)[None, :] < jnp.arange(pair_count)[:, None]
    slot_rank = jnp.sum(same_holder & before[None, :, :], axis=2)
    chosen = (holder == own_index)[:, None, :] & (
        slot_rank[:, None, :] == jnp.arange(capacity)[None, :, None]
    )
    send_index = jnp.sum(jnp.where(chosen, inside[:, None, :], 0), axis=2)
    prob_blocks = teacher_prob.reshape(row_count, teacher_blocks, BLK)
    outgoing = jnp.take(prob_blocks, send_index.reshape(-1), axis=1).reshape(row_count, vocab_count, capacity, BLK)
    incoming = lax.all_to_all(outgoing, "vocab", split_axis=1, concat_axis=1, tiled=True)
    own_holder = jnp.take(holder, own_index, axis=0)
    own_rank = jnp.take(slot_rank, own_index, axis=0)
    recv_slot = own_holder * capacity + own_rank
    gathered = jnp.take(incoming.reshape(row_count, vocab_count * capacity, BLK), recv_slot, axis=1).reshape(
        row_count, student_blocks, K, BLK
    )
    weights = weights.swapaxes(0, 1).reshape(student_blocks, K, BLK, BLK)
    mapped = jnp.einsum("rbkc,bkcd->rbd", gathered, weights, preferred_element_type=jnp.float32).reshape(
        row_count, student_cols
    )
    total_mass = lax.psum(jnp.sum(mapped, axis=1), "vocab")
    normed = mapped / total_mass[:, None]
    return lax.psum(
        jnp.sum(jax.scipy.special.xlogy(normed, normed) - normed * student_logprob, axis=1), "vocab"
    )


def shards(teacher_logits, student_logits, alignment, src_block, margin_weight):
    doc_count, pos_count, teacher_cols = teacher_logits.shape
    student_cols = student_logits.shape[2]
    teacher_blocks = teacher_cols // BLK
    student_blocks = student_cols // BLK
    row_count = doc_count * pos_count
    pair_count = student_blocks * K
    vocab_count = lax.axis_size("vocab")
    steps = vocab_count // 2
    home = teacher_blocks + 1
    vocab_index = lax.axis_index("vocab")
    seq_index = lax.axis_index("seq")
    sign = 1 - 2 * (seq_index % 2)
    span = pos_count + 2 * W

    with jax.named_scope("halo"):
        low, high = halo(teacher_logits, W)
    with jax.named_scope("weights"):
        weights = lax.all_gather(
            margin_weight.reshape(pair_count, -1, BLK), "dp", axis=0, tiled=False
        )

    with jax.named_scope("rows"):
        cand = (alignment - seq_index * pos_count + W + jnp.arange(doc_count)[:, None] * span).reshape(-1)
        cand = jnp.clip(cand, 0, doc_count * span - 1)
        places = jnp.arange(doc_count * span)
        used = jnp.any(cand[:, None] == places[None, :], axis=0)
        place_rank = jnp.sum(used[:, None] & (places[:, None] < places[None, :]), axis=0)
        cand_rank = jnp.sum(used[None, :] & (places[None, :] < cand[:, None]), axis=1)
        row_ids = jnp.arange(ROWS)
        pick = ((row_ids[:, None] == place_rank[None, :]) & used[None, :]).astype(jnp.bfloat16)
        spread = (cand_rank[:, None] == row_ids[None, :]).astype(jnp.bfloat16)
        rows_fit = jnp.sum(used.astype(jnp.int32)) <= ROWS

    vmem = pl.BlockSpec(memory_space=pltpu.VMEM)
    smem = pl.BlockSpec(memory_space=pltpu.SMEM)
    anywhere = pl.BlockSpec(memory_space=pl.ANY)
    room = pltpu.CompilerParams(vmem_limit_bytes=20 * 1024 * 1024)

    def planes(count):
        return jax.ShapeDtypeStruct((count, ROWS, BLK), jnp.bfloat16)

    with jax.named_scope("pack"):
        listed = src_block.reshape(vocab_count, pair_count)
        place = jnp.stack([vocab_index, sign]).astype(jnp.int32)
        own, ahead, behind, packed = pl.pallas_call(
            pack_kernel,
            out_shape=(planes(home), planes(SIZES[0][0]), planes(SIZES[1][0]), jax.ShapeDtypeStruct((8, BLK), jnp.int32)),
            in_specs=[vmem] * 6,
            out_specs=(vmem,) * 4,
            scratch_shapes=[
                pltpu.VMEM((doc_count * span, teacher_cols), jnp.bfloat16),
                pltpu.VMEM((teacher_blocks, ROWS, BLK), jnp.bfloat16),
            ],
            compiler_params=room,
        )(jnp.broadcast_to(place[:, None], (2, BLK)), listed, teacher_logits, low, high, pick)

    with jax.named_scope("plan"):
        table = jax.ShapeDtypeStruct((8, BLK), jnp.int32)
        send, items, left = pl.pallas_call(
            functools.partial(plan_kernel, teacher_blocks),
            out_shape=(jax.ShapeDtypeStruct((8, 2 * BLK), jnp.int32), table, table),
            in_specs=[smem, vmem, vmem],
            out_specs=(vmem,) * 3,
            scratch_shapes=[pltpu.VMEM((6 * steps, vocab_count, BLK), jnp.float32)],
            compiler_params=room,
        )(place, listed, packed)

    def ready(chain, step, after, frames):
        return pl.pallas_call(
            functools.partial(ready_kernel, chain, step),
            out_shape=planes(SIZES[chain][step]),
            in_specs=[anywhere] + [vmem] * (2 + len(frames)),
            out_specs=vmem,
            compiler_params=room,
        )(after, send, own, *frames)

    def passed(chain, step, part, newest):
        return pl.pallas_call(
            functools.partial(pass_kernel, chain, step, home),
            out_shape=planes(SIZES[chain][step]),
            in_specs=[vmem] * 3,
            out_specs=vmem,
            compiler_params=room,
        )(send, part, newest)

    with jax.named_scope("ring"):
        forward, backward = ring_pairs(1), ring_pairs(-1)
        came_behind = [lax.ppermute(behind, ("seq", "vocab"), backward)]
        came_ahead = [lax.ppermute(ahead, ("seq", "vocab"), forward)]
        for step in range(1, steps):
            part = ready(1, step, ahead, came_behind[:-1])
            behind = passed(1, step, part, came_behind[-1])
            came_behind.append(lax.ppermute(behind, ("seq", "vocab"), backward))
            part = ready(0, step, behind, came_ahead[:-1])
            ahead = passed(0, step, part, came_ahead[-1])
            came_ahead.append(lax.ppermute(ahead, ("seq", "vocab"), forward))

    with jax.named_scope("student"):
        top, total = pl.pallas_call(
            student_kernel,
            out_shape=(jax.ShapeDtypeStruct((row_count, BLK), jnp.float32),) * 2,
            in_specs=[vmem],
            out_specs=(vmem,) * 2,
            compiler_params=room,
        )(student_logits)

    with jax.named_scope("stage"):
        early = (own, *came_ahead[:-1], *came_behind[:-1])
        held = pl.pallas_call(
            functools.partial(stage_kernel, steps),
            out_shape=planes(pair_count + vocab_count),
            in_specs=[smem] + [vmem] * len(early),
            out_specs=vmem,
            compiler_params=room,
        )(items, *early)

    with jax.named_scope("map"):
        sums = pl.pallas_call(
            functools.partial(map_kernel, steps),
            out_shape=jax.ShapeDtypeStruct((vocab_count, 4, row_count), jnp.float32),
            in_specs=[smem] + [vmem] * 8,
            out_specs=vmem,
            scratch_shapes=[
                pltpu.VMEM((pair_count + vocab_count, ROWS, BLK), jnp.bfloat16),
                pltpu.VMEM((vocab_count, row_count, BLK), jnp.float32),
            ],
            compiler_params=room,
        )(items, held, came_ahead[-1], came_behind[-1], spread, weights, student_logits, top, total)

    with jax.named_scope("finish"):
        parts = lax.all_to_all(sums, "vocab", split_axis=0, concat_axis=0, tiled=True)
        mass_part, cross_part, top_part, total_part = (parts[:, i] for i in range(4))
        student_top = jnp.max(top_part, axis=0)
        log_total = student_top + jnp.log(jnp.sum(jnp.exp(top_part - student_top) * total_part, axis=0))
        mass = jnp.sum(mass_part, axis=0)
        result = jnp.sum(cross_part + mass_part * (log_total - top_part), axis=0) / mass - jnp.log(mass)

    result = lax.cond(
        rows_fit & (left[0, 0] == 0),
        lambda *_: result,
        lambda *operands: whole(operands[:3], *operands[3:]),
        low,
        teacher_logits,
        high,
        cand,
        src_block,
        weights,
        student_logits,
    )
    return result.reshape(doc_count, pos_count)


def solution(mesh):
    in_specs = (
        P("dp", "seq", "vocab"),
        P("dp", "seq", "vocab"),
        P("dp", "seq"),
        P(),
        P("vocab", None, "dp", None),
    )
    out_specs = P("dp", "seq")
    return jax.shard_map(shards, mesh=mesh, in_specs=in_specs, out_specs=out_specs, check_vma=False)
```
